32 devices in a mesh: groups: 2 (over x), shard: 16 (over z, y, core).
Axes of the slice: x: 2, y: 2, z: 4, core: 2. Of those that a mesh axis runs over, the one named last changes fastest.
Arguments:
- query_hidden: bfloat16 [128, 32, 768], P(('groups', 'shard')), parts along dimension 0, may hold values from -6 to 6
- query_lengths: int32 [128], P(('groups', 'shard')), parts along dimension 0, may hold values from 8 to 32
- inner_weight: bfloat16 [768, 3072], replicated, may hold values from -0.21875 to 0.21875
- outer_weight: bfloat16 [3072, 768], replicated, may hold values from -0.109375 to 0.109375
- norm_gain: float32 [768], replicated, may hold values from 0.1 to 1.9
- embed_weight: bfloat16 [768, 128], replicated, may hold values from -0.21875 to 0.21875
- passage_vectors: bfloat16 [1536, 128, 128], P(('groups', 'shard')), parts along dimension 0, may hold values from -0.52734375 to 0.52734375
- passage_lengths: int32 [1536], P(('groups', 'shard')), parts along dimension 0, may hold values from 16 to 128
- passage_row: int32 [1536], P('groups'), parts along dimension 0, may hold values from 0 to 767, as said below
- candidates: int32 [128, 64], P(('groups', 'shard')), parts along dimension 0, may hold values from 0 to 767, as said below
Outputs:
- scores: float32 [128, 64], P(('groups', 'shard')), parts along dimension 0
- best_scores: float32 [128, 10], P(('groups', 'shard')), parts along dimension 0
The draws below stay inside these ranges and needn't reach their ends.
There are 2 independent parts, one for each index of `groups`. The reference program is written for one: setup_inputs(seed, part) draws one part's arguments, and reference() takes and returns one part's arrays. A program takes and returns all parts, laid end to end along the dimension named above; an argument that names none is the same for every part. Nothing has to cross between parts.
Inputs may be any that keep to these rules, and one draw needn't show every extreme that they name: A permutation: passage p is stored at row passage_row[p] of passage_vectors and passage_lengths, which lies on shard index passage_row[p] // 48. All candidate entries of the queries of one shard (aligned blocks of 4 queries) name distinct passages; queries of different shards may share candidates. Among the candidate entries of one shard's queries, at most 24 are stored on any one shard, and in every draw one shard stores exactly 24 entries of every shard's queries.
All inputs are finite; a program needn't handle non-finite values.
Results may differ from the reference program's by a relative error of at most 0.00046.
Values may be sent and summed in bfloat16 or wider, within the bound.
No kernel may reach another device: no remote copies, remote signals or barrier semaphores. Data moves between devices by JAX's collectives and lax.ppermute only.
A program may use at most 128 MiB of HBM per device.

```python
import jax
import jax.numpy as jnp
from jax import lax

D = 768
FF = 3072
EMBED = 128
QLEN = 32
PLEN = 128
CANDS = 64
TOPN = 10
Q_DEV = 4
P_DEV = 48
QUERIES = 64
PASSAGES = 768
CAP = 24


def candidate_layout(key):
    shard_count = PASSAGES // P_DEV
    per_device = Q_DEV * CANDS
    ordering = jax.random.permutation(jax.random.fold_in(key, 11), PASSAGES).astype(jnp.int32)
    hot_owner = jax.random.randint(jax.random.fold_in(key, 12), (), 0, shard_count).astype(jnp.int32)

    def per_source(source):
        source_key = jax.random.fold_in(jax.random.fold_in(key, 13), source)
        owner_pool = jnp.arange((shard_count - 1) * CAP, dtype=jnp.int32) // CAP
        owner_pool = owner_pool + (owner_pool >= hot_owner).astype(jnp.int32)
        picked = jax.random.permutation(jax.random.fold_in(source_key, 1), owner_pool)[:per_device - CAP]
        owners = jnp.concatenate([jnp.full((CAP,), hot_owner, jnp.int32), picked])
        owners = jax.random.permutation(jax.random.fold_in(source_key, 2), owners)
        onehot = (owners[:, None] == jnp.arange(shard_count, dtype=jnp.int32)[None, :]).astype(jnp.int32)
        ranking = jnp.sum((jnp.cumsum(onehot, axis=0) - onehot) * onehot, axis=1)
        row_keys = jax.random.split(jax.random.fold_in(source_key, 3), shard_count)
        row_orders = jax.vmap(lambda one_key: jax.random.permutation(one_key, P_DEV).astype(jnp.int32))(row_keys)
        local_row = row_orders[owners, ranking]
        return owners * P_DEV + local_row
    slab_rows = jax.vmap(per_source)(jnp.arange(shard_count, dtype=jnp.int32))
    return (ordering, slab_rows.reshape(QUERIES, CANDS))


def draw_passage_row(key, part):
    return candidate_layout(key)[0]


def draw_candidates(key, part):
    layout = candidate_layout(key)
    inverse = jnp.zeros((PASSAGES,), jnp.int32).at[layout[0]].set(jnp.arange(PASSAGES, dtype=jnp.int32))
    return inverse[layout[1]]


def with_ends(result, key, low, largest):
    place = [jax.random.randint(jax.random.fold_in(key, axis), (), 0, length) for axis, length in enumerate(result.shape)]
    longest = result.shape.index(max(result.shape))
    beside = place[:longest] + [(place[longest] + 1) % result.shape[longest]] + place[longest + 1:]
    return result.at[tuple(place)].set(low).at[tuple(beside)].set(largest)


def level_of(rng, extent, cuts, low, high):
    gain, own = 1.0, jax.random.fold_in(rng, 6)
    for dim, parts in cuts:
        heights = jnp.exp(jax.random.uniform(jax.random.fold_in(own, dim), (parts,), jnp.float32, low / len(cuts), high / len(cuts)))
        gain = gain * jnp.repeat(heights, extent[dim] // parts).reshape([-1 if axis == dim else 1 for axis in range(len(extent))])
    return gain


def noise(rng, dims, width, bound, pieces=(), kind=jnp.bfloat16):
    gain = level_of(rng, dims, pieces, -0.22, 0.18) if pieces else 1.0
    entries = jax.random.normal(rng, dims, jnp.float32) * width * gain
    return jnp.minimum(jnp.maximum(entries, -bound), bound).astype(kind)


def setup_inputs(seed: int = 0, part: int = 0) -> dict:
    seeds = jax.random.split(jax.random.key(seed), 11)
    part_keys = jax.random.split(jax.random.fold_in(seeds[10], part), 11)
    query_hidden = noise(part_keys[0], (QUERIES, QLEN, D), 1.0, 6.0, ((0, 16),))
    query_lengths = with_ends(jax.random.randint(part_keys[1], (QUERIES,), max(QLEN // 4, 1), QLEN + 1), jax.random.fold_in(part_keys[1], 1), max(QLEN // 4, 1), QLEN).astype(jnp.int32)
    inner_weight = noise(seeds[2], (D, FF), D ** -0.5, 0.21875)
    outer_weight = noise(seeds[3], (FF, D), FF ** -0.5, 0.109375)
    norm_gain = jnp.clip(1.0 + 0.18 * jax.random.normal(seeds[4], (D,), jnp.float32), 0.1, 1.9)
    embed_weight = noise(seeds[5], (D, EMBED), D ** -0.5, 0.21875)
    passage_vectors = noise(part_keys[6], (PASSAGES, PLEN, EMBED), (EMBED ** -0.5), 0.52734375, ((0, 16),))
    passage_lengths = with_ends(jax.random.randint(part_keys[7], (PASSAGES,), max(PLEN // 8, 1), PLEN + 1), jax.random.fold_in(part_keys[7], 1), max(PLEN // 8, 1), PLEN).astype(jnp.int32)
    passage_row = draw_passage_row(jax.random.fold_in(jax.random.fold_in(seeds[10], part), 71), part)
    candidates = draw_candidates(jax.random.fold_in(jax.random.fold_in(seeds[10], part), 71), part)
    return dict(query_hidden=query_hidden, query_lengths=query_lengths, inner_weight=inner_weight, outer_weight=outer_weight, norm_gain=norm_gain, embed_weight=embed_weight, passage_vectors=passage_vectors, passage_lengths=passage_lengths, passage_row=passage_row, candidates=candidates)


def encode(query_hidden, inner_weight, outer_weight, norm_gain, embed_weight):
    tokens = query_hidden.reshape(-1, query_hidden.shape[-1])
    inner_sum = jnp.dot(tokens, inner_weight, preferred_element_type=jnp.float32)
    activated = jax.nn.gelu(inner_sum, approximate=False).astype(jnp.bfloat16)
    summed = tokens.astype(jnp.float32) + jnp.dot(activated, outer_weight, preferred_element_type=jnp.float32)
    center = lax.optimization_barrier(jnp.mean(summed, axis=-1, keepdims=True))
    spread = lax.optimization_barrier(jnp.mean(jnp.square(summed - center), axis=-1, keepdims=True))
    layer_out = ((summed - center) * lax.rsqrt(spread + 1e-12) * norm_gain.astype(jnp.float32)).astype(jnp.bfloat16)
    embedded = jnp.dot(layer_out, embed_weight, preferred_element_type=jnp.float32)
    length = lax.optimization_barrier(jnp.sum(jnp.square(embedded), axis=-1, keepdims=True))
    vectors = (embedded * lax.rsqrt(length + 1e-06)).astype(jnp.bfloat16)
    return vectors.reshape(query_hidden.shape[0], query_hidden.shape[1], -1)

def reference(query_hidden, query_lengths, inner_weight, outer_weight, norm_gain, embed_weight, passage_vectors, passage_lengths, passage_row, candidates):
    query_vectors = encode(query_hidden, inner_weight, outer_weight, norm_gain, embed_weight)

    def score_query(packed):
        vectors, query_len, passage_ids = packed
        slab_rows = passage_row[passage_ids]
        blocks = passage_vectors[slab_rows]
        block_lens = passage_lengths[slab_rows]
        similar = jnp.einsum('te,cpe->ctp', vectors.astype(jnp.float32), blocks.astype(jnp.float32))
        pass_mask = jnp.arange(PLEN, dtype=jnp.int32)[None, None, :] < block_lens[:, None, None]
        best_match = lax.optimization_barrier(jnp.max(jnp.where(pass_mask, similar, -1e+30), axis=2))
        token_mask = jnp.arange(QLEN, dtype=jnp.int32)[None, :] < query_len
        return lax.optimization_barrier(jnp.sum(jnp.where(token_mask, best_match, 0.0), axis=1))
    scores = lax.map(score_query, (query_vectors, query_lengths, candidates))
    best_scores = lax.top_k(scores, TOPN)[0]
    return (scores, best_scores)
```

```python
import jax
import jax.numpy as jnp
from jax import lax
from jax.experimental import pallas as pl
from jax.experimental.pallas import tpu as pltpu
from jax.sharding import PartitionSpec as P

TOPN = 10
F32 = jnp.float32
BF16 = jnp.bfloat16
NT = (((1,), (1,)), ((), ()))
VMEM = pl.BlockSpec(memory_space=pltpu.VMEM)
SMEM = pl.BlockSpec(memory_space=pltpu.SMEM)
ANY = pl.BlockSpec(memory_space=pl.ANY)


def split3(value):
    high = value.astype(BF16)
    rest = value - high.astype(F32)
    middle = rest.astype(BF16)
    low = (rest - middle.astype(F32)).astype(BF16)
    return high, middle, low


def encode_kernel(lens_ref, x_ref, w1_ref, w2_ref, gain_ref, embed_ref, out_ref, w1_buf, w2_buf, sems):
    chunks, _, width = w1_buf.shape
    copies = []
    for c in range(chunks):
        first = pltpu.make_async_copy(w1_ref.at[:, pl.ds(c * width, width)], w1_buf.at[c], sems.at[0, c])
        second = pltpu.make_async_copy(w2_ref.at[pl.ds(c * width, width), :], w2_buf.at[c], sems.at[1, c])
        first.start()
        second.start()
        copies.append((first, second))
    query_count, token_count, width_in = x_ref.shape
    x = x_ref[...].reshape(query_count * token_count, width_in)
    total = x.astype(F32)
    copies[0][0].wait()
    inner = jnp.dot(x, w1_buf[0], preferred_element_type=F32)
    for c in range(chunks):
        copies[c][1].wait()
        if c + 1 < chunks:
            copies[c + 1][0].wait()
            later = jnp.dot(x, w1_buf[c + 1], preferred_element_type=F32)
        active = (0.5 * inner * (1.0 + lax.erf(inner * (0.5 ** 0.5)))).astype(BF16)
        total = total + jnp.dot(active, w2_buf[c], preferred_element_type=F32)
        if c + 1 < chunks:
            inner = later
    centered = total - jnp.mean(total, axis=-1, keepdims=True)
    spread = jnp.mean(jnp.square(centered), axis=-1, keepdims=True)
    layer_out = (centered * lax.rsqrt(spread + 1e-12) * gain_ref[...]).astype(BF16)
    embedded = jnp.dot(layer_out, embed_ref[...], preferred_element_type=F32)
    length = jnp.sum(jnp.square(embedded), axis=-1, keepdims=True)
    vectors = embedded * lax.rsqrt(length + 1e-06)
    token = lax.broadcasted_iota(jnp.int32, vectors.shape, 0)
    for i in range(query_count):
        padded = (token >= i * token_count + lens_ref[i]) & (token < (i + 1) * token_count)
        vectors = jnp.where(padded, 0.0, vectors)
    out_ref[...] = vectors.astype(BF16)


def encode(query_lengths, query_hidden, inner_weight, outer_weight, norm_gain, embed_weight):
    query_count, token_count, d = query_hidden.shape
    ff = inner_weight.shape[1]
    e = embed_weight.shape[1]
    chunks = 6
    width = ff // chunks
    tokens = query_count * token_count
    return pl.pallas_call(
        encode_kernel,
        out_shape=jax.ShapeDtypeStruct((tokens, e), BF16),
        in_specs=[SMEM, VMEM, ANY, ANY, VMEM, VMEM],
        out_specs=VMEM,
        scratch_shapes=[
            pltpu.VMEM((chunks, d, width), BF16),
            pltpu.VMEM((chunks, width, d), BF16),
            pltpu.SemaphoreType.DMA((2, chunks)),
        ],
        compiler_params=pltpu.CompilerParams(vmem_limit_bytes=40 * 2 ** 20),
        cost_estimate=pl.CostEstimate(
            flops=4 * tokens * d * ff, bytes_accessed=4 * d * ff, transcendentals=tokens * ff
        ),
        name="encode",
    )(query_lengths, query_hidden, inner_weight, outer_weight, norm_gain.reshape(1, d), embed_weight)


def prepare_kernel(
    me_ref, lens_ref, row_ref, own_ref, row_lanes_ref, cand_ref, pass_ref, _, masked_ref, index_ref, rows_ref
):
    passage_count, plen, _ = pass_ref.shape
    query_count, cand_count = own_ref.shape
    shard_count = cand_ref.shape[0] // query_count
    token_count = 32

    def lookup(k, carry):
        for i in range(query_count):
            rows_ref[i, k] = row_ref[own_ref[i, k]]
        return carry

    lax.fori_loop(0, cand_count, lookup, 0, unroll=4)

    position = lax.broadcasted_iota(jnp.int32, (plen, 1), 0)

    def mask(p, carry):
        block = pass_ref[p]
        keep = lax.broadcasted_iota(jnp.int32, block.shape, 0) < lens_ref[p]
        first = jnp.broadcast_to(block[0:1].astype(F32), block.shape)
        masked_ref[p] = jnp.where(keep, block.astype(F32), first).astype(BF16)
        return carry

    lax.fori_loop(0, passage_count, mask, 0, unroll=4)

    base = me_ref[0] * passage_count
    local = lax.broadcasted_iota(jnp.int32, (passage_count, 128), 0) + base
    lane = lax.broadcasted_iota(jnp.int32, (passage_count, 128), 1)

    def find(j, found):
        return jnp.where(row_lanes_ref[pl.ds(j, 1), :] == local, (lane + j * 128).astype(F32), found)

    found = lax.fori_loop(0, row_lanes_ref.shape[0], find, jnp.zeros((passage_count, 128), F32))
    passage_id = jnp.sum(found, axis=1, keepdims=True).astype(jnp.int32)
    passage_id = jnp.broadcast_to(passage_id, (passage_count, cand_count))

    slot_lane = lax.broadcasted_iota(jnp.int32, index_ref.shape, 1)

    def choose(s, index):
        hit = jnp.zeros((passage_count, cand_count), F32)
        for i in range(1, query_count):
            hit = jnp.where(cand_ref[pl.ds(s * query_count + i, 1), :] == passage_id, float(i), hit)
        query = jnp.sum(hit, axis=1, keepdims=True).astype(jnp.int32)
        return jnp.where(slot_lane == s, (s * query_count + query) * token_count, index)

    index_ref[...] = lax.fori_loop(0, shard_count, choose, jnp.zeros(index_ref.shape, jnp.int32))


def prepare(me, passage_lengths, passage_row, candidates, all_candidates, passage_vectors, after):
    passage_count = passage_vectors.shape[0]
    shard_count = all_candidates.shape[0] // candidates.shape[0]
    return pl.pallas_call(
        prepare_kernel,
        out_shape=(
            jax.ShapeDtypeStruct(passage_vectors.shape, BF16),
            jax.ShapeDtypeStruct((passage_count, shard_count), jnp.int32),
            jax.ShapeDtypeStruct(candidates.shape, jnp.int32),
        ),
        in_specs=[SMEM, SMEM, SMEM, SMEM, VMEM, VMEM, VMEM, ANY],
        out_specs=(VMEM, VMEM, SMEM),
        cost_estimate=pl.CostEstimate(
            flops=4 * passage_vectors.size, bytes_accessed=4 * passage_vectors.size, transcendentals=0
        ),
        name="prepare",
    )(
        me,
        passage_lengths,
        passage_row,
        candidates,
        passage_row.reshape(-1, 128),
        all_candidates,
        passage_vectors,
        after,
    )


def score_kernel(index_ref, query_ref, pass_ref, out_ref, best_ref):
    passage_count = pass_ref.shape[0]
    shard_count = index_ref.shape[1]
    token_count = best_ref.shape[1] // shard_count
    group = min(shard_count, 256 // token_count)

    def eight(step, carry):
        for part in range(shard_count // group):
            rows = []
            for j in range(8):
                p = step * 8 + j
                picked = jnp.concatenate(
                    [
                        query_ref[pl.ds(pl.multiple_of(index_ref[p, s], token_count), token_count), :]
                        for s in range(part * group, (part + 1) * group)
                    ],
                    axis=0,
                )
                similar = lax.dot_general(pass_ref[p], picked, NT, preferred_element_type=F32)
                rows.append(jnp.max(similar, axis=0, keepdims=True))
            best_ref[pl.ds(pl.multiple_of(step * 8, 8), 8), pl.ds(part * group * token_count, group * token_count)] = (
                jnp.concatenate(rows, axis=0)
            )
        return carry

    lax.fori_loop(0, passage_count // 8, eight, 0)
    wide = best_ref.shape[1]
    source = lax.broadcasted_iota(jnp.int32, (shard_count, wide), 0)
    column = lax.broadcasted_iota(jnp.int32, (shard_count, wide), 1)
    first = source * token_count
    ones = jnp.where((column >= first) & (column < first + token_count), 1.0, 0.0).astype(BF16)
    total = sum(lax.dot_general(ones, part, NT, preferred_element_type=F32) for part in split3(best_ref[...]))
    out_ref[...] = jnp.zeros(out_ref.shape, F32)
    out_ref[:, pl.ds(0, passage_count)] = total


def score(index, queries, passages, token_count):
    passage_count, plen, e = passages.shape
    shard_count = index.shape[1]
    lanes = -(-passage_count // 128) * 128
    return pl.pallas_call(
        score_kernel,
        out_shape=jax.ShapeDtypeStruct((shard_count, lanes), F32),
        in_specs=[SMEM, VMEM, VMEM],
        out_specs=VMEM,
        scratch_shapes=[pltpu.VMEM((passage_count, shard_count * token_count), F32)],
        compiler_params=pltpu.CompilerParams(vmem_limit_bytes=32 * 2 ** 20),
        cost_estimate=pl.CostEstimate(
            flops=2 * passage_count * shard_count * token_count * plen * e,
            bytes_accessed=2 * (passages.size + queries.size),
            transcendentals=0,
        ),
        name="score",
    )(index, queries, passages)


def finish_kernel(passage_count, got_ref, rows_ref, scores_ref, best_ref):
    shard_count, lanes = got_ref.shape
    query_count, cand_count = scores_ref.shape
    parts = split3(got_ref[...])
    owner_iota = lax.broadcasted_iota(jnp.int32, (shard_count, cand_count), 0)
    local_iota = lax.broadcasted_iota(jnp.int32, (lanes, cand_count), 0)
    row_iota = lax.broadcasted_iota(jnp.int32, (cand_count, cand_count), 0)
    col_iota = lax.broadcasted_iota(jnp.int32, (cand_count, cand_count), 1)
    place = lax.broadcasted_iota(jnp.int32, (cand_count, 128), 1)
    for i in range(query_count):
        row = rows_ref[i:i + 1, :]
        owner = row // passage_count
        local = row - owner * passage_count
        onehot = jnp.where(local_iota == local, 1.0, 0.0).astype(BF16)
        picked = sum(jnp.dot(part, onehot, preferred_element_type=F32) for part in parts)
        score_row = jnp.sum(jnp.where(owner_iota == owner, picked, 0.0), axis=0, keepdims=True)
        scores_ref[i:i + 1, :] = score_row
        across = jnp.broadcast_to(score_row, (cand_count, cand_count))
        score_col = jnp.sum(jnp.where(row_iota == col_iota, across, 0.0), axis=1, keepdims=True)
        ahead = (across > score_col) | ((across == score_col) & (col_iota < row_iota))
        rank = jnp.sum(jnp.where(ahead, 1.0, 0.0), axis=1, keepdims=True).astype(jnp.int32)
        ordered = jnp.sum(jnp.where(rank == place, score_col, 0.0), axis=0, keepdims=True)
        best_ref[i:i + 1, :] = ordered[:, :TOPN]


def finish(got, rows, passage_count):
    def kernel(*refs):
        finish_kernel(passage_count, *refs)

    query_count = rows.shape[0]
    return pl.pallas_call(
        kernel,
        out_shape=(
            jax.ShapeDtypeStruct(rows.shape, F32),
            jax.ShapeDtypeStruct((query_count, TOPN), F32),
        ),
        in_specs=[VMEM, VMEM],
        out_specs=(VMEM, VMEM),
        name="finish",
    )(got, rows)


def per_device(
    query_hidden,
    query_lengths,
    inner_weight,
    outer_weight,
    norm_gain,
    embed_weight,
    passage_vectors,
    passage_lengths,
    passage_row,
    candidates,
):
    passage_count = passage_vectors.shape[0]
    token_count = query_hidden.shape[1]
    me = lax.axis_index("shard").astype(jnp.int32).reshape(1)
    all_candidates = lax.all_gather(candidates, "shard", axis=0, tiled=True)
    vectors = encode(query_lengths, query_hidden, inner_weight, outer_weight, norm_gain, embed_weight)
    all_vectors = lax.all_gather(vectors, "shard", axis=0, tiled=True)
    masked, index, rows = prepare(
        me, passage_lengths, passage_row, candidates, all_candidates, passage_vectors, vectors
    )
    sums = score(index, all_vectors, masked, token_count)
    got = lax.all_to_all(sums, "shard", split_axis=0, concat_axis=0, tiled=True)
    return finish(got, rows, passage_count)


def solution(mesh):
    in_specs = (
        P(("groups", "shard"), None, None),
        P(("groups", "shard")),
        P(),
        P(),
        P(),
        P(),
        P(("groups", "shard"), None, None),
        P(("groups", "shard")),
        P("groups"),
        P(("groups", "shard"), None),
    )
    out_specs = (P(("groups", "shard"), None), P(("groups", "shard"), None))
    return jax.shard_map(
        per_device, mesh=mesh, in_specs=in_specs, out_specs=out_specs, check_vma=False
    )
```

```python
import jax
import jax.numpy as jnp
from jax import lax
from jax.experimental import pallas as pl
from jax.experimental.pallas import tpu as pltpu
from jax.sharding import PartitionSpec as P

TOPN = 10
F32 = jnp.float32
BF16 = jnp.bfloat16
NT = (((1,), (1,)), ((), ()))
VMEM = pl.BlockSpec(memory_space=pltpu.VMEM)
SMEM = pl.BlockSpec(memory_space=pltpu.SMEM)
ANY = pl.BlockSpec(memory_space=pl.ANY)


def split3(value):
    high = value.astype(BF16)
    rest = value - high.astype(F32)
    middle = rest.astype(BF16)
    low = (rest - middle.astype(F32)).astype(BF16)
    return high, middle, low


def encode_kernel(lens_ref, x_ref, w1_ref, w2_ref, gain_ref, embed_ref, out_ref, w1_buf, w2_buf, sems):
    chunks, _, width = w1_buf.shape
    copies = []
    for c in range(chunks):
        first = pltpu.make_async_copy(w1_ref.at[:, pl.ds(c * width, width)], w1_buf.at[c], sems.at[0, c])
        second = pltpu.make_async_copy(w2_ref.at[pl.ds(c * width, width), :], w2_buf.at[c], sems.at[1, c])
        first.start()
        second.start()
        copies.append((first, second))
    query_count, token_count, width_in = x_ref.shape
    x = x_ref[...].reshape(query_count * token_count, width_in)
    total = x.astype(F32)
    copies[0][0].wait()
    inner = jnp.dot(x, w1_buf[0], preferred_element_type=F32)
    for c in range(chunks):
        copies[c][1].wait()
        if c + 1 < chunks:
            copies[c + 1][0].wait()
            later = jnp.dot(x, w1_buf[c + 1], preferred_element_type=F32)
        active = (0.5 * inner * (1.0 + lax.erf(inner * (0.5 ** 0.5)))).astype(BF16)
        total = total + jnp.dot(active, w2_buf[c], preferred_element_type=F32)
        if c + 1 < chunks:
            inner = later
    centered = total - jnp.mean(total, axis=-1, keepdims=True)
    spread = jnp.mean(jnp.square(centered), axis=-1, keepdims=True)
    layer_out = (centered * lax.rsqrt(spread + 1e-12) * gain_ref[...]).astype(BF16)
    embedded = jnp.dot(layer_out, embed_ref[...], preferred_element_type=F32)
    length = jnp.sum(jnp.square(embedded), axis=-1, keepdims=True)
    vectors = embedded * lax.rsqrt(length + 1e-06)
    token = lax.broadcasted_iota(jnp.int32, vectors.shape, 0)
    for i in range(query_count):
        padded = (token >= i * token_count + lens_ref[i]) & (token < (i + 1) * token_count)
        vectors = jnp.where(padded, 0.0, vectors)
    out_ref[...] = vectors.astype(BF16)


def encode(query_lengths, query_hidden, inner_weight, outer_weight, norm_gain, embed_weight):
    query_count, token_count, d = query_hidden.shape
    ff = inner_weight.shape[1]
    e = embed_weight.shape[1]
    chunks = 6
    width = ff // chunks
    tokens = query_count * token_count
    return pl.pallas_call(
        encode_kernel,
        out_shape=jax.ShapeDtypeStruct((tokens, e), BF16),
        in_specs=[SMEM, VMEM, ANY, ANY, VMEM, VMEM],
        out_specs=VMEM,
        scratch_shapes=[
            pltpu.VMEM((chunks, d, width), BF16),
            pltpu.VMEM((chunks, width, d), BF16),
            pltpu.SemaphoreType.DMA((2, chunks)),
        ],
        compiler_params=pltpu.CompilerParams(vmem_limit_bytes=56 * 2 ** 20),
        cost_estimate=pl.CostEstimate(
            flops=4 * tokens * d * ff, bytes_accessed=4 * d * ff, transcendentals=tokens * ff
        ),
        name="encode",
    )(query_lengths, query_hidden, inner_weight, outer_weight, norm_gain.reshape(1, d), embed_weight)


def prepare_kernel(slots, token_count, me_ref, row_ref, own_ref, row_lanes_ref, *refs):
    cand_refs = refs[:slots]
    index_ref, rows_ref = refs[slots + 1:]
    passage_count = index_ref.shape[0]
    half = passage_count // 2
    query_count, cand_count = own_ref.shape

    def lookup(k, carry):
        for i in range(query_count):
            rows_ref[i, k] = row_ref[own_ref[i, k]]
        return carry

    lax.fori_loop(0, cand_count, lookup, 0, unroll=4)

    position = lax.broadcasted_iota(jnp.int32, (passage_count, 128), 0)
    local = jnp.where(position < half, position + me_ref[0] * half, position - half + me_ref[1] * half)
    lane = lax.broadcasted_iota(jnp.int32, (passage_count, 128), 1)

    def find(j, found):
        return jnp.where(row_lanes_ref[pl.ds(j, 1), :] == local, (lane + j * 128).astype(F32), found)

    found = lax.fori_loop(0, row_lanes_ref.shape[0], find, jnp.zeros((passage_count, 128), F32))
    passage_id = jnp.sum(found, axis=1, keepdims=True).astype(jnp.int32)
    passage_id = jnp.broadcast_to(passage_id, (passage_count, cand_count))

    slot_lane = lax.broadcasted_iota(jnp.int32, index_ref.shape, 1)
    index = jnp.zeros(index_ref.shape, jnp.int32)
    for s in range(slots):
        hit = jnp.zeros((passage_count, cand_count), F32)
        for i in range(1, query_count):
            hit = jnp.where(cand_refs[s][i:i + 1, :] == passage_id, float(i), hit)
        query = jnp.sum(hit, axis=1, keepdims=True).astype(jnp.int32)
        index = jnp.where(slot_lane == s, query * token_count, index)
    index_ref[...] = index


def prepare(me, passage_row, candidates, passage_count, token_count, after):
    slots = len(candidates)

    def kernel(*refs):
        prepare_kernel(slots, token_count, *refs)

    return pl.pallas_call(
        kernel,
        out_shape=(
            jax.ShapeDtypeStruct((passage_count, slots), jnp.int32),
            jax.ShapeDtypeStruct(candidates[0].shape, jnp.int32),
        ),
        in_specs=[SMEM, SMEM, SMEM, VMEM] + [VMEM] * slots + [ANY],
        out_specs=(VMEM, SMEM),
        cost_estimate=pl.CostEstimate(flops=10 ** 6, bytes_accessed=10 ** 6, transcendentals=0),
        name="prepare",
    )(me, passage_row, candidates[0], passage_row.reshape(-1, 128), *candidates, after)


def score_kernel(slots, index_ref, len0_ref, len1_ref, pass0_ref, pass1_ref, *refs):
    query_refs = refs[:slots]
    out_refs = refs[slots:2 * slots]
    best_ref = refs[2 * slots]
    half, plen, _ = pass0_ref.shape
    token_count = best_ref.shape[1] // slots
    group = min(slots, 256 // token_count)
    position = lax.broadcasted_iota(jnp.int32, (plen, group * token_count), 0)

    for side, (len_ref, pass_ref) in enumerate(((len0_ref, pass0_ref), (len1_ref, pass1_ref))):

        def eight(step, carry):
            for part in range(slots // group):
                rows = []
                for j in range(8):
                    p = step * 8 + j
                    picked = jnp.concatenate(
                        [
                            query_refs[s][
                                pl.ds(pl.multiple_of(index_ref[side * half + p, s], token_count), token_count), :
                            ]
                            for s in range(part * group, (part + 1) * group)
                        ],
                        axis=0,
                    )
                    similar = lax.dot_general(pass_ref[p], picked, NT, preferred_element_type=F32)
                    similar = jnp.where(position < len_ref[p], similar, -1e30)
                    rows.append(jnp.max(similar, axis=0, keepdims=True))
                best_ref[
                    pl.ds(pl.multiple_of(side * half + step * 8, 8), 8),
                    pl.ds(part * group * token_count, group * token_count),
                ] = jnp.concatenate(rows, axis=0)
            return carry

        lax.fori_loop(0, half // 8, eight, 0)
    wide = best_ref.shape[1]
    source = lax.broadcasted_iota(jnp.int32, (slots, wide), 0)
    column = lax.broadcasted_iota(jnp.int32, (slots, wide), 1)
    first = source * token_count
    ones = jnp.where((column >= first) & (column < first + token_count), 1.0, 0.0).astype(BF16)
    total = sum(lax.dot_general(ones, part, NT, preferred_element_type=F32) for part in split3(best_ref[...]))
    for s in range(slots):
        out_refs[s][...] = jnp.zeros(out_refs[s].shape, F32)
        out_refs[s][:, pl.ds(0, 2 * half)] = total[s:s + 1]


def score(index, lengths, passages, queries, token_count):
    half, plen, e = passages[0].shape
    slots = len(queries)
    lanes = -(-2 * half // 128) * 128

    def kernel(*refs):
        score_kernel(slots, *refs)

    return pl.pallas_call(
        kernel,
        out_shape=[jax.ShapeDtypeStruct((1, lanes), F32)] * slots,
        in_specs=[SMEM, SMEM, SMEM, VMEM, VMEM] + [VMEM] * slots,
        out_specs=[VMEM] * slots,
        scratch_shapes=[pltpu.VMEM((2 * half, slots * token_count), F32)],
        cost_estimate=pl.CostEstimate(
            flops=4 * half * slots * token_count * plen * e,
            bytes_accessed=4 * passages[0].size,
            transcendentals=0,
        ),
        name="score",
    )(index, *lengths, *passages, *queries)


def finish_kernel(slots, half, me_ref, rows_ref, *refs):
    got_refs = refs[:slots]
    scores_ref, best_ref = refs[slots:]
    query_count, cand_count = scores_ref.shape
    got = jnp.concatenate([ref[...] for ref in got_refs], axis=0)
    lanes = got.shape[1]
    parts = split3(got)
    slot_iota = lax.broadcasted_iota(jnp.int32, (slots, cand_count), 0)
    local_iota = lax.broadcasted_iota(jnp.int32, (lanes, cand_count), 0)
    row_iota = lax.broadcasted_iota(jnp.int32, (cand_count, cand_count), 0)
    col_iota = lax.broadcasted_iota(jnp.int32, (cand_count, cand_count), 1)
    place = lax.broadcasted_iota(jnp.int32, (cand_count, 128), 1)
    me = me_ref[0]
    for i in range(query_count):
        row = rows_ref[i:i + 1, :]
        owner = row // half
        side = jnp.bitwise_and(jnp.bitwise_xor(owner, me), 1)
        local = row - owner * half + side * half
        slot = jnp.right_shift(jnp.bitwise_xor(owner, me), 1)
        onehot = jnp.where(local_iota == local, 1.0, 0.0).astype(BF16)
        picked = sum(jnp.dot(part, onehot, preferred_element_type=F32) for part in parts)
        score_row = jnp.sum(jnp.where(slot_iota == slot, picked, 0.0), axis=0, keepdims=True)
        scores_ref[i:i + 1, :] = score_row
        across = jnp.broadcast_to(score_row, (cand_count, cand_count))
        score_col = jnp.sum(jnp.where(row_iota == col_iota, across, 0.0), axis=1, keepdims=True)
        ahead = (across > score_col) | ((across == score_col) & (col_iota < row_iota))
        rank = jnp.sum(jnp.where(ahead, 1.0, 0.0), axis=1, keepdims=True).astype(jnp.int32)
        ordered = jnp.sum(jnp.where(rank == place, score_col, 0.0), axis=0, keepdims=True)
        best_ref[i:i + 1, :] = ordered[:, :TOPN]


def finish(me, rows, got, half):
    slots = len(got)

    def kernel(*refs):
        finish_kernel(slots, half, *refs)

    return pl.pallas_call(
        kernel,
        out_shape=(
            jax.ShapeDtypeStruct(rows.shape, F32),
            jax.ShapeDtypeStruct((rows.shape[0], TOPN), F32),
        ),
        in_specs=[SMEM, VMEM] + [VMEM] * slots,
        out_specs=(VMEM, VMEM),
        name="finish",
    )(me, rows, *got)


def swap(value, distance):
    size = lax.axis_size("shard")
    return lax.ppermute(value, "shard", [(i, i ^ distance) for i in range(size)])


def spread(value, slots):
    return [value] + [swap(value, 2 * d) for d in range(1, slots)]


def per_device(
    query_hidden,
    query_lengths,
    inner_weight,
    outer_weight,
    norm_gain,
    embed_weight,
    passage_vectors,
    passage_lengths,
    passage_row,
    candidates,
):
    half = passage_vectors.shape[0]
    token_count = query_hidden.shape[1]
    slots = lax.axis_size("shard") // 2
    shard = lax.axis_index("shard").astype(jnp.int32)
    me = jnp.stack([shard, jnp.bitwise_xor(shard, 1)])
    all_candidates = spread(candidates, slots)
    passages = (passage_vectors, swap(passage_vectors, 1))
    lengths = (passage_lengths, swap(passage_lengths, 1))
    vectors = encode(query_lengths, query_hidden, inner_weight, outer_weight, norm_gain, embed_weight)
    all_vectors = spread(vectors, slots)
    index, rows = prepare(me, passage_row, all_candidates, 2 * half, token_count, vectors)
    sums = score(index, lengths, passages, all_vectors, token_count)
    got = [sums[0]] + [swap(sums[d], 2 * d) for d in range(1, slots)]
    return finish(me, rows, got, half)


def solution(mesh):
    in_specs = (
        P(("groups", "shard"), None, None),
        P(("groups", "shard")),
        P(),
        P(),
        P(),
        P(),
        P(("groups", "shard"), None, None),
        P(("groups", "shard")),
        P("groups"),
        P(("groups", "shard"), None),
    )
    out_specs = (P(("groups", "shard"), None), P(("groups", "shard"), None))
    return jax.shard_map(
        per_device, mesh=mesh, in_specs=in_specs, out_specs=out_specs, check_vma=False
    )
```

```python
import jax
import jax.numpy as jnp
from jax import lax
from jax.experimental import pallas as pl
from jax.experimental.pallas import tpu as pltpu
from jax.sharding import PartitionSpec as P

TOPN = 10
F32 = jnp.float32
BF16 = jnp.bfloat16
NT = (((1,), (1,)), ((), ()))
VMEM = pl.BlockSpec(memory_space=pltpu.VMEM)
SMEM = pl.BlockSpec(memory_space=pltpu.SMEM)
ANY = pl.BlockSpec(memory_space=pl.ANY)


def split3(value):
    high = value.astype(BF16)
    rest = value - high.astype(F32)
    middle = rest.astype(BF16)
    low = (rest - middle.astype(F32)).astype(BF16)
    return high, middle, low


def encode_kernel(
    inverse,
    lens_ref,
    me_ref,
    row_ref,
    cand_ref,
    plen_ref,
    x_ref,
    w1_ref,
    w2_ref,
    gain_ref,
    embed_ref,
    pass_ref,
    out_ref,
    masked_ref,
    spot_ref,
    w1_buf,
    w2_buf,
    pass_buf,
    table,
    table_v,
    sems,
    pass_sem,
    table_sem,
):
    chunks, _, width = w1_buf.shape
    half, plen, _ = pass_buf.shape
    slots, lanes = table_v.shape
    query_count, token_count, width_in = x_ref.shape
    cand_count = cand_ref.shape[1]
    table_v[...] = jnp.zeros(table_v.shape, jnp.int32)
    clear = pltpu.make_async_copy(table_v, table, table_sem)
    clear.start()
    copies = []
    for c in range(chunks):
        first = pltpu.make_async_copy(w1_ref.at[:, pl.ds(c * width, width)], w1_buf.at[c], sems.at[0, c])
        second = pltpu.make_async_copy(w2_ref.at[pl.ds(c * width, width), :], w2_buf.at[c], sems.at[1, c])
        first.start()
        second.start()
        copies.append((first, second))
    load = pltpu.make_async_copy(pass_ref, pass_buf, pass_sem)
    load.start()
    clear.wait()

    side = jnp.bitwise_and(me_ref[0], 1)

    def enter(k, carry):
        for i in range(query_count):
            row = row_ref[cand_ref[i, k]]
            owner = inverse(row)
            chip = jnp.right_shift(owner, 1)
            place = row - owner * half + jnp.bitwise_xor(jnp.bitwise_and(owner, 1), side) * half
            table[chip, place] = i
            spot_ref[i, k] = chip * lanes + place
        return carry

    lax.fori_loop(0, cand_count, enter, 0, unroll=4)
    fetch = pltpu.make_async_copy(table, table_v, table_sem)
    fetch.start()

    x = x_ref[...].reshape(query_count * token_count, width_in)
    total = x.astype(F32)
    copies[0][0].wait()
    inner = jnp.dot(x, w1_buf[0], preferred_element_type=F32)
    for c in range(chunks):
        copies[c][1].wait()
        if c + 1 < chunks:
            copies[c + 1][0].wait()
            later = jnp.dot(x, w1_buf[c + 1], preferred_element_type=F32)
        active = (0.5 * inner * (1.0 + lax.erf(inner * (0.5 ** 0.5)))).astype(BF16)
        total = total + jnp.dot(active, w2_buf[c], preferred_element_type=F32)
        if c + 1 < chunks:
            inner = later

    load.wait()

    def mask(p, carry):
        block = pass_buf[p]
        keep = lax.broadcasted_iota(jnp.int32, block.shape, 0) < plen_ref[p]
        block = block.astype(F32)
        pass_buf[p] = jnp.where(keep, block, jnp.broadcast_to(block[0:1], block.shape)).astype(BF16)
        return carry

    lax.fori_loop(0, half, mask, 0, unroll=4)
    save = pltpu.make_async_copy(pass_buf, masked_ref, pass_sem)
    save.start()

    centered = total - jnp.mean(total, axis=-1, keepdims=True)
    variance = jnp.mean(jnp.square(centered), axis=-1, keepdims=True)
    layer_out = (centered * lax.rsqrt(variance + 1e-12) * gain_ref[...]).astype(BF16)
    embedded = jnp.dot(layer_out, embed_ref[...], preferred_element_type=F32)
    length = jnp.sum(jnp.square(embedded), axis=-1, keepdims=True)
    vectors = embedded * lax.rsqrt(length + 1e-06)
    token = lax.broadcasted_iota(jnp.int32, vectors.shape, 0)
    for i in range(query_count):
        padded = (token >= i * token_count + lens_ref[i]) & (token < (i + 1) * token_count)
        vectors = jnp.where(padded, 0.0, vectors)
    vectors = vectors.astype(BF16)
    fetch.wait()
    tokens = query_count * token_count
    tail = out_ref.shape[1] - tokens
    for s in range(slots):
        out_ref[s, pl.ds(0, tokens), :] = vectors
        out_ref[s, pl.ds(tokens, tail), :] = jnp.broadcast_to(
            table_v[s:s + 1, :].astype(F32), (tail, lanes)
        ).astype(BF16)
    save.wait()


def divider(divisor, limit):
    magic = -(-(2 ** 20) // divisor)
    if limit * magic < 2 ** 31 and all((v * magic) >> 20 == v // divisor for v in range(limit)):
        return lambda value: jnp.right_shift(value * magic, 20)
    return lambda value: value // divisor


def encode(
    me,
    query_hidden,
    query_lengths,
    inner_weight,
    outer_weight,
    norm_gain,
    embed_weight,
    passage_vectors,
    passage_lengths,
    passage_row,
    candidates,
    slots,
):
    query_count, token_count, d = query_hidden.shape
    ff = inner_weight.shape[1]
    e = embed_weight.shape[1]
    half = passage_vectors.shape[0]
    assert 2 * half <= e
    chunks = 6
    width = ff // chunks
    tokens = query_count * token_count
    inverse = divider(half, passage_row.shape[0])

    def kernel(*refs):
        encode_kernel(inverse, *refs)

    return pl.pallas_call(
        kernel,
        out_shape=(
            jax.ShapeDtypeStruct((slots, tokens + 16, e), BF16),
            jax.ShapeDtypeStruct(passage_vectors.shape, BF16),
            jax.ShapeDtypeStruct(candidates.shape, jnp.int32),
        ),
        in_specs=[SMEM] * 5 + [VMEM, ANY, ANY, VMEM, VMEM, ANY],
        out_specs=(VMEM, ANY, SMEM),
        scratch_shapes=[
            pltpu.VMEM((chunks, d, width), BF16),
            pltpu.VMEM((chunks, width, d), BF16),
            pltpu.VMEM(passage_vectors.shape, BF16),
            pltpu.SMEM((slots, e), jnp.int32),
            pltpu.VMEM((slots, e), jnp.int32),
            pltpu.SemaphoreType.DMA((2, chunks)),
            pltpu.SemaphoreType.DMA,
            pltpu.SemaphoreType.DMA,
        ],
        compiler_params=pltpu.CompilerParams(vmem_limit_bytes=56 * 2 ** 20),
        cost_estimate=pl.CostEstimate(
            flops=4 * tokens * d * ff, bytes_accessed=4 * d * ff, transcendentals=tokens * ff
        ),
        name="encode",
    )(
        query_lengths,
        me,
        passage_row,
        candidates,
        passage_lengths,
        query_hidden,
        inner_weight,
        outer_weight,
        norm_gain.reshape(1, d),
        embed_weight,
        passage_vectors,
    )


def score_kernel(token_count, got_ref, pass0_ref, pass1_ref, out_ref, best_ref, index_v, index, sem):
    slots, message, lanes = got_ref.shape
    half = pass0_ref.shape[0]
    tokens = message - 16
    group = min(slots, 256 // token_count)
    for s in range(slots):
        index_v[s:s + 1, :] = got_ref[s, pl.ds(tokens, 16), :].astype(F32)[0:1].astype(jnp.int32) * token_count
    copy = pltpu.make_async_copy(index_v, index, sem)
    copy.start()
    copy.wait()

    for side, pass_ref in enumerate((pass0_ref, pass1_ref)):

        def eight(step, carry):
            for part in range(slots // group):
                rows = []
                for j in range(8):
                    p = step * 8 + j
                    picked = jnp.concatenate(
                        [
                            got_ref[s, pl.ds(pl.multiple_of(index[s, side * half + p], token_count), token_count), :]
                            for s in range(part * group, (part + 1) * group)
                        ],
                        axis=0,
                    )
                    similar = lax.dot_general(pass_ref[p], picked, NT, preferred_element_type=F32)
                    rows.append(jnp.max(similar, axis=0, keepdims=True))
                best_ref[
                    pl.ds(pl.multiple_of(side * half + step * 8, 8), 8),
                    pl.ds(part * group * token_count, group * token_count),
                ] = jnp.concatenate(rows, axis=0)
            return carry

        lax.fori_loop(0, half // 8, eight, 0)
    wide = best_ref.shape[1]
    source = lax.broadcasted_iota(jnp.int32, (slots, wide), 0)
    column = lax.broadcasted_iota(jnp.int32, (slots, wide), 1)
    first = source * token_count
    ones = jnp.where((column >= first) & (column < first + token_count), 1.0, 0.0).astype(BF16)
    total = sum(lax.dot_general(ones, part, NT, preferred_element_type=F32) for part in split3(best_ref[...]))
    out_ref[...] = jnp.zeros(out_ref.shape, F32)
    out_ref[:, pl.ds(0, 2 * half)] = total


def score(got, own, other, token_count):
    half, plen, e = own.shape
    slots = got.shape[0]

    def kernel(*refs):
        score_kernel(token_count, *refs)

    return pl.pallas_call(
        kernel,
        out_shape=jax.ShapeDtypeStruct((slots, e), F32),
        in_specs=[VMEM] * 3,
        out_specs=VMEM,
        scratch_shapes=[
            pltpu.VMEM((2 * half, slots * token_count), F32),
            pltpu.VMEM((slots, e), jnp.int32),
            pltpu.SMEM((slots, e), jnp.int32),
            pltpu.SemaphoreType.DMA,
        ],
        cost_estimate=pl.CostEstimate(
            flops=4 * half * slots * token_count * plen * e, bytes_accessed=4 * own.size, transcendentals=0
        ),
        name="score",
    )(got, own, other)


def finish_kernel(got_ref, spot_ref, scores_ref, best_ref):
    slots, lanes = got_ref.shape
    query_count, cand_count = scores_ref.shape
    parts = split3(got_ref[...])
    slot_iota = lax.broadcasted_iota(jnp.int32, (slots, cand_count), 0) * lanes
    lane_iota = lax.broadcasted_iota(jnp.int32, (lanes, cand_count), 0)
    row_iota = lax.broadcasted_iota(jnp.int32, (cand_count, cand_count), 0)
    col_iota = lax.broadcasted_iota(jnp.int32, (cand_count, cand_count), 1)
    place = lax.broadcasted_iota(jnp.int32, (cand_count, 128), 1)
    for i in range(query_count):
        spot = spot_ref[i:i + 1, :]
        lane = jnp.bitwise_and(spot, lanes - 1)
        onehot = jnp.where(lane_iota == lane, 1.0, 0.0).astype(BF16)
        picked = sum(jnp.dot(part, onehot, preferred_element_type=F32) for part in parts)
        score_row = jnp.sum(jnp.where(slot_iota == spot - lane, picked, 0.0), axis=0, keepdims=True)
        scores_ref[i:i + 1, :] = score_row
        across = jnp.broadcast_to(score_row, (cand_count, cand_count))
        score_col = jnp.sum(jnp.where(row_iota == col_iota, across, 0.0), axis=1, keepdims=True)
        ahead = (across > score_col) | ((across == score_col) & (col_iota < row_iota))
        rank = jnp.sum(jnp.where(ahead, 1.0, 0.0), axis=1, keepdims=True).astype(jnp.int32)
        ordered = jnp.sum(jnp.where(rank == place, score_col, 0.0), axis=0, keepdims=True)
        best_ref[i:i + 1, :] = ordered[:, :TOPN]


def finish(got, spots):
    return pl.pallas_call(
        finish_kernel,
        out_shape=(
            jax.ShapeDtypeStruct(spots.shape, F32),
            jax.ShapeDtypeStruct((spots.shape[0], TOPN), F32),
        ),
        in_specs=[VMEM, VMEM],
        out_specs=(VMEM, VMEM),
        name="finish",
    )(got, spots)


def per_device(
    query_hidden,
    query_lengths,
    inner_weight,
    outer_weight,
    norm_gain,
    embed_weight,
    passage_vectors,
    passage_lengths,
    passage_row,
    candidates,
):
    size = lax.axis_size("shard")
    slots = size // 2
    groups = [list(range(core, size, 2)) for core in range(2)]
    me = lax.axis_index("shard").astype(jnp.int32).reshape(1)
    message, own, spots = encode(
        me,
        query_hidden,
        query_lengths,
        inner_weight,
        outer_weight,
        norm_gain,
        embed_weight,
        passage_vectors,
        passage_lengths,
        passage_row,
        candidates,
        slots,
    )
    other = lax.ppermute(own, "shard", [(i, i ^ 1) for i in range(size)])
    got = lax.all_to_all(message, "shard", split_axis=0, concat_axis=0, axis_index_groups=groups, tiled=True)
    sums = score(got, own, other, query_hidden.shape[1])
    back = lax.all_to_all(sums, "shard", split_axis=0, concat_axis=0, axis_index_groups=groups, tiled=True)
    return finish(back, spots)


def solution(mesh):
    in_specs = (
        P(("groups", "shard"), None, None),
        P(("groups", "shard")),
        P(),
        P(),
        P(),
        P(),
        P(("groups", "shard"), None, None),
        P(("groups", "shard")),
        P("groups"),
        P(("groups", "shard"), None),
    )
    out_specs = (P(("groups", "shard"), None), P(("groups", "shard"), None))
    return jax.shard_map(
        per_device, mesh=mesh, in_specs=in_specs, out_specs=out_specs, check_vma=False
    )
```

```python
import jax
import jax.numpy as jnp
from jax import lax
from jax.experimental import pallas as pl
from jax.experimental.pallas import tpu as pltpu
from jax.sharding import PartitionSpec as P

TOPN = 10
F32 = jnp.float32
BF16 = jnp.bfloat16
NT = (((1,), (1,)), ((), ()))
VMEM = pl.BlockSpec(memory_space=pltpu.VMEM)
SMEM = pl.BlockSpec(memory_space=pltpu.SMEM)
ANY = pl.BlockSpec(memory_space=pl.ANY)


def split3(value):
    high = value.astype(BF16)
    rest = value - high.astype(F32)
    middle = rest.astype(BF16)
    low = (rest - middle.astype(F32)).astype(BF16)
    return high, middle, low


def encode_kernel(
    inverse,
    half,
    me_ref,
    lens_hbm,
    row_hbm,
    cand_hbm,
    x_hbm,
    w1_ref,
    w2_ref,
    gain_hbm,
    embed_hbm,
    out_ref,
    spot_ref,
    w1_buf,
    w2_buf,
    lens_ref,
    row_ref,
    cand_ref,
    x_ref,
    gain_ref,
    embed_ref,
    table,
    table_v,
    sems,
    small_sems,
    table_sem,
):
    chunks, _, width = w1_buf.shape
    slots, lanes = table_v.shape
    query_count, token_count, width_in = x_ref.shape
    cand_count = cand_ref.shape[1]
    table_v[...] = jnp.zeros(table_v.shape, jnp.int32)
    clear = pltpu.make_async_copy(table_v, table, table_sem)
    clear.start()
    copies = []
    for c in range(chunks):
        first = pltpu.make_async_copy(w1_ref.at[:, pl.ds(c * width, width)], w1_buf.at[c], sems.at[0, c])
        second = pltpu.make_async_copy(w2_ref.at[pl.ds(c * width, width), :], w2_buf.at[c], sems.at[1, c])
        copies.append((first, second))
    small = [
        pltpu.make_async_copy(source, target, small_sems.at[n])
        for n, (source, target) in enumerate(
            (
                (row_hbm, row_ref),
                (cand_hbm, cand_ref),
                (x_hbm, x_ref),
                (lens_hbm, lens_ref),
                (gain_hbm, gain_ref),
                (embed_hbm, embed_ref),
            )
        )
    ]
    for copy in small[:3]:
        copy.start()
    for first, _ in copies:
        first.start()
    for _, second in copies:
        second.start()
    for copy in small[3:]:
        copy.start()
    clear.wait()
    small[0].wait()
    small[1].wait()

    side = jnp.bitwise_and(me_ref[0], 1)

    def enter(k, carry):
        for i in range(query_count):
            row = row_ref[cand_ref[i, k]]
            owner = inverse(row)
            chip = jnp.right_shift(owner, 1)
            place = row - owner * half + jnp.bitwise_xor(jnp.bitwise_and(owner, 1), side) * half
            table[chip, place] = i
            spot_ref[i, k] = chip * lanes + place
        return carry

    lax.fori_loop(0, cand_count, enter, 0, unroll=4)
    fetch = pltpu.make_async_copy(table, table_v, table_sem)
    fetch.start()

    small[2].wait()
    x = x_ref[...].reshape(query_count * token_count, width_in)
    actives = []
    for c in range(chunks):
        copies[c][0].wait()
        inner = jnp.dot(x, w1_buf[c], preferred_element_type=F32)
        actives.append((0.5 * inner * (1.0 + lax.erf(inner * (0.5 ** 0.5)))).astype(BF16))
    total = x.astype(F32)
    for c in range(chunks):
        copies[c][1].wait()
        total = total + jnp.dot(actives[c], w2_buf[c], preferred_element_type=F32)

    for copy in small[3:]:
        copy.wait()
    centered = total - jnp.mean(total, axis=-1, keepdims=True)
    variance = jnp.mean(jnp.square(centered), axis=-1, keepdims=True)
    layer_out = (centered * lax.rsqrt(variance + 1e-12) * gain_ref[...].reshape(1, width_in)).astype(BF16)
    embedded = jnp.dot(layer_out, embed_ref[...], preferred_element_type=F32)
    length = jnp.sum(jnp.square(embedded), axis=-1, keepdims=True)
    vectors = embedded * lax.rsqrt(length + 1e-06)
    token = lax.broadcasted_iota(jnp.int32, vectors.shape, 0)
    for i in range(query_count):
        padded = (token >= i * token_count + lens_ref[i]) & (token < (i + 1) * token_count)
        vectors = jnp.where(padded, 0.0, vectors)
    vectors = vectors.astype(BF16)
    fetch.wait()
    tokens = query_count * token_count
    tail = out_ref.shape[1] - tokens
    for s in range(slots):
        out_ref[s, pl.ds(0, tokens), :] = vectors
        out_ref[s, pl.ds(tokens, tail), :] = jnp.broadcast_to(
            table_v[s:s + 1, :].astype(F32), (tail, lanes)
        ).astype(BF16)


def divider(divisor, limit):
    magic = -(-(2 ** 20) // divisor)
    if limit * magic < 2 ** 31 and all((v * magic) >> 20 == v // divisor for v in range(limit)):
        return lambda value: jnp.right_shift(value * magic, 20)
    return lambda value: value // divisor


def encode(
    me,
    query_hidden,
    query_lengths,
    inner_weight,
    outer_weight,
    norm_gain,
    embed_weight,
    passage_row,
    candidates,
    slots,
    half,
):
    query_count, token_count, d = query_hidden.shape
    ff = inner_weight.shape[1]
    e = embed_weight.shape[1]
    assert 2 * half <= e
    chunks = 6
    width = ff // chunks
    tokens = query_count * token_count
    inverse = divider(half, passage_row.shape[0])

    def kernel(*refs):
        encode_kernel(inverse, half, *refs)

    return pl.pallas_call(
        kernel,
        out_shape=(
            jax.ShapeDtypeStruct((slots, tokens + 16, e), BF16),
            jax.ShapeDtypeStruct(candidates.shape, jnp.int32),
        ),
        in_specs=[SMEM] + [ANY] * 8,
        out_specs=(VMEM, SMEM),
        scratch_shapes=[
            pltpu.VMEM((chunks, d, width), BF16),
            pltpu.VMEM((chunks, width, d), BF16),
            pltpu.SMEM(query_lengths.shape, jnp.int32),
            pltpu.SMEM(passage_row.shape, jnp.int32),
            pltpu.SMEM(candidates.shape, jnp.int32),
            pltpu.VMEM(query_hidden.shape, BF16),
            pltpu.VMEM(norm_gain.shape, F32),
            pltpu.VMEM(embed_weight.shape, BF16),
            pltpu.SMEM((slots, e), jnp.int32),
            pltpu.VMEM((slots, e), jnp.int32),
            pltpu.SemaphoreType.DMA((2, chunks)),
            pltpu.SemaphoreType.DMA((6,)),
            pltpu.SemaphoreType.DMA,
        ],
        compiler_params=pltpu.CompilerParams(vmem_limit_bytes=60 * 2 ** 20),
        cost_estimate=pl.CostEstimate(
            flops=4 * tokens * d * ff, bytes_accessed=4 * d * ff, transcendentals=tokens * ff
        ),
        name="encode",
    )(
        me,
        query_lengths,
        passage_row,
        candidates,
        query_hidden,
        inner_weight,
        outer_weight,
        norm_gain,
        embed_weight,
    )


def mask_kernel(len0_ref, len1_ref, pass0_ref, pass1_ref, _, out_ref):
    half = pass0_ref.shape[0]
    for side, (len_ref, pass_ref) in enumerate(((len0_ref, pass0_ref), (len1_ref, pass1_ref))):

        def mask(p, carry):
            block = pass_ref[p]
            keep = lax.broadcasted_iota(jnp.int32, block.shape, 0) < len_ref[p]
            block = block.astype(F32)
            out_ref[side * half + p] = jnp.where(keep, block, jnp.broadcast_to(block[0:1], block.shape)).astype(BF16)
            return carry

        lax.fori_loop(0, half, mask, 0, unroll=4)


def mask(lengths, passages, after):
    half, plen, e = passages[0].shape
    return pl.pallas_call(
        mask_kernel,
        out_shape=jax.ShapeDtypeStruct((2 * half, plen, e), BF16),
        in_specs=[SMEM, SMEM, VMEM, VMEM, ANY],
        out_specs=VMEM,
        compiler_params=pltpu.CompilerParams(vmem_limit_bytes=8 * 2 ** 20),
        cost_estimate=pl.CostEstimate(
            flops=8 * half * plen * e, bytes_accessed=8 * half * plen * e, transcendentals=0
        ),
        name="mask",
    )(*lengths, *passages, after)


def score_kernel(token_count, got_ref, pass_ref, out_ref, best_ref, index_v, index, sem):
    slots, message, lanes = got_ref.shape
    passage_count = pass_ref.shape[0]
    tokens = message - 16
    group = min(slots, 256 // token_count)
    for s in range(slots):
        index_v[s:s + 1, :] = got_ref[s, pl.ds(tokens, 16), :].astype(F32)[0:1].astype(jnp.int32) * token_count
    copy = pltpu.make_async_copy(index_v, index, sem)
    copy.start()
    copy.wait()

    def eight(step, carry):
        for part in range(slots // group):
            rows = []
            for j in range(8):
                p = step * 8 + j
                picked = jnp.concatenate(
                    [
                        got_ref[s, pl.ds(pl.multiple_of(index[s, p], token_count), token_count), :]
                        for s in range(part * group, (part + 1) * group)
                    ],
                    axis=0,
                )
                similar = lax.dot_general(pass_ref[p], picked, NT, preferred_element_type=F32)
                rows.append(jnp.max(similar, axis=0, keepdims=True))
            best_ref[
                pl.ds(pl.multiple_of(step * 8, 8), 8),
                pl.ds(part * group * token_count, group * token_count),
            ] = jnp.concatenate(rows, axis=0)
        return carry

    lax.fori_loop(0, passage_count // 8, eight, 0)
    wide = best_ref.shape[1]
    source = lax.broadcasted_iota(jnp.int32, (slots, wide), 0)
    column = lax.broadcasted_iota(jnp.int32, (slots, wide), 1)
    first = source * token_count
    ones = jnp.where((column >= first) & (column < first + token_count), 1.0, 0.0).astype(BF16)
    total = sum(lax.dot_general(ones, part, NT, preferred_element_type=F32) for part in split3(best_ref[...]))
    out_ref[...] = jnp.zeros(out_ref.shape, F32)
    out_ref[:, pl.ds(0, passage_count)] = total


def score(got, passages, token_count):
    passage_count, plen, e = passages.shape
    slots = got.shape[0]

    def kernel(*refs):
        score_kernel(token_count, *refs)

    return pl.pallas_call(
        kernel,
        out_shape=jax.ShapeDtypeStruct((slots, e), F32),
        in_specs=[VMEM] * 2,
        out_specs=VMEM,
        scratch_shapes=[
            pltpu.VMEM((passage_count, slots * token_count), F32),
            pltpu.VMEM((slots, e), jnp.int32),
            pltpu.SMEM((slots, e), jnp.int32),
            pltpu.SemaphoreType.DMA,
        ],
        compiler_params=pltpu.CompilerParams(vmem_limit_bytes=12 * 2 ** 20),
        cost_estimate=pl.CostEstimate(
            flops=2 * passage_count * slots * token_count * plen * e,
            bytes_accessed=2 * passages.size,
            transcendentals=0,
        ),
        name="score",
    )(got, passages)


def finish_kernel(got_ref, spot_ref, scores_ref, best_ref):
    slots, lanes = got_ref.shape
    query_count, cand_count = scores_ref.shape
    parts = split3(got_ref[...])
    slot_iota = lax.broadcasted_iota(jnp.int32, (slots, cand_count), 0) * lanes
    lane_iota = lax.broadcasted_iota(jnp.int32, (lanes, cand_count), 0)
    row_iota = lax.broadcasted_iota(jnp.int32, (cand_count, cand_count), 0)
    col_iota = lax.broadcasted_iota(jnp.int32, (cand_count, cand_count), 1)
    place = lax.broadcasted_iota(jnp.int32, (cand_count, 128), 1)
    for i in range(query_count):
        spot = spot_ref[i:i + 1, :]
        lane = jnp.bitwise_and(spot, lanes - 1)
        onehot = jnp.where(lane_iota == lane, 1.0, 0.0).astype(BF16)
        picked = sum(jnp.dot(part, onehot, preferred_element_type=F32) for part in parts)
        score_row = jnp.sum(jnp.where(slot_iota == spot - lane, picked, 0.0), axis=0, keepdims=True)
        scores_ref[i:i + 1, :] = score_row
        across = jnp.broadcast_to(score_row, (cand_count, cand_count))
        score_col = jnp.sum(jnp.where(row_iota == col_iota, across, 0.0), axis=1, keepdims=True)
        ahead = (across > score_col) | ((across == score_col) & (col_iota < row_iota))
        rank = jnp.sum(jnp.where(ahead, 1.0, 0.0), axis=1, keepdims=True).astype(jnp.int32)
        ordered = jnp.sum(jnp.where(rank == place, score_col, 0.0), axis=0, keepdims=True)
        best_ref[i:i + 1, :] = ordered[:, :TOPN]


def finish(got, spots):
    return pl.pallas_call(
        finish_kernel,
        out_shape=(
            jax.ShapeDtypeStruct(spots.shape, F32),
            jax.ShapeDtypeStruct((spots.shape[0], TOPN), F32),
        ),
        in_specs=[VMEM, VMEM],
        out_specs=(VMEM, VMEM),
        compiler_params=pltpu.CompilerParams(vmem_limit_bytes=2 ** 21),
        name="finish",
    )(got, spots)


def per_device(
    query_hidden,
    query_lengths,
    inner_weight,
    outer_weight,
    norm_gain,
    embed_weight,
    passage_vectors,
    passage_lengths,
    passage_row,
    candidates,
):
    size = lax.axis_size("shard")
    slots = size // 2
    groups = [list(range(core, size, 2)) for core in range(2)]
    me = lax.axis_index("shard").astype(jnp.int32).reshape(1)
    half = passage_vectors.shape[0]
    across = [(i, i ^ 1) for i in range(size)]
    passages = (passage_vectors, lax.ppermute(passage_vectors, "shard", across))
    lengths = (passage_lengths, lax.ppermute(passage_lengths, "shard", across))
    message, spots = encode(
        me,
        query_hidden,
        query_lengths,
        inner_weight,
        outer_weight,
        norm_gain,
        embed_weight,
        passage_row,
        candidates,
        slots,
        half,
    )
    got = lax.all_to_all(message, "shard", split_axis=0, concat_axis=0, axis_index_groups=groups, tiled=True)
    masked = mask(lengths, passages, spots)
    sums = score(got, masked, query_hidden.shape[1])
    back = lax.all_to_all(sums, "shard", split_axis=0, concat_axis=0, axis_index_groups=groups, tiled=True)
    return finish(back, spots)


def solution(mesh):
    in_specs = (
        P(("groups", "shard"), None, None),
        P(("groups", "shard")),
        P(),
        P(),
        P(),
        P(),
        P(("groups", "shard"), None, None),
        P(("groups", "shard")),
        P("groups"),
        P(("groups", "shard"), None),
    )
    out_specs = (P(("groups", "shard"), None), P(("groups", "shard"), None))
    return jax.shard_map(
        per_device, mesh=mesh, in_specs=in_specs, out_specs=out_specs, check_vma=False
    )
```

```python
import jax
import jax.numpy as jnp
from jax import lax
from jax.experimental import pallas as pl
from jax.experimental.pallas import tpu as pltpu
from jax.sharding import PartitionSpec as P

TOPN = 10
F32 = jnp.float32
BF16 = jnp.bfloat16
NT = (((1,), (1,)), ((), ()))
VMEM = pl.BlockSpec(memory_space=pltpu.VMEM)
SMEM = pl.BlockSpec(memory_space=pltpu.SMEM)
ANY = pl.BlockSpec(memory_space=pl.ANY)


def split3(value):
    high = value.astype(BF16)
    rest = value - high.astype(F32)
    middle = rest.astype(BF16)
    low = (rest - middle.astype(F32)).astype(BF16)
    return high, middle, low


def encode_kernel(
    inverse,
    half,
    me_ref,
    lens_hbm,
    row_hbm,
    cand_hbm,
    x_hbm,
    w1_ref,
    w2_ref,
    gain_hbm,
    embed_hbm,
    out_ref,
    spot_ref,
    w1_buf,
    w2_buf,
    lens_ref,
    row_ref,
    cand_ref,
    x_ref,
    gain_ref,
    embed_ref,
    table,
    table_v,
    sems,
    small_sems,
    table_sem,
):
    chunks, _, width = w1_buf.shape
    slots, lanes = table_v.shape
    query_count, token_count, width_in = x_ref.shape
    cand_count = cand_ref.shape[1]
    table_v[...] = jnp.zeros(table_v.shape, jnp.int32)
    clear = pltpu.make_async_copy(table_v, table, table_sem)
    clear.start()
    copies = []
    for c in range(chunks):
        first = pltpu.make_async_copy(w1_ref.at[:, pl.ds(c * width, width)], w1_buf.at[c], sems.at[0, c])
        second = pltpu.make_async_copy(w2_ref.at[pl.ds(c * width, width), :], w2_buf.at[c], sems.at[1, c])
        copies.append((first, second))
    small = [
        pltpu.make_async_copy(source, target, small_sems.at[n])
        for n, (source, target) in enumerate(
            (
                (row_hbm, row_ref),
                (cand_hbm, cand_ref),
                (x_hbm, x_ref),
                (lens_hbm, lens_ref),
                (gain_hbm, gain_ref),
                (embed_hbm, embed_ref),
            )
        )
    ]
    for copy in small[:3]:
        copy.start()
    for first, _ in copies:
        first.start()
    for _, second in copies:
        second.start()
    for copy in small[3:]:
        copy.start()
    clear.wait()
    small[0].wait()
    small[1].wait()

    side = jnp.bitwise_and(me_ref[0], 1)

    entries = [(i, k) for k in range(cand_count) for i in range(query_count)]
    share = -(-len(entries) // (2 * chunks - 2))

    def enter():
        for i, k in entries[:share]:
            row = row_ref[cand_ref[i, k]]
            owner = inverse(row)
            chip = jnp.right_shift(owner, 1)
            place = row - owner * half + jnp.bitwise_xor(jnp.bitwise_and(owner, 1), side) * half
            table[chip, place] = i
            spot_ref[i, k] = chip * lanes + place
        del entries[:share]

    small[2].wait()
    x = x_ref[...].reshape(query_count * token_count, width_in)
    actives = []
    for c in range(chunks):
        copies[c][0].wait()
        enter()
        inner = jnp.dot(x, w1_buf[c], preferred_element_type=F32)
        actives.append((0.5 * inner * (1.0 + lax.erf(inner * (0.5 ** 0.5)))).astype(BF16))
    total = x.astype(F32)
    for c in range(chunks):
        copies[c][1].wait()
        enter()
        if c == chunks - 2:
            fetch = pltpu.make_async_copy(table, table_v, table_sem)
            fetch.start()
        total = total + jnp.dot(actives[c], w2_buf[c], preferred_element_type=F32)

    for copy in small[3:]:
        copy.wait()
    centered = total - jnp.mean(total, axis=-1, keepdims=True)
    variance = jnp.mean(jnp.square(centered), axis=-1, keepdims=True)
    layer_out = (centered * lax.rsqrt(variance + 1e-12) * gain_ref[...].reshape(1, width_in)).astype(BF16)
    embedded = jnp.dot(layer_out, embed_ref[...], preferred_element_type=F32)
    length = jnp.sum(jnp.square(embedded), axis=-1, keepdims=True)
    vectors = embedded * lax.rsqrt(length + 1e-06)
    token = lax.broadcasted_iota(jnp.int32, vectors.shape, 0)
    for i in range(query_count):
        padded = (token >= i * token_count + lens_ref[i]) & (token < (i + 1) * token_count)
        vectors = jnp.where(padded, 0.0, vectors)
    vectors = vectors.astype(BF16)
    fetch.wait()
    tokens = query_count * token_count
    tail = out_ref.shape[1] - tokens
    for s in range(slots):
        out_ref[s, pl.ds(0, tokens), :] = vectors
        out_ref[s, pl.ds(tokens, tail), :] = jnp.broadcast_to(
            table_v[s:s + 1, :].astype(F32), (tail, lanes)
        ).astype(BF16)


def divider(divisor, limit):
    magic = -(-(2 ** 20) // divisor)
    if limit * magic < 2 ** 31 and all((v * magic) >> 20 == v // divisor for v in range(limit)):
        return lambda value: jnp.right_shift(value * magic, 20)
    return lambda value: value // divisor


def encode(
    me,
    query_hidden,
    query_lengths,
    inner_weight,
    outer_weight,
    norm_gain,
    embed_weight,
    passage_row,
    candidates,
    slots,
    half,
):
    query_count, token_count, d = query_hidden.shape
    ff = inner_weight.shape[1]
    e = embed_weight.shape[1]
    assert 2 * half <= e
    chunks = 6
    width = ff // chunks
    tokens = query_count * token_count
    inverse = divider(half, passage_row.shape[0])

    def kernel(*refs):
        encode_kernel(inverse, half, *refs)

    return pl.pallas_call(
        kernel,
        out_shape=(
            jax.ShapeDtypeStruct((slots, tokens + 16, e), BF16),
            jax.ShapeDtypeStruct(candidates.shape, jnp.int32),
        ),
        in_specs=[SMEM] + [ANY] * 8,
        out_specs=(VMEM, SMEM),
        scratch_shapes=[
            pltpu.VMEM((chunks, d, width), BF16),
            pltpu.VMEM((chunks, width, d), BF16),
            pltpu.SMEM(query_lengths.shape, jnp.int32),
            pltpu.SMEM(passage_row.shape, jnp.int32),
            pltpu.SMEM(candidates.shape, jnp.int32),
            pltpu.VMEM(query_hidden.shape, BF16),
            pltpu.VMEM(norm_gain.shape, F32),
            pltpu.VMEM(embed_weight.shape, BF16),
            pltpu.SMEM((slots, e), jnp.int32),
            pltpu.VMEM((slots, e), jnp.int32),
            pltpu.SemaphoreType.DMA((2, chunks)),
            pltpu.SemaphoreType.DMA((6,)),
            pltpu.SemaphoreType.DMA,
        ],
        compiler_params=pltpu.CompilerParams(vmem_limit_bytes=60 * 2 ** 20),
        cost_estimate=pl.CostEstimate(
            flops=4 * tokens * d * ff, bytes_accessed=4 * d * ff, transcendentals=tokens * ff
        ),
        name="encode",
    )(
        me,
        query_lengths,
        passage_row,
        candidates,
        query_hidden,
        inner_weight,
        outer_weight,
        norm_gain,
        embed_weight,
    )


def mask_kernel(len_ref, pass_ref, _, out_ref):
    def mask(p, carry):
        block = pass_ref[p]
        keep = lax.broadcasted_iota(jnp.int32, block.shape, 0) < len_ref[p]
        block = block.astype(F32)
        out_ref[p] = jnp.where(keep, block, jnp.broadcast_to(block[0:1], block.shape)).astype(BF16)
        return carry

    lax.fori_loop(0, pass_ref.shape[0], mask, 0, unroll=4)


def mask(lengths, passages, after):
    return pl.pallas_call(
        mask_kernel,
        out_shape=jax.ShapeDtypeStruct(passages.shape, BF16),
        in_specs=[SMEM, VMEM, ANY],
        out_specs=VMEM,
        compiler_params=pltpu.CompilerParams(vmem_limit_bytes=8 * 2 ** 20),
        cost_estimate=pl.CostEstimate(flops=8 * passages.size, bytes_accessed=4 * passages.size, transcendentals=0),
        name="mask",
    )(lengths, passages, after)


def score_kernel(token_count, got_ref, pass0_ref, pass1_ref, out_ref, best_ref, index_v, index, sem):
    slots, message, lanes = got_ref.shape
    half = pass0_ref.shape[0]
    tokens = message - 16
    group = min(slots, 256 // token_count)
    for s in range(slots):
        index_v[s:s + 1, :] = got_ref[s, pl.ds(tokens, 16), :].astype(F32)[0:1].astype(jnp.int32) * token_count
    copy = pltpu.make_async_copy(index_v, index, sem)
    copy.start()
    copy.wait()

    for side, pass_ref in enumerate((pass0_ref, pass1_ref)):

        def eight(step, carry):
            for part in range(slots // group):
                rows = []
                for j in range(8):
                    p = step * 8 + j
                    picked = jnp.concatenate(
                        [
                            got_ref[s, pl.ds(pl.multiple_of(index[s, side * half + p], token_count), token_count), :]
                            for s in range(part * group, (part + 1) * group)
                        ],
                        axis=0,
                    )
                    similar = lax.dot_general(pass_ref[p], picked, NT, preferred_element_type=F32)
                    rows.append(jnp.max(similar, axis=0, keepdims=True))
                best_ref[
                    pl.ds(pl.multiple_of(side * half + step * 8, 8), 8),
                    pl.ds(part * group * token_count, group * token_count),
                ] = jnp.concatenate(rows, axis=0)
            return carry

        lax.fori_loop(0, half // 8, eight, 0)
    wide = best_ref.shape[1]
    source = lax.broadcasted_iota(jnp.int32, (slots, wide), 0)
    column = lax.broadcasted_iota(jnp.int32, (slots, wide), 1)
    first = source * token_count
    ones = jnp.where((column >= first) & (column < first + token_count), 1.0, 0.0).astype(BF16)
    total = sum(lax.dot_general(ones, part, NT, preferred_element_type=F32) for part in split3(best_ref[...]))
    out_ref[...] = jnp.zeros(out_ref.shape, F32)
    out_ref[:, pl.ds(0, 2 * half)] = total


def score(got, own, other, token_count):
    half, plen, e = own.shape
    passage_count = 2 * half
    slots = got.shape[0]

    def kernel(*refs):
        score_kernel(token_count, *refs)

    return pl.pallas_call(
        kernel,
        out_shape=jax.ShapeDtypeStruct((slots, e), F32),
        in_specs=[VMEM] * 3,
        out_specs=VMEM,
        scratch_shapes=[
            pltpu.VMEM((passage_count, slots * token_count), F32),
            pltpu.VMEM((slots, e), jnp.int32),
            pltpu.SMEM((slots, e), jnp.int32),
            pltpu.SemaphoreType.DMA,
        ],
        compiler_params=pltpu.CompilerParams(vmem_limit_bytes=12 * 2 ** 20),
        cost_estimate=pl.CostEstimate(
            flops=2 * passage_count * slots * token_count * plen * e,
            bytes_accessed=4 * own.size,
            transcendentals=0,
        ),
        name="score",
    )(got, own, other)


def finish_kernel(me_ref, got_ref, spot_ref, scores_ref, best_ref):
    slots, _, lanes = got_ref.shape
    query_count, cand_count = scores_ref.shape
    chip = jnp.right_shift(me_ref[0], 1)
    parts = split3(jnp.concatenate([got_ref[s, pl.ds(chip, 1), :] for s in range(slots)], axis=0))
    slot_iota = lax.broadcasted_iota(jnp.int32, (slots, cand_count), 0) * lanes
    lane_iota = lax.broadcasted_iota(jnp.int32, (lanes, cand_count), 0)
    row_iota = lax.broadcasted_iota(jnp.int32, (cand_count, cand_count), 0)
    col_iota = lax.broadcasted_iota(jnp.int32, (cand_count, cand_count), 1)
    place = lax.broadcasted_iota(jnp.int32, (cand_count, 128), 1)
    for i in range(query_count):
        spot = spot_ref[i:i + 1, :]
        lane = jnp.bitwise_and(spot, lanes - 1)
        onehot = jnp.where(lane_iota == lane, 1.0, 0.0).astype(BF16)
        picked = sum(jnp.dot(part, onehot, preferred_element_type=F32) for part in parts)
        score_row = jnp.sum(jnp.where(slot_iota == spot - lane, picked, 0.0), axis=0, keepdims=True)
        scores_ref[i:i + 1, :] = score_row
        across = jnp.broadcast_to(score_row, (cand_count, cand_count))
        score_col = jnp.sum(jnp.where(row_iota == col_iota, across, 0.0), axis=1, keepdims=True)
        ahead = (across > score_col) | ((across == score_col) & (col_iota < row_iota))
        rank = jnp.sum(jnp.where(ahead, 1.0, 0.0), axis=1, keepdims=True).astype(jnp.int32)
        ordered = jnp.sum(jnp.where(rank == place, score_col, 0.0), axis=0, keepdims=True)
        best_ref[i:i + 1, :] = ordered[:, :TOPN]


def finish(me, got, spots):
    return pl.pallas_call(
        finish_kernel,
        out_shape=(
            jax.ShapeDtypeStruct(spots.shape, F32),
            jax.ShapeDtypeStruct((spots.shape[0], TOPN), F32),
        ),
        in_specs=[SMEM, VMEM, VMEM],
        out_specs=(VMEM, VMEM),
        compiler_params=pltpu.CompilerParams(vmem_limit_bytes=2 ** 21),
        name="finish",
    )(me, got, spots)


def per_device(
    query_hidden,
    query_lengths,
    inner_weight,
    outer_weight,
    norm_gain,
    embed_weight,
    passage_vectors,
    passage_lengths,
    passage_row,
    candidates,
):
    size = lax.axis_size("shard")
    slots = size // 2
    groups = [list(range(core, size, 2)) for core in range(2)]
    me = lax.axis_index("shard").astype(jnp.int32).reshape(1)
    half = passage_vectors.shape[0]
    across = [(i, i ^ 1) for i in range(size)]
    message, spots = encode(
        me,
        query_hidden,
        query_lengths,
        inner_weight,
        outer_weight,
        norm_gain,
        embed_weight,
        passage_row,
        candidates,
        slots,
        half,
    )
    got = lax.all_to_all(message, "shard", split_axis=0, concat_axis=0, axis_index_groups=groups, tiled=True)
    own = mask(passage_lengths, passage_vectors, spots)
    other = lax.ppermute(own, "shard", across)
    sums = score(got, own, other, query_hidden.shape[1])
    back = lax.all_gather(sums, "shard", axis=0, axis_index_groups=groups)
    return finish(me, back, spots)


def solution(mesh):
    in_specs = (
        P(("groups", "shard"), None, None),
        P(("groups", "shard")),
        P(),
        P(),
        P(),
        P(),
        P(("groups", "shard"), None, None),
        P(("groups", "shard")),
        P("groups"),
        P(("groups", "shard"), None),
    )
    out_specs = (P(("groups", "shard"), None), P(("groups", "shard"), None))
    return jax.shard_map(
        per_device, mesh=mesh, in_specs=in_specs, out_specs=out_specs, check_vma=False
    )
```

```python
import jax
import jax.numpy as jnp
from jax import lax
from jax.experimental import pallas as pl
from jax.experimental.pallas import tpu as pltpu
from jax.sharding import PartitionSpec as P

TOPN = 10
F32 = jnp.float32
BF16 = jnp.bfloat16
NT = (((1,), (1,)), ((), ()))
VMEM = pl.BlockSpec(memory_space=pltpu.VMEM)
SMEM = pl.BlockSpec(memory_space=pltpu.SMEM)
ANY = pl.BlockSpec(memory_space=pl.ANY)


def split3(value):
    high = value.astype(BF16)
    rest = value - high.astype(F32)
    middle = rest.astype(BF16)
    low = (rest - middle.astype(F32)).astype(BF16)
    return high, middle, low


def encode_kernel(
    inverse,
    half,
    me_ref,
    lens_hbm,
    plen_hbm,
    row_hbm,
    cand_hbm,
    x_hbm,
    w1_ref,
    w2_ref,
    gain_hbm,
    embed_hbm,
    pass_hbm,
    out_ref,
    masked_hbm,
    spot_ref,
    w1_buf,
    w2_buf,
    pass_buf,
    lens_ref,
    plen_ref,
    row_ref,
    cand_ref,
    x_ref,
    gain_ref,
    embed_ref,
    table,
    table_v,
    sems,
    small_sems,
    table_sem,
    pass_sems,
):
    chunks, _, width = w1_buf.shape
    slots, lanes = table_v.shape
    query_count, token_count, width_in = x_ref.shape
    cand_count = cand_ref.shape[1]
    table_v[...] = jnp.zeros(table_v.shape, jnp.int32)
    clear = pltpu.make_async_copy(table_v, table, table_sem)
    clear.start()
    copies = []
    for c in range(chunks):
        first = pltpu.make_async_copy(w1_ref.at[:, pl.ds(c * width, width)], w1_buf.at[c], sems.at[0, c])
        second = pltpu.make_async_copy(w2_ref.at[pl.ds(c * width, width), :], w2_buf.at[c], sems.at[1, c])
        copies.append((first, second))
    small = [
        pltpu.make_async_copy(source, target, small_sems.at[n])
        for n, (source, target) in enumerate(
            (
                (row_hbm, row_ref),
                (cand_hbm, cand_ref),
                (x_hbm, x_ref),
                (plen_hbm, plen_ref),
                (lens_hbm, lens_ref),
                (gain_hbm, gain_ref),
                (embed_hbm, embed_ref),
            )
        )
    ]
    for copy in small[:4]:
        copy.start()
    batch = half // chunks
    loads, saves = [], []
    for c in range(chunks):
        rows = pl.ds(c * batch, batch)
        loads.append(pltpu.make_async_copy(pass_hbm.at[rows], pass_buf.at[rows], pass_sems.at[0, c]))
        saves.append(pltpu.make_async_copy(pass_buf.at[rows], masked_hbm.at[rows], pass_sems.at[1, c]))
    copies[0][0].start()
    copies[1][0].start()
    copies[0][1].start()
    for c in range(2, chunks):
        loads[c - 2].start()
        copies[c][0].start()
        copies[c - 1][1].start()
    copies[-1][1].start()
    loads[-2].start()
    loads[-1].start()
    for copy in small[4:]:
        copy.start()
    clear.wait()
    small[0].wait()
    small[1].wait()

    side = jnp.bitwise_and(me_ref[0], 1)

    entries = [(i, k) for k in range(cand_count) for i in range(query_count)]
    share = -(-len(entries) // (chunks + 1))

    def enter():
        for i, k in entries[:share]:
            row = row_ref[cand_ref[i, k]]
            owner = inverse(row)
            chip = jnp.right_shift(owner, 1)
            place = row - owner * half + jnp.bitwise_xor(jnp.bitwise_and(owner, 1), side) * half
            table[chip, place] = i
            spot_ref[i, k] = chip * lanes + place
        del entries[:share]

    def mask(c):
        loads[c].wait()
        for p in range(c * batch, (c + 1) * batch):
            block = pass_buf[p]
            keep = lax.broadcasted_iota(jnp.int32, block.shape, 0) < plen_ref[p]
            block = block.astype(F32)
            pass_buf[p] = jnp.where(keep, block, jnp.broadcast_to(block[0:1], block.shape)).astype(BF16)
        saves[c].start()

    small[2].wait()
    small[3].wait()
    x = x_ref[...].reshape(query_count * token_count, width_in)
    total = x.astype(F32)
    inner = active = None
    for step in range(chunks + 2):
        if step < chunks:
            copies[step][0].wait()
        if step >= 2:
            copies[step - 2][1].wait()
        if 2 <= step < chunks:
            mask(step - 2)
        enter()
        later = jnp.dot(x, w1_buf[step], preferred_element_type=F32) if step < chunks else None
        if step >= 2:
            total = total + jnp.dot(active, w2_buf[step - 2], preferred_element_type=F32)
        if 1 <= step <= chunks:
            active = (0.5 * inner * (1.0 + lax.erf(inner * (0.5 ** 0.5)))).astype(BF16)
        inner = later
        if step == chunks:
            fetch = pltpu.make_async_copy(table, table_v, table_sem)
            fetch.start()
    mask(chunks - 2)
    mask(chunks - 1)

    for copy in small[4:]:
        copy.wait()
    centered = total - jnp.mean(total, axis=-1, keepdims=True)
    variance = jnp.mean(jnp.square(centered), axis=-1, keepdims=True)
    layer_out = (centered * lax.rsqrt(variance + 1e-12) * gain_ref[...].reshape(1, width_in)).astype(BF16)
    embedded = jnp.dot(layer_out, embed_ref[...], preferred_element_type=F32)
    length = jnp.sum(jnp.square(embedded), axis=-1, keepdims=True)
    vectors = embedded * lax.rsqrt(length + 1e-06)
    token = lax.broadcasted_iota(jnp.int32, vectors.shape, 0)
    for i in range(query_count):
        padded = (token >= i * token_count + lens_ref[i]) & (token < (i + 1) * token_count)
        vectors = jnp.where(padded, 0.0, vectors)
    vectors = vectors.astype(BF16)
    fetch.wait()
    tokens = query_count * token_count
    out_ref[pl.ds(0, tokens), :] = vectors
    out_ref[pl.ds(tokens, slots), :] = table_v[...].astype(F32).astype(BF16)
    for save in saves:
        save.wait()


def divider(divisor, limit):
    magic = -(-(2 ** 20) // divisor)
    if limit * magic < 2 ** 31 and all((v * magic) >> 20 == v // divisor for v in range(limit)):
        return lambda value: jnp.right_shift(value * magic, 20)
    return lambda value: value // divisor


def encode(
    me,
    query_hidden,
    query_lengths,
    inner_weight,
    outer_weight,
    norm_gain,
    embed_weight,
    passage_vectors,
    passage_lengths,
    passage_row,
    candidates,
    slots,
):
    query_count, token_count, d = query_hidden.shape
    ff = inner_weight.shape[1]
    e = embed_weight.shape[1]
    half = passage_vectors.shape[0]
    slots = -(-slots // 16) * 16
    assert 2 * half <= e
    chunks = 6
    width = ff // chunks
    tokens = query_count * token_count
    inverse = divider(half, passage_row.shape[0])

    def kernel(*refs):
        encode_kernel(inverse, half, *refs)

    return pl.pallas_call(
        kernel,
        out_shape=(
            jax.ShapeDtypeStruct((tokens + slots, e), BF16),
            jax.ShapeDtypeStruct(passage_vectors.shape, BF16),
            jax.ShapeDtypeStruct(candidates.shape, jnp.int32),
        ),
        in_specs=[SMEM] + [ANY] * 10,
        out_specs=(VMEM, ANY, SMEM),
        scratch_shapes=[
            pltpu.VMEM((chunks, d, width), BF16),
            pltpu.VMEM((chunks, width, d), BF16),
            pltpu.VMEM(passage_vectors.shape, BF16),
            pltpu.SMEM(query_lengths.shape, jnp.int32),
            pltpu.SMEM(passage_lengths.shape, jnp.int32),
            pltpu.SMEM(passage_row.shape, jnp.int32),
            pltpu.SMEM(candidates.shape, jnp.int32),
            pltpu.VMEM(query_hidden.shape, BF16),
            pltpu.VMEM(norm_gain.shape, F32),
            pltpu.VMEM(embed_weight.shape, BF16),
            pltpu.SMEM((slots, e), jnp.int32),
            pltpu.VMEM((slots, e), jnp.int32),
            pltpu.SemaphoreType.DMA((2, chunks)),
            pltpu.SemaphoreType.DMA((7,)),
            pltpu.SemaphoreType.DMA,
            pltpu.SemaphoreType.DMA((2, chunks)),
        ],
        compiler_params=pltpu.CompilerParams(vmem_limit_bytes=60 * 2 ** 20),
        cost_estimate=pl.CostEstimate(
            flops=4 * tokens * d * ff, bytes_accessed=4 * d * ff, transcendentals=tokens * ff
        ),
        name="encode",
    )(
        me,
        query_lengths,
        passage_lengths,
        passage_row,
        candidates,
        query_hidden,
        inner_weight,
        outer_weight,
        norm_gain,
        embed_weight,
        passage_vectors,
    )


def score_kernel(slots, token_count, me_ref, pass0_ref, pass1_ref, *refs):
    got_refs = refs[:slots]
    out_ref, best_ref, index_v, index, sem = refs[slots:]
    message, lanes = got_refs[0].shape
    half = pass0_ref.shape[0]
    rows = -(-slots // 16) * 16
    tokens = message - rows
    group = min(slots, 256 // token_count)
    chip = jnp.right_shift(me_ref[0], 1)
    mine = lax.broadcasted_iota(jnp.int32, (rows, lanes), 0) == chip
    for s in range(slots):
        table = got_refs[s][pl.ds(tokens, rows), :].astype(F32)
        query = jnp.sum(jnp.where(mine, table, 0.0), axis=0, keepdims=True)
        index_v[s:s + 1, :] = query.astype(jnp.int32) * token_count
    copy = pltpu.make_async_copy(index_v, index, sem)
    copy.start()
    copy.wait()

    for side, pass_ref in enumerate((pass0_ref, pass1_ref)):

        def eight(step, carry):
            for part in range(slots // group):
                rows = []
                for j in range(8):
                    p = step * 8 + j
                    picked = jnp.concatenate(
                        [
                            got_refs[s][pl.ds(pl.multiple_of(index[s, side * half + p], token_count), token_count), :]
                            for s in range(part * group, (part + 1) * group)
                        ],
                        axis=0,
                    )
                    similar = lax.dot_general(pass_ref[p], picked, NT, preferred_element_type=F32)
                    rows.append(jnp.max(similar, axis=0, keepdims=True))
                best_ref[
                    pl.ds(pl.multiple_of(side * half + step * 8, 8), 8),
                    pl.ds(part * group * token_count, group * token_count),
                ] = jnp.concatenate(rows, axis=0)
            return carry

        lax.fori_loop(0, half // 8, eight, 0)
    wide = best_ref.shape[1]
    source = lax.broadcasted_iota(jnp.int32, (slots, wide), 0)
    column = lax.broadcasted_iota(jnp.int32, (slots, wide), 1)
    first = source * token_count
    ones = jnp.where((column >= first) & (column < first + token_count), 1.0, 0.0).astype(BF16)
    total = sum(lax.dot_general(ones, part, NT, preferred_element_type=F32) for part in split3(best_ref[...]))
    out_ref[...] = jnp.zeros(out_ref.shape, F32)
    for s in range(slots):
        out_ref[pl.ds(jnp.bitwise_xor(chip, s), 1), pl.ds(0, 2 * half)] = total[s:s + 1]


def score(me, got, own, other, token_count):
    half, plen, e = own.shape
    passage_count = 2 * half
    slots = len(got)

    def kernel(*refs):
        score_kernel(slots, token_count, *refs)

    return pl.pallas_call(
        kernel,
        out_shape=jax.ShapeDtypeStruct((slots, e), F32),
        in_specs=[SMEM] + [VMEM] * (2 + slots),
        out_specs=VMEM,
        scratch_shapes=[
            pltpu.VMEM((passage_count, slots * token_count), F32),
            pltpu.VMEM((slots, e), jnp.int32),
            pltpu.SMEM((slots, e), jnp.int32),
            pltpu.SemaphoreType.DMA,
        ],
        compiler_params=pltpu.CompilerParams(vmem_limit_bytes=12 * 2 ** 20),
        cost_estimate=pl.CostEstimate(
            flops=2 * passage_count * slots * token_count * plen * e,
            bytes_accessed=4 * own.size,
            transcendentals=0,
        ),
        name="score",
    )(me, own, other, *got)


def finish_kernel(got_ref, spot_ref, scores_ref, best_ref):
    slots, lanes = got_ref.shape
    query_count, cand_count = scores_ref.shape
    parts = split3(got_ref[...])
    slot_iota = lax.broadcasted_iota(jnp.int32, (slots, cand_count), 0) * lanes
    lane_iota = lax.broadcasted_iota(jnp.int32, (lanes, cand_count), 0)
    row_iota = lax.broadcasted_iota(jnp.int32, (cand_count, cand_count), 0)
    col_iota = lax.broadcasted_iota(jnp.int32, (cand_count, cand_count), 1)
    place = lax.broadcasted_iota(jnp.int32, (cand_count, 128), 1)
    for i in range(query_count):
        spot = spot_ref[i:i + 1, :]
        lane = jnp.bitwise_and(spot, lanes - 1)
        onehot = jnp.where(lane_iota == lane, 1.0, 0.0).astype(BF16)
        picked = sum(jnp.dot(part, onehot, preferred_element_type=F32) for part in parts)
        score_row = jnp.sum(jnp.where(slot_iota == spot - lane, picked, 0.0), axis=0, keepdims=True)
        scores_ref[i:i + 1, :] = score_row
        across = jnp.broadcast_to(score_row, (cand_count, cand_count))
        score_col = jnp.sum(jnp.where(row_iota == col_iota, across, 0.0), axis=1, keepdims=True)
        ahead = (across > score_col) | ((across == score_col) & (col_iota < row_iota))
        rank = jnp.sum(jnp.where(ahead, 1.0, 0.0), axis=1, keepdims=True).astype(jnp.int32)
        ordered = jnp.sum(jnp.where(rank == place, score_col, 0.0), axis=0, keepdims=True)
        best_ref[i:i + 1, :] = ordered[:, :TOPN]


def finish(got, spots):
    return pl.pallas_call(
        finish_kernel,
        out_shape=(
            jax.ShapeDtypeStruct(spots.shape, F32),
            jax.ShapeDtypeStruct((spots.shape[0], TOPN), F32),
        ),
        in_specs=[VMEM, VMEM],
        out_specs=(VMEM, VMEM),
        compiler_params=pltpu.CompilerParams(vmem_limit_bytes=2 ** 21),
        name="finish",
    )(got, spots)


def swap(value, distance):
    size = lax.axis_size("shard")
    return lax.ppermute(value, "shard", [(i, i ^ distance) for i in range(size)])


def per_device(
    query_hidden,
    query_lengths,
    inner_weight,
    outer_weight,
    norm_gain,
    embed_weight,
    passage_vectors,
    passage_lengths,
    passage_row,
    candidates,
):
    size = lax.axis_size("shard")
    slots = size // 2
    groups = [list(range(core, size, 2)) for core in range(2)]
    me = lax.axis_index("shard").astype(jnp.int32).reshape(1)
    message, own, spots = encode(
        me,
        query_hidden,
        query_lengths,
        inner_weight,
        outer_weight,
        norm_gain,
        embed_weight,
        passage_vectors,
        passage_lengths,
        passage_row,
        candidates,
        slots,
    )
    got = [message] + [swap(message, 2 * d) for d in range(1, slots)]
    other = swap(own, 1)
    sums = score(me, got, own, other, query_hidden.shape[1])
    back = lax.all_to_all(sums, "shard", split_axis=0, concat_axis=0, axis_index_groups=groups, tiled=True)
    return finish(back, spots)


def solution(mesh):
    in_specs = (
        P(("groups", "shard"), None, None),
        P(("groups", "shard")),
        P(),
        P(),
        P(),
        P(),
        P(("groups", "shard"), None, None),
        P(("groups", "shard")),
        P("groups"),
        P(("groups", "shard"), None),
    )
    out_specs = (P(("groups", "shard"), None), P(("groups", "shard"), None))
    return jax.shard_map(
        per_device, mesh=mesh, in_specs=in_specs, out_specs=out_specs, check_vma=False
    )
```

```python
import jax
import jax.numpy as jnp
from jax import lax
from jax.experimental import pallas as pl
from jax.experimental.pallas import tpu as pltpu
from jax.sharding import PartitionSpec as P

TOPN = 10
F32 = jnp.float32
BF16 = jnp.bfloat16
NT = (((1,), (1,)), ((), ()))
VMEM = pl.BlockSpec(memory_space=pltpu.VMEM)
SMEM = pl.BlockSpec(memory_space=pltpu.SMEM)
ANY = pl.BlockSpec(memory_space=pl.ANY)


def split3(value):
    high = value.astype(BF16)
    rest = value - high.astype(F32)
    middle = rest.astype(BF16)
    low = (rest - middle.astype(F32)).astype(BF16)
    return high, middle, low


def gelu(value):
    size = jnp.abs(value)
    inverse = 1.0 / (1.0 + (0.3275911 * 0.5 ** 0.5) * size)
    tail = 0.5 * 1.061405429
    for factor in (-1.453152027, 1.421413741, -0.284496736, 0.254829592):
        tail = tail * inverse + 0.5 * factor
    tail = tail * inverse * jnp.exp(-0.5 * value * value)
    return jnp.maximum(value, 0.0) - size * tail


def mask_into(out_ref, pass_ref, len_ref, first, count):
    def mask(p, carry):
        block = pass_ref[p]
        keep = lax.broadcasted_iota(jnp.int32, block.shape, 0) < len_ref[p]
        block = block.astype(F32)
        out_ref[p] = jnp.where(keep, block, jnp.broadcast_to(block[0:1], block.shape)).astype(BF16)
        return carry

    if count <= 8:
        for p in range(first, first + count):
            mask(p, 0)
    else:
        lax.fori_loop(first, first + count, mask, 0, unroll=8)


def encode_kernel(
    inverse,
    half,
    me_ref,
    lens_hbm,
    plen_hbm,
    row_hbm,
    cand_hbm,
    x_hbm,
    w1_ref,
    w2_ref,
    gain_hbm,
    embed_hbm,
    pass_hbm,
    out_ref,
    masked_hbm,
    spot_ref,
    w1_buf,
    w2_buf,
    pass_buf,
    lens_ref,
    plen_ref,
    row_ref,
    cand_ref,
    x_ref,
    gain_ref,
    embed_ref,
    table,
    table_v,
    sems,
    small_sems,
    table_sem,
    pass_sems,
):
    chunks, _, width = w1_buf.shape
    slots, lanes = table_v.shape
    query_count, token_count, width_in = x_ref.shape
    cand_count = cand_ref.shape[1]
    table_v[...] = jnp.zeros(table_v.shape, jnp.int32)
    clear = pltpu.make_async_copy(table_v, table, table_sem)
    clear.start()
    copies = []
    for c in range(chunks):
        first = pltpu.make_async_copy(w1_ref.at[:, pl.ds(c * width, width)], w1_buf.at[c], sems.at[0, c])
        second = pltpu.make_async_copy(w2_ref.at[pl.ds(c * width, width), :], w2_buf.at[c], sems.at[1, c])
        copies.append((first, second))
    small = [
        pltpu.make_async_copy(source, target, small_sems.at[n])
        for n, (source, target) in enumerate(
            (
                (row_hbm, row_ref),
                (cand_hbm, cand_ref),
                (x_hbm, x_ref),
                (plen_hbm, plen_ref),
                (lens_hbm, lens_ref),
                (gain_hbm, gain_ref),
                (embed_hbm, embed_ref),
            )
        )
    ]
    for copy in small[:4]:
        copy.start()
    batch = half // chunks
    loads, saves = [], []
    for c in range(chunks):
        rows = pl.ds(c * batch, batch)
        loads.append(pltpu.make_async_copy(pass_hbm.at[rows], pass_buf.at[rows], pass_sems.at[0, c]))
        saves.append(pltpu.make_async_copy(pass_buf.at[rows], masked_hbm.at[rows], pass_sems.at[1, c]))
    copies[0][0].start()
    copies[1][0].start()
    copies[0][1].start()
    for c in range(2, chunks):
        loads[c - 2].start()
        copies[c][0].start()
        copies[c - 1][1].start()
    copies[-1][1].start()
    loads[-2].start()
    loads[-1].start()
    for copy in small[4:]:
        copy.start()
    clear.wait()
    small[0].wait()
    small[1].wait()

    side = jnp.bitwise_and(me_ref[0], 1)

    entries = [(i, k) for k in range(cand_count) for i in range(query_count)]
    share = -(-len(entries) // (chunks + 1))

    def enter():
        for i, k in entries[:share]:
            row = row_ref[cand_ref[i, k]]
            owner = inverse(row)
            chip = jnp.right_shift(owner, 1)
            place = row - owner * half + jnp.bitwise_xor(jnp.bitwise_and(owner, 1), side) * half
            table[chip, place] = i
            spot_ref[i, k] = chip * lanes + place
        del entries[:share]

    def mask(c):
        loads[c].wait()
        mask_into(pass_buf, pass_buf, plen_ref, c * batch, batch)
        saves[c].start()

    small[2].wait()
    small[3].wait()
    x = x_ref[...].reshape(query_count * token_count, width_in)
    total = x.astype(F32)
    inner = active = None
    for step in range(chunks + 2):
        if step < chunks:
            copies[step][0].wait()
        if step >= 2:
            copies[step - 2][1].wait()
        if 2 <= step < chunks:
            mask(step - 2)
        enter()
        later = jnp.dot(x, w1_buf[step], preferred_element_type=F32) if step < chunks else None
        if step >= 2:
            total = total + jnp.dot(active, w2_buf[step - 2], preferred_element_type=F32)
        if 1 <= step <= chunks:
            active = gelu(inner).astype(BF16)
        inner = later
        if step == chunks:
            fetch = pltpu.make_async_copy(table, table_v, table_sem)
            fetch.start()
    mask(chunks - 2)
    mask(chunks - 1)

    for copy in small[4:]:
        copy.wait()
    centered = total - jnp.mean(total, axis=-1, keepdims=True)
    variance = jnp.mean(jnp.square(centered), axis=-1, keepdims=True)
    layer_out = (centered * lax.rsqrt(variance + 1e-12) * gain_ref[...].reshape(1, width_in)).astype(BF16)
    embedded = jnp.dot(layer_out, embed_ref[...], preferred_element_type=F32)
    length = jnp.sum(jnp.square(embedded), axis=-1, keepdims=True)
    vectors = embedded * lax.rsqrt(length + 1e-06)
    token = lax.broadcasted_iota(jnp.int32, vectors.shape, 0)
    for i in range(query_count):
        padded = (token >= i * token_count + lens_ref[i]) & (token < (i + 1) * token_count)
        vectors = jnp.where(padded, 0.0, vectors)
    vectors = vectors.astype(BF16)
    fetch.wait()
    tokens = query_count * token_count
    wanted = table_v[...].astype(F32).astype(BF16)
    for z in range(out_ref.shape[0]):
        out_ref[z, pl.ds(0, tokens), :] = vectors
        out_ref[z, pl.ds(tokens, slots), :] = wanted
    for save in saves:
        save.wait()


def divider(divisor, limit):
    magic = -(-(2 ** 20) // divisor)
    if limit * magic < 2 ** 31 and all((v * magic) >> 20 == v // divisor for v in range(limit)):
        return lambda value: jnp.right_shift(value * magic, 20)
    return lambda value: value // divisor


def encode(
    me,
    query_hidden,
    query_lengths,
    inner_weight,
    outer_weight,
    norm_gain,
    embed_weight,
    passage_vectors,
    passage_lengths,
    passage_row,
    candidates,
    slots,
    outer,
):
    query_count, token_count, d = query_hidden.shape
    ff = inner_weight.shape[1]
    e = embed_weight.shape[1]
    half = passage_vectors.shape[0]
    slots = -(-slots // 16) * 16
    assert 2 * half <= e
    chunks = 6
    width = ff // chunks
    tokens = query_count * token_count
    inverse = divider(half, passage_row.shape[0])

    def kernel(*refs):
        encode_kernel(inverse, half, *refs)

    return pl.pallas_call(
        kernel,
        out_shape=(
            jax.ShapeDtypeStruct((outer, tokens + slots, e), BF16),
            jax.ShapeDtypeStruct(passage_vectors.shape, BF16),
            jax.ShapeDtypeStruct(candidates.shape, jnp.int32),
        ),
        in_specs=[SMEM] + [ANY] * 10,
        out_specs=(VMEM, ANY, SMEM),
        scratch_shapes=[
            pltpu.VMEM((chunks, d, width), BF16),
            pltpu.VMEM((chunks, width, d), BF16),
            pltpu.VMEM(passage_vectors.shape, BF16),
            pltpu.SMEM(query_lengths.shape, jnp.int32),
            pltpu.SMEM(passage_lengths.shape, jnp.int32),
            pltpu.SMEM(passage_row.shape, jnp.int32),
            pltpu.SMEM(candidates.shape, jnp.int32),
            pltpu.VMEM(query_hidden.shape, BF16),
            pltpu.VMEM(norm_gain.shape, F32),
            pltpu.VMEM(embed_weight.shape, BF16),
            pltpu.SMEM((slots, e), jnp.int32),
            pltpu.VMEM((slots, e), jnp.int32),
            pltpu.SemaphoreType.DMA((2, chunks)),
            pltpu.SemaphoreType.DMA((7,)),
            pltpu.SemaphoreType.DMA,
            pltpu.SemaphoreType.DMA((2, chunks)),
        ],
        compiler_params=pltpu.CompilerParams(vmem_limit_bytes=60 * 2 ** 20),
        cost_estimate=pl.CostEstimate(
            flops=4 * tokens * d * ff, bytes_accessed=4 * d * ff, transcendentals=tokens * ff
        ),
        name="encode",
    )(
        me,
        query_lengths,
        passage_lengths,
        passage_row,
        candidates,
        query_hidden,
        inner_weight,
        outer_weight,
        norm_gain,
        embed_weight,
        passage_vectors,
    )


def score_kernel(inner, token_count, me_ref, len_ref, raw_ref, other_ref, *refs):
    got_refs = refs[:inner]
    out_ref, best_ref, own_ref, index_v, index, sem = refs[inner:]
    outer, message, lanes = got_refs[0].shape
    half = own_ref.shape[0]
    slots = inner * outer
    rows = -(-slots // 16) * 16
    tokens = message - rows
    group = min(slots, 256 // token_count)
    chip = jnp.right_shift(me_ref[0], 1)
    mine = lax.broadcasted_iota(jnp.int32, (rows, lanes), 0) == chip
    for s in range(slots):
        table = got_refs[s // outer][s % outer, pl.ds(tokens, rows), :].astype(F32)
        query = jnp.sum(jnp.where(mine, table, 0.0), axis=0, keepdims=True)
        index_v[s:s + 1, :] = query.astype(jnp.int32) * token_count
    copy = pltpu.make_async_copy(index_v, index, sem)
    copy.start()
    mask_into(own_ref, raw_ref, len_ref, 0, half)
    copy.wait()

    for first, pass_ref in ((half, other_ref), (0, own_ref)):

        def eight(step, carry):
            for part in range(slots // group):
                rows = []
                for j in range(8):
                    p = step * 8 + j
                    picked = jnp.concatenate(
                        [
                            got_refs[s // outer][
                                s % outer, pl.ds(pl.multiple_of(index[s, first + p], token_count), token_count), :
                            ]
                            for s in range(part * group, (part + 1) * group)
                        ],
                        axis=0,
                    )
                    similar = lax.dot_general(pass_ref[p], picked, NT, preferred_element_type=F32)
                    rows.append(jnp.max(similar, axis=0, keepdims=True))
                best_ref[
                    pl.ds(pl.multiple_of(first + step * 8, 8), 8),
                    pl.ds(part * group * token_count, group * token_count),
                ] = jnp.concatenate(rows, axis=0)
            return carry

        lax.fori_loop(0, half // 8, eight, 0)
    wide = best_ref.shape[1]
    source = lax.broadcasted_iota(jnp.int32, (slots, wide), 0)
    column = lax.broadcasted_iota(jnp.int32, (slots, wide), 1)
    start = source * token_count
    ones = jnp.where((column >= start) & (column < start + token_count), 1.0, 0.0).astype(BF16)
    total = sum(lax.dot_general(ones, part, NT, preferred_element_type=F32) for part in split3(best_ref[...]))
    out_ref[...] = jnp.zeros(out_ref.shape, F32)
    for s in range(slots):
        out_ref[s % outer, s // outer:s // outer + 1, pl.ds(0, 2 * half)] = total[s:s + 1]


def score(me, lengths, got, own, other, token_count):
    half, plen, e = own.shape
    passage_count = 2 * half
    inner = len(got)
    outer = got[0].shape[0]
    slots = inner * outer

    def kernel(*refs):
        score_kernel(inner, token_count, *refs)

    return pl.pallas_call(
        kernel,
        out_shape=jax.ShapeDtypeStruct((outer, inner, e), F32),
        in_specs=[SMEM, SMEM, VMEM, VMEM] + [VMEM] * inner,
        out_specs=VMEM,
        scratch_shapes=[
            pltpu.VMEM((passage_count, slots * token_count), F32),
            pltpu.VMEM(own.shape, BF16),
            pltpu.VMEM((slots, e), jnp.int32),
            pltpu.SMEM((slots, e), jnp.int32),
            pltpu.SemaphoreType.DMA,
        ],
        compiler_params=pltpu.CompilerParams(vmem_limit_bytes=12 * 2 ** 20),
        cost_estimate=pl.CostEstimate(
            flops=2 * passage_count * slots * token_count * plen * e,
            bytes_accessed=4 * own.size,
            transcendentals=0,
        ),
        name="score",
    )(me, lengths, own, other, *got)


def finish_kernel(inner, me_ref, *refs):
    got_refs = refs[:inner]
    spot_ref, scores_ref, best_ref = refs[inner:]
    outer, _, lanes = got_refs[0].shape
    slots = inner * outer
    query_count, cand_count = scores_ref.shape
    chip = jnp.right_shift(me_ref[0], 1)
    parts = split3(jnp.concatenate([got_refs[d][z, d:d + 1, :] for z in range(outer) for d in range(inner)], axis=0))
    slot_iota = lax.broadcasted_iota(jnp.int32, (slots, cand_count), 0) * lanes
    lane_iota = lax.broadcasted_iota(jnp.int32, (lanes, cand_count), 0)
    row_iota = lax.broadcasted_iota(jnp.int32, (cand_count, cand_count), 0)
    col_iota = lax.broadcasted_iota(jnp.int32, (cand_count, cand_count), 1)
    place = lax.broadcasted_iota(jnp.int32, (cand_count, 128), 1)
    for i in range(query_count):
        spot = jnp.bitwise_xor(spot_ref[i:i + 1, :], jnp.bitwise_and(chip, inner - 1) * lanes)
        lane = jnp.bitwise_and(spot, lanes - 1)
        onehot = jnp.where(lane_iota == lane, 1.0, 0.0).astype(BF16)
        picked = sum(jnp.dot(part, onehot, preferred_element_type=F32) for part in parts)
        score_row = jnp.sum(jnp.where(slot_iota == spot - lane, picked, 0.0), axis=0, keepdims=True)
        scores_ref[i:i + 1, :] = score_row
        across = jnp.broadcast_to(score_row, (cand_count, cand_count))
        score_col = jnp.sum(jnp.where(row_iota == col_iota, across, 0.0), axis=1, keepdims=True)
        ahead = (across > score_col) | ((across == score_col) & (col_iota < row_iota))
        rank = jnp.sum(jnp.where(ahead, 1.0, 0.0), axis=1, keepdims=True).astype(jnp.int32)
        ordered = jnp.sum(jnp.where(rank == place, score_col, 0.0), axis=0, keepdims=True)
        best_ref[i:i + 1, :] = ordered[:, :TOPN]


def finish(me, got, spots):
    inner = len(got)

    def kernel(*refs):
        finish_kernel(inner, *refs)

    return pl.pallas_call(
        kernel,
        out_shape=(
            jax.ShapeDtypeStruct(spots.shape, F32),
            jax.ShapeDtypeStruct((spots.shape[0], TOPN), F32),
        ),
        in_specs=[SMEM] + [VMEM] * (inner + 1),
        out_specs=(VMEM, VMEM),
        compiler_params=pltpu.CompilerParams(vmem_limit_bytes=2 ** 21),
        name="finish",
    )(me, *got, spots)


def swap(value, distance):
    size = lax.axis_size("shard")
    return lax.ppermute(value, "shard", [(i, i ^ distance) for i in range(size)])


def per_device(
    query_hidden,
    query_lengths,
    inner_weight,
    outer_weight,
    norm_gain,
    embed_weight,
    passage_vectors,
    passage_lengths,
    passage_row,
    candidates,
):
    size = lax.axis_size("shard")
    slots = size // 2
    inner = 1
    while 4 * inner * inner <= slots:
        inner *= 2
    outer = slots // inner
    lines = [[(z * inner + y) * 2 + core for z in range(outer)] for y in range(inner) for core in range(2)]
    me = lax.axis_index("shard").astype(jnp.int32).reshape(1)
    message, masked, spots = encode(
        me,
        query_hidden,
        query_lengths,
        inner_weight,
        outer_weight,
        norm_gain,
        embed_weight,
        passage_vectors,
        passage_lengths,
        passage_row,
        candidates,
        slots,
        outer,
    )
    other = swap(masked, 1)

    def exchange(value):
        line = lax.all_to_all(value, "shard", split_axis=0, concat_axis=0, axis_index_groups=lines, tiled=True)
        return [line] + [swap(line, 2 * d) for d in range(1, inner)]

    got = exchange(message)
    sums = score(me, passage_lengths, got, passage_vectors, other, query_hidden.shape[1])
    return finish(me, exchange(sums), spots)


def solution(mesh):
    in_specs = (
        P(("groups", "shard"), None, None),
        P(("groups", "shard")),
        P(),
        P(),
        P(),
        P(),
        P(("groups", "shard"), None, None),
        P(("groups", "shard")),
        P("groups"),
        P(("groups", "shard"), None),
    )
    out_specs = (P(("groups", "shard"), None), P(("groups", "shard"), None))
    return jax.shard_map(
        per_device, mesh=mesh, in_specs=in_specs, out_specs=out_specs, check_vma=False
    )
```

```python
import jax
import jax.numpy as jnp
from jax import lax
from jax.experimental import pallas as pl
from jax.experimental.pallas import tpu as pltpu
from jax.sharding import PartitionSpec as P

TOPN = 10
F32 = jnp.float32
BF16 = jnp.bfloat16
NT = (((1,), (1,)), ((), ()))
VMEM = pl.BlockSpec(memory_space=pltpu.VMEM)
SMEM = pl.BlockSpec(memory_space=pltpu.SMEM)
ANY = pl.BlockSpec(memory_space=pl.ANY)


def split3(value):
    high = value.astype(BF16)
    rest = value - high.astype(F32)
    middle = rest.astype(BF16)
    low = (rest - middle.astype(F32)).astype(BF16)
    return high, middle, low


def mask_into(out_ref, pass_ref, len_ref, first, count):
    def mask(p, carry):
        block = pass_ref[p]
        keep = lax.broadcasted_iota(jnp.int32, block.shape, 0) < len_ref[p]
        block = block.astype(F32)
        out_ref[p] = jnp.where(keep, block, jnp.broadcast_to(block[0:1], block.shape)).astype(BF16)
        return carry

    if count <= 8:
        for p in range(first, first + count):
            mask(p, 0)
    else:
        lax.fori_loop(first, first + count, mask, 0, unroll=8)


def encode_kernel(
    inverse,
    half,
    me_ref,
    lens_hbm,
    plen_hbm,
    row_hbm,
    cand_hbm,
    x_hbm,
    w1_ref,
    w2_ref,
    gain_hbm,
    embed_hbm,
    pass_hbm,
    out_ref,
    masked_hbm,
    spot_ref,
    w1_buf,
    w2_buf,
    pass_buf,
    lens_ref,
    plen_ref,
    row_ref,
    cand_ref,
    x_ref,
    gain_ref,
    embed_ref,
    table,
    table_v,
    sems,
    small_sems,
    table_sem,
    pass_sems,
):
    chunks, _, width = w1_buf.shape
    slots, lanes = table_v.shape
    query_count, token_count, width_in = x_ref.shape
    cand_count = cand_ref.shape[1]
    table_v[...] = jnp.zeros(table_v.shape, jnp.int32)
    clear = pltpu.make_async_copy(table_v, table, table_sem)
    clear.start()
    copies = []
    for c in range(chunks):
        first = pltpu.make_async_copy(w1_ref.at[:, pl.ds(c * width, width)], w1_buf.at[c], sems.at[0, c])
        second = pltpu.make_async_copy(w2_ref.at[pl.ds(c * width, width), :], w2_buf.at[c], sems.at[1, c])
        copies.append((first, second))
    small = [
        pltpu.make_async_copy(source, target, small_sems.at[n])
        for n, (source, target) in enumerate(
            (
                (row_hbm, row_ref),
                (cand_hbm, cand_ref),
                (x_hbm, x_ref),
                (plen_hbm, plen_ref),
                (lens_hbm, lens_ref),
                (gain_hbm, gain_ref),
                (embed_hbm, embed_ref),
            )
        )
    ]
    for copy in small[:4]:
        copy.start()
    batch = half // chunks
    loads, saves = [], []
    for c in range(chunks):
        rows = pl.ds(c * batch, batch)
        loads.append(pltpu.make_async_copy(pass_hbm.at[rows], pass_buf.at[rows], pass_sems.at[0, c]))
        saves.append(pltpu.make_async_copy(pass_buf.at[rows], masked_hbm.at[rows], pass_sems.at[1, c]))
    copies[0][0].start()
    copies[1][0].start()
    copies[0][1].start()
    for c in range(2, chunks):
        loads[c - 2].start()
        copies[c][0].start()
        copies[c - 1][1].start()
    copies[-1][1].start()
    loads[-2].start()
    loads[-1].start()
    for copy in small[4:]:
        copy.start()
    clear.wait()
    small[0].wait()
    small[1].wait()

    side = jnp.bitwise_and(me_ref[0], 1)

    entries = [(i, k) for k in range(cand_count) for i in range(query_count)]
    share = -(-len(entries) // (chunks + 1))

    def enter():
        for i, k in entries[:share]:
            row = row_ref[cand_ref[i, k]]
            owner = inverse(row)
            chip = jnp.right_shift(owner, 1)
            place = row - owner * half + jnp.bitwise_xor(jnp.bitwise_and(owner, 1), side) * half
            table[chip, place] = i
            spot_ref[i, k] = chip * lanes + place
        del entries[:share]

    def mask(c):
        loads[c].wait()
        mask_into(pass_buf, pass_buf, plen_ref, c * batch, batch)
        saves[c].start()

    small[2].wait()
    small[3].wait()
    x = x_ref[...].reshape(query_count * token_count, width_in)
    total = x.astype(F32)
    inner = active = None
    for step in range(chunks + 2):
        if step < chunks:
            copies[step][0].wait()
        if step >= 2:
            copies[step - 2][1].wait()
        if 2 <= step < chunks:
            mask(step - 2)
        enter()
        later = jnp.dot(x, w1_buf[step], preferred_element_type=F32) if step < chunks else None
        if step >= 2:
            total = total + jnp.dot(active, w2_buf[step - 2], preferred_element_type=F32)
        if 1 <= step <= chunks:
            active = (0.5 * inner * (1.0 + lax.erf(inner * (0.5 ** 0.5)))).astype(BF16)
        inner = later
        if step == chunks:
            fetch = pltpu.make_async_copy(table, table_v, table_sem)
            fetch.start()
    mask(chunks - 2)
    mask(chunks - 1)

    for copy in small[4:]:
        copy.wait()
    centered = total - jnp.mean(total, axis=-1, keepdims=True)
    variance = jnp.mean(jnp.square(centered), axis=-1, keepdims=True)
    layer_out = (centered * lax.rsqrt(variance + 1e-12) * gain_ref[...].reshape(1, width_in)).astype(BF16)
    embedded = jnp.dot(layer_out, embed_ref[...], preferred_element_type=F32)
    length = jnp.sum(jnp.square(embedded), axis=-1, keepdims=True)
    vectors = embedded * lax.rsqrt(length + 1e-06)
    token = lax.broadcasted_iota(jnp.int32, vectors.shape, 0)
    for i in range(query_count):
        padded = (token >= i * token_count + lens_ref[i]) & (token < (i + 1) * token_count)
        vectors = jnp.where(padded, 0.0, vectors)
    vectors = vectors.astype(BF16)
    fetch.wait()
    tokens = query_count * token_count
    wanted = table_v[...].astype(F32).astype(BF16)
    out_ref[pl.ds(0, tokens), :] = vectors
    out_ref[pl.ds(tokens, slots), :] = wanted
    for save in saves:
        save.wait()


def divider(divisor, limit):
    magic = -(-(2 ** 20) // divisor)
    if limit * magic < 2 ** 31 and all((v * magic) >> 20 == v // divisor for v in range(limit)):
        return lambda value: jnp.right_shift(value * magic, 20)
    return lambda value: value // divisor


def encode(
    me,
    query_hidden,
    query_lengths,
    inner_weight,
    outer_weight,
    norm_gain,
    embed_weight,
    passage_vectors,
    passage_lengths,
    passage_row,
    candidates,
    slots,
):
    query_count, token_count, d = query_hidden.shape
    ff = inner_weight.shape[1]
    e = embed_weight.shape[1]
    half = passage_vectors.shape[0]
    slots = -(-slots // 16) * 16
    assert 2 * half <= e
    chunks = 6
    width = ff // chunks
    tokens = query_count * token_count
    inverse = divider(half, passage_row.shape[0])

    def kernel(*refs):
        encode_kernel(inverse, half, *refs)

    return pl.pallas_call(
        kernel,
        out_shape=(
            jax.ShapeDtypeStruct((tokens + slots, e), BF16),
            jax.ShapeDtypeStruct(passage_vectors.shape, BF16),
            jax.ShapeDtypeStruct(candidates.shape, jnp.int32),
        ),
        in_specs=[SMEM] + [ANY] * 10,
        out_specs=(VMEM, ANY, SMEM),
        scratch_shapes=[
            pltpu.VMEM((chunks, d, width), BF16),
            pltpu.VMEM((chunks, width, d), BF16),
            pltpu.VMEM(passage_vectors.shape, BF16),
            pltpu.SMEM(query_lengths.shape, jnp.int32),
            pltpu.SMEM(passage_lengths.shape, jnp.int32),
            pltpu.SMEM(passage_row.shape, jnp.int32),
            pltpu.SMEM(candidates.shape, jnp.int32),
            pltpu.VMEM(query_hidden.shape, BF16),
            pltpu.VMEM(norm_gain.shape, F32),
            pltpu.VMEM(embed_weight.shape, BF16),
            pltpu.SMEM((slots, e), jnp.int32),
            pltpu.VMEM((slots, e), jnp.int32),
            pltpu.SemaphoreType.DMA((2, chunks)),
            pltpu.SemaphoreType.DMA((7,)),
            pltpu.SemaphoreType.DMA,
            pltpu.SemaphoreType.DMA((2, chunks)),
        ],
        compiler_params=pltpu.CompilerParams(vmem_limit_bytes=60 * 2 ** 20),
        cost_estimate=pl.CostEstimate(
            flops=4 * tokens * d * ff, bytes_accessed=4 * d * ff, transcendentals=tokens * ff
        ),
        name="encode",
    )(
        me,
        query_lengths,
        passage_lengths,
        passage_row,
        candidates,
        query_hidden,
        inner_weight,
        outer_weight,
        norm_gain,
        embed_weight,
        passage_vectors,
    )


def score_kernel(slots, token_count, me_ref, len_ref, raw_ref, other_ref, *refs):
    got_refs = refs[:slots]
    out_ref, best_ref, own_ref, index_v, index, sem = refs[slots:]
    message, lanes = got_refs[0].shape
    half = own_ref.shape[0]
    rows = -(-slots // 16) * 16
    tokens = message - rows
    group = min(slots, 256 // token_count)
    chip = jnp.right_shift(me_ref[0], 1)
    mine = lax.broadcasted_iota(jnp.int32, (rows, lanes), 0) == chip
    for s in range(slots):
        table = got_refs[s][pl.ds(tokens, rows), :].astype(F32)
        query = jnp.sum(jnp.where(mine, table, 0.0), axis=0, keepdims=True)
        index_v[s:s + 1, :] = query.astype(jnp.int32) * token_count
    copy = pltpu.make_async_copy(index_v, index, sem)
    copy.start()
    mask_into(own_ref, raw_ref, len_ref, 0, half)
    copy.wait()

    for first, pass_ref in ((half, other_ref), (0, own_ref)):

        def eight(step, carry):
            for part in range(slots // group):
                rows = []
                for j in range(8):
                    p = step * 8 + j
                    picked = jnp.concatenate(
                        [
                            got_refs[s][pl.ds(pl.multiple_of(index[s, first + p], token_count), token_count), :]
                            for s in range(part * group, (part + 1) * group)
                        ],
                        axis=0,
                    )
                    similar = lax.dot_general(pass_ref[p], picked, NT, preferred_element_type=F32)
                    rows.append(jnp.max(similar, axis=0, keepdims=True))
                best_ref[
                    pl.ds(pl.multiple_of(first + step * 8, 8), 8),
                    pl.ds(part * group * token_count, group * token_count),
                ] = jnp.concatenate(rows, axis=0)
            return carry

        lax.fori_loop(0, half // 8, eight, 0)
    wide = best_ref.shape[1]
    source = lax.broadcasted_iota(jnp.int32, (slots, wide), 0)
    column = lax.broadcasted_iota(jnp.int32, (slots, wide), 1)
    start = source * token_count
    ones = jnp.where((column >= start) & (column < start + token_count), 1.0, 0.0).astype(BF16)
    total = sum(lax.dot_general(ones, part, NT, preferred_element_type=F32) for part in split3(best_ref[...]))
    out_ref[...] = jnp.zeros(out_ref.shape, F32)
    for s in range(slots):
        out_ref[pl.ds(jnp.bitwise_xor(chip, s), 1), pl.ds(0, 2 * half)] = total[s:s + 1]


def score(me, lengths, got, own, other, token_count):
    half, plen, e = own.shape
    passage_count = 2 * half
    slots = len(got)

    def kernel(*refs):
        score_kernel(slots, token_count, *refs)

    return pl.pallas_call(
        kernel,
        out_shape=jax.ShapeDtypeStruct((slots, e), F32),
        in_specs=[SMEM, SMEM, VMEM, VMEM] + [VMEM] * slots,
        out_specs=VMEM,
        scratch_shapes=[
            pltpu.VMEM((passage_count, slots * token_count), F32),
            pltpu.VMEM(own.shape, BF16),
            pltpu.VMEM((slots, e), jnp.int32),
            pltpu.SMEM((slots, e), jnp.int32),
            pltpu.SemaphoreType.DMA,
        ],
        compiler_params=pltpu.CompilerParams(vmem_limit_bytes=12 * 2 ** 20),
        cost_estimate=pl.CostEstimate(
            flops=2 * passage_count * slots * token_count * plen * e,
            bytes_accessed=4 * own.size,
            transcendentals=0,
        ),
        name="score",
    )(me, lengths, own, other, *got)


def finish_kernel(got_ref, spot_ref, scores_ref, best_ref):
    slots, lanes = got_ref.shape
    query_count, cand_count = scores_ref.shape
    parts = split3(got_ref[...])
    slot_iota = lax.broadcasted_iota(jnp.int32, (slots, cand_count), 0) * lanes
    lane_iota = lax.broadcasted_iota(jnp.int32, (lanes, cand_count), 0)
    row_iota = lax.broadcasted_iota(jnp.int32, (cand_count, cand_count), 0)
    col_iota = lax.broadcasted_iota(jnp.int32, (cand_count, cand_count), 1)
    place = lax.broadcasted_iota(jnp.int32, (cand_count, 128), 1)
    for i in range(query_count):
        spot = spot_ref[i:i + 1, :]
        lane = jnp.bitwise_and(spot, lanes - 1)
        onehot = jnp.where(lane_iota == lane, 1.0, 0.0).astype(BF16)
        picked = sum(jnp.dot(part, onehot, preferred_element_type=F32) for part in parts)
        score_row = jnp.sum(jnp.where(slot_iota == spot - lane, picked, 0.0), axis=0, keepdims=True)
        scores_ref[i:i + 1, :] = score_row
        across = jnp.broadcast_to(score_row, (cand_count, cand_count))
        score_col = jnp.sum(jnp.where(row_iota == col_iota, across, 0.0), axis=1, keepdims=True)
        ahead = (across > score_col) | ((across == score_col) & (col_iota < row_iota))
        rank = jnp.sum(jnp.where(ahead, 1.0, 0.0), axis=1, keepdims=True).astype(jnp.int32)
        ordered = jnp.sum(jnp.where(rank == place, score_col, 0.0), axis=0, keepdims=True)
        best_ref[i:i + 1, :] = ordered[:, :TOPN]


def finish(got, spots):
    return pl.pallas_call(
        finish_kernel,
        out_shape=(
            jax.ShapeDtypeStruct(spots.shape, F32),
            jax.ShapeDtypeStruct((spots.shape[0], TOPN), F32),
        ),
        in_specs=[VMEM, VMEM],
        out_specs=(VMEM, VMEM),
        compiler_params=pltpu.CompilerParams(vmem_limit_bytes=2 ** 21),
        name="finish",
    )(got, spots)


def swap(value, distance):
    size = lax.axis_size("shard")
    return lax.ppermute(value, "shard", [(i, i ^ distance) for i in range(size)])


def per_device(
    query_hidden,
    query_lengths,
    inner_weight,
    outer_weight,
    norm_gain,
    embed_weight,
    passage_vectors,
    passage_lengths,
    passage_row,
    candidates,
):
    size = lax.axis_size("shard")
    slots = size // 2
    inner = 1
    while 4 * inner * inner <= slots:
        inner *= 2
    groups = [list(range(core, size, 2)) for core in range(2)]
    me = lax.axis_index("shard").astype(jnp.int32).reshape(1)
    message, masked, spots = encode(
        me,
        query_hidden,
        query_lengths,
        inner_weight,
        outer_weight,
        norm_gain,
        embed_weight,
        passage_vectors,
        passage_lengths,
        passage_row,
        candidates,
        slots,
    )
    other = swap(masked, 1)

    line = [message] + [swap(message, 2 * d) for d in range(slots - inner, 0, -inner)][::-1]
    got = [line[s // inner] if s % inner == 0 else swap(line[s // inner], 2 * (s % inner)) for s in range(slots)]
    sums = score(me, passage_lengths, got, passage_vectors, other, query_hidden.shape[1])
    back = lax.all_to_all(sums, "shard", split_axis=0, concat_axis=0, axis_index_groups=groups, tiled=True)
    return finish(back, spots)


def solution(mesh):
    in_specs = (
        P(("groups", "shard"), None, None),
        P(("groups", "shard")),
        P(),
        P(),
        P(),
        P(),
        P(("groups", "shard"), None, None),
        P(("groups", "shard")),
        P("groups"),
        P(("groups", "shard"), None),
    )
    out_specs = (P(("groups", "shard"), None), P(("groups", "shard"), None))
    return jax.shard_map(
        per_device, mesh=mesh, in_specs=in_specs, out_specs=out_specs, check_vma=False
    )
```

```python
import jax
import jax.numpy as jnp
from jax import lax
from jax.experimental import pallas as pl
from jax.experimental.pallas import tpu as pltpu
from jax.sharding import PartitionSpec as P

TOPN = 10
F32 = jnp.float32
BF16 = jnp.bfloat16
NT = (((1,), (1,)), ((), ()))
VMEM = pl.BlockSpec(memory_space=pltpu.VMEM)
SMEM = pl.BlockSpec(memory_space=pltpu.SMEM)
ANY = pl.BlockSpec(memory_space=pl.ANY)


def split3(value):
    high = value.astype(BF16)
    rest = value - high.astype(F32)
    middle = rest.astype(BF16)
    low = (rest - middle.astype(F32)).astype(BF16)
    return high, middle, low


def mask_into(out_ref, pass_ref, len_ref, first, count):
    def mask(p, carry):
        block = pass_ref[p]
        keep = lax.broadcasted_iota(jnp.int32, block.shape, 0) < len_ref[p]
        block = block.astype(F32)
        out_ref[p] = jnp.where(keep, block, jnp.broadcast_to(block[0:1], block.shape)).astype(BF16)
        return carry

    if count <= 8:
        for p in range(first, first + count):
            mask(p, 0)
    else:
        lax.fori_loop(first, first + count, mask, 0, unroll=8)


def encode_kernel(
    half,
    me_ref,
    lens_hbm,
    plen_hbm,
    row_hbm,
    cand_hbm,
    x_hbm,
    w1_ref,
    w2_ref,
    gain_hbm,
    embed_hbm,
    pass_hbm,
    out_ref,
    masked_hbm,
    spot_ref,
    w1_buf,
    w2_buf,
    pass_buf,
    lens_ref,
    plen_ref,
    row_ref,
    place_ref,
    cand_ref,
    x_ref,
    gain_ref,
    embed_ref,
    table,
    table_v,
    sems,
    small_sems,
    place_sem,
    table_sem,
    pass_sems,
):
    chunks, _, width = w1_buf.shape
    slots, lanes = table_v.shape
    query_count, token_count, width_in = x_ref.shape
    cand_count = cand_ref.shape[1]
    table_v[...] = jnp.zeros(table_v.shape, jnp.int32)
    clear = pltpu.make_async_copy(table_v, table, table_sem)
    clear.start()
    copies = []
    for c in range(chunks):
        first = pltpu.make_async_copy(w1_ref.at[:, pl.ds(c * width, width)], w1_buf.at[c], sems.at[0, c])
        second = pltpu.make_async_copy(w2_ref.at[pl.ds(c * width, width), :], w2_buf.at[c], sems.at[1, c])
        copies.append((first, second))
    small = [
        pltpu.make_async_copy(source, target, small_sems.at[n])
        for n, (source, target) in enumerate(
            (
                (x_hbm, x_ref),
                (row_hbm, row_ref),
                (cand_hbm, cand_ref),
                (plen_hbm, plen_ref),
                (lens_hbm, lens_ref),
                (gain_hbm, gain_ref),
                (embed_hbm, embed_ref),
            )
        )
    ]
    for copy in small[:3]:
        copy.start()
    copies[0][0].start()
    small[3].start()
    batch = half // chunks
    loads, saves = [], []
    for c in range(chunks):
        rows = pl.ds(c * batch, batch)
        loads.append(pltpu.make_async_copy(pass_hbm.at[rows], pass_buf.at[rows], pass_sems.at[0, c]))
        saves.append(pltpu.make_async_copy(pass_buf.at[rows], masked_hbm.at[rows], pass_sems.at[1, c]))
    copies[1][0].start()
    copies[0][1].start()
    for c in range(2, chunks):
        loads[c - 2].start()
        copies[c][0].start()
        copies[c - 1][1].start()
    copies[-1][1].start()
    loads[-2].start()
    loads[-1].start()
    for copy in small[4:]:
        copy.start()
    clear.wait()
    side = jnp.bitwise_and(me_ref[0], 1)
    small[1].wait()
    row = row_ref[...]
    owner = jnp.floor((row.astype(F32) + 0.5) * (1.0 / half)).astype(jnp.int32)
    opposite = jnp.bitwise_xor(jnp.bitwise_and(owner, 1), side)
    row_ref[...] = jnp.right_shift(owner, 1) * lanes + row - owner * half + opposite * half
    placed = pltpu.make_async_copy(row_ref, place_ref, place_sem)
    placed.start()
    small[2].wait()
    placed.wait()

    entries = [(i, k) for k in range(cand_count) for i in range(query_count)]
    share = -(-len(entries) // (chunks + 1))

    def enter():
        for i, k in entries[:share]:
            spot = place_ref[cand_ref[i, k]]
            table[jnp.right_shift(spot, 7), jnp.bitwise_and(spot, 127)] = i
            spot_ref[i, k] = spot
        del entries[:share]

    def mask(c):
        loads[c].wait()
        mask_into(pass_buf, pass_buf, plen_ref, c * batch, batch)
        saves[c].start()

    small[0].wait()
    small[3].wait()
    x = x_ref[...].reshape(query_count * token_count, width_in)
    total = x.astype(F32)
    inner = active = None
    for step in range(chunks + 2):
        if step < chunks:
            copies[step][0].wait()
        if step >= 2:
            copies[step - 2][1].wait()
        if 2 <= step < chunks:
            mask(step - 2)
        enter()
        later = jnp.dot(x, w1_buf[step], preferred_element_type=F32) if step < chunks else None
        if step >= 2:
            total = total + jnp.dot(active, w2_buf[step - 2], preferred_element_type=F32)
        if 1 <= step <= chunks:
            active = (0.5 * inner * (1.0 + lax.erf(inner * (0.5 ** 0.5)))).astype(BF16)
        inner = later
        if step == chunks:
            fetch = pltpu.make_async_copy(table, table_v, table_sem)
            fetch.start()
    mask(chunks - 2)
    mask(chunks - 1)

    for copy in small[4:]:
        copy.wait()
    centered = total - jnp.mean(total, axis=-1, keepdims=True)
    variance = jnp.mean(jnp.square(centered), axis=-1, keepdims=True)
    layer_out = (centered * lax.rsqrt(variance + 1e-12) * gain_ref[...].reshape(1, width_in)).astype(BF16)
    embedded = jnp.dot(layer_out, embed_ref[...], preferred_element_type=F32)
    length = jnp.sum(jnp.square(embedded), axis=-1, keepdims=True)
    vectors = embedded * lax.rsqrt(length + 1e-06)
    token = lax.broadcasted_iota(jnp.int32, vectors.shape, 0)
    for i in range(query_count):
        padded = (token >= i * token_count + lens_ref[i]) & (token < (i + 1) * token_count)
        vectors = jnp.where(padded, 0.0, vectors)
    vectors = vectors.astype(BF16)
    fetch.wait()
    tokens = query_count * token_count
    wanted = table_v[...].astype(F32).astype(BF16)
    out_ref[pl.ds(0, tokens), :] = vectors
    out_ref[pl.ds(tokens, slots), :] = wanted
    for save in saves:
        save.wait()


def encode(
    me,
    query_hidden,
    query_lengths,
    inner_weight,
    outer_weight,
    norm_gain,
    embed_weight,
    passage_vectors,
    passage_lengths,
    passage_row,
    candidates,
    slots,
):
    query_count, token_count, d = query_hidden.shape
    ff = inner_weight.shape[1]
    e = embed_weight.shape[1]
    half = passage_vectors.shape[0]
    slots = -(-slots // 16) * 16
    assert 2 * half <= e == 128
    chunks = 6
    width = ff // chunks
    tokens = query_count * token_count

    def kernel(*refs):
        encode_kernel(half, *refs)

    return pl.pallas_call(
        kernel,
        out_shape=(
            jax.ShapeDtypeStruct((tokens + slots, e), BF16),
            jax.ShapeDtypeStruct(passage_vectors.shape, BF16),
            jax.ShapeDtypeStruct(candidates.shape, jnp.int32),
        ),
        in_specs=[SMEM] + [ANY] * 10,
        out_specs=(VMEM, ANY, SMEM),
        scratch_shapes=[
            pltpu.VMEM((chunks, d, width), BF16),
            pltpu.VMEM((chunks, width, d), BF16),
            pltpu.VMEM(passage_vectors.shape, BF16),
            pltpu.SMEM(query_lengths.shape, jnp.int32),
            pltpu.SMEM(passage_lengths.shape, jnp.int32),
            pltpu.VMEM(passage_row.shape, jnp.int32),
            pltpu.SMEM(passage_row.shape, jnp.int32),
            pltpu.SMEM(candidates.shape, jnp.int32),
            pltpu.VMEM(query_hidden.shape, BF16),
            pltpu.VMEM(norm_gain.shape, F32),
            pltpu.VMEM(embed_weight.shape, BF16),
            pltpu.SMEM((slots, e), jnp.int32),
            pltpu.VMEM((slots, e), jnp.int32),
            pltpu.SemaphoreType.DMA((2, chunks)),
            pltpu.SemaphoreType.DMA((7,)),
            pltpu.SemaphoreType.DMA,
            pltpu.SemaphoreType.DMA,
            pltpu.SemaphoreType.DMA((2, chunks)),
        ],
        compiler_params=pltpu.CompilerParams(vmem_limit_bytes=60 * 2 ** 20),
        cost_estimate=pl.CostEstimate(
            flops=4 * tokens * d * ff, bytes_accessed=4 * d * ff, transcendentals=tokens * ff
        ),
        name="encode",
    )(
        me,
        query_lengths,
        passage_lengths,
        passage_row,
        candidates,
        query_hidden,
        inner_weight,
        outer_weight,
        norm_gain,
        embed_weight,
        passage_vectors,
    )


def mask_kernel(len_ref, pass_ref, *refs):
    mask_into(refs[-1], pass_ref, len_ref, 0, pass_ref.shape[0])


def mask(lengths, passages, late):
    return pl.pallas_call(
        mask_kernel,
        out_shape=jax.ShapeDtypeStruct(passages.shape, BF16),
        in_specs=[SMEM, VMEM, VMEM],
        out_specs=VMEM,
        compiler_params=pltpu.CompilerParams(vmem_limit_bytes=2 ** 22),
        cost_estimate=pl.CostEstimate(flops=8 * passages.size, bytes_accessed=4 * passages.size, transcendentals=0),
        name="mask",
    )(lengths, passages, late)


def score_kernel(slots, token_count, me_ref, own_ref, other_ref, *refs):
    got_refs = refs[:slots]
    out_ref, best_ref, index_v, index, sem = refs[slots:]
    message, lanes = got_refs[0].shape
    half = own_ref.shape[0]
    rows = -(-slots // 16) * 16
    tokens = message - rows
    group = min(slots, 256 // token_count)
    chip = jnp.right_shift(me_ref[0], 1)
    mine = lax.broadcasted_iota(jnp.int32, (rows, lanes), 0) == chip
    for s in range(slots):
        table = got_refs[s][pl.ds(tokens, rows), :].astype(F32)
        query = jnp.sum(jnp.where(mine, table, 0.0), axis=0, keepdims=True)
        index_v[s:s + 1, :] = query.astype(jnp.int32) * token_count
    copy = pltpu.make_async_copy(index_v, index, sem)
    copy.start()
    copy.wait()

    for first, pass_ref in ((half, other_ref), (0, own_ref)):

        def eight(step, carry):
            for part in range(slots // group):
                rows = []
                for j in range(8):
                    p = step * 8 + j
                    picked = jnp.concatenate(
                        [
                            got_refs[s][pl.ds(pl.multiple_of(index[s, first + p], token_count), token_count), :]
                            for s in range(part * group, (part + 1) * group)
                        ],
                        axis=0,
                    )
                    similar = lax.dot_general(pass_ref[p], picked, NT, preferred_element_type=F32)
                    rows.append(jnp.max(similar, axis=0, keepdims=True))
                best_ref[
                    pl.ds(pl.multiple_of(first + step * 8, 8), 8),
                    pl.ds(part * group * token_count, group * token_count),
                ] = jnp.concatenate(rows, axis=0)
            return carry

        lax.fori_loop(0, half // 8, eight, 0)
    wide = best_ref.shape[1]
    source = lax.broadcasted_iota(jnp.int32, (slots, wide), 0)
    column = lax.broadcasted_iota(jnp.int32, (slots, wide), 1)
    start = source * token_count
    ones = jnp.where((column >= start) & (column < start + token_count), 1.0, 0.0).astype(BF16)
    total = sum(lax.dot_general(ones, part, NT, preferred_element_type=F32) for part in split3(best_ref[...]))
    out_ref[...] = jnp.zeros(out_ref.shape, F32)
    for s in range(slots):
        out_ref[pl.ds(jnp.bitwise_xor(chip, s), 1), pl.ds(0, 2 * half)] = total[s:s + 1]


def score(me, got, own, other, token_count):
    half, plen, e = own.shape
    passage_count = 2 * half
    slots = len(got)

    def kernel(*refs):
        score_kernel(slots, token_count, *refs)

    return pl.pallas_call(
        kernel,
        out_shape=jax.ShapeDtypeStruct((slots, e), F32),
        in_specs=[SMEM, VMEM, VMEM] + [VMEM] * slots,
        out_specs=VMEM,
        scratch_shapes=[
            pltpu.VMEM((passage_count, slots * token_count), F32),
            pltpu.VMEM((slots, e), jnp.int32),
            pltpu.SMEM((slots, e), jnp.int32),
            pltpu.SemaphoreType.DMA,
        ],
        compiler_params=pltpu.CompilerParams(vmem_limit_bytes=12 * 2 ** 20),
        cost_estimate=pl.CostEstimate(
            flops=2 * passage_count * slots * token_count * plen * e,
            bytes_accessed=4 * own.size,
            transcendentals=0,
        ),
        name="score",
    )(me, own, other, *got)


def finish_kernel(got_ref, spot_ref, scores_ref, best_ref):
    slots, lanes = got_ref.shape
    query_count, cand_count = scores_ref.shape
    parts = split3(got_ref[...])
    slot_iota = lax.broadcasted_iota(jnp.int32, (slots, cand_count), 0) * lanes
    lane_iota = lax.broadcasted_iota(jnp.int32, (lanes, cand_count), 0)
    row_iota = lax.broadcasted_iota(jnp.int32, (cand_count, cand_count), 0)
    col_iota = lax.broadcasted_iota(jnp.int32, (cand_count, cand_count), 1)
    place = lax.broadcasted_iota(jnp.int32, (cand_count, 128), 1)
    for i in range(query_count):
        spot = spot_ref[i:i + 1, :]
        lane = jnp.bitwise_and(spot, lanes - 1)
        onehot = jnp.where(lane_iota == lane, 1.0, 0.0).astype(BF16)
        picked = sum(jnp.dot(part, onehot, preferred_element_type=F32) for part in parts)
        score_row = jnp.sum(jnp.where(slot_iota == spot - lane, picked, 0.0), axis=0, keepdims=True)
        scores_ref[i:i + 1, :] = score_row
        across = jnp.broadcast_to(score_row, (cand_count, cand_count))
        score_col = jnp.sum(jnp.where(row_iota == col_iota, across, 0.0), axis=1, keepdims=True)
        ahead = (across > score_col) | ((across == score_col) & (col_iota < row_iota))
        rank = jnp.sum(jnp.where(ahead, 1.0, 0.0), axis=1, keepdims=True).astype(jnp.int32)
        ordered = jnp.sum(jnp.where(rank == place, score_col, 0.0), axis=0, keepdims=True)
        best_ref[i:i + 1, :] = ordered[:, :TOPN]


def finish(got, spots):
    return pl.pallas_call(
        finish_kernel,
        out_shape=(
            jax.ShapeDtypeStruct(spots.shape, F32),
            jax.ShapeDtypeStruct((spots.shape[0], TOPN), F32),
        ),
        in_specs=[VMEM, VMEM],
        out_specs=(VMEM, VMEM),
        compiler_params=pltpu.CompilerParams(vmem_limit_bytes=2 ** 21),
        name="finish",
    )(got, spots)


def swap(value, distance):
    size = lax.axis_size("shard")
    return lax.ppermute(value, "shard", [(i, i ^ distance) for i in range(size)])


def per_device(
    query_hidden,
    query_lengths,
    inner_weight,
    outer_weight,
    norm_gain,
    embed_weight,
    passage_vectors,
    passage_lengths,
    passage_row,
    candidates,
):
    size = lax.axis_size("shard")
    slots = size // 2
    inner = 1
    while 4 * inner * inner <= slots:
        inner *= 2
    groups = [list(range(core, size, 2)) for core in range(2)]
    me = lax.axis_index("shard").astype(jnp.int32).reshape(1)
    message, masked, spots = encode(
        me,
        query_hidden,
        query_lengths,
        inner_weight,
        outer_weight,
        norm_gain,
        embed_weight,
        passage_vectors,
        passage_lengths,
        passage_row,
        candidates,
        slots,
    )
    other = swap(masked, 1)

    line = [message] + [swap(message, 2 * d) for d in range(slots - inner, 0, -inner)][::-1]
    got = [line[s // inner] if s % inner == 0 else swap(line[s // inner], 2 * (s % inner)) for s in range(slots)]
    own = mask(passage_lengths, passage_vectors, got[inner + 1])
    sums = score(me, got, own, other, query_hidden.shape[1])
    back = lax.all_to_all(sums, "shard", split_axis=0, concat_axis=0, axis_index_groups=groups, tiled=True)
    return finish(back, spots)


def solution(mesh):
    in_specs = (
        P(("groups", "shard"), None, None),
        P(("groups", "shard")),
        P(),
        P(),
        P(),
        P(),
        P(("groups", "shard"), None, None),
        P(("groups", "shard")),
        P("groups"),
        P(("groups", "shard"), None),
    )
    out_specs = (P(("groups", "shard"), None), P(("groups", "shard"), None))
    return jax.shard_map(
        per_device, mesh=mesh, in_specs=in_specs, out_specs=out_specs, check_vma=False
    )
```

```python
import jax
import jax.numpy as jnp
from jax import lax
from jax.experimental import pallas as pl
from jax.experimental.pallas import tpu as pltpu
from jax.sharding import PartitionSpec as P

TOPN = 10
F32 = jnp.float32
BF16 = jnp.bfloat16
NT = (((1,), (1,)), ((), ()))
VMEM = pl.BlockSpec(memory_space=pltpu.VMEM)
SMEM = pl.BlockSpec(memory_space=pltpu.SMEM)
ANY = pl.BlockSpec(memory_space=pl.ANY)


def split3(value):
    high = value.astype(BF16)
    rest = value - high.astype(F32)
    middle = rest.astype(BF16)
    low = (rest - middle.astype(F32)).astype(BF16)
    return high, middle, low


def mask_into(out_ref, pass_ref, len_ref, first, count):
    def mask(p, carry):
        block = pass_ref[p]
        keep = lax.broadcasted_iota(jnp.int32, block.shape, 0) < len_ref[p]
        block = block.astype(F32)
        out_ref[p] = jnp.where(keep, block, jnp.broadcast_to(block[0:1], block.shape)).astype(BF16)
        return carry

    if count <= 8:
        for p in range(first, first + count):
            mask(p, 0)
    else:
        lax.fori_loop(first, first + count, mask, 0, unroll=8)


def encode_kernel(
    half,
    color,
    me_ref,
    lens_hbm,
    plen_hbm,
    row_hbm,
    cand_hbm,
    x_hbm,
    w1_ref,
    w2_ref,
    gain_hbm,
    embed_hbm,
    pass_hbm,
    out_ref,
    masked_hbm,
    spot_ref,
    w1_buf,
    w2_buf,
    pass_buf,
    lens_ref,
    plen_ref,
    row_ref,
    place_ref,
    cand_ref,
    x_ref,
    gain_ref,
    embed_ref,
    table,
    table_v,
    sems,
    small_sems,
    place_sem,
    table_sem,
    pass_sems,
):
    chunks, _, width = w1_buf.shape
    slots, lanes = table_v.shape
    query_count, token_count, width_in = x_ref.shape
    cand_count = cand_ref.shape[1]
    table_v[...] = jnp.zeros(table_v.shape, jnp.int32)
    clear = pltpu.make_async_copy(table_v, table, table_sem)
    clear.start()
    copies = []
    for c in range(chunks):
        first = pltpu.make_async_copy(w1_ref.at[:, pl.ds(c * width, width)], w1_buf.at[c], sems.at[0, c])
        second = pltpu.make_async_copy(w2_ref.at[pl.ds(c * width, width), :], w2_buf.at[c], sems.at[1, c])
        copies.append((first, second))
    small = [
        pltpu.make_async_copy(source, target, small_sems.at[n])
        for n, (source, target) in enumerate(
            (
                (x_hbm, x_ref),
                (row_hbm, row_ref),
                (cand_hbm, cand_ref),
                (plen_hbm, plen_ref),
                (lens_hbm, lens_ref),
                (gain_hbm, gain_ref),
                (embed_hbm, embed_ref),
            )
        )
    ]
    for copy in small[:3]:
        copy.start()
    copies[0][0].start()
    small[3].start()
    batch = half // chunks
    loads, saves = [], []
    for c in range(chunks):
        rows = pl.ds(c * batch, batch)
        loads.append(pltpu.make_async_copy(pass_hbm.at[rows], pass_buf.at[rows], pass_sems.at[0, c]))
        saves.append(pltpu.make_async_copy(pass_buf.at[rows], masked_hbm.at[rows], pass_sems.at[1, c]))
    copies[1][0].start()
    copies[0][1].start()
    for c in range(2, chunks):
        loads[c - 2].start()
        copies[c][0].start()
        copies[c - 1][1].start()
    copies[-1][1].start()
    loads[-2].start()
    loads[-1].start()
    for copy in small[4:]:
        copy.start()
    clear.wait()
    small[1].wait()
    row = row_ref[...]
    owner = jnp.floor((row.astype(F32) + 0.5) * (1.0 / half)).astype(jnp.int32)
    opposite = jnp.bitwise_xor(color(owner), color(me_ref[0]))
    row_ref[...] = jnp.right_shift(owner, 1) * lanes + row - owner * half + opposite * half
    placed = pltpu.make_async_copy(row_ref, place_ref, place_sem)
    placed.start()

    entries = [(i, k) for k in range(cand_count) for i in range(query_count)]
    share = -(-len(entries) // chunks)

    def enter():
        for i, k in entries[:share]:
            spot = place_ref[cand_ref[i, k]]
            table[jnp.right_shift(spot, 7), jnp.bitwise_and(spot, 127)] = i
            spot_ref[i, k] = spot
        del entries[:share]

    def mask(c):
        loads[c].wait()
        mask_into(pass_buf, pass_buf, plen_ref, c * batch, batch)
        saves[c].start()

    small[0].wait()
    small[3].wait()
    x = x_ref[...].reshape(query_count * token_count, width_in)
    total = x.astype(F32)
    inner = active = None
    for step in range(chunks + 2):
        if step < chunks:
            copies[step][0].wait()
        if step >= 2:
            copies[step - 2][1].wait()
        if 2 <= step < chunks:
            mask(step - 2)
        if step == 1:
            small[2].wait()
            placed.wait()
        if step >= 1:
            enter()
        later = jnp.dot(x, w1_buf[step], preferred_element_type=F32) if step < chunks else None
        if step >= 2:
            total = total + jnp.dot(active, w2_buf[step - 2], preferred_element_type=F32)
        if 1 <= step <= chunks:
            active = (0.5 * inner * (1.0 + lax.erf(inner * (0.5 ** 0.5)))).astype(BF16)
        inner = later
        if step == chunks:
            fetch = pltpu.make_async_copy(table, table_v, table_sem)
            fetch.start()
    mask(chunks - 2)
    mask(chunks - 1)

    for copy in small[4:]:
        copy.wait()
    centered = total - jnp.mean(total, axis=-1, keepdims=True)
    variance = jnp.mean(jnp.square(centered), axis=-1, keepdims=True)
    layer_out = (centered * lax.rsqrt(variance + 1e-12) * gain_ref[...].reshape(1, width_in)).astype(BF16)
    embedded = jnp.dot(layer_out, embed_ref[...], preferred_element_type=F32)
    length = jnp.sum(jnp.square(embedded), axis=-1, keepdims=True)
    vectors = embedded * lax.rsqrt(length + 1e-06)
    token = lax.broadcasted_iota(jnp.int32, vectors.shape, 0)
    for i in range(query_count):
        padded = (token >= i * token_count + lens_ref[i]) & (token < (i + 1) * token_count)
        vectors = jnp.where(padded, 0.0, vectors)
    vectors = vectors.astype(BF16)
    fetch.wait()
    tokens = query_count * token_count
    wanted = table_v[...].astype(F32).astype(BF16)
    out_ref[pl.ds(0, tokens), :] = vectors
    out_ref[pl.ds(tokens, slots), :] = wanted
    for save in saves:
        save.wait()


def encode(
    me,
    query_hidden,
    query_lengths,
    inner_weight,
    outer_weight,
    norm_gain,
    embed_weight,
    passage_vectors,
    passage_lengths,
    passage_row,
    candidates,
    slots,
    color,
):
    query_count, token_count, d = query_hidden.shape
    ff = inner_weight.shape[1]
    e = embed_weight.shape[1]
    half = passage_vectors.shape[0]
    slots = -(-slots // 16) * 16
    assert 2 * half <= e == 128
    chunks = 6
    width = ff // chunks
    tokens = query_count * token_count

    def kernel(*refs):
        encode_kernel(half, color, *refs)

    return pl.pallas_call(
        kernel,
        out_shape=(
            jax.ShapeDtypeStruct((tokens + slots, e), BF16),
            jax.ShapeDtypeStruct(passage_vectors.shape, BF16),
            jax.ShapeDtypeStruct(candidates.shape, jnp.int32),
        ),
        in_specs=[SMEM] + [ANY] * 10,
        out_specs=(VMEM, ANY, SMEM),
        scratch_shapes=[
            pltpu.VMEM((chunks, d, width), BF16),
            pltpu.VMEM((chunks, width, d), BF16),
            pltpu.VMEM(passage_vectors.shape, BF16),
            pltpu.SMEM(query_lengths.shape, jnp.int32),
            pltpu.SMEM(passage_lengths.shape, jnp.int32),
            pltpu.VMEM(passage_row.shape, jnp.int32),
            pltpu.SMEM(passage_row.shape, jnp.int32),
            pltpu.SMEM(candidates.shape, jnp.int32),
            pltpu.VMEM(query_hidden.shape, BF16),
            pltpu.VMEM(norm_gain.shape, F32),
            pltpu.VMEM(embed_weight.shape, BF16),
            pltpu.SMEM((slots, e), jnp.int32),
            pltpu.VMEM((slots, e), jnp.int32),
            pltpu.SemaphoreType.DMA((2, chunks)),
            pltpu.SemaphoreType.DMA((7,)),
            pltpu.SemaphoreType.DMA,
            pltpu.SemaphoreType.DMA,
            pltpu.SemaphoreType.DMA((2, chunks)),
        ],
        compiler_params=pltpu.CompilerParams(vmem_limit_bytes=60 * 2 ** 20),
        cost_estimate=pl.CostEstimate(
            flops=4 * tokens * d * ff, bytes_accessed=4 * d * ff, transcendentals=tokens * ff
        ),
        name="encode",
    )(
        me,
        query_lengths,
        passage_lengths,
        passage_row,
        candidates,
        query_hidden,
        inner_weight,
        outer_weight,
        norm_gain,
        embed_weight,
        passage_vectors,
    )


def mask_kernel(len_ref, pass_ref, *refs):
    mask_into(refs[-1], pass_ref, len_ref, 0, pass_ref.shape[0])


def mask(lengths, passages, late):
    return pl.pallas_call(
        mask_kernel,
        out_shape=jax.ShapeDtypeStruct(passages.shape, BF16),
        in_specs=[SMEM, VMEM, VMEM],
        out_specs=VMEM,
        compiler_params=pltpu.CompilerParams(vmem_limit_bytes=2 ** 22),
        cost_estimate=pl.CostEstimate(flops=8 * passages.size, bytes_accessed=4 * passages.size, transcendentals=0),
        name="mask",
    )(lengths, passages, late)


def score_kernel(slots, token_count, me_ref, own_ref, other_ref, *refs):
    got_refs = refs[:slots]
    out_ref, best_ref, index_v, index, sem = refs[slots:]
    message, lanes = got_refs[0].shape
    half = own_ref.shape[0]
    rows = -(-slots // 16) * 16
    tokens = message - rows
    group = min(slots, 256 // token_count)
    chip = jnp.right_shift(me_ref[0], 1)
    mine = lax.broadcasted_iota(jnp.int32, (rows, lanes), 0) == chip
    for s in range(slots):
        table = got_refs[s][pl.ds(tokens, rows), :].astype(F32)
        query = jnp.sum(jnp.where(mine, table, 0.0), axis=0, keepdims=True)
        index_v[s:s + 1, :] = query.astype(jnp.int32) * token_count
    copy = pltpu.make_async_copy(index_v, index, sem)
    copy.start()
    copy.wait()

    for first, pass_ref in ((half, other_ref), (0, own_ref)):

        def eight(step, carry):
            for part in range(slots // group):
                rows = []
                for j in range(8):
                    p = step * 8 + j
                    picked = jnp.concatenate(
                        [
                            got_refs[s][pl.ds(pl.multiple_of(index[s, first + p], token_count), token_count), :]
                            for s in range(part * group, (part + 1) * group)
                        ],
                        axis=0,
                    )
                    similar = lax.dot_general(pass_ref[p], picked, NT, preferred_element_type=F32)
                    rows.append(jnp.max(similar, axis=0, keepdims=True))
                best_ref[
                    pl.ds(pl.multiple_of(first + step * 8, 8), 8),
                    pl.ds(part * group * token_count, group * token_count),
                ] = jnp.concatenate(rows, axis=0)
            return carry

        lax.fori_loop(0, half // 8, eight, 0)
    wide = best_ref.shape[1]
    source = lax.broadcasted_iota(jnp.int32, (slots, wide), 0)
    column = lax.broadcasted_iota(jnp.int32, (slots, wide), 1)
    start = source * token_count
    ones = jnp.where((column >= start) & (column < start + token_count), 1.0, 0.0).astype(BF16)
    total = sum(lax.dot_general(ones, part, NT, preferred_element_type=F32) for part in split3(best_ref[...]))
    out_ref[...] = jnp.zeros(out_ref.shape, F32)
    for s in range(slots):
        out_ref[pl.ds(jnp.bitwise_xor(chip, s), 1), pl.ds(0, 2 * half)] = total[s:s + 1]


def score(me, got, own, other, token_count):
    half, plen, e = own.shape
    passage_count = 2 * half
    slots = len(got)

    def kernel(*refs):
        score_kernel(slots, token_count, *refs)

    return pl.pallas_call(
        kernel,
        out_shape=jax.ShapeDtypeStruct((slots, e), F32),
        in_specs=[SMEM, VMEM, VMEM] + [VMEM] * slots,
        out_specs=VMEM,
        scratch_shapes=[
            pltpu.VMEM((passage_count, slots * token_count), F32),
            pltpu.VMEM((slots, e), jnp.int32),
            pltpu.SMEM((slots, e), jnp.int32),
            pltpu.SemaphoreType.DMA,
        ],
        compiler_params=pltpu.CompilerParams(vmem_limit_bytes=12 * 2 ** 20),
        cost_estimate=pl.CostEstimate(
            flops=2 * passage_count * slots * token_count * plen * e,
            bytes_accessed=4 * own.size,
            transcendentals=0,
        ),
        name="score",
    )(me, own, other, *got)


def finish_kernel(got_ref, spot_ref, scores_ref, best_ref):
    slots, lanes = got_ref.shape
    query_count, cand_count = scores_ref.shape
    parts = split3(got_ref[...])
    slot_iota = lax.broadcasted_iota(jnp.int32, (slots, cand_count), 0) * lanes
    lane_iota = lax.broadcasted_iota(jnp.int32, (lanes, cand_count), 0)
    row_iota = lax.broadcasted_iota(jnp.int32, (cand_count, cand_count), 0)
    col_iota = lax.broadcasted_iota(jnp.int32, (cand_count, cand_count), 1)
    place = lax.broadcasted_iota(jnp.int32, (cand_count, 128), 1)
    for i in range(query_count):
        spot = spot_ref[i:i + 1, :]
        lane = jnp.bitwise_and(spot, lanes - 1)
        onehot = jnp.where(lane_iota == lane, 1.0, 0.0).astype(BF16)
        picked = sum(jnp.dot(part, onehot, preferred_element_type=F32) for part in parts)
        score_row = jnp.sum(jnp.where(slot_iota == spot - lane, picked, 0.0), axis=0, keepdims=True)
        scores_ref[i:i + 1, :] = score_row
        across = jnp.broadcast_to(score_row, (cand_count, cand_count))
        score_col = jnp.sum(jnp.where(row_iota == col_iota, across, 0.0), axis=1, keepdims=True)
        ahead = (across > score_col) | ((across == score_col) & (col_iota < row_iota))
        rank = jnp.sum(jnp.where(ahead, 1.0, 0.0), axis=1, keepdims=True).astype(jnp.int32)
        ordered = jnp.sum(jnp.where(rank == place, score_col, 0.0), axis=0, keepdims=True)
        best_ref[i:i + 1, :] = ordered[:, :TOPN]


def finish(got, spots):
    return pl.pallas_call(
        finish_kernel,
        out_shape=(
            jax.ShapeDtypeStruct(spots.shape, F32),
            jax.ShapeDtypeStruct((spots.shape[0], TOPN), F32),
        ),
        in_specs=[VMEM, VMEM],
        out_specs=(VMEM, VMEM),
        compiler_params=pltpu.CompilerParams(vmem_limit_bytes=2 ** 21),
        name="finish",
    )(got, spots)


def swap(value, distance):
    size = lax.axis_size("shard")
    return lax.ppermute(value, "shard", [(i, i ^ distance) for i in range(size)])


def per_device(
    query_hidden,
    query_lengths,
    inner_weight,
    outer_weight,
    norm_gain,
    embed_weight,
    passage_vectors,
    passage_lengths,
    passage_row,
    candidates,
):
    size = lax.axis_size("shard")
    slots = size // 2
    inner = 1
    while 4 * inner * inner <= slots:
        inner *= 2
    shift = inner.bit_length()

    def color(index):
        return (index ^ (index >> 1) ^ (index >> shift)) & 1

    groups = [[i for i in range(size) if color(i) == c] for c in range(2)]

    def send(value, distance):
        return swap(value, 2 * distance + color(2 * distance))

    me = lax.axis_index("shard").astype(jnp.int32).reshape(1)
    message, masked, spots = encode(
        me,
        query_hidden,
        query_lengths,
        inner_weight,
        outer_weight,
        norm_gain,
        embed_weight,
        passage_vectors,
        passage_lengths,
        passage_row,
        candidates,
        slots,
        color,
    )
    other = swap(masked, 1)

    line = [message] + [send(message, d) for d in range(slots - inner, 0, -inner)][::-1]
    got = [line[s // inner] if s % inner == 0 else send(line[s // inner], s % inner) for s in range(slots)]
    own = mask(passage_lengths, passage_vectors, got[inner + 1])
    sums = score(me, got, own, other, query_hidden.shape[1])
    back = lax.all_to_all(sums, "shard", split_axis=0, concat_axis=0, axis_index_groups=groups, tiled=True)
    return finish(back, spots)


def solution(mesh):
    in_specs = (
        P(("groups", "shard"), None, None),
        P(("groups", "shard")),
        P(),
        P(),
        P(),
        P(),
        P(("groups", "shard"), None, None),
        P(("groups", "shard")),
        P("groups"),
        P(("groups", "shard"), None),
    )
    out_specs = (P(("groups", "shard"), None), P(("groups", "shard"), None))
    return jax.shard_map(
        per_device, mesh=mesh, in_specs=in_specs, out_specs=out_specs, check_vma=False
    )
```

```python
import jax
import jax.numpy as jnp
from jax import lax
from jax.experimental import pallas as pl
from jax.experimental.pallas import tpu as pltpu
from jax.sharding import PartitionSpec as P

TOPN = 10
F32 = jnp.float32
BF16 = jnp.bfloat16
NT = (((1,), (1,)), ((), ()))
VMEM = pl.BlockSpec(memory_space=pltpu.VMEM)
SMEM = pl.BlockSpec(memory_space=pltpu.SMEM)
ANY = pl.BlockSpec(memory_space=pl.ANY)


def split3(value):
    high = value.astype(BF16)
    rest = value - high.astype(F32)
    middle = rest.astype(BF16)
    low = (rest - middle.astype(F32)).astype(BF16)
    return high, middle, low


def mask_into(out_ref, pass_ref, len_ref, first, count):
    def mask(p, carry):
        block = pass_ref[p]
        keep = lax.broadcasted_iota(jnp.int32, block.shape, 0) < len_ref[p]
        block = block.astype(F32)
        out_ref[p] = jnp.where(keep, block, jnp.broadcast_to(block[0:1], block.shape)).astype(BF16)
        return carry

    if count <= 8:
        for p in range(first, first + count):
            mask(p, 0)
    else:
        lax.fori_loop(first, first + count, mask, 0, unroll=8)


def encode_kernel(
    half,
    color,
    me_ref,
    lens_hbm,
    plen_hbm,
    row_hbm,
    cand_hbm,
    x_hbm,
    w1_ref,
    w2_ref,
    gain_hbm,
    embed_hbm,
    pass_hbm,
    out_ref,
    masked_hbm,
    spot_ref,
    w1_buf,
    w2_buf,
    pass_buf,
    lens_ref,
    plen_ref,
    row_ref,
    place_ref,
    cand_ref,
    x_ref,
    gain_ref,
    embed_ref,
    table,
    table_v,
    sems,
    small_sems,
    place_sem,
    table_sem,
    pass_sems,
):
    chunks, _, width = w1_buf.shape
    slots, lanes = table_v.shape
    query_count, token_count, width_in = x_ref.shape
    cand_count = cand_ref.shape[1]
    table_v[...] = jnp.zeros(table_v.shape, jnp.int32)
    clear = pltpu.make_async_copy(table_v, table, table_sem)
    clear.start()
    copies = []
    for c in range(chunks):
        first = pltpu.make_async_copy(w1_ref.at[:, pl.ds(c * width, width)], w1_buf.at[c], sems.at[0, c])
        second = pltpu.make_async_copy(w2_ref.at[pl.ds(c * width, width), :], w2_buf.at[c], sems.at[1, c])
        copies.append((first, second))
    small = [
        pltpu.make_async_copy(source, target, small_sems.at[n])
        for n, (source, target) in enumerate(
            (
                (x_hbm, x_ref),
                (row_hbm, row_ref),
                (cand_hbm, cand_ref),
                (plen_hbm, plen_ref),
                (lens_hbm, lens_ref),
                (gain_hbm, gain_ref),
                (embed_hbm, embed_ref),
            )
        )
    ]
    for copy in small[:3]:
        copy.start()
    copies[0][0].start()
    small[3].start()
    batch = half // chunks
    loads, saves = [], []
    for c in range(chunks):
        rows = pl.ds(c * batch, batch)
        loads.append(pltpu.make_async_copy(pass_hbm.at[rows], pass_buf.at[rows], pass_sems.at[0, c]))
        saves.append(pltpu.make_async_copy(pass_buf.at[rows], masked_hbm.at[rows], pass_sems.at[1, c]))
    copies[1][0].start()
    copies[0][1].start()
    for c in range(2, chunks):
        loads[c - 2].start()
        copies[c][0].start()
        copies[c - 1][1].start()
    copies[-1][1].start()
    loads[-2].start()
    loads[-1].start()
    for copy in small[4:]:
        copy.start()
    clear.wait()
    small[1].wait()
    row = row_ref[...]
    owner = jnp.floor((row.astype(F32) + 0.5) * (1.0 / half)).astype(jnp.int32)
    opposite = jnp.bitwise_xor(color(owner), color(me_ref[0]))
    row_ref[...] = jnp.right_shift(owner, 1) * lanes + row - owner * half + opposite * half
    placed = pltpu.make_async_copy(row_ref, place_ref, place_sem)
    placed.start()

    entries = [(i, k) for k in range(cand_count) for i in range(query_count)]
    share = -(-len(entries) // chunks)

    def enter():
        for first in range(0, share, 12):
            batch = entries[first:min(first + 12, share)]
            names = [cand_ref[i, k] for i, k in batch]
            spots = [place_ref[name] for name in names]
            for (i, k), spot in zip(batch, spots):
                table[jnp.right_shift(spot, 7), jnp.bitwise_and(spot, 127)] = i
                spot_ref[i, k] = spot
        del entries[:share]

    def mask(c):
        loads[c].wait()
        mask_into(pass_buf, pass_buf, plen_ref, c * batch, batch)
        saves[c].start()

    small[0].wait()
    small[3].wait()
    x = x_ref[...].reshape(query_count * token_count, width_in)
    total = x.astype(F32)
    inner = active = None
    for step in range(chunks + 2):
        if step < chunks:
            copies[step][0].wait()
        if step >= 2:
            copies[step - 2][1].wait()
        if 2 <= step < chunks:
            mask(step - 2)
        if step == 1:
            small[2].wait()
            placed.wait()
        if step >= 1:
            enter()
        later = jnp.dot(x, w1_buf[step], preferred_element_type=F32) if step < chunks else None
        if step >= 2:
            total = total + jnp.dot(active, w2_buf[step - 2], preferred_element_type=F32)
        if 1 <= step <= chunks:
            active = (0.5 * inner * (1.0 + lax.erf(inner * (0.5 ** 0.5)))).astype(BF16)
        inner = later
        if step == chunks:
            fetch = pltpu.make_async_copy(table, table_v, table_sem)
            fetch.start()
    mask(chunks - 2)
    mask(chunks - 1)

    for copy in small[4:]:
        copy.wait()
    centered = total - jnp.mean(total, axis=-1, keepdims=True)
    variance = jnp.mean(jnp.square(centered), axis=-1, keepdims=True)
    layer_out = (centered * lax.rsqrt(variance + 1e-12) * gain_ref[...].reshape(1, width_in)).astype(BF16)
    embedded = jnp.dot(layer_out, embed_ref[...], preferred_element_type=F32)
    length = jnp.sum(jnp.square(embedded), axis=-1, keepdims=True)
    vectors = embedded * lax.rsqrt(length + 1e-06)
    token = lax.broadcasted_iota(jnp.int32, vectors.shape, 0)
    for i in range(query_count):
        padded = (token >= i * token_count + lens_ref[i]) & (token < (i + 1) * token_count)
        vectors = jnp.where(padded, 0.0, vectors)
    vectors = vectors.astype(BF16)
    fetch.wait()
    tokens = query_count * token_count
    wanted = table_v[...].astype(F32).astype(BF16)
    out_ref[pl.ds(0, tokens), :] = vectors
    out_ref[pl.ds(tokens, slots), :] = wanted
    for save in saves:
        save.wait()


def encode(
    me,
    query_hidden,
    query_lengths,
    inner_weight,
    outer_weight,
    norm_gain,
    embed_weight,
    passage_vectors,
    passage_lengths,
    passage_row,
    candidates,
    slots,
    color,
):
    query_count, token_count, d = query_hidden.shape
    ff = inner_weight.shape[1]
    e = embed_weight.shape[1]
    half = passage_vectors.shape[0]
    slots = -(-slots // 16) * 16
    assert 2 * half <= e == 128
    chunks = 6
    width = ff // chunks
    tokens = query_count * token_count

    def kernel(*refs):
        encode_kernel(half, color, *refs)

    return pl.pallas_call(
        kernel,
        out_shape=(
            jax.ShapeDtypeStruct((tokens + slots, e), BF16),
            jax.ShapeDtypeStruct(passage_vectors.shape, BF16),
            jax.ShapeDtypeStruct(candidates.shape, jnp.int32),
        ),
        in_specs=[SMEM] + [ANY] * 10,
        out_specs=(VMEM, ANY, SMEM),
        scratch_shapes=[
            pltpu.VMEM((chunks, d, width), BF16),
            pltpu.VMEM((chunks, width, d), BF16),
            pltpu.VMEM(passage_vectors.shape, BF16),
            pltpu.SMEM(query_lengths.shape, jnp.int32),
            pltpu.SMEM(passage_lengths.shape, jnp.int32),
            pltpu.VMEM(passage_row.shape, jnp.int32),
            pltpu.SMEM(passage_row.shape, jnp.int32),
            pltpu.SMEM(candidates.shape, jnp.int32),
            pltpu.VMEM(query_hidden.shape, BF16),
            pltpu.VMEM(norm_gain.shape, F32),
            pltpu.VMEM(embed_weight.shape, BF16),
            pltpu.SMEM((slots, e), jnp.int32),
            pltpu.VMEM((slots, e), jnp.int32),
            pltpu.SemaphoreType.DMA((2, chunks)),
            pltpu.SemaphoreType.DMA((7,)),
            pltpu.SemaphoreType.DMA,
            pltpu.SemaphoreType.DMA,
            pltpu.SemaphoreType.DMA((2, chunks)),
        ],
        compiler_params=pltpu.CompilerParams(vmem_limit_bytes=60 * 2 ** 20),
        cost_estimate=pl.CostEstimate(
            flops=4 * tokens * d * ff, bytes_accessed=4 * d * ff, transcendentals=tokens * ff
        ),
        name="encode",
    )(
        me,
        query_lengths,
        passage_lengths,
        passage_row,
        candidates,
        query_hidden,
        inner_weight,
        outer_weight,
        norm_gain,
        embed_weight,
        passage_vectors,
    )


def mask_kernel(len_ref, pass_ref, *refs):
    mask_into(refs[-1], pass_ref, len_ref, 0, pass_ref.shape[0])


def mask(lengths, passages, late):
    return pl.pallas_call(
        mask_kernel,
        out_shape=jax.ShapeDtypeStruct(passages.shape, BF16),
        in_specs=[SMEM, VMEM, VMEM],
        out_specs=VMEM,
        compiler_params=pltpu.CompilerParams(vmem_limit_bytes=2 ** 22),
        cost_estimate=pl.CostEstimate(flops=8 * passages.size, bytes_accessed=4 * passages.size, transcendentals=0),
        name="mask",
    )(lengths, passages, late)


def score_kernel(slots, token_count, me_ref, own_ref, other_ref, *refs):
    got_refs = refs[:slots]
    out_ref, best_ref, index_v, index, sem = refs[slots:]
    message, lanes = got_refs[0].shape
    half = own_ref.shape[0]
    rows = -(-slots // 16) * 16
    tokens = message - rows
    group = min(slots, 256 // token_count)
    chip = jnp.right_shift(me_ref[0], 1)
    mine = lax.broadcasted_iota(jnp.int32, (rows, lanes), 0) == chip
    for s in range(slots):
        table = got_refs[s][pl.ds(tokens, rows), :].astype(F32)
        query = jnp.sum(jnp.where(mine, table, 0.0), axis=0, keepdims=True)
        index_v[s:s + 1, :] = query.astype(jnp.int32) * token_count
    copy = pltpu.make_async_copy(index_v, index, sem)
    copy.start()
    copy.wait()

    for first, pass_ref in ((half, other_ref), (0, own_ref)):

        def eight(step, carry):
            for part in range(slots // group):
                rows = []
                for j in range(8):
                    p = step * 8 + j
                    picked = jnp.concatenate(
                        [
                            got_refs[s][pl.ds(pl.multiple_of(index[s, first + p], token_count), token_count), :]
                            for s in range(part * group, (part + 1) * group)
                        ],
                        axis=0,
                    )
                    similar = lax.dot_general(pass_ref[p], picked, NT, preferred_element_type=F32)
                    rows.append(jnp.max(similar, axis=0, keepdims=True))
                best_ref[
                    pl.ds(pl.multiple_of(first + step * 8, 8), 8),
                    pl.ds(part * group * token_count, group * token_count),
                ] = jnp.concatenate(rows, axis=0)
            return carry

        lax.fori_loop(0, half // 8, eight, 0)
    wide = best_ref.shape[1]
    source = lax.broadcasted_iota(jnp.int32, (slots, wide), 0)
    column = lax.broadcasted_iota(jnp.int32, (slots, wide), 1)
    start = source * token_count
    ones = jnp.where((column >= start) & (column < start + token_count), 1.0, 0.0).astype(BF16)
    total = sum(lax.dot_general(ones, part, NT, preferred_element_type=F32) for part in split3(best_ref[...]))
    out_ref[...] = jnp.zeros(out_ref.shape, F32)
    for s in range(slots):
        out_ref[pl.ds(jnp.bitwise_xor(chip, s), 1), pl.ds(0, 2 * half)] = total[s:s + 1]


def score(me, got, own, other, token_count):
    half, plen, e = own.shape
    passage_count = 2 * half
    slots = len(got)

    def kernel(*refs):
        score_kernel(slots, token_count, *refs)

    return pl.pallas_call(
        kernel,
        out_shape=jax.ShapeDtypeStruct((slots, e), F32),
        in_specs=[SMEM, VMEM, VMEM] + [VMEM] * slots,
        out_specs=VMEM,
        scratch_shapes=[
            pltpu.VMEM((passage_count, slots * token_count), F32),
            pltpu.VMEM((slots, e), jnp.int32),
            pltpu.SMEM((slots, e), jnp.int32),
            pltpu.SemaphoreType.DMA,
        ],
        compiler_params=pltpu.CompilerParams(vmem_limit_bytes=12 * 2 ** 20),
        cost_estimate=pl.CostEstimate(
            flops=2 * passage_count * slots * token_count * plen * e,
            bytes_accessed=4 * own.size,
            transcendentals=0,
        ),
        name="score",
    )(me, own, other, *got)


def finish_kernel(got_ref, spot_ref, scores_ref, best_ref):
    slots, lanes = got_ref.shape
    query_count, cand_count = scores_ref.shape
    parts = split3(got_ref[...])
    slot_iota = lax.broadcasted_iota(jnp.int32, (slots, cand_count), 0) * lanes
    lane_iota = lax.broadcasted_iota(jnp.int32, (lanes, cand_count), 0)
    row_iota = lax.broadcasted_iota(jnp.int32, (cand_count, cand_count), 0)
    col_iota = lax.broadcasted_iota(jnp.int32, (cand_count, cand_count), 1)
    place = lax.broadcasted_iota(jnp.int32, (cand_count, 128), 1)
    for i in range(query_count):
        spot = spot_ref[i:i + 1, :]
        lane = jnp.bitwise_and(spot, lanes - 1)
        onehot = jnp.where(lane_iota == lane, 1.0, 0.0).astype(BF16)
        picked = sum(jnp.dot(part, onehot, preferred_element_type=F32) for part in parts)
        score_row = jnp.sum(jnp.where(slot_iota == spot - lane, picked, 0.0), axis=0, keepdims=True)
        scores_ref[i:i + 1, :] = score_row
        across = jnp.broadcast_to(score_row, (cand_count, cand_count))
        score_col = jnp.sum(jnp.where(row_iota == col_iota, across, 0.0), axis=1, keepdims=True)
        ahead = (across > score_col) | ((across == score_col) & (col_iota < row_iota))
        rank = jnp.sum(jnp.where(ahead, 1.0, 0.0), axis=1, keepdims=True).astype(jnp.int32)
        ordered = jnp.sum(jnp.where(rank == place, score_col, 0.0), axis=0, keepdims=True)
        best_ref[i:i + 1, :] = ordered[:, :TOPN]


def finish(got, spots):
    return pl.pallas_call(
        finish_kernel,
        out_shape=(
            jax.ShapeDtypeStruct(spots.shape, F32),
            jax.ShapeDtypeStruct((spots.shape[0], TOPN), F32),
        ),
        in_specs=[VMEM, VMEM],
        out_specs=(VMEM, VMEM),
        compiler_params=pltpu.CompilerParams(vmem_limit_bytes=2 ** 21),
        name="finish",
    )(got, spots)


def swap(value, distance):
    size = lax.axis_size("shard")
    return lax.ppermute(value, "shard", [(i, i ^ distance) for i in range(size)])


def per_device(
    query_hidden,
    query_lengths,
    inner_weight,
    outer_weight,
    norm_gain,
    embed_weight,
    passage_vectors,
    passage_lengths,
    passage_row,
    candidates,
):
    size = lax.axis_size("shard")
    slots = size // 2
    inner = 1
    while 4 * inner * inner <= slots:
        inner *= 2
    shift = inner.bit_length()

    def color(index):
        return (index ^ (index >> 1) ^ (index >> shift)) & 1

    groups = [[i for i in range(size) if color(i) == c] for c in range(2)]

    def send(value, distance):
        return swap(value, 2 * distance + color(2 * distance))

    me = lax.axis_index("shard").astype(jnp.int32).reshape(1)
    message, masked, spots = encode(
        me,
        query_hidden,
        query_lengths,
        inner_weight,
        outer_weight,
        norm_gain,
        embed_weight,
        passage_vectors,
        passage_lengths,
        passage_row,
        candidates,
        slots,
        color,
    )
    other = swap(masked, 1)

    line = [message] + [send(message, d) for d in range(slots - inner, 0, -inner)][::-1]
    got = [line[s // inner] if s % inner == 0 else send(line[s // inner], s % inner) for s in range(slots)]
    own = mask(passage_lengths, passage_vectors, got[inner + 1])
    sums = score(me, got, own, other, query_hidden.shape[1])
    back = lax.all_to_all(sums, "shard", split_axis=0, concat_axis=0, axis_index_groups=groups, tiled=True)
    return finish(back, spots)


def solution(mesh):
    in_specs = (
        P(("groups", "shard"), None, None),
        P(("groups", "shard")),
        P(),
        P(),
        P(),
        P(),
        P(("groups", "shard"), None, None),
        P(("groups", "shard")),
        P("groups"),
        P(("groups", "shard"), None),
    )
    out_specs = (P(("groups", "shard"), None), P(("groups", "shard"), None))
    return jax.shard_map(
        per_device, mesh=mesh, in_specs=in_specs, out_specs=out_specs, check_vma=False
    )
```

```python
import jax
import jax.numpy as jnp
from jax import lax
from jax.experimental import pallas as pl
from jax.experimental.pallas import tpu as pltpu
from jax.sharding import PartitionSpec as P

TOPN = 10
F32 = jnp.float32
BF16 = jnp.bfloat16
NT = (((1,), (1,)), ((), ()))
VMEM = pl.BlockSpec(memory_space=pltpu.VMEM)
SMEM = pl.BlockSpec(memory_space=pltpu.SMEM)
ANY = pl.BlockSpec(memory_space=pl.ANY)


def split3(value):
    high = value.astype(BF16)
    rest = value - high.astype(F32)
    middle = rest.astype(BF16)
    low = (rest - middle.astype(F32)).astype(BF16)
    return high, middle, low


def mask_into(out_ref, pass_ref, len_ref, first, count):
    def mask(p, carry):
        block = pass_ref[p]
        keep = lax.broadcasted_iota(jnp.int32, block.shape, 0) < len_ref[p]
        block = block.astype(F32)
        out_ref[p] = jnp.where(keep, block, jnp.broadcast_to(block[0:1], block.shape)).astype(BF16)
        return carry

    if count <= 8:
        for p in range(first, first + count):
            mask(p, 0)
    else:
        lax.fori_loop(first, first + count, mask, 0, unroll=8)


def encode_kernel(
    half,
    color,
    me_ref,
    lens_hbm,
    row_hbm,
    cand_hbm,
    x_hbm,
    w1_ref,
    w2_ref,
    gain_hbm,
    embed_hbm,
    out_ref,
    spot_ref,
    w1_buf,
    w2_buf,
    lens_ref,
    row_ref,
    place_ref,
    cand_ref,
    x_ref,
    gain_ref,
    embed_ref,
    table,
    table_v,
    sems,
    small_sems,
    place_sem,
    table_sem,
):
    chunks, _, width = w1_buf.shape
    slots, lanes = table_v.shape
    query_count, token_count, width_in = x_ref.shape
    cand_count = cand_ref.shape[1]
    table_v[...] = jnp.zeros(table_v.shape, jnp.int32)
    clear = pltpu.make_async_copy(table_v, table, table_sem)
    clear.start()
    copies = []
    for c in range(chunks):
        first = pltpu.make_async_copy(w1_ref.at[:, pl.ds(c * width, width)], w1_buf.at[c], sems.at[0, c])
        second = pltpu.make_async_copy(w2_ref.at[pl.ds(c * width, width), :], w2_buf.at[c], sems.at[1, c])
        copies.append((first, second))
    small = [
        pltpu.make_async_copy(source, target, small_sems.at[n])
        for n, (source, target) in enumerate(
            (
                (x_hbm, x_ref),
                (row_hbm, row_ref),
                (cand_hbm, cand_ref),
                (lens_hbm, lens_ref),
                (gain_hbm, gain_ref),
                (embed_hbm, embed_ref),
            )
        )
    ]
    for copy in small[:3]:
        copy.start()
    copies[0][0].start()
    copies[1][0].start()
    copies[0][1].start()
    for c in range(2, chunks):
        copies[c][0].start()
        copies[c - 1][1].start()
    copies[-1][1].start()
    for copy in small[3:]:
        copy.start()
    clear.wait()
    small[1].wait()
    row = row_ref[...]
    owner = jnp.floor((row.astype(F32) + 0.5) * (1.0 / half)).astype(jnp.int32)
    opposite = jnp.bitwise_xor(color(owner), color(me_ref[0]))
    row_ref[...] = jnp.right_shift(owner, 1) * lanes + row - owner * half + opposite * half
    placed = pltpu.make_async_copy(row_ref, place_ref, place_sem)
    placed.start()

    entries = [(i, k) for k in range(cand_count) for i in range(query_count)]
    share = -(-len(entries) // chunks)

    def enter():
        for first in range(0, share, 12):
            batch = entries[first:min(first + 12, share)]
            names = [cand_ref[i, k] for i, k in batch]
            spots = [place_ref[name] for name in names]
            for (i, k), spot in zip(batch, spots):
                table[jnp.right_shift(spot, 7), jnp.bitwise_and(spot, 127)] = i
                spot_ref[i, k] = spot
        del entries[:share]

    small[0].wait()
    x = x_ref[...].reshape(query_count * token_count, width_in)
    total = x.astype(F32)
    inner = active = None
    for step in range(chunks + 2):
        if step < chunks:
            copies[step][0].wait()
        if step >= 2:
            copies[step - 2][1].wait()
        if step == 1:
            small[2].wait()
            placed.wait()
        if step >= 1:
            enter()
        later = jnp.dot(x, w1_buf[step], preferred_element_type=F32) if step < chunks else None
        if step >= 2:
            total = total + jnp.dot(active, w2_buf[step - 2], preferred_element_type=F32)
        if 1 <= step <= chunks:
            active = (0.5 * inner * (1.0 + lax.erf(inner * (0.5 ** 0.5)))).astype(BF16)
        inner = later
        if step == chunks:
            fetch = pltpu.make_async_copy(table, table_v, table_sem)
            fetch.start()

    for copy in small[3:]:
        copy.wait()
    centered = total - jnp.mean(total, axis=-1, keepdims=True)
    variance = jnp.mean(jnp.square(centered), axis=-1, keepdims=True)
    layer_out = (centered * lax.rsqrt(variance + 1e-12) * gain_ref[...].reshape(1, width_in)).astype(BF16)
    embedded = jnp.dot(layer_out, embed_ref[...], preferred_element_type=F32)
    length = jnp.sum(jnp.square(embedded), axis=-1, keepdims=True)
    vectors = embedded * lax.rsqrt(length + 1e-06)
    token = lax.broadcasted_iota(jnp.int32, vectors.shape, 0)
    for i in range(query_count):
        padded = (token >= i * token_count + lens_ref[i]) & (token < (i + 1) * token_count)
        vectors = jnp.where(padded, 0.0, vectors)
    vectors = vectors.astype(BF16)
    fetch.wait()
    tokens = query_count * token_count
    wanted = table_v[...].astype(F32).astype(BF16)
    out_ref[pl.ds(0, tokens), :] = vectors
    out_ref[pl.ds(tokens, slots), :] = wanted


def encode(
    me,
    query_hidden,
    query_lengths,
    inner_weight,
    outer_weight,
    norm_gain,
    embed_weight,
    half,
    passage_row,
    candidates,
    slots,
    color,
):
    query_count, token_count, d = query_hidden.shape
    ff = inner_weight.shape[1]
    e = embed_weight.shape[1]
    slots = -(-slots // 16) * 16
    assert 2 * half <= e == 128
    chunks = 6
    width = ff // chunks
    tokens = query_count * token_count

    def kernel(*refs):
        encode_kernel(half, color, *refs)

    return pl.pallas_call(
        kernel,
        out_shape=(
            jax.ShapeDtypeStruct((tokens + slots, e), BF16),
            jax.ShapeDtypeStruct(candidates.shape, jnp.int32),
        ),
        in_specs=[SMEM] + [ANY] * 8,
        out_specs=(VMEM, SMEM),
        scratch_shapes=[
            pltpu.VMEM((chunks, d, width), BF16),
            pltpu.VMEM((chunks, width, d), BF16),
            pltpu.SMEM(query_lengths.shape, jnp.int32),
            pltpu.VMEM(passage_row.shape, jnp.int32),
            pltpu.SMEM(passage_row.shape, jnp.int32),
            pltpu.SMEM(candidates.shape, jnp.int32),
            pltpu.VMEM(query_hidden.shape, BF16),
            pltpu.VMEM(norm_gain.shape, F32),
            pltpu.VMEM(embed_weight.shape, BF16),
            pltpu.SMEM((slots, e), jnp.int32),
            pltpu.VMEM((slots, e), jnp.int32),
            pltpu.SemaphoreType.DMA((2, chunks)),
            pltpu.SemaphoreType.DMA((6,)),
            pltpu.SemaphoreType.DMA,
            pltpu.SemaphoreType.DMA,
        ],
        compiler_params=pltpu.CompilerParams(vmem_limit_bytes=60 * 2 ** 20),
        cost_estimate=pl.CostEstimate(
            flops=4 * tokens * d * ff, bytes_accessed=4 * d * ff, transcendentals=tokens * ff
        ),
        name="encode",
    )(
        me,
        query_lengths,
        passage_row,
        candidates,
        query_hidden,
        inner_weight,
        outer_weight,
        norm_gain,
        embed_weight,
    )


def mask_kernel(len0_ref, len1_ref, pass0_ref, pass1_ref, _, out0_ref, out1_ref):
    mask_into(out0_ref, pass0_ref, len0_ref, 0, pass0_ref.shape[0])
    mask_into(out1_ref, pass1_ref, len1_ref, 0, pass1_ref.shape[0])


def mask(lengths, passages, late):
    shape = passages[0].shape
    size = 2 * passages[0].size
    return pl.pallas_call(
        mask_kernel,
        out_shape=[jax.ShapeDtypeStruct(shape, BF16)] * 2,
        in_specs=[SMEM, SMEM, VMEM, VMEM, VMEM],
        out_specs=[VMEM, VMEM],
        compiler_params=pltpu.CompilerParams(vmem_limit_bytes=2 ** 22),
        cost_estimate=pl.CostEstimate(flops=8 * size, bytes_accessed=4 * size, transcendentals=0),
        name="mask",
    )(*lengths, *passages, late)


def score_kernel(slots, token_count, me_ref, own_ref, other_ref, *refs):
    got_refs = refs[:slots]
    out_ref, best_ref, index_v, index, sem = refs[slots:]
    message, lanes = got_refs[0].shape
    half = own_ref.shape[0]
    rows = -(-slots // 16) * 16
    tokens = message - rows
    group = min(slots, 256 // token_count)
    chip = jnp.right_shift(me_ref[0], 1)
    mine = lax.broadcasted_iota(jnp.int32, (rows, lanes), 0) == chip
    for s in range(slots):
        table = got_refs[s][pl.ds(tokens, rows), :].astype(F32)
        query = jnp.sum(jnp.where(mine, table, 0.0), axis=0, keepdims=True)
        index_v[s:s + 1, :] = query.astype(jnp.int32) * token_count
    copy = pltpu.make_async_copy(index_v, index, sem)
    copy.start()
    copy.wait()

    for first, pass_ref in ((half, other_ref), (0, own_ref)):

        def eight(step, carry):
            for part in range(slots // group):
                rows = []
                for j in range(8):
                    p = step * 8 + j
                    picked = jnp.concatenate(
                        [
                            got_refs[s][pl.ds(pl.multiple_of(index[s, first + p], token_count), token_count), :]
                            for s in range(part * group, (part + 1) * group)
                        ],
                        axis=0,
                    )
                    similar = lax.dot_general(pass_ref[p], picked, NT, preferred_element_type=F32)
                    rows.append(jnp.max(similar, axis=0, keepdims=True))
                best_ref[
                    pl.ds(pl.multiple_of(first + step * 8, 8), 8),
                    pl.ds(part * group * token_count, group * token_count),
                ] = jnp.concatenate(rows, axis=0)
            return carry

        lax.fori_loop(0, half // 8, eight, 0)
    wide = best_ref.shape[1]
    source = lax.broadcasted_iota(jnp.int32, (slots, wide), 0)
    column = lax.broadcasted_iota(jnp.int32, (slots, wide), 1)
    start = source * token_count
    ones = jnp.where((column >= start) & (column < start + token_count), 1.0, 0.0).astype(BF16)
    total = sum(lax.dot_general(ones, part, NT, preferred_element_type=F32) for part in split3(best_ref[...]))
    out_ref[...] = jnp.zeros(out_ref.shape, F32)
    for s in range(slots):
        out_ref[pl.ds(jnp.bitwise_xor(chip, s), 1), pl.ds(0, 2 * half)] = total[s:s + 1]


def score(me, got, own, other, token_count):
    half, plen, e = own.shape
    passage_count = 2 * half
    slots = len(got)

    def kernel(*refs):
        score_kernel(slots, token_count, *refs)

    return pl.pallas_call(
        kernel,
        out_shape=jax.ShapeDtypeStruct((slots, e), F32),
        in_specs=[SMEM, VMEM, VMEM] + [VMEM] * slots,
        out_specs=VMEM,
        scratch_shapes=[
            pltpu.VMEM((passage_count, slots * token_count), F32),
            pltpu.VMEM((slots, e), jnp.int32),
            pltpu.SMEM((slots, e), jnp.int32),
            pltpu.SemaphoreType.DMA,
        ],
        compiler_params=pltpu.CompilerParams(vmem_limit_bytes=12 * 2 ** 20),
        cost_estimate=pl.CostEstimate(
            flops=2 * passage_count * slots * token_count * plen * e,
            bytes_accessed=4 * own.size,
            transcendentals=0,
        ),
        name="score",
    )(me, own, other, *got)


def finish_kernel(got_ref, spot_ref, scores_ref, best_ref):
    slots, lanes = got_ref.shape
    query_count, cand_count = scores_ref.shape
    parts = split3(got_ref[...])
    slot_iota = lax.broadcasted_iota(jnp.int32, (slots, cand_count), 0) * lanes
    lane_iota = lax.broadcasted_iota(jnp.int32, (lanes, cand_count), 0)
    row_iota = lax.broadcasted_iota(jnp.int32, (cand_count, cand_count), 0)
    col_iota = lax.broadcasted_iota(jnp.int32, (cand_count, cand_count), 1)
    place = lax.broadcasted_iota(jnp.int32, (cand_count, 128), 1)
    for i in range(query_count):
        spot = spot_ref[i:i + 1, :]
        lane = jnp.bitwise_and(spot, lanes - 1)
        onehot = jnp.where(lane_iota == lane, 1.0, 0.0).astype(BF16)
        picked = sum(jnp.dot(part, onehot, preferred_element_type=F32) for part in parts)
        score_row = jnp.sum(jnp.where(slot_iota == spot - lane, picked, 0.0), axis=0, keepdims=True)
        scores_ref[i:i + 1, :] = score_row
        across = jnp.broadcast_to(score_row, (cand_count, cand_count))
        score_col = jnp.sum(jnp.where(row_iota == col_iota, across, 0.0), axis=1, keepdims=True)
        ahead = (across > score_col) | ((across == score_col) & (col_iota < row_iota))
        rank = jnp.sum(jnp.where(ahead, 1.0, 0.0), axis=1, keepdims=True).astype(jnp.int32)
        ordered = jnp.sum(jnp.where(rank == place, score_col, 0.0), axis=0, keepdims=True)
        best_ref[i:i + 1, :] = ordered[:, :TOPN]


def finish(got, spots):
    return pl.pallas_call(
        finish_kernel,
        out_shape=(
            jax.ShapeDtypeStruct(spots.shape, F32),
            jax.ShapeDtypeStruct((spots.shape[0], TOPN), F32),
        ),
        in_specs=[VMEM, VMEM],
        out_specs=(VMEM, VMEM),
        compiler_params=pltpu.CompilerParams(vmem_limit_bytes=2 ** 21),
        name="finish",
    )(got, spots)


def swap(value, distance):
    size = lax.axis_size("shard")
    return lax.ppermute(value, "shard", [(i, i ^ distance) for i in range(size)])


def per_device(
    query_hidden,
    query_lengths,
    inner_weight,
    outer_weight,
    norm_gain,
    embed_weight,
    passage_vectors,
    passage_lengths,
    passage_row,
    candidates,
):
    size = lax.axis_size("shard")
    slots = size // 2
    inner = 1
    while 4 * inner * inner <= slots:
        inner *= 2
    shift = inner.bit_length()

    def color(index):
        return (index ^ (index >> 1) ^ (index >> shift)) & 1

    groups = [[i for i in range(size) if color(i) == c] for c in range(2)]

    def send(value, distance):
        return swap(value, 2 * distance + color(2 * distance))

    me = lax.axis_index("shard").astype(jnp.int32).reshape(1)
    across = swap(passage_lengths, 1)
    message, spots = encode(
        me,
        query_hidden,
        query_lengths,
        inner_weight,
        outer_weight,
        norm_gain,
        embed_weight,
        passage_vectors.shape[0],
        passage_row,
        candidates,
        slots,
        color,
    )
    message, across, raw = lax.optimization_barrier((message, across, passage_vectors))
    raw = swap(raw, 1)

    line = [message] + [send(message, d) for d in range(slots - inner, 0, -inner)][::-1]
    got = [line[s // inner] if s % inner == 0 else send(line[s // inner], s % inner) for s in range(slots)]
    own, other = mask((passage_lengths, across), (passage_vectors, raw), got[inner + 1])
    sums = score(me, got, own, other, query_hidden.shape[1])
    back = lax.all_to_all(sums, "shard", split_axis=0, concat_axis=0, axis_index_groups=groups, tiled=True)
    return finish(back, spots)


def solution(mesh):
    in_specs = (
        P(("groups", "shard"), None, None),
        P(("groups", "shard")),
        P(),
        P(),
        P(),
        P(),
        P(("groups", "shard"), None, None),
        P(("groups", "shard")),
        P("groups"),
        P(("groups", "shard"), None),
    )
    out_specs = (P(("groups", "shard"), None), P(("groups", "shard"), None))
    return jax.shard_map(
        per_device, mesh=mesh, in_specs=in_specs, out_specs=out_specs, check_vma=False
    )
```

```python
import jax
import jax.numpy as jnp
from jax import lax
from jax.experimental import pallas as pl
from jax.experimental.pallas import tpu as pltpu
from jax.sharding import PartitionSpec as P

TOPN = 10
F32 = jnp.float32
BF16 = jnp.bfloat16
NT = (((1,), (1,)), ((), ()))
VMEM = pl.BlockSpec(memory_space=pltpu.VMEM)
SMEM = pl.BlockSpec(memory_space=pltpu.SMEM)
ANY = pl.BlockSpec(memory_space=pl.ANY)


def split3(value):
    high = value.astype(BF16)
    rest = value - high.astype(F32)
    middle = rest.astype(BF16)
    low = (rest - middle.astype(F32)).astype(BF16)
    return high, middle, low


def mask_into(out_ref, pass_ref, len_ref, first, count):
    def mask(p, carry):
        block = pass_ref[p]
        keep = lax.broadcasted_iota(jnp.int32, block.shape, 0) < len_ref[p]
        block = block.astype(F32)
        out_ref[p] = jnp.where(keep, block, jnp.broadcast_to(block[0:1], block.shape)).astype(BF16)
        return carry

    if count <= 8:
        for p in range(first, first + count):
            mask(p, 0)
    else:
        lax.fori_loop(first, first + count, mask, 0, unroll=8)


def encode_kernel(
    half,
    color,
    me_ref,
    lens_hbm,
    row_hbm,
    cand_hbm,
    x_hbm,
    w1_ref,
    w2_ref,
    gain_hbm,
    embed_hbm,
    out_ref,
    spot_ref,
    w1_buf,
    w2_buf,
    lens_ref,
    row_ref,
    place_ref,
    cand_ref,
    x_ref,
    gain_ref,
    embed_ref,
    table,
    table_v,
    sems,
    small_sems,
    place_sem,
    table_sem,
):
    chunks, _, width = w1_buf.shape
    slots, lanes = table_v.shape
    query_count, token_count, width_in = x_ref.shape
    cand_count = cand_ref.shape[1]
    table_v[...] = jnp.zeros(table_v.shape, jnp.int32)
    clear = pltpu.make_async_copy(table_v, table, table_sem)
    clear.start()
    copies = []
    for c in range(chunks):
        first = pltpu.make_async_copy(w1_ref.at[:, pl.ds(c * width, width)], w1_buf.at[c], sems.at[0, c])
        second = pltpu.make_async_copy(w2_ref.at[pl.ds(c * width, width), :], w2_buf.at[c], sems.at[1, c])
        copies.append((first, second))
    small = [
        pltpu.make_async_copy(source, target, small_sems.at[n])
        for n, (source, target) in enumerate(
            (
                (x_hbm, x_ref),
                (row_hbm, row_ref),
                (cand_hbm, cand_ref),
                (lens_hbm, lens_ref),
                (gain_hbm, gain_ref),
                (embed_hbm, embed_ref),
            )
        )
    ]
    for copy in small[:3]:
        copy.start()
    copies[0][0].start()
    copies[1][0].start()
    copies[0][1].start()
    for c in range(2, chunks):
        copies[c][0].start()
        copies[c - 1][1].start()
    copies[-1][1].start()
    for copy in small[3:]:
        copy.start()
    clear.wait()
    small[1].wait()
    row = row_ref[...]
    owner = jnp.floor((row.astype(F32) + 0.5) * (1.0 / half)).astype(jnp.int32)
    opposite = jnp.bitwise_xor(color(owner), color(me_ref[0]))
    row_ref[...] = jnp.right_shift(owner, 1) * lanes + row - owner * half + opposite * half
    placed = pltpu.make_async_copy(row_ref, place_ref, place_sem)
    placed.start()

    entries = [(i, k) for k in range(cand_count) for i in range(query_count)]
    share = -(-len(entries) // chunks)

    def enter():
        for first in range(0, share, 12):
            batch = entries[first:min(first + 12, share)]
            names = [cand_ref[i, k] for i, k in batch]
            spots = [place_ref[name] for name in names]
            for (i, k), spot in zip(batch, spots):
                table[jnp.right_shift(spot, 7), jnp.bitwise_and(spot, 127)] = i
                spot_ref[i, k] = spot
        del entries[:share]

    small[0].wait()
    x = x_ref[...].reshape(query_count * token_count, width_in)
    total = x.astype(F32)
    inner = active = None
    for step in range(chunks + 2):
        if step < chunks:
            copies[step][0].wait()
        if step >= 2:
            copies[step - 2][1].wait()
        if step == 1:
            small[2].wait()
            placed.wait()
        if step >= 1:
            enter()
        later = jnp.dot(x, w1_buf[step], preferred_element_type=F32) if step < chunks else None
        if step >= 2:
            total = total + jnp.dot(active, w2_buf[step - 2], preferred_element_type=F32)
        if 1 <= step <= chunks:
            active = (0.5 * inner * (1.0 + lax.erf(inner * (0.5 ** 0.5)))).astype(BF16)
        inner = later
        if step == chunks:
            fetch = pltpu.make_async_copy(table, table_v, table_sem)
            fetch.start()

    for copy in small[3:]:
        copy.wait()
    centered = total - jnp.mean(total, axis=-1, keepdims=True)
    variance = jnp.mean(jnp.square(centered), axis=-1, keepdims=True)
    layer_out = (centered * lax.rsqrt(variance + 1e-12) * gain_ref[...].reshape(1, width_in)).astype(BF16)
    embedded = jnp.dot(layer_out, embed_ref[...], preferred_element_type=F32)
    length = jnp.sum(jnp.square(embedded), axis=-1, keepdims=True)
    vectors = embedded * lax.rsqrt(length + 1e-06)
    token = lax.broadcasted_iota(jnp.int32, vectors.shape, 0)
    for i in range(query_count):
        padded = (token >= i * token_count + lens_ref[i]) & (token < (i + 1) * token_count)
        vectors = jnp.where(padded, 0.0, vectors)
    vectors = vectors.astype(BF16)
    fetch.wait()
    tokens = query_count * token_count
    wanted = table_v[...].astype(F32).astype(BF16)
    out_ref[pl.ds(0, tokens), :] = vectors
    out_ref[pl.ds(tokens, slots), :] = wanted


def encode(
    me,
    query_hidden,
    query_lengths,
    inner_weight,
    outer_weight,
    norm_gain,
    embed_weight,
    half,
    passage_row,
    candidates,
    slots,
    color,
):
    query_count, token_count, d = query_hidden.shape
    ff = inner_weight.shape[1]
    e = embed_weight.shape[1]
    slots = -(-slots // 16) * 16
    assert 2 * half <= e == 128
    chunks = 6
    width = ff // chunks
    tokens = query_count * token_count

    def kernel(*refs):
        encode_kernel(half, color, *refs)

    return pl.pallas_call(
        kernel,
        out_shape=(
            jax.ShapeDtypeStruct((tokens + slots, e), BF16),
            jax.ShapeDtypeStruct(candidates.shape, jnp.int32),
        ),
        in_specs=[SMEM] + [ANY] * 8,
        out_specs=(VMEM, SMEM),
        scratch_shapes=[
            pltpu.VMEM((chunks, d, width), BF16),
            pltpu.VMEM((chunks, width, d), BF16),
            pltpu.SMEM(query_lengths.shape, jnp.int32),
            pltpu.VMEM(passage_row.shape, jnp.int32),
            pltpu.SMEM(passage_row.shape, jnp.int32),
            pltpu.SMEM(candidates.shape, jnp.int32),
            pltpu.VMEM(query_hidden.shape, BF16),
            pltpu.VMEM(norm_gain.shape, F32),
            pltpu.VMEM(embed_weight.shape, BF16),
            pltpu.SMEM((slots, e), jnp.int32),
            pltpu.VMEM((slots, e), jnp.int32),
            pltpu.SemaphoreType.DMA((2, chunks)),
            pltpu.SemaphoreType.DMA((6,)),
            pltpu.SemaphoreType.DMA,
            pltpu.SemaphoreType.DMA,
        ],
        compiler_params=pltpu.CompilerParams(vmem_limit_bytes=60 * 2 ** 20),
        cost_estimate=pl.CostEstimate(
            flops=4 * tokens * d * ff, bytes_accessed=4 * d * ff, transcendentals=tokens * ff
        ),
        name="encode",
    )(
        me,
        query_lengths,
        passage_row,
        candidates,
        query_hidden,
        inner_weight,
        outer_weight,
        norm_gain,
        embed_weight,
    )


def mask_kernel(len0_ref, len1_ref, pass0_ref, pass1_ref, _, out0_ref, out1_ref):
    mask_into(out0_ref, pass0_ref, len0_ref, 0, pass0_ref.shape[0])
    mask_into(out1_ref, pass1_ref, len1_ref, 0, pass1_ref.shape[0])


def mask(lengths, passages, late):
    shape = passages[0].shape
    size = 2 * passages[0].size
    return pl.pallas_call(
        mask_kernel,
        out_shape=[jax.ShapeDtypeStruct(shape, BF16)] * 2,
        in_specs=[SMEM, SMEM, VMEM, VMEM, VMEM],
        out_specs=[VMEM, VMEM],
        compiler_params=pltpu.CompilerParams(vmem_limit_bytes=2 ** 22),
        cost_estimate=pl.CostEstimate(flops=8 * size, bytes_accessed=4 * size, transcendentals=0),
        name="mask",
    )(*lengths, *passages, late)


def score_kernel(slots, token_count, me_ref, own_ref, other_ref, *refs):
    got_refs = refs[:slots]
    out_ref, best_ref, index_v, index, sem = refs[slots:]
    message, lanes = got_refs[0].shape
    half = own_ref.shape[0]
    rows = -(-slots // 16) * 16
    tokens = message - rows
    group = min(slots, 256 // token_count)
    chip = jnp.right_shift(me_ref[0], 1)
    mine = lax.broadcasted_iota(jnp.int32, (rows, lanes), 0) == chip
    for s in range(slots):
        table = got_refs[s][pl.ds(tokens, rows), :].astype(F32)
        query = jnp.sum(jnp.where(mine, table, 0.0), axis=0, keepdims=True)
        index_v[s:s + 1, :] = query.astype(jnp.int32) * token_count
    copy = pltpu.make_async_copy(index_v, index, sem)
    copy.start()
    copy.wait()

    for first, pass_ref in ((half, other_ref), (0, own_ref)):

        def eight(step, carry):
            for part in range(slots // group):
                rows = []
                for j in range(8):
                    p = step * 8 + j
                    picked = jnp.concatenate(
                        [
                            got_refs[s][pl.ds(pl.multiple_of(index[s, first + p], token_count), token_count), :]
                            for s in range(part * group, (part + 1) * group)
                        ],
                        axis=0,
                    )
                    similar = lax.dot_general(pass_ref[p], picked, NT, preferred_element_type=F32)
                    rows.append(jnp.max(similar, axis=0, keepdims=True))
                best_ref[
                    pl.ds(pl.multiple_of(first + step * 8, 8), 8),
                    pl.ds(part * group * token_count, group * token_count),
                ] = jnp.concatenate(rows, axis=0)
            return carry

        lax.fori_loop(0, half // 8, eight, 0)
    wide = best_ref.shape[1]
    source = lax.broadcasted_iota(jnp.int32, (slots, wide), 0)
    column = lax.broadcasted_iota(jnp.int32, (slots, wide), 1)
    start = source * token_count
    ones = jnp.where((column >= start) & (column < start + token_count), 1.0, 0.0).astype(BF16)
    total = sum(lax.dot_general(ones, part, NT, preferred_element_type=F32) for part in split3(best_ref[...]))
    out_ref[...] = jnp.zeros(out_ref.shape, F32)
    for s in range(slots):
        out_ref[pl.ds(jnp.bitwise_xor(chip, s), 1), pl.ds(0, 2 * half)] = total[s:s + 1]


def score(me, got, own, other, token_count):
    half, plen, e = own.shape
    passage_count = 2 * half
    slots = len(got)

    def kernel(*refs):
        score_kernel(slots, token_count, *refs)

    return pl.pallas_call(
        kernel,
        out_shape=jax.ShapeDtypeStruct((slots, e), F32),
        in_specs=[SMEM, VMEM, VMEM] + [VMEM] * slots,
        out_specs=VMEM,
        scratch_shapes=[
            pltpu.VMEM((passage_count, slots * token_count), F32),
            pltpu.VMEM((slots, e), jnp.int32),
            pltpu.SMEM((slots, e), jnp.int32),
            pltpu.SemaphoreType.DMA,
        ],
        compiler_params=pltpu.CompilerParams(vmem_limit_bytes=12 * 2 ** 20),
        cost_estimate=pl.CostEstimate(
            flops=2 * passage_count * slots * token_count * plen * e,
            bytes_accessed=4 * own.size,
            transcendentals=0,
        ),
        name="score",
    )(me, own, other, *got)


def finish_kernel(got_ref, spot_ref, scores_ref, best_ref):
    slots, lanes = got_ref.shape
    query_count, cand_count = scores_ref.shape
    parts = split3(got_ref[...])
    slot_iota = lax.broadcasted_iota(jnp.int32, (slots, cand_count), 0) * lanes
    lane_iota = lax.broadcasted_iota(jnp.int32, (lanes, cand_count), 0)
    row_iota = lax.broadcasted_iota(jnp.int32, (cand_count, cand_count), 0)
    col_iota = lax.broadcasted_iota(jnp.int32, (cand_count, cand_count), 1)
    place = lax.broadcasted_iota(jnp.int32, (cand_count, 128), 1)
    for i in range(query_count):
        spot = spot_ref[i:i + 1, :]
        lane = jnp.bitwise_and(spot, lanes - 1)
        onehot = jnp.where(lane_iota == lane, 1.0, 0.0).astype(BF16)
        picked = sum(jnp.dot(part, onehot, preferred_element_type=F32) for part in parts)
        score_row = jnp.sum(jnp.where(slot_iota == spot - lane, picked, 0.0), axis=0, keepdims=True)
        scores_ref[i:i + 1, :] = score_row
        across = jnp.broadcast_to(score_row, (cand_count, cand_count))
        score_col = jnp.sum(jnp.where(row_iota == col_iota, across, 0.0), axis=1, keepdims=True)
        ahead = (across > score_col) | ((across == score_col) & (col_iota < row_iota))
        rank = jnp.sum(jnp.where(ahead, 1.0, 0.0), axis=1, keepdims=True).astype(jnp.int32)
        ordered = jnp.sum(jnp.where(rank == place, score_col, 0.0), axis=0, keepdims=True)
        best_ref[i:i + 1, :] = ordered[:, :TOPN]


def finish(got, spots):
    return pl.pallas_call(
        finish_kernel,
        out_shape=(
            jax.ShapeDtypeStruct(spots.shape, F32),
            jax.ShapeDtypeStruct((spots.shape[0], TOPN), F32),
        ),
        in_specs=[VMEM, VMEM],
        out_specs=(VMEM, VMEM),
        compiler_params=pltpu.CompilerParams(vmem_limit_bytes=2 ** 21),
        name="finish",
    )(got, spots)


def swap(value, distance):
    size = lax.axis_size("shard")
    return lax.ppermute(value, "shard", [(i, i ^ distance) for i in range(size)])


def per_device(
    query_hidden,
    query_lengths,
    inner_weight,
    outer_weight,
    norm_gain,
    embed_weight,
    passage_vectors,
    passage_lengths,
    passage_row,
    candidates,
):
    size = lax.axis_size("shard")
    slots = size // 2
    inner = 1
    while 4 * inner * inner <= slots:
        inner *= 2
    shift = inner.bit_length()

    def color(index):
        return (index ^ (index >> 1) ^ (index >> shift)) & 1

    groups = [[i for i in range(size) if color(i) == c] for c in range(2)]

    def send(value, distance):
        return swap(value, 2 * distance + color(2 * distance))

    me = lax.axis_index("shard").astype(jnp.int32).reshape(1)
    across = swap(passage_lengths, 1)
    message, spots = encode(
        me,
        query_hidden,
        query_lengths,
        inner_weight,
        outer_weight,
        norm_gain,
        embed_weight,
        passage_vectors.shape[0],
        passage_row,
        candidates,
        slots,
        color,
    )
    message, across, raw = lax.optimization_barrier((message, across, passage_vectors))
    raw = swap(raw, 1)

    got = {0: message}
    distance = slots
    while distance > 1:
        distance //= 2
        got.update({s + distance: send(value, distance) for s, value in got.items()})
    got = [got[s] for s in range(slots)]
    own, other = mask((passage_lengths, across), (passage_vectors, raw), got[inner + 1])
    sums = score(me, got, own, other, query_hidden.shape[1])
    back = lax.all_to_all(sums, "shard", split_axis=0, concat_axis=0, axis_index_groups=groups, tiled=True)
    return finish(back, spots)


def solution(mesh):
    in_specs = (
        P(("groups", "shard"), None, None),
        P(("groups", "shard")),
        P(),
        P(),
        P(),
        P(),
        P(("groups", "shard"), None, None),
        P(("groups", "shard")),
        P("groups"),
        P(("groups", "shard"), None),
    )
    out_specs = (P(("groups", "shard"), None), P(("groups", "shard"), None))
    return jax.shard_map(
        per_device, mesh=mesh, in_specs=in_specs, out_specs=out_specs, check_vma=False
    )
```

```python
import jax
import jax.numpy as jnp
from jax import lax
from jax.experimental import pallas as pl
from jax.experimental.pallas import tpu as pltpu
from jax.sharding import PartitionSpec as P

TOPN = 10
F32 = jnp.float32
BF16 = jnp.bfloat16
NT = (((1,), (1,)), ((), ()))
VMEM = pl.BlockSpec(memory_space=pltpu.VMEM)
SMEM = pl.BlockSpec(memory_space=pltpu.SMEM)
ANY = pl.BlockSpec(memory_space=pl.ANY)


def split3(value):
    high = value.astype(BF16)
    rest = value - high.astype(F32)
    middle = rest.astype(BF16)
    low = (rest - middle.astype(F32)).astype(BF16)
    return high, middle, low


def mask_into(out_ref, pass_ref, len_ref, first, count):
    def mask(p, carry):
        block = pass_ref[p]
        keep = lax.broadcasted_iota(jnp.int32, block.shape, 0) < len_ref[p]
        block = block.astype(F32)
        out_ref[p] = jnp.where(keep, block, jnp.broadcast_to(block[0:1], block.shape)).astype(BF16)
        return carry

    if count <= 8:
        for p in range(first, first + count):
            mask(p, 0)
    else:
        lax.fori_loop(first, first + count, mask, 0, unroll=8)


def encode_kernel(
    half,
    color,
    me_ref,
    lens_hbm,
    row_hbm,
    cand_hbm,
    x_hbm,
    w1_ref,
    w2_ref,
    gain_hbm,
    embed_hbm,
    out_ref,
    spot_ref,
    w1_buf,
    w2_buf,
    lens_ref,
    row_ref,
    place_ref,
    cand_ref,
    x_ref,
    gain_ref,
    embed_ref,
    table,
    table_v,
    sems,
    small_sems,
    place_sem,
    table_sem,
):
    chunks, _, width = w1_buf.shape
    slots, lanes = table_v.shape
    query_count, token_count, width_in = x_ref.shape
    cand_count = cand_ref.shape[1]
    table_v[...] = jnp.zeros(table_v.shape, jnp.int32)
    clear = pltpu.make_async_copy(table_v, table, table_sem)
    clear.start()
    copies = []
    for c in range(chunks):
        first = pltpu.make_async_copy(w1_ref.at[:, pl.ds(c * width, width)], w1_buf.at[c], sems.at[0, c])
        second = pltpu.make_async_copy(w2_ref.at[pl.ds(c * width, width), :], w2_buf.at[c], sems.at[1, c])
        copies.append((first, second))
    small = [
        pltpu.make_async_copy(source, target, small_sems.at[n])
        for n, (source, target) in enumerate(
            (
                (x_hbm, x_ref),
                (row_hbm, row_ref),
                (cand_hbm, cand_ref),
                (lens_hbm, lens_ref),
                (gain_hbm, gain_ref),
                (embed_hbm, embed_ref),
            )
        )
    ]
    for copy in small[:3]:
        copy.start()
    copies[0][0].start()
    copies[1][0].start()
    copies[0][1].start()
    for c in range(2, chunks):
        copies[c][0].start()
        copies[c - 1][1].start()
    copies[-1][1].start()
    for copy in small[3:]:
        copy.start()
    clear.wait()
    small[1].wait()
    row = row_ref[...]
    owner = jnp.floor((row.astype(F32) + 0.5) * (1.0 / half)).astype(jnp.int32)
    opposite = jnp.bitwise_xor(color(owner), color(me_ref[0]))
    row_ref[...] = jnp.right_shift(owner, 1) * lanes + row - owner * half + opposite * half
    placed = pltpu.make_async_copy(row_ref, place_ref, place_sem)
    placed.start()

    entries = [(i, k) for k in range(cand_count) for i in range(query_count)]
    share = -(-len(entries) // chunks)

    def enter():
        for first in range(0, share, 12):
            batch = entries[first:min(first + 12, share)]
            names = [cand_ref[i, k] for i, k in batch]
            spots = [place_ref[name] for name in names]
            for (i, k), spot in zip(batch, spots):
                table[jnp.right_shift(spot, 7), jnp.bitwise_and(spot, 127)] = i
                spot_ref[i, k] = spot
        del entries[:share]

    small[0].wait()
    x = x_ref[...].reshape(query_count * token_count, width_in)
    total = x.astype(F32)
    inner = active = None
    for step in range(chunks + 2):
        if step < chunks:
            copies[step][0].wait()
        if step >= 2:
            copies[step - 2][1].wait()
        if step == 1:
            small[2].wait()
            placed.wait()
        if step >= 1:
            enter()
        later = jnp.dot(x, w1_buf[step], preferred_element_type=F32) if step < chunks else None
        if step >= 2:
            total = total + jnp.dot(active, w2_buf[step - 2], preferred_element_type=F32)
        if 1 <= step <= chunks:
            active = (0.5 * inner * (1.0 + lax.erf(inner * (0.5 ** 0.5)))).astype(BF16)
        inner = later
        if step == chunks:
            fetch = pltpu.make_async_copy(table, table_v, table_sem)
            fetch.start()

    for copy in small[3:]:
        copy.wait()
    centered = total - jnp.mean(total, axis=-1, keepdims=True)
    variance = jnp.mean(jnp.square(centered), axis=-1, keepdims=True)
    layer_out = (centered * lax.rsqrt(variance + 1e-12) * gain_ref[...].reshape(1, width_in)).astype(BF16)
    embedded = jnp.dot(layer_out, embed_ref[...], preferred_element_type=F32)
    length = jnp.sum(jnp.square(embedded), axis=-1, keepdims=True)
    vectors = embedded * lax.rsqrt(length + 1e-06)
    token = lax.broadcasted_iota(jnp.int32, vectors.shape, 0)
    for i in range(query_count):
        padded = (token >= i * token_count + lens_ref[i]) & (token < (i + 1) * token_count)
        vectors = jnp.where(padded, 0.0, vectors)
    vectors = vectors.astype(BF16)
    fetch.wait()
    tokens = query_count * token_count
    wanted = table_v[...].astype(F32).astype(BF16)
    out_ref[pl.ds(0, tokens), :] = vectors
    out_ref[pl.ds(tokens, slots), :] = wanted


def encode(
    me,
    query_hidden,
    query_lengths,
    inner_weight,
    outer_weight,
    norm_gain,
    embed_weight,
    half,
    passage_row,
    candidates,
    slots,
    color,
):
    query_count, token_count, d = query_hidden.shape
    ff = inner_weight.shape[1]
    e = embed_weight.shape[1]
    slots = -(-slots // 16) * 16
    assert 2 * half <= e == 128
    chunks = 6
    width = ff // chunks
    tokens = query_count * token_count

    def kernel(*refs):
        encode_kernel(half, color, *refs)

    return pl.pallas_call(
        kernel,
        out_shape=(
            jax.ShapeDtypeStruct((tokens + slots, e), BF16),
            jax.ShapeDtypeStruct(candidates.shape, jnp.int32),
        ),
        in_specs=[SMEM] + [ANY] * 8,
        out_specs=(VMEM, SMEM),
        scratch_shapes=[
            pltpu.VMEM((chunks, d, width), BF16),
            pltpu.VMEM((chunks, width, d), BF16),
            pltpu.SMEM(query_lengths.shape, jnp.int32),
            pltpu.VMEM(passage_row.shape, jnp.int32),
            pltpu.SMEM(passage_row.shape, jnp.int32),
            pltpu.SMEM(candidates.shape, jnp.int32),
            pltpu.VMEM(query_hidden.shape, BF16),
            pltpu.VMEM(norm_gain.shape, F32),
            pltpu.VMEM(embed_weight.shape, BF16),
            pltpu.SMEM((slots, e), jnp.int32),
            pltpu.VMEM((slots, e), jnp.int32),
            pltpu.SemaphoreType.DMA((2, chunks)),
            pltpu.SemaphoreType.DMA((6,)),
            pltpu.SemaphoreType.DMA,
            pltpu.SemaphoreType.DMA,
        ],
        compiler_params=pltpu.CompilerParams(vmem_limit_bytes=60 * 2 ** 20),
        cost_estimate=pl.CostEstimate(
            flops=4 * tokens * d * ff, bytes_accessed=4 * d * ff, transcendentals=tokens * ff
        ),
        name="encode",
    )(
        me,
        query_lengths,
        passage_row,
        candidates,
        query_hidden,
        inner_weight,
        outer_weight,
        norm_gain,
        embed_weight,
    )


def mask_kernel(len0_ref, len1_ref, pass0_ref, pass1_ref, _, out0_ref, out1_ref):
    mask_into(out0_ref, pass0_ref, len0_ref, 0, pass0_ref.shape[0])
    mask_into(out1_ref, pass1_ref, len1_ref, 0, pass1_ref.shape[0])


def mask(lengths, passages, late):
    shape = passages[0].shape
    size = 2 * passages[0].size
    return pl.pallas_call(
        mask_kernel,
        out_shape=[jax.ShapeDtypeStruct(shape, BF16)] * 2,
        in_specs=[SMEM, SMEM, VMEM, VMEM, VMEM],
        out_specs=[VMEM, VMEM],
        compiler_params=pltpu.CompilerParams(vmem_limit_bytes=2 ** 22),
        cost_estimate=pl.CostEstimate(flops=8 * size, bytes_accessed=4 * size, transcendentals=0),
        name="mask",
    )(*lengths, *passages, late)


def score_kernel(slots, token_count, me_ref, own_ref, other_ref, *refs):
    got_refs = refs[:slots]
    out_ref, best_ref, index_v, index, sem = refs[slots:]
    message, lanes = got_refs[0].shape
    half = own_ref.shape[0]
    rows = -(-slots // 16) * 16
    tokens = message - rows
    group = min(slots, 256 // token_count)
    chip = jnp.right_shift(me_ref[0], 1)
    mine = lax.broadcasted_iota(jnp.int32, (rows, lanes), 0) == chip
    for s in range(slots):
        table = got_refs[s][pl.ds(tokens, rows), :].astype(F32)
        query = jnp.sum(jnp.where(mine, table, 0.0), axis=0, keepdims=True)
        index_v[s:s + 1, :] = query.astype(jnp.int32) * token_count
    copy = pltpu.make_async_copy(index_v, index, sem)
    copy.start()
    copy.wait()

    for first, pass_ref in ((half, other_ref), (0, own_ref)):

        def eight(step, carry):
            for part in range(slots // group):
                rows = []
                for j in range(8):
                    p = step * 8 + j
                    picked = jnp.concatenate(
                        [
                            got_refs[s][pl.ds(pl.multiple_of(index[s, first + p], token_count), token_count), :]
                            for s in range(part * group, (part + 1) * group)
                        ],
                        axis=0,
                    )
                    similar = lax.dot_general(pass_ref[p], picked, NT, preferred_element_type=F32)
                    rows.append(jnp.max(similar, axis=0, keepdims=True))
                best_ref[
                    pl.ds(pl.multiple_of(first + step * 8, 8), 8),
                    pl.ds(part * group * token_count, group * token_count),
                ] = jnp.concatenate(rows, axis=0)
            return carry

        lax.fori_loop(0, half // 8, eight, 0)
    wide = best_ref.shape[1]
    source = lax.broadcasted_iota(jnp.int32, (slots, wide), 0)
    column = lax.broadcasted_iota(jnp.int32, (slots, wide), 1)
    start = source * token_count
    ones = jnp.where((column >= start) & (column < start + token_count), 1.0, 0.0).astype(BF16)
    total = sum(lax.dot_general(ones, part, NT, preferred_element_type=F32) for part in split3(best_ref[...]))
    out_ref[...] = jnp.zeros(out_ref.shape, F32)
    for s in range(slots):
        out_ref[pl.ds(jnp.bitwise_xor(chip, s), 1), pl.ds(0, 2 * half)] = total[s:s + 1]


def score(me, got, own, other, token_count):
    half, plen, e = own.shape
    passage_count = 2 * half
    slots = len(got)

    def kernel(*refs):
        score_kernel(slots, token_count, *refs)

    return pl.pallas_call(
        kernel,
        out_shape=jax.ShapeDtypeStruct((slots, e), F32),
        in_specs=[SMEM, VMEM, VMEM] + [VMEM] * slots,
        out_specs=VMEM,
        scratch_shapes=[
            pltpu.VMEM((passage_count, slots * token_count), F32),
            pltpu.VMEM((slots, e), jnp.int32),
            pltpu.SMEM((slots, e), jnp.int32),
            pltpu.SemaphoreType.DMA,
        ],
        compiler_params=pltpu.CompilerParams(vmem_limit_bytes=12 * 2 ** 20),
        cost_estimate=pl.CostEstimate(
            flops=2 * passage_count * slots * token_count * plen * e,
            bytes_accessed=4 * own.size,
            transcendentals=0,
        ),
        name="score",
    )(me, own, other, *got)


def finish_kernel(got_ref, spot_ref, scores_ref, best_ref):
    slots, lanes = got_ref.shape
    query_count, cand_count = scores_ref.shape
    parts = split3(got_ref[...])
    slot_iota = lax.broadcasted_iota(jnp.int32, (slots, cand_count), 0) * lanes
    lane_iota = lax.broadcasted_iota(jnp.int32, (lanes, cand_count), 0)
    row_iota = lax.broadcasted_iota(jnp.int32, (cand_count, cand_count), 0)
    col_iota = lax.broadcasted_iota(jnp.int32, (cand_count, cand_count), 1)
    place = lax.broadcasted_iota(jnp.int32, (cand_count, 128), 1)
    for i in range(query_count):
        spot = spot_ref[i:i + 1, :]
        lane = jnp.bitwise_and(spot, lanes - 1)
        onehot = jnp.where(lane_iota == lane, 1.0, 0.0).astype(BF16)
        picked = sum(jnp.dot(part, onehot, preferred_element_type=F32) for part in parts)
        score_row = jnp.sum(jnp.where(slot_iota == spot - lane, picked, 0.0), axis=0, keepdims=True)
        scores_ref[i:i + 1, :] = score_row
        across = jnp.broadcast_to(score_row, (cand_count, cand_count))
        score_col = jnp.sum(jnp.where(row_iota == col_iota, across, 0.0), axis=1, keepdims=True)
        ahead = (across > score_col) | ((across == score_col) & (col_iota < row_iota))
        rank = jnp.sum(jnp.where(ahead, 1.0, 0.0), axis=1, keepdims=True).astype(jnp.int32)
        ordered = jnp.sum(jnp.where(rank == place, score_col, 0.0), axis=0, keepdims=True)
        best_ref[i:i + 1, :] = ordered[:, :TOPN]


def finish(got, spots):
    return pl.pallas_call(
        finish_kernel,
        out_shape=(
            jax.ShapeDtypeStruct(spots.shape, F32),
            jax.ShapeDtypeStruct((spots.shape[0], TOPN), F32),
        ),
        in_specs=[VMEM, VMEM],
        out_specs=(VMEM, VMEM),
        compiler_params=pltpu.CompilerParams(vmem_limit_bytes=2 ** 21),
        name="finish",
    )(got, spots)


def swap(value, distance):
    size = lax.axis_size("shard")
    return lax.ppermute(value, "shard", [(i, i ^ distance) for i in range(size)])


def per_device(
    query_hidden,
    query_lengths,
    inner_weight,
    outer_weight,
    norm_gain,
    embed_weight,
    passage_vectors,
    passage_lengths,
    passage_row,
    candidates,
):
    size = lax.axis_size("shard")
    slots = size // 2
    inner = 1
    while 4 * inner * inner <= slots:
        inner *= 2
    shift = inner.bit_length()

    def color(index):
        return (index ^ (index >> 1) ^ (index >> shift)) & 1

    groups = [[i for i in range(size) if color(i) == c] for c in range(2)]

    def send(value, distance):
        return swap(value, 2 * distance + color(2 * distance))

    me = lax.axis_index("shard").astype(jnp.int32).reshape(1)
    raw = swap(passage_vectors, 1)
    across = swap(passage_lengths, 1)
    message, spots = encode(
        me,
        query_hidden,
        query_lengths,
        inner_weight,
        outer_weight,
        norm_gain,
        embed_weight,
        passage_vectors.shape[0],
        passage_row,
        candidates,
        slots,
        color,
    )
    message, across = lax.optimization_barrier((message, across))

    got = {0: message}
    distance = slots
    while distance > 1:
        distance //= 2
        got.update({s + distance: send(value, distance) for s, value in got.items()})
    got = [got[s] for s in range(slots)]
    own, other = mask((passage_lengths, across), (passage_vectors, raw), got[inner + 1])
    sums = score(me, got, own, other, query_hidden.shape[1])
    back = lax.all_to_all(sums, "shard", split_axis=0, concat_axis=0, axis_index_groups=groups, tiled=True)
    return finish(back, spots)


def solution(mesh):
    in_specs = (
        P(("groups", "shard"), None, None),
        P(("groups", "shard")),
        P(),
        P(),
        P(),
        P(),
        P(("groups", "shard"), None, None),
        P(("groups", "shard")),
        P("groups"),
        P(("groups", "shard"), None),
    )
    out_specs = (P(("groups", "shard"), None), P(("groups", "shard"), None))
    return jax.shard_map(
        per_device, mesh=mesh, in_specs=in_specs, out_specs=out_specs, check_vma=False
    )
```

```python
import jax
import jax.numpy as jnp
from jax import lax
from jax.experimental import pallas as pl
from jax.experimental.pallas import tpu as pltpu
from jax.sharding import PartitionSpec as P

TOPN = 10
F32 = jnp.float32
BF16 = jnp.bfloat16
NT = (((1,), (1,)), ((), ()))
VMEM = pl.BlockSpec(memory_space=pltpu.VMEM)
SMEM = pl.BlockSpec(memory_space=pltpu.SMEM)
ANY = pl.BlockSpec(memory_space=pl.ANY)


def split3(value):
    high = value.astype(BF16)
    rest = value - high.astype(F32)
    middle = rest.astype(BF16)
    low = (rest - middle.astype(F32)).astype(BF16)
    return high, middle, low


ERF_AS_TANH = (
    0.7978849414561846,
    0.0363330845700197,
    -3.259496904628066e-05,
    -5.53061960886502e-05,
    3.964744776164795e-06,
    -1.3226336338657016e-07,
    1.7561713006335889e-09,
)


def gelu(value):
    square = value * value
    factor = ERF_AS_TANH[-1] * square + ERF_AS_TANH[-2]
    for coefficient in ERF_AS_TANH[-3::-1]:
        factor = factor * square + coefficient
    half = 0.5 * value
    return half + half * jnp.tanh(value * factor)


def mask_into(out_ref, pass_ref, len_ref, first, count):
    def mask(p, carry):
        block = pass_ref[p]
        keep = lax.broadcasted_iota(jnp.int32, block.shape, 0) < len_ref[p]
        block = block.astype(F32)
        out_ref[p] = jnp.where(keep, block, jnp.broadcast_to(block[0:1], block.shape)).astype(BF16)
        return carry

    if count <= 8:
        for p in range(first, first + count):
            mask(p, 0)
    else:
        lax.fori_loop(first, first + count, mask, 0, unroll=8)


def encode_kernel(
    half,
    color,
    me_ref,
    lens_hbm,
    row_hbm,
    cand_hbm,
    x_hbm,
    w1_ref,
    w2_ref,
    gain_hbm,
    embed_hbm,
    out_ref,
    spot_ref,
    w1_buf,
    w2_buf,
    lens_ref,
    row_ref,
    place_ref,
    cand_ref,
    x_ref,
    gain_ref,
    embed_ref,
    table,
    table_v,
    sems,
    small_sems,
    place_sem,
    table_sem,
):
    chunks, _, width = w1_buf.shape
    slots, lanes = table_v.shape
    query_count, token_count, width_in = x_ref.shape
    cand_count = cand_ref.shape[1]
    table_v[...] = jnp.zeros(table_v.shape, jnp.int32)
    clear = pltpu.make_async_copy(table_v, table, table_sem)
    clear.start()
    copies = []
    for c in range(chunks):
        first = pltpu.make_async_copy(w1_ref.at[:, pl.ds(c * width, width)], w1_buf.at[c], sems.at[0, c])
        second = pltpu.make_async_copy(w2_ref.at[pl.ds(c * width, width), :], w2_buf.at[c], sems.at[1, c])
        copies.append((first, second))
    small = [
        pltpu.make_async_copy(source, target, small_sems.at[n])
        for n, (source, target) in enumerate(
            (
                (x_hbm, x_ref),
                (row_hbm, row_ref),
                (cand_hbm, cand_ref),
                (lens_hbm, lens_ref),
                (gain_hbm, gain_ref),
                (embed_hbm, embed_ref),
            )
        )
    ]
    for copy in small[:3]:
        copy.start()
    copies[0][0].start()
    copies[1][0].start()
    copies[0][1].start()
    for c in range(2, chunks):
        copies[c][0].start()
        copies[c - 1][1].start()
    copies[-1][1].start()
    for copy in small[3:]:
        copy.start()
    clear.wait()
    small[1].wait()
    row = row_ref[...]
    owner = jnp.floor((row.astype(F32) + 0.5) * (1.0 / half)).astype(jnp.int32)
    opposite = jnp.bitwise_xor(color(owner), color(me_ref[0]))
    row_ref[...] = jnp.right_shift(owner, 1) * lanes + row - owner * half + opposite * half
    placed = pltpu.make_async_copy(row_ref, place_ref, place_sem)
    placed.start()

    entries = [(i, k) for k in range(cand_count) for i in range(query_count)]
    share = -(-len(entries) // chunks)

    def enter():
        for first in range(0, share, 12):
            batch = entries[first:min(first + 12, share)]
            names = [cand_ref[i, k] for i, k in batch]
            spots = [place_ref[name] for name in names]
            for (i, k), spot in zip(batch, spots):
                table[jnp.right_shift(spot, 7), jnp.bitwise_and(spot, 127)] = i
                spot_ref[i, k] = spot
        del entries[:share]

    small[0].wait()
    x = x_ref[...].reshape(query_count * token_count, width_in)
    total = x.astype(F32)
    inner = active = None
    for step in range(chunks + 2):
        if step < chunks:
            copies[step][0].wait()
        if step >= 2:
            copies[step - 2][1].wait()
        if step == 1:
            small[2].wait()
            placed.wait()
        if step >= 1:
            enter()
        later = jnp.dot(x, w1_buf[step], preferred_element_type=F32) if step < chunks else None
        if step >= 2:
            total = total + jnp.dot(active, w2_buf[step - 2], preferred_element_type=F32)
        if 1 <= step <= chunks:
            active = gelu(inner).astype(BF16)
        inner = later
        if step == chunks:
            fetch = pltpu.make_async_copy(table, table_v, table_sem)
            fetch.start()

    for copy in small[3:]:
        copy.wait()
    centered = total - jnp.mean(total, axis=-1, keepdims=True)
    variance = jnp.mean(jnp.square(centered), axis=-1, keepdims=True)
    layer_out = (centered * lax.rsqrt(variance + 1e-12) * gain_ref[...].reshape(1, width_in)).astype(BF16)
    embedded = jnp.dot(layer_out, embed_ref[...], preferred_element_type=F32)
    length = jnp.sum(jnp.square(embedded), axis=-1, keepdims=True)
    vectors = embedded * lax.rsqrt(length + 1e-06)
    token = lax.broadcasted_iota(jnp.int32, vectors.shape, 0)
    for i in range(query_count):
        padded = (token >= i * token_count + lens_ref[i]) & (token < (i + 1) * token_count)
        vectors = jnp.where(padded, 0.0, vectors)
    vectors = vectors.astype(BF16)
    fetch.wait()
    tokens = query_count * token_count
    wanted = table_v[...].astype(F32).astype(BF16)
    out_ref[pl.ds(0, tokens), :] = vectors
    out_ref[pl.ds(tokens, slots), :] = wanted


def encode(
    me,
    query_hidden,
    query_lengths,
    inner_weight,
    outer_weight,
    norm_gain,
    embed_weight,
    half,
    passage_row,
    candidates,
    slots,
    color,
):
    query_count, token_count, d = query_hidden.shape
    ff = inner_weight.shape[1]
    e = embed_weight.shape[1]
    slots = -(-slots // 16) * 16
    assert 2 * half <= e == 128
    chunks = 6
    width = ff // chunks
    tokens = query_count * token_count

    def kernel(*refs):
        encode_kernel(half, color, *refs)

    return pl.pallas_call(
        kernel,
        out_shape=(
            jax.ShapeDtypeStruct((tokens + slots, e), BF16),
            jax.ShapeDtypeStruct(candidates.shape, jnp.int32),
        ),
        in_specs=[SMEM] + [ANY] * 8,
        out_specs=(VMEM, SMEM),
        scratch_shapes=[
            pltpu.VMEM((chunks, d, width), BF16),
            pltpu.VMEM((chunks, width, d), BF16),
            pltpu.SMEM(query_lengths.shape, jnp.int32),
            pltpu.VMEM(passage_row.shape, jnp.int32),
            pltpu.SMEM(passage_row.shape, jnp.int32),
            pltpu.SMEM(candidates.shape, jnp.int32),
            pltpu.VMEM(query_hidden.shape, BF16),
            pltpu.VMEM(norm_gain.shape, F32),
            pltpu.VMEM(embed_weight.shape, BF16),
            pltpu.SMEM((slots, e), jnp.int32),
            pltpu.VMEM((slots, e), jnp.int32),
            pltpu.SemaphoreType.DMA((2, chunks)),
            pltpu.SemaphoreType.DMA((6,)),
            pltpu.SemaphoreType.DMA,
            pltpu.SemaphoreType.DMA,
        ],
        compiler_params=pltpu.CompilerParams(vmem_limit_bytes=60 * 2 ** 20),
        cost_estimate=pl.CostEstimate(
            flops=4 * tokens * d * ff, bytes_accessed=4 * d * ff, transcendentals=tokens * ff
        ),
        name="encode",
    )(
        me,
        query_lengths,
        passage_row,
        candidates,
        query_hidden,
        inner_weight,
        outer_weight,
        norm_gain,
        embed_weight,
    )


def mask_kernel(len0_ref, len1_ref, pass0_ref, pass1_ref, _, out0_ref, out1_ref):
    mask_into(out0_ref, pass0_ref, len0_ref, 0, pass0_ref.shape[0])
    mask_into(out1_ref, pass1_ref, len1_ref, 0, pass1_ref.shape[0])


def mask(lengths, passages, late):
    shape = passages[0].shape
    size = 2 * passages[0].size
    return pl.pallas_call(
        mask_kernel,
        out_shape=[jax.ShapeDtypeStruct(shape, BF16)] * 2,
        in_specs=[SMEM, SMEM, VMEM, VMEM, VMEM],
        out_specs=[VMEM, VMEM],
        compiler_params=pltpu.CompilerParams(vmem_limit_bytes=2 ** 22),
        cost_estimate=pl.CostEstimate(flops=8 * size, bytes_accessed=4 * size, transcendentals=0),
        name="mask",
    )(*lengths, *passages, late)


def score_kernel(slots, token_count, me_ref, own_ref, other_ref, *refs):
    got_refs = refs[:slots]
    out_ref, best_ref, index_v, index, sem = refs[slots:]
    message, lanes = got_refs[0].shape
    half = own_ref.shape[0]
    rows = -(-slots // 16) * 16
    tokens = message - rows
    group = min(slots, 256 // token_count)
    chip = jnp.right_shift(me_ref[0], 1)
    mine = lax.broadcasted_iota(jnp.int32, (rows, lanes), 0) == chip
    for s in range(slots):
        table = got_refs[s][pl.ds(tokens, rows), :].astype(F32)
        query = jnp.sum(jnp.where(mine, table, 0.0), axis=0, keepdims=True)
        index_v[s:s + 1, :] = query.astype(jnp.int32) * token_count
    copy = pltpu.make_async_copy(index_v, index, sem)
    copy.start()
    copy.wait()

    for first, pass_ref in ((half, other_ref), (0, own_ref)):

        def eight(step, carry):
            for part in range(slots // group):
                rows = []
                for j in range(8):
                    p = step * 8 + j
                    picked = jnp.concatenate(
                        [
                            got_refs[s][pl.ds(pl.multiple_of(index[s, first + p], token_count), token_count), :]
                            for s in range(part * group, (part + 1) * group)
                        ],
                        axis=0,
                    )
                    similar = lax.dot_general(pass_ref[p], picked, NT, preferred_element_type=F32)
                    rows.append(jnp.max(similar, axis=0, keepdims=True))
                best_ref[
                    pl.ds(pl.multiple_of(first + step * 8, 8), 8),
                    pl.ds(part * group * token_count, group * token_count),
                ] = jnp.concatenate(rows, axis=0)
            return carry

        lax.fori_loop(0, half // 8, eight, 0)
    wide = best_ref.shape[1]
    source = lax.broadcasted_iota(jnp.int32, (slots, wide), 0)
    column = lax.broadcasted_iota(jnp.int32, (slots, wide), 1)
    start = source * token_count
    ones = jnp.where((column >= start) & (column < start + token_count), 1.0, 0.0).astype(BF16)
    total = sum(lax.dot_general(ones, part, NT, preferred_element_type=F32) for part in split3(best_ref[...]))
    out_ref[...] = jnp.zeros(out_ref.shape, F32)
    for s in range(slots):
        out_ref[pl.ds(jnp.bitwise_xor(chip, s), 1), pl.ds(0, 2 * half)] = total[s:s + 1]


def score(me, got, own, other, token_count):
    half, plen, e = own.shape
    passage_count = 2 * half
    slots = len(got)

    def kernel(*refs):
        score_kernel(slots, token_count, *refs)

    return pl.pallas_call(
        kernel,
        out_shape=jax.ShapeDtypeStruct((slots, e), F32),
        in_specs=[SMEM, VMEM, VMEM] + [VMEM] * slots,
        out_specs=VMEM,
        scratch_shapes=[
            pltpu.VMEM((passage_count, slots * token_count), F32),
            pltpu.VMEM((slots, e), jnp.int32),
            pltpu.SMEM((slots, e), jnp.int32),
            pltpu.SemaphoreType.DMA,
        ],
        compiler_params=pltpu.CompilerParams(vmem_limit_bytes=12 * 2 ** 20),
        cost_estimate=pl.CostEstimate(
            flops=2 * passage_count * slots * token_count * plen * e,
            bytes_accessed=4 * own.size,
            transcendentals=0,
        ),
        name="score",
    )(me, own, other, *got)


def finish_kernel(got_ref, spot_ref, scores_ref, best_ref):
    slots, lanes = got_ref.shape
    query_count, cand_count = scores_ref.shape
    parts = split3(got_ref[...])
    slot_iota = lax.broadcasted_iota(jnp.int32, (slots, cand_count), 0) * lanes
    lane_iota = lax.broadcasted_iota(jnp.int32, (lanes, cand_count), 0)
    row_iota = lax.broadcasted_iota(jnp.int32, (cand_count, cand_count), 0)
    col_iota = lax.broadcasted_iota(jnp.int32, (cand_count, cand_count), 1)
    place = lax.broadcasted_iota(jnp.int32, (cand_count, 128), 1)
    for i in range(query_count):
        spot = spot_ref[i:i + 1, :]
        lane = jnp.bitwise_and(spot, lanes - 1)
        onehot = jnp.where(lane_iota == lane, 1.0, 0.0).astype(BF16)
        picked = sum(jnp.dot(part, onehot, preferred_element_type=F32) for part in parts)
        score_row = jnp.sum(jnp.where(slot_iota == spot - lane, picked, 0.0), axis=0, keepdims=True)
        scores_ref[i:i + 1, :] = score_row
        across = jnp.broadcast_to(score_row, (cand_count, cand_count))
        score_col = jnp.sum(jnp.where(row_iota == col_iota, across, 0.0), axis=1, keepdims=True)
        ahead = (across > score_col) | ((across == score_col) & (col_iota < row_iota))
        rank = jnp.sum(jnp.where(ahead, 1.0, 0.0), axis=1, keepdims=True).astype(jnp.int32)
        ordered = jnp.sum(jnp.where(rank == place, score_col, 0.0), axis=0, keepdims=True)
        best_ref[i:i + 1, :] = ordered[:, :TOPN]


def finish(got, spots):
    return pl.pallas_call(
        finish_kernel,
        out_shape=(
            jax.ShapeDtypeStruct(spots.shape, F32),
            jax.ShapeDtypeStruct((spots.shape[0], TOPN), F32),
        ),
        in_specs=[VMEM, VMEM],
        out_specs=(VMEM, VMEM),
        compiler_params=pltpu.CompilerParams(vmem_limit_bytes=2 ** 21),
        name="finish",
    )(got, spots)


def swap(value, distance):
    size = lax.axis_size("shard")
    return lax.ppermute(value, "shard", [(i, i ^ distance) for i in range(size)])


def per_device(
    query_hidden,
    query_lengths,
    inner_weight,
    outer_weight,
    norm_gain,
    embed_weight,
    passage_vectors,
    passage_lengths,
    passage_row,
    candidates,
):
    size = lax.axis_size("shard")
    slots = size // 2
    inner = 1
    while 4 * inner * inner <= slots:
        inner *= 2
    shift = inner.bit_length()

    def color(index):
        return (index ^ (index >> 1) ^ (index >> shift)) & 1

    groups = [[i for i in range(size) if color(i) == c] for c in range(2)]

    def send(value, distance):
        return swap(value, 2 * distance + color(2 * distance))

    me = lax.axis_index("shard").astype(jnp.int32).reshape(1)
    across = swap(passage_lengths, 1)
    message, spots = encode(
        me,
        query_hidden,
        query_lengths,
        inner_weight,
        outer_weight,
        norm_gain,
        embed_weight,
        passage_vectors.shape[0],
        passage_row,
        candidates,
        slots,
        color,
    )
    message, across, raw = lax.optimization_barrier((message, across, passage_vectors))
    raw = swap(raw, 1)

    line = [message] + [send(message, d) for d in range(slots - inner, 0, -inner)][::-1]
    got = [line[s // inner] if s % inner == 0 else send(line[s // inner], s % inner) for s in range(slots)]
    own, other = mask((passage_lengths, across), (passage_vectors, raw), got[inner + 1])
    sums = score(me, got, own, other, query_hidden.shape[1])
    back = lax.all_to_all(sums, "shard", split_axis=0, concat_axis=0, axis_index_groups=groups, tiled=True)
    return finish(back, spots)


def solution(mesh):
    in_specs = (
        P(("groups", "shard"), None, None),
        P(("groups", "shard")),
        P(),
        P(),
        P(),
        P(),
        P(("groups", "shard"), None, None),
        P(("groups", "shard")),
        P("groups"),
        P(("groups", "shard"), None),
    )
    out_specs = (P(("groups", "shard"), None), P(("groups", "shard"), None))
    return jax.shard_map(
        per_device, mesh=mesh, in_specs=in_specs, out_specs=out_specs, check_vma=False
    )
```

```python
import jax
import jax.numpy as jnp
from jax import lax
from jax.experimental import pallas as pl
from jax.experimental.pallas import tpu as pltpu
from jax.sharding import PartitionSpec as P

TOPN = 10
F32 = jnp.float32
BF16 = jnp.bfloat16
NT = (((1,), (1,)), ((), ()))
VMEM = pl.BlockSpec(memory_space=pltpu.VMEM)
SMEM = pl.BlockSpec(memory_space=pltpu.SMEM)
ANY = pl.BlockSpec(memory_space=pl.ANY)


def split3(value):
    high = value.astype(BF16)
    rest = value - high.astype(F32)
    middle = rest.astype(BF16)
    low = (rest - middle.astype(F32)).astype(BF16)
    return high, middle, low


def mask_into(out_ref, pass_ref, len_ref, first, count):
    def mask(p, carry):
        block = pass_ref[p]
        keep = lax.broadcasted_iota(jnp.int32, block.shape, 0) < len_ref[p]
        block = block.astype(F32)
        out_ref[p] = jnp.where(keep, block, jnp.broadcast_to(block[0:1], block.shape)).astype(BF16)
        return carry

    if count <= 8:
        for p in range(first, first + count):
            mask(p, 0)
    else:
        lax.fori_loop(first, first + count, mask, 0, unroll=8)


def encode_kernel(
    half,
    color,
    me_ref,
    lens_hbm,
    row_hbm,
    cand_hbm,
    x_hbm,
    w1_ref,
    w2_ref,
    gain_hbm,
    embed_hbm,
    out_ref,
    spot_ref,
    w1_buf,
    w2_buf,
    lens_ref,
    row_ref,
    place_ref,
    cand_ref,
    x_ref,
    gain_ref,
    embed_ref,
    table,
    table_v,
    sems,
    small_sems,
    place_sem,
    table_sem,
):
    chunks, _, width = w1_buf.shape
    slots, lanes = table_v.shape
    query_count, token_count, width_in = x_ref.shape
    cand_count = cand_ref.shape[1]
    table_v[...] = jnp.zeros(table_v.shape, jnp.int32)
    clear = pltpu.make_async_copy(table_v, table, table_sem)
    clear.start()
    copies = []
    for c in range(chunks):
        first = pltpu.make_async_copy(w1_ref.at[:, pl.ds(c * width, width)], w1_buf.at[c], sems.at[0, c])
        second = pltpu.make_async_copy(w2_ref.at[pl.ds(c * width, width), :], w2_buf.at[c], sems.at[1, c])
        copies.append((first, second))
    small = [
        pltpu.make_async_copy(source, target, small_sems.at[n])
        for n, (source, target) in enumerate(
            (
                (x_hbm, x_ref),
                (row_hbm, row_ref),
                (cand_hbm, cand_ref),
                (lens_hbm, lens_ref),
                (gain_hbm, gain_ref),
                (embed_hbm, embed_ref),
            )
        )
    ]
    for copy in small[:3]:
        copy.start()
    copies[0][0].start()
    copies[1][0].start()
    copies[0][1].start()
    for c in range(2, chunks):
        copies[c][0].start()
        copies[c - 1][1].start()
    copies[-1][1].start()
    for copy in small[3:]:
        copy.start()
    clear.wait()
    small[1].wait()
    row = row_ref[...]
    owner = jnp.floor((row.astype(F32) + 0.5) * (1.0 / half)).astype(jnp.int32)
    opposite = jnp.bitwise_xor(color(owner), color(me_ref[0]))
    row_ref[...] = jnp.right_shift(owner, 1) * lanes + row - owner * half + opposite * half
    placed = pltpu.make_async_copy(row_ref, place_ref, place_sem)
    placed.start()

    entries = [(i, k) for k in range(cand_count) for i in range(query_count)]
    share = -(-len(entries) // chunks)

    def enter():
        for first in range(0, share, 12):
            batch = entries[first:min(first + 12, share)]
            names = [cand_ref[i, k] for i, k in batch]
            spots = [place_ref[name] for name in names]
            for (i, k), spot in zip(batch, spots):
                table[jnp.right_shift(spot, 7), jnp.bitwise_and(spot, 127)] = i
                spot_ref[i, k] = spot
        del entries[:share]

    small[0].wait()
    x = x_ref[...].reshape(query_count * token_count, width_in)
    total = x.astype(F32)
    inner = active = None
    for step in range(chunks + 2):
        if step < chunks:
            copies[step][0].wait()
        if step >= 2:
            copies[step - 2][1].wait()
        if step == 1:
            small[2].wait()
            placed.wait()
        if step >= 1:
            enter()
        later = jnp.dot(x, w1_buf[step], preferred_element_type=F32) if step < chunks else None
        if step >= 2:
            total = total + jnp.dot(active, w2_buf[step - 2], preferred_element_type=F32)
        if 1 <= step <= chunks:
            active = (0.5 * inner * (1.0 + lax.erf(inner * (0.5 ** 0.5)))).astype(BF16)
        inner = later
        if step == chunks:
            fetch = pltpu.make_async_copy(table, table_v, table_sem)
            fetch.start()

    for copy in small[3:]:
        copy.wait()
    centered = total - jnp.mean(total, axis=-1, keepdims=True)
    variance = jnp.mean(jnp.square(centered), axis=-1, keepdims=True)
    layer_out = (centered * lax.rsqrt(variance + 1e-12) * gain_ref[...].reshape(1, width_in)).astype(BF16)
    embedded = jnp.dot(layer_out, embed_ref[...], preferred_element_type=F32)
    length = jnp.sum(jnp.square(embedded), axis=-1, keepdims=True)
    vectors = embedded * lax.rsqrt(length + 1e-06)
    token = lax.broadcasted_iota(jnp.int32, vectors.shape, 0)
    for i in range(query_count):
        padded = (token >= i * token_count + lens_ref[i]) & (token < (i + 1) * token_count)
        vectors = jnp.where(padded, 0.0, vectors)
    vectors = vectors.astype(BF16)
    fetch.wait()
    tokens = query_count * token_count
    wanted = table_v[...].astype(F32).astype(BF16)
    out_ref[pl.ds(0, tokens), :] = vectors
    out_ref[pl.ds(tokens, slots), :] = wanted


def encode(
    me,
    query_hidden,
    query_lengths,
    inner_weight,
    outer_weight,
    norm_gain,
    embed_weight,
    half,
    passage_row,
    candidates,
    slots,
    color,
):
    query_count, token_count, d = query_hidden.shape
    ff = inner_weight.shape[1]
    e = embed_weight.shape[1]
    slots = -(-slots // 16) * 16
    assert 2 * half <= e == 128
    chunks = 6
    width = ff // chunks
    tokens = query_count * token_count

    def kernel(*refs):
        encode_kernel(half, color, *refs)

    return pl.pallas_call(
        kernel,
        out_shape=(
            jax.ShapeDtypeStruct((tokens + slots, e), BF16),
            jax.ShapeDtypeStruct(candidates.shape, jnp.int32),
        ),
        in_specs=[SMEM] + [ANY] * 8,
        out_specs=(VMEM, SMEM),
        scratch_shapes=[
            pltpu.VMEM((chunks, d, width), BF16),
            pltpu.VMEM((chunks, width, d), BF16),
            pltpu.SMEM(query_lengths.shape, jnp.int32),
            pltpu.VMEM(passage_row.shape, jnp.int32),
            pltpu.SMEM(passage_row.shape, jnp.int32),
            pltpu.SMEM(candidates.shape, jnp.int32),
            pltpu.VMEM(query_hidden.shape, BF16),
            pltpu.VMEM(norm_gain.shape, F32),
            pltpu.VMEM(embed_weight.shape, BF16),
            pltpu.SMEM((slots, e), jnp.int32),
            pltpu.VMEM((slots, e), jnp.int32),
            pltpu.SemaphoreType.DMA((2, chunks)),
            pltpu.SemaphoreType.DMA((6,)),
            pltpu.SemaphoreType.DMA,
            pltpu.SemaphoreType.DMA,
        ],
        compiler_params=pltpu.CompilerParams(vmem_limit_bytes=60 * 2 ** 20),
        cost_estimate=pl.CostEstimate(
            flops=4 * tokens * d * ff, bytes_accessed=4 * d * ff, transcendentals=tokens * ff
        ),
        name="encode",
    )(
        me,
        query_lengths,
        passage_row,
        candidates,
        query_hidden,
        inner_weight,
        outer_weight,
        norm_gain,
        embed_weight,
    )


def mask_kernel(len0_ref, len1_ref, pass0_ref, pass1_ref, _, out0_ref, out1_ref):
    mask_into(out0_ref, pass0_ref, len0_ref, 0, pass0_ref.shape[0])
    mask_into(out1_ref, pass1_ref, len1_ref, 0, pass1_ref.shape[0])


def mask(lengths, passages, late):
    shape = passages[0].shape
    size = 2 * passages[0].size
    return pl.pallas_call(
        mask_kernel,
        out_shape=[jax.ShapeDtypeStruct(shape, BF16)] * 2,
        in_specs=[SMEM, SMEM, VMEM, VMEM, VMEM],
        out_specs=[VMEM, VMEM],
        compiler_params=pltpu.CompilerParams(vmem_limit_bytes=2 ** 22),
        cost_estimate=pl.CostEstimate(flops=8 * size, bytes_accessed=4 * size, transcendentals=0),
        name="mask",
    )(*lengths, *passages, late)


def score_kernel(slots, token_count, me_ref, own_ref, other_ref, *refs):
    got_refs = refs[:slots]
    out_ref, best_ref, index_v, index, sem = refs[slots:]
    message, lanes = got_refs[0].shape
    half = own_ref.shape[0]
    rows = -(-slots // 16) * 16
    tokens = message - rows
    group = min(slots, 256 // token_count)
    unroll = 24 if slots == group else 8
    chip = jnp.right_shift(me_ref[0], 1)
    mine = lax.broadcasted_iota(jnp.int32, (rows, lanes), 0) == chip
    for s in range(slots):
        table = got_refs[s][pl.ds(tokens, rows), :].astype(F32)
        query = jnp.sum(jnp.where(mine, table, 0.0), axis=0, keepdims=True)
        index_v[s:s + 1, :] = query.astype(jnp.int32) * token_count
    copy = pltpu.make_async_copy(index_v, index, sem)
    copy.start()
    copy.wait()

    for first, pass_ref in ((half, other_ref), (0, own_ref)):

        def several(step, carry):
            for part in range(slots // group):
                rows = []
                for j in range(unroll):
                    p = step * unroll + j
                    picked = jnp.concatenate(
                        [
                            got_refs[s][pl.ds(pl.multiple_of(index[s, first + p], token_count), token_count), :]
                            for s in range(part * group, (part + 1) * group)
                        ],
                        axis=0,
                    )
                    similar = lax.dot_general(pass_ref[p], picked, NT, preferred_element_type=F32)
                    rows.append(jnp.max(similar, axis=0, keepdims=True))
                    if len(rows) == 8:
                        best_ref[
                            pl.ds(pl.multiple_of(first + step * unroll + j - 7, 8), 8),
                            pl.ds(part * group * token_count, group * token_count),
                        ] = jnp.concatenate(rows, axis=0)
                        rows = []
            return carry

        lax.fori_loop(0, half // unroll, several, 0)
    wide = best_ref.shape[1]
    source = lax.broadcasted_iota(jnp.int32, (slots, wide), 0)
    column = lax.broadcasted_iota(jnp.int32, (slots, wide), 1)
    start = source * token_count
    ones = jnp.where((column >= start) & (column < start + token_count), 1.0, 0.0).astype(BF16)
    total = sum(lax.dot_general(ones, part, NT, preferred_element_type=F32) for part in split3(best_ref[...]))
    out_ref[...] = jnp.zeros(out_ref.shape, F32)
    for s in range(slots):
        out_ref[pl.ds(jnp.bitwise_xor(chip, s), 1), pl.ds(0, 2 * half)] = total[s:s + 1]


def score(me, got, own, other, token_count):
    half, plen, e = own.shape
    passage_count = 2 * half
    slots = len(got)

    def kernel(*refs):
        score_kernel(slots, token_count, *refs)

    return pl.pallas_call(
        kernel,
        out_shape=jax.ShapeDtypeStruct((slots, e), F32),
        in_specs=[SMEM, VMEM, VMEM] + [VMEM] * slots,
        out_specs=VMEM,
        scratch_shapes=[
            pltpu.VMEM((passage_count, slots * token_count), F32),
            pltpu.VMEM((slots, e), jnp.int32),
            pltpu.SMEM((slots, e), jnp.int32),
            pltpu.SemaphoreType.DMA,
        ],
        compiler_params=pltpu.CompilerParams(vmem_limit_bytes=12 * 2 ** 20),
        cost_estimate=pl.CostEstimate(
            flops=2 * passage_count * slots * token_count * plen * e,
            bytes_accessed=4 * own.size,
            transcendentals=0,
        ),
        name="score",
    )(me, own, other, *got)


def finish_kernel(got_ref, spot_ref, scores_ref, best_ref):
    slots, lanes = got_ref.shape
    query_count, cand_count = scores_ref.shape
    parts = split3(got_ref[...])
    slot_iota = lax.broadcasted_iota(jnp.int32, (slots, cand_count), 0) * lanes
    lane_iota = lax.broadcasted_iota(jnp.int32, (lanes, cand_count), 0)
    row_iota = lax.broadcasted_iota(jnp.int32, (cand_count, cand_count), 0)
    col_iota = lax.broadcasted_iota(jnp.int32, (cand_count, cand_count), 1)
    place = lax.broadcasted_iota(jnp.int32, (cand_count, 128), 1)
    for i in range(query_count):
        spot = spot_ref[i:i + 1, :]
        lane = jnp.bitwise_and(spot, lanes - 1)
        onehot = jnp.where(lane_iota == lane, 1.0, 0.0).astype(BF16)
        picked = sum(jnp.dot(part, onehot, preferred_element_type=F32) for part in parts)
        score_row = jnp.sum(jnp.where(slot_iota == spot - lane, picked, 0.0), axis=0, keepdims=True)
        scores_ref[i:i + 1, :] = score_row
        across = jnp.broadcast_to(score_row, (cand_count, cand_count))
        score_col = jnp.sum(jnp.where(row_iota == col_iota, across, 0.0), axis=1, keepdims=True)
        ahead = (across > score_col) | ((across == score_col) & (col_iota < row_iota))
        rank = jnp.sum(jnp.where(ahead, 1.0, 0.0), axis=1, keepdims=True).astype(jnp.int32)
        ordered = jnp.sum(jnp.where(rank == place, score_col, 0.0), axis=0, keepdims=True)
        best_ref[i:i + 1, :] = ordered[:, :TOPN]


def finish(got, spots):
    return pl.pallas_call(
        finish_kernel,
        out_shape=(
            jax.ShapeDtypeStruct(spots.shape, F32),
            jax.ShapeDtypeStruct((spots.shape[0], TOPN), F32),
        ),
        in_specs=[VMEM, VMEM],
        out_specs=(VMEM, VMEM),
        compiler_params=pltpu.CompilerParams(vmem_limit_bytes=2 ** 21),
        name="finish",
    )(got, spots)


def swap(value, distance):
    size = lax.axis_size("shard")
    return lax.ppermute(value, "shard", [(i, i ^ distance) for i in range(size)])


def per_device(
    query_hidden,
    query_lengths,
    inner_weight,
    outer_weight,
    norm_gain,
    embed_weight,
    passage_vectors,
    passage_lengths,
    passage_row,
    candidates,
):
    size = lax.axis_size("shard")
    slots = size // 2
    inner = 1
    while 4 * inner * inner <= slots:
        inner *= 2
    shift = inner.bit_length()

    def color(index):
        return (index ^ (index >> 1) ^ (index >> shift)) & 1

    groups = [[i for i in range(size) if color(i) == c] for c in range(2)]

    def send(value, distance):
        return swap(value, 2 * distance + color(2 * distance))

    me = lax.axis_index("shard").astype(jnp.int32).reshape(1)
    across = swap(passage_lengths, 1)
    message, spots = encode(
        me,
        query_hidden,
        query_lengths,
        inner_weight,
        outer_weight,
        norm_gain,
        embed_weight,
        passage_vectors.shape[0],
        passage_row,
        candidates,
        slots,
        color,
    )
    message, across, raw = lax.optimization_barrier((message, across, passage_vectors))
    raw = swap(raw, 1)

    line = [message] + [send(message, d) for d in range(slots - inner, 0, -inner)][::-1]
    got = [line[s // inner] if s % inner == 0 else send(line[s // inner], s % inner) for s in range(slots)]
    own, other = mask((passage_lengths, across), (passage_vectors, raw), got[inner + 1])
    sums = score(me, got, own, other, query_hidden.shape[1])
    back = lax.all_to_all(sums, "shard", split_axis=0, concat_axis=0, axis_index_groups=groups, tiled=True)
    return finish(back, spots)


def solution(mesh):
    in_specs = (
        P(("groups", "shard"), None, None),
        P(("groups", "shard")),
        P(),
        P(),
        P(),
        P(),
        P(("groups", "shard"), None, None),
        P(("groups", "shard")),
        P("groups"),
        P(("groups", "shard"), None),
    )
    out_specs = (P(("groups", "shard"), None), P(("groups", "shard"), None))
    return jax.shard_map(
        per_device, mesh=mesh, in_specs=in_specs, out_specs=out_specs, check_vma=False
    )
```

```python
import jax
import jax.numpy as jnp
from jax import lax
from jax.experimental import pallas as pl
from jax.experimental.pallas import tpu as pltpu
from jax.sharding import PartitionSpec as P

TOPN = 10
F32 = jnp.float32
BF16 = jnp.bfloat16
NT = (((1,), (1,)), ((), ()))
VMEM = pl.BlockSpec(memory_space=pltpu.VMEM)
SMEM = pl.BlockSpec(memory_space=pltpu.SMEM)
ANY = pl.BlockSpec(memory_space=pl.ANY)


def split3(value):
    high = value.astype(BF16)
    rest = value - high.astype(F32)
    middle = rest.astype(BF16)
    low = (rest - middle.astype(F32)).astype(BF16)
    return high, middle, low


def mask_into(out_ref, pass_ref, len_ref, first, count):
    def mask(p, carry):
        block = pass_ref[p]
        keep = lax.broadcasted_iota(jnp.int32, block.shape, 0) < len_ref[p]
        block = block.astype(F32)
        out_ref[p] = jnp.where(keep, block, jnp.broadcast_to(block[0:1], block.shape)).astype(BF16)
        return carry

    if count <= 8:
        for p in range(first, first + count):
            mask(p, 0)
    else:
        lax.fori_loop(first, first + count, mask, 0, unroll=8)


def encode_kernel(
    half,
    color,
    me_ref,
    lens_hbm,
    row_hbm,
    cand_hbm,
    x_hbm,
    w1_ref,
    w2_ref,
    gain_hbm,
    embed_hbm,
    out_ref,
    spot_ref,
    w1_buf,
    w2_buf,
    lens_ref,
    row_ref,
    place_ref,
    cand_ref,
    x_ref,
    gain_ref,
    embed_ref,
    table,
    table_v,
    sems,
    small_sems,
    place_sem,
    table_sem,
):
    chunks, _, width = w1_buf.shape
    slots, lanes = table_v.shape
    query_count, token_count, width_in = x_ref.shape
    cand_count = cand_ref.shape[1]
    table_v[...] = jnp.zeros(table_v.shape, jnp.int32)
    clear = pltpu.make_async_copy(table_v, table, table_sem)
    clear.start()
    copies = []
    for c in range(chunks):
        first = pltpu.make_async_copy(w1_ref.at[:, pl.ds(c * width, width)], w1_buf.at[c], sems.at[0, c])
        second = pltpu.make_async_copy(w2_ref.at[pl.ds(c * width, width), :], w2_buf.at[c], sems.at[1, c])
        copies.append((first, second))
    small = [
        pltpu.make_async_copy(source, target, small_sems.at[n])
        for n, (source, target) in enumerate(
            (
                (x_hbm, x_ref),
                (row_hbm, row_ref),
                (cand_hbm, cand_ref),
                (lens_hbm, lens_ref),
                (gain_hbm, gain_ref),
                (embed_hbm, embed_ref),
            )
        )
    ]
    for copy in small[:3]:
        copy.start()
    copies[0][0].start()
    copies[1][0].start()
    copies[0][1].start()
    for c in range(2, chunks):
        copies[c][0].start()
        copies[c - 1][1].start()
    copies[-1][1].start()
    for copy in small[3:]:
        copy.start()
    clear.wait()
    small[1].wait()
    row = row_ref[...]
    owner = jnp.floor((row.astype(F32) + 0.5) * (1.0 / half)).astype(jnp.int32)
    opposite = jnp.bitwise_xor(color(owner), color(me_ref[0]))
    row_ref[...] = jnp.right_shift(owner, 1) * lanes + row - owner * half + opposite * half
    placed = pltpu.make_async_copy(row_ref, place_ref, place_sem)
    placed.start()

    entries = [(i, k) for k in range(cand_count) for i in range(query_count)]
    share = -(-len(entries) // chunks)

    def enter():
        for first in range(0, share, 12):
            batch = entries[first:min(first + 12, share)]
            names = [cand_ref[i, k] for i, k in batch]
            spots = [place_ref[name] for name in names]
            for (i, k), spot in zip(batch, spots):
                table[jnp.right_shift(spot, 7), jnp.bitwise_and(spot, 127)] = i
                spot_ref[i, k] = spot
        del entries[:share]

    small[0].wait()
    x = x_ref[...].reshape(query_count * token_count, width_in)
    total = x.astype(F32)
    inner = active = None
    for step in range(chunks + 2):
        if step < chunks:
            copies[step][0].wait()
        if step >= 2:
            copies[step - 2][1].wait()
        if step == 1:
            small[2].wait()
            placed.wait()
        if step >= 1:
            enter()
        later = jnp.dot(x, w1_buf[step], preferred_element_type=F32) if step < chunks else None
        if step >= 2:
            total = total + jnp.dot(active, w2_buf[step - 2], preferred_element_type=F32)
        if 1 <= step <= chunks:
            active = (0.5 * inner * (1.0 + lax.erf(inner * (0.5 ** 0.5)))).astype(BF16)
        inner = later
        if step == chunks:
            fetch = pltpu.make_async_copy(table, table_v, table_sem)
            fetch.start()

    for copy in small[3:]:
        copy.wait()
    centered = total - jnp.mean(total, axis=-1, keepdims=True)
    variance = jnp.mean(jnp.square(centered), axis=-1, keepdims=True)
    layer_out = (centered * lax.rsqrt(variance + 1e-12) * gain_ref[...].reshape(1, width_in)).astype(BF16)
    embedded = jnp.dot(layer_out, embed_ref[...], preferred_element_type=F32)
    length = jnp.sum(jnp.square(embedded), axis=-1, keepdims=True)
    vectors = embedded * lax.rsqrt(length + 1e-06)
    token = lax.broadcasted_iota(jnp.int32, vectors.shape, 0)
    for i in range(query_count):
        padded = (token >= i * token_count + lens_ref[i]) & (token < (i + 1) * token_count)
        vectors = jnp.where(padded, 0.0, vectors)
    vectors = vectors.astype(BF16)
    fetch.wait()
    tokens = query_count * token_count
    wanted = table_v[...].astype(F32).astype(BF16)
    out_ref[pl.ds(0, tokens), :] = vectors
    out_ref[pl.ds(tokens, slots), :] = wanted


def encode(
    me,
    query_hidden,
    query_lengths,
    inner_weight,
    outer_weight,
    norm_gain,
    embed_weight,
    half,
    passage_row,
    candidates,
    slots,
    color,
):
    query_count, token_count, d = query_hidden.shape
    ff = inner_weight.shape[1]
    e = embed_weight.shape[1]
    slots = -(-slots // 16) * 16
    assert 2 * half <= e == 128
    chunks = 4
    width = ff // chunks
    tokens = query_count * token_count

    def kernel(*refs):
        encode_kernel(half, color, *refs)

    return pl.pallas_call(
        kernel,
        out_shape=(
            jax.ShapeDtypeStruct((tokens + slots, e), BF16),
            jax.ShapeDtypeStruct(candidates.shape, jnp.int32),
        ),
        in_specs=[SMEM] + [ANY] * 8,
        out_specs=(VMEM, SMEM),
        scratch_shapes=[
            pltpu.VMEM((chunks, d, width), BF16),
            pltpu.VMEM((chunks, width, d), BF16),
            pltpu.SMEM(query_lengths.shape, jnp.int32),
            pltpu.VMEM(passage_row.shape, jnp.int32),
            pltpu.SMEM(passage_row.shape, jnp.int32),
            pltpu.SMEM(candidates.shape, jnp.int32),
            pltpu.VMEM(query_hidden.shape, BF16),
            pltpu.VMEM(norm_gain.shape, F32),
            pltpu.VMEM(embed_weight.shape, BF16),
            pltpu.SMEM((slots, e), jnp.int32),
            pltpu.VMEM((slots, e), jnp.int32),
            pltpu.SemaphoreType.DMA((2, chunks)),
            pltpu.SemaphoreType.DMA((6,)),
            pltpu.SemaphoreType.DMA,
            pltpu.SemaphoreType.DMA,
        ],
        compiler_params=pltpu.CompilerParams(vmem_limit_bytes=60 * 2 ** 20),
        cost_estimate=pl.CostEstimate(
            flops=4 * tokens * d * ff, bytes_accessed=4 * d * ff, transcendentals=tokens * ff
        ),
        name="encode",
    )(
        me,
        query_lengths,
        passage_row,
        candidates,
        query_hidden,
        inner_weight,
        outer_weight,
        norm_gain,
        embed_weight,
    )


def mask_kernel(len0_ref, len1_ref, pass0_ref, pass1_ref, _, out0_ref, out1_ref):
    mask_into(out0_ref, pass0_ref, len0_ref, 0, pass0_ref.shape[0])
    mask_into(out1_ref, pass1_ref, len1_ref, 0, pass1_ref.shape[0])


def mask(lengths, passages, late):
    shape = passages[0].shape
    size = 2 * passages[0].size
    return pl.pallas_call(
        mask_kernel,
        out_shape=[jax.ShapeDtypeStruct(shape, BF16)] * 2,
        in_specs=[SMEM, SMEM, VMEM, VMEM, VMEM],
        out_specs=[VMEM, VMEM],
        compiler_params=pltpu.CompilerParams(vmem_limit_bytes=2 ** 22),
        cost_estimate=pl.CostEstimate(flops=8 * size, bytes_accessed=4 * size, transcendentals=0),
        name="mask",
    )(*lengths, *passages, late)


def score_kernel(slots, token_count, me_ref, own_ref, other_ref, *refs):
    got_refs = refs[:slots]
    out_ref, best_ref, index_v, index, sem = refs[slots:]
    message, lanes = got_refs[0].shape
    half = own_ref.shape[0]
    rows = -(-slots // 16) * 16
    tokens = message - rows
    group = min(slots, 256 // token_count)
    unroll = half if slots == group else 8
    chip = jnp.right_shift(me_ref[0], 1)
    mine = lax.broadcasted_iota(jnp.int32, (rows, lanes), 0) == chip
    for s in range(slots):
        table = got_refs[s][pl.ds(tokens, rows), :].astype(F32)
        query = jnp.sum(jnp.where(mine, table, 0.0), axis=0, keepdims=True)
        index_v[s:s + 1, :] = query.astype(jnp.int32) * token_count
    copy = pltpu.make_async_copy(index_v, index, sem)
    copy.start()
    copy.wait()

    for first, pass_ref in ((half, other_ref), (0, own_ref)):

        def several(step, carry):
            for part in range(slots // group):
                rows = []
                for j in range(unroll):
                    p = step * unroll + j
                    picked = jnp.concatenate(
                        [
                            got_refs[s][pl.ds(pl.multiple_of(index[s, first + p], token_count), token_count), :]
                            for s in range(part * group, (part + 1) * group)
                        ],
                        axis=0,
                    )
                    similar = lax.dot_general(pass_ref[p], picked, NT, preferred_element_type=F32)
                    rows.append(jnp.max(similar, axis=0, keepdims=True))
                    if len(rows) == 8:
                        best_ref[
                            pl.ds(pl.multiple_of(first + step * unroll + j - 7, 8), 8),
                            pl.ds(part * group * token_count, group * token_count),
                        ] = jnp.concatenate(rows, axis=0)
                        rows = []
            return carry

        lax.fori_loop(0, half // unroll, several, 0)
    wide = best_ref.shape[1]
    source = lax.broadcasted_iota(jnp.int32, (slots, wide), 0)
    column = lax.broadcasted_iota(jnp.int32, (slots, wide), 1)
    start = source * token_count
    ones = jnp.where((column >= start) & (column < start + token_count), 1.0, 0.0).astype(BF16)
    total = sum(lax.dot_general(ones, part, NT, preferred_element_type=F32) for part in split3(best_ref[...]))
    out_ref[...] = jnp.zeros(out_ref.shape, F32)
    for s in range(slots):
        out_ref[pl.ds(jnp.bitwise_xor(chip, s), 1), pl.ds(0, 2 * half)] = total[s:s + 1]


def score(me, got, own, other, token_count):
    half, plen, e = own.shape
    passage_count = 2 * half
    slots = len(got)

    def kernel(*refs):
        score_kernel(slots, token_count, *refs)

    return pl.pallas_call(
        kernel,
        out_shape=jax.ShapeDtypeStruct((slots, e), F32),
        in_specs=[SMEM, VMEM, VMEM] + [VMEM] * slots,
        out_specs=VMEM,
        scratch_shapes=[
            pltpu.VMEM((passage_count, slots * token_count), F32),
            pltpu.VMEM((slots, e), jnp.int32),
            pltpu.SMEM((slots, e), jnp.int32),
            pltpu.SemaphoreType.DMA,
        ],
        compiler_params=pltpu.CompilerParams(vmem_limit_bytes=12 * 2 ** 20),
        cost_estimate=pl.CostEstimate(
            flops=2 * passage_count * slots * token_count * plen * e,
            bytes_accessed=4 * own.size,
            transcendentals=0,
        ),
        name="score",
    )(me, own, other, *got)


def finish_kernel(got_ref, spot_ref, scores_ref, best_ref):
    slots, lanes = got_ref.shape
    query_count, cand_count = scores_ref.shape
    parts = split3(got_ref[...])
    slot_iota = lax.broadcasted_iota(jnp.int32, (slots, cand_count), 0) * lanes
    lane_iota = lax.broadcasted_iota(jnp.int32, (lanes, cand_count), 0)
    row_iota = lax.broadcasted_iota(jnp.int32, (cand_count, cand_count), 0)
    col_iota = lax.broadcasted_iota(jnp.int32, (cand_count, cand_count), 1)
    place = lax.broadcasted_iota(jnp.int32, (cand_count, 128), 1)
    for i in range(query_count):
        spot = spot_ref[i:i + 1, :]
        lane = jnp.bitwise_and(spot, lanes - 1)
        onehot = jnp.where(lane_iota == lane, 1.0, 0.0).astype(BF16)
        picked = sum(jnp.dot(part, onehot, preferred_element_type=F32) for part in parts)
        score_row = jnp.sum(jnp.where(slot_iota == spot - lane, picked, 0.0), axis=0, keepdims=True)
        scores_ref[i:i + 1, :] = score_row
        across = jnp.broadcast_to(score_row, (cand_count, cand_count))
        score_col = jnp.sum(jnp.where(row_iota == col_iota, across, 0.0), axis=1, keepdims=True)
        ahead = (across > score_col) | ((across == score_col) & (col_iota < row_iota))
        rank = jnp.sum(jnp.where(ahead, 1.0, 0.0), axis=1, keepdims=True).astype(jnp.int32)
        ordered = jnp.sum(jnp.where(rank == place, score_col, 0.0), axis=0, keepdims=True)
        best_ref[i:i + 1, :] = ordered[:, :TOPN]


def finish(got, spots):
    return pl.pallas_call(
        finish_kernel,
        out_shape=(
            jax.ShapeDtypeStruct(spots.shape, F32),
            jax.ShapeDtypeStruct((spots.shape[0], TOPN), F32),
        ),
        in_specs=[VMEM, VMEM],
        out_specs=(VMEM, VMEM),
        compiler_params=pltpu.CompilerParams(vmem_limit_bytes=2 ** 21),
        name="finish",
    )(got, spots)


def swap(value, distance):
    size = lax.axis_size("shard")
    return lax.ppermute(value, "shard", [(i, i ^ distance) for i in range(size)])


def per_device(
    query_hidden,
    query_lengths,
    inner_weight,
    outer_weight,
    norm_gain,
    embed_weight,
    passage_vectors,
    passage_lengths,
    passage_row,
    candidates,
):
    size = lax.axis_size("shard")
    slots = size // 2
    inner = 1
    while 4 * inner * inner <= slots:
        inner *= 2
    shift = inner.bit_length()

    def color(index):
        return (index ^ (index >> 1) ^ (index >> shift)) & 1

    groups = [[i for i in range(size) if color(i) == c] for c in range(2)]

    def send(value, distance):
        return swap(value, 2 * distance + color(2 * distance))

    me = lax.axis_index("shard").astype(jnp.int32).reshape(1)
    across = swap(passage_lengths, 1)
    message, spots = encode(
        me,
        query_hidden,
        query_lengths,
        inner_weight,
        outer_weight,
        norm_gain,
        embed_weight,
        passage_vectors.shape[0],
        passage_row,
        candidates,
        slots,
        color,
    )
    message, across, raw = lax.optimization_barrier((message, across, passage_vectors))
    raw = swap(raw, 1)

    line = [message] + [send(message, d) for d in range(slots - inner, 0, -inner)][::-1]
    got = [line[s // inner] if s % inner == 0 else send(line[s // inner], s % inner) for s in range(slots)]
    own, other = mask((passage_lengths, across), (passage_vectors, raw), got[inner + 1])
    sums = score(me, got, own, other, query_hidden.shape[1])
    back = lax.all_to_all(sums, "shard", split_axis=0, concat_axis=0, axis_index_groups=groups, tiled=True)
    return finish(back, spots)


def solution(mesh):
    in_specs = (
        P(("groups", "shard"), None, None),
        P(("groups", "shard")),
        P(),
        P(),
        P(),
        P(),
        P(("groups", "shard"), None, None),
        P(("groups", "shard")),
        P("groups"),
        P(("groups", "shard"), None),
    )
    out_specs = (P(("groups", "shard"), None), P(("groups", "shard"), None))
    return jax.shard_map(
        per_device, mesh=mesh, in_specs=in_specs, out_specs=out_specs, check_vma=False
    )
```

```python
import jax
import jax.numpy as jnp
from jax import lax
from jax.experimental import pallas as pl
from jax.experimental.pallas import tpu as pltpu
from jax.sharding import PartitionSpec as P

TOPN = 10
F32 = jnp.float32
BF16 = jnp.bfloat16
NT = (((1,), (1,)), ((), ()))
VMEM = pl.BlockSpec(memory_space=pltpu.VMEM)
SMEM = pl.BlockSpec(memory_space=pltpu.SMEM)
ANY = pl.BlockSpec(memory_space=pl.ANY)


def split3(value):
    high = value.astype(BF16)
    rest = value - high.astype(F32)
    middle = rest.astype(BF16)
    low = (rest - middle.astype(F32)).astype(BF16)
    return high, middle, low


def mask_into(out_ref, pass_ref, len_ref, first, count):
    def mask(p, carry):
        block = pass_ref[p]
        keep = lax.broadcasted_iota(jnp.int32, block.shape, 0) < len_ref[p]
        block = block.astype(F32)
        out_ref[p] = jnp.where(keep, block, jnp.broadcast_to(block[0:1], block.shape)).astype(BF16)
        return carry

    if count <= 8:
        for p in range(first, first + count):
            mask(p, 0)
    else:
        lax.fori_loop(first, first + count, mask, 0, unroll=16)


def encode_kernel(
    half,
    color,
    me_ref,
    lens_hbm,
    row_hbm,
    cand_hbm,
    x_hbm,
    w1_ref,
    w2_ref,
    gain_hbm,
    embed_hbm,
    out_ref,
    spot_ref,
    w1_buf,
    w2_buf,
    lens_ref,
    row_ref,
    place_ref,
    cand_ref,
    x_ref,
    gain_ref,
    embed_ref,
    table,
    table_v,
    sems,
    small_sems,
    place_sem,
    table_sem,
):
    chunks, _, width = w1_buf.shape
    slots, lanes = table_v.shape
    query_count, token_count, width_in = x_ref.shape
    cand_count = cand_ref.shape[1]
    table_v[...] = jnp.zeros(table_v.shape, jnp.int32)
    clear = pltpu.make_async_copy(table_v, table, table_sem)
    clear.start()
    copies = []
    for c in range(chunks):
        first = pltpu.make_async_copy(w1_ref.at[:, pl.ds(c * width, width)], w1_buf.at[c], sems.at[0, c])
        second = pltpu.make_async_copy(w2_ref.at[pl.ds(c * width, width), :], w2_buf.at[c], sems.at[1, c])
        copies.append((first, second))
    small = [
        pltpu.make_async_copy(source, target, small_sems.at[n])
        for n, (source, target) in enumerate(
            (
                (x_hbm, x_ref),
                (row_hbm, row_ref),
                (cand_hbm, cand_ref),
                (lens_hbm, lens_ref),
                (gain_hbm, gain_ref),
                (embed_hbm, embed_ref),
            )
        )
    ]
    for copy in small[:3]:
        copy.start()
    copies[0][0].start()
    copies[1][0].start()
    copies[0][1].start()
    for c in range(2, chunks):
        copies[c][0].start()
        copies[c - 1][1].start()
    copies[-1][1].start()
    for copy in small[3:]:
        copy.start()
    clear.wait()
    small[1].wait()
    row = row_ref[...]
    owner = jnp.floor((row.astype(F32) + 0.5) * (1.0 / half)).astype(jnp.int32)
    opposite = jnp.bitwise_xor(color(owner), color(me_ref[0]))
    row_ref[...] = jnp.right_shift(owner, 1) * lanes + row - owner * half + opposite * half
    placed = pltpu.make_async_copy(row_ref, place_ref, place_sem)
    placed.start()

    entries = [(i, k) for k in range(cand_count) for i in range(query_count)]
    share = -(-len(entries) // chunks)

    def enter():
        for first in range(0, share, 12):
            batch = entries[first:min(first + 12, share)]
            names = [cand_ref[i, k] for i, k in batch]
            spots = [place_ref[name] for name in names]
            for (i, k), spot in zip(batch, spots):
                table[jnp.right_shift(spot, 7), jnp.bitwise_and(spot, 127)] = i
                spot_ref[i, k] = spot
        del entries[:share]

    small[0].wait()
    x = x_ref[...].reshape(query_count * token_count, width_in)
    total = x.astype(F32)
    inner = active = None
    for step in range(chunks + 2):
        if step < chunks:
            copies[step][0].wait()
        if step >= 2:
            copies[step - 2][1].wait()
        if step == 1:
            small[2].wait()
            placed.wait()
        if step >= 1:
            enter()
        later = jnp.dot(x, w1_buf[step], preferred_element_type=F32) if step < chunks else None
        if step >= 2:
            total = total + jnp.dot(active, w2_buf[step - 2], preferred_element_type=F32)
        if 1 <= step <= chunks:
            active = (0.5 * inner * (1.0 + lax.erf(inner * (0.5 ** 0.5)))).astype(BF16)
        inner = later
        if step == chunks:
            fetch = pltpu.make_async_copy(table, table_v, table_sem)
            fetch.start()

    for copy in small[3:]:
        copy.wait()
    centered = total - jnp.mean(total, axis=-1, keepdims=True)
    variance = jnp.mean(jnp.square(centered), axis=-1, keepdims=True)
    layer_out = (centered * lax.rsqrt(variance + 1e-12) * gain_ref[...].reshape(1, width_in)).astype(BF16)
    embedded = jnp.dot(layer_out, embed_ref[...], preferred_element_type=F32)
    length = jnp.sum(jnp.square(embedded), axis=-1, keepdims=True)
    vectors = embedded * lax.rsqrt(length + 1e-06)
    token = lax.broadcasted_iota(jnp.int32, vectors.shape, 0)
    for i in range(query_count):
        padded = (token >= i * token_count + lens_ref[i]) & (token < (i + 1) * token_count)
        vectors = jnp.where(padded, 0.0, vectors)
    vectors = vectors.astype(BF16)
    fetch.wait()
    tokens = query_count * token_count
    wanted = table_v[...].astype(F32).astype(BF16)
    out_ref[pl.ds(0, tokens), :] = vectors
    out_ref[pl.ds(tokens, slots), :] = wanted


def encode(
    me,
    query_hidden,
    query_lengths,
    inner_weight,
    outer_weight,
    norm_gain,
    embed_weight,
    half,
    passage_row,
    candidates,
    slots,
    color,
):
    query_count, token_count, d = query_hidden.shape
    ff = inner_weight.shape[1]
    e = embed_weight.shape[1]
    slots = -(-slots // 16) * 16
    assert 2 * half <= e == 128
    chunks = 3
    width = ff // chunks
    tokens = query_count * token_count

    def kernel(*refs):
        encode_kernel(half, color, *refs)

    return pl.pallas_call(
        kernel,
        out_shape=(
            jax.ShapeDtypeStruct((tokens + slots, e), BF16),
            jax.ShapeDtypeStruct(candidates.shape, jnp.int32),
        ),
        in_specs=[SMEM] + [ANY] * 8,
        out_specs=(VMEM, SMEM),
        scratch_shapes=[
            pltpu.VMEM((chunks, d, width), BF16),
            pltpu.VMEM((chunks, width, d), BF16),
            pltpu.SMEM(query_lengths.shape, jnp.int32),
            pltpu.VMEM(passage_row.shape, jnp.int32),
            pltpu.SMEM(passage_row.shape, jnp.int32),
            pltpu.SMEM(candidates.shape, jnp.int32),
            pltpu.VMEM(query_hidden.shape, BF16),
            pltpu.VMEM(norm_gain.shape, F32),
            pltpu.VMEM(embed_weight.shape, BF16),
            pltpu.SMEM((slots, e), jnp.int32),
            pltpu.VMEM((slots, e), jnp.int32),
            pltpu.SemaphoreType.DMA((2, chunks)),
            pltpu.SemaphoreType.DMA((6,)),
            pltpu.SemaphoreType.DMA,
            pltpu.SemaphoreType.DMA,
        ],
        compiler_params=pltpu.CompilerParams(vmem_limit_bytes=60 * 2 ** 20),
        cost_estimate=pl.CostEstimate(
            flops=4 * tokens * d * ff, bytes_accessed=4 * d * ff, transcendentals=tokens * ff
        ),
        name="encode",
    )(
        me,
        query_lengths,
        passage_row,
        candidates,
        query_hidden,
        inner_weight,
        outer_weight,
        norm_gain,
        embed_weight,
    )


def mask_kernel(len0_ref, len1_ref, pass0_ref, pass1_ref, _, out0_ref, out1_ref):
    mask_into(out0_ref, pass0_ref, len0_ref, 0, pass0_ref.shape[0])
    mask_into(out1_ref, pass1_ref, len1_ref, 0, pass1_ref.shape[0])


def mask(lengths, passages, late):
    shape = passages[0].shape
    size = 2 * passages[0].size
    return pl.pallas_call(
        mask_kernel,
        out_shape=[jax.ShapeDtypeStruct(shape, BF16)] * 2,
        in_specs=[SMEM, SMEM, VMEM, VMEM, VMEM],
        out_specs=[VMEM, VMEM],
        compiler_params=pltpu.CompilerParams(vmem_limit_bytes=2 ** 22),
        cost_estimate=pl.CostEstimate(flops=8 * size, bytes_accessed=4 * size, transcendentals=0),
        name="mask",
    )(*lengths, *passages, late)


def score_kernel(slots, token_count, me_ref, own_ref, other_ref, *refs):
    got_refs = refs[:slots]
    out_ref, best_ref, index_v, index, sem = refs[slots:]
    message, lanes = got_refs[0].shape
    half = own_ref.shape[0]
    rows = -(-slots // 16) * 16
    tokens = message - rows
    group = min(slots, 256 // token_count)
    unroll = half if slots == group else 8
    chip = jnp.right_shift(me_ref[0], 1)
    mine = lax.broadcasted_iota(jnp.int32, (rows, lanes), 0) == chip
    for s in range(slots):
        table = got_refs[s][pl.ds(tokens, rows), :].astype(F32)
        query = jnp.sum(jnp.where(mine, table, 0.0), axis=0, keepdims=True)
        index_v[s:s + 1, :] = query.astype(jnp.int32) * token_count
    copy = pltpu.make_async_copy(index_v, index, sem)
    copy.start()
    copy.wait()

    for first, pass_ref in ((half, other_ref), (0, own_ref)):

        def several(step, carry):
            for part in range(slots // group):
                rows = []
                for j in range(unroll):
                    p = step * unroll + j
                    picked = jnp.concatenate(
                        [
                            got_refs[s][pl.ds(pl.multiple_of(index[s, first + p], token_count), token_count), :]
                            for s in range(part * group, (part + 1) * group)
                        ],
                        axis=0,
                    )
                    similar = lax.dot_general(pass_ref[p], picked, NT, preferred_element_type=F32)
                    rows.append(jnp.max(similar, axis=0, keepdims=True))
                    if len(rows) == 8:
                        best_ref[
                            pl.ds(pl.multiple_of(first + step * unroll + j - 7, 8), 8),
                            pl.ds(part * group * token_count, group * token_count),
                        ] = jnp.concatenate(rows, axis=0)
                        rows = []
            return carry

        if unroll == half:
            several(0, 0)
        else:
            lax.fori_loop(0, half // unroll, several, 0)
    wide = best_ref.shape[1]
    source = lax.broadcasted_iota(jnp.int32, (slots, wide), 0)
    column = lax.broadcasted_iota(jnp.int32, (slots, wide), 1)
    start = source * token_count
    ones = jnp.where((column >= start) & (column < start + token_count), 1.0, 0.0).astype(BF16)
    total = sum(lax.dot_general(ones, part, NT, preferred_element_type=F32) for part in split3(best_ref[...]))
    out_ref[...] = jnp.zeros(out_ref.shape, F32)
    for s in range(slots):
        out_ref[pl.ds(jnp.bitwise_xor(chip, s), 1), pl.ds(0, 2 * half)] = total[s:s + 1]


def score(me, got, own, other, token_count):
    half, plen, e = own.shape
    passage_count = 2 * half
    slots = len(got)

    def kernel(*refs):
        score_kernel(slots, token_count, *refs)

    return pl.pallas_call(
        kernel,
        out_shape=jax.ShapeDtypeStruct((slots, e), F32),
        in_specs=[SMEM, VMEM, VMEM] + [VMEM] * slots,
        out_specs=VMEM,
        scratch_shapes=[
            pltpu.VMEM((passage_count, slots * token_count), F32),
            pltpu.VMEM((slots, e), jnp.int32),
            pltpu.SMEM((slots, e), jnp.int32),
            pltpu.SemaphoreType.DMA,
        ],
        compiler_params=pltpu.CompilerParams(vmem_limit_bytes=12 * 2 ** 20),
        cost_estimate=pl.CostEstimate(
            flops=2 * passage_count * slots * token_count * plen * e,
            bytes_accessed=4 * own.size,
            transcendentals=0,
        ),
        name="score",
    )(me, own, other, *got)


def finish_kernel(got_ref, spot_ref, scores_ref, best_ref):
    slots, lanes = got_ref.shape
    query_count, cand_count = scores_ref.shape
    parts = split3(got_ref[...])
    slot_iota = lax.broadcasted_iota(jnp.int32, (slots, cand_count), 0) * lanes
    lane_iota = lax.broadcasted_iota(jnp.int32, (lanes, cand_count), 0)
    row_iota = lax.broadcasted_iota(jnp.int32, (cand_count, cand_count), 0)
    col_iota = lax.broadcasted_iota(jnp.int32, (cand_count, cand_count), 1)
    place = lax.broadcasted_iota(jnp.int32, (cand_count, 128), 1)
    for i in range(query_count):
        spot = spot_ref[i:i + 1, :]
        lane = jnp.bitwise_and(spot, lanes - 1)
        onehot = jnp.where(lane_iota == lane, 1.0, 0.0).astype(BF16)
        picked = sum(jnp.dot(part, onehot, preferred_element_type=F32) for part in parts)
        score_row = jnp.sum(jnp.where(slot_iota == spot - lane, picked, 0.0), axis=0, keepdims=True)
        scores_ref[i:i + 1, :] = score_row
        across = jnp.broadcast_to(score_row, (cand_count, cand_count))
        score_col = jnp.sum(jnp.where(row_iota == col_iota, across, 0.0), axis=1, keepdims=True)
        ahead = (across > score_col) | ((across == score_col) & (col_iota < row_iota))
        rank = jnp.sum(jnp.where(ahead, 1.0, 0.0), axis=1, keepdims=True).astype(jnp.int32)
        ordered = jnp.sum(jnp.where(rank == place, score_col, 0.0), axis=0, keepdims=True)
        best_ref[i:i + 1, :] = ordered[:, :TOPN]


def finish(got, spots):
    return pl.pallas_call(
        finish_kernel,
        out_shape=(
            jax.ShapeDtypeStruct(spots.shape, F32),
            jax.ShapeDtypeStruct((spots.shape[0], TOPN), F32),
        ),
        in_specs=[VMEM, VMEM],
        out_specs=(VMEM, VMEM),
        compiler_params=pltpu.CompilerParams(vmem_limit_bytes=2 ** 21),
        name="finish",
    )(got, spots)


def swap(value, distance):
    size = lax.axis_size("shard")
    return lax.ppermute(value, "shard", [(i, i ^ distance) for i in range(size)])


def per_device(
    query_hidden,
    query_lengths,
    inner_weight,
    outer_weight,
    norm_gain,
    embed_weight,
    passage_vectors,
    passage_lengths,
    passage_row,
    candidates,
):
    size = lax.axis_size("shard")
    slots = size // 2
    inner = 1
    while 4 * inner * inner <= slots:
        inner *= 2
    shift = inner.bit_length()

    def color(index):
        return (index ^ (index >> 1) ^ (index >> shift)) & 1

    groups = [[i for i in range(size) if color(i) == c] for c in range(2)]

    def send(value, distance):
        return swap(value, 2 * distance + color(2 * distance))

    me = lax.axis_index("shard").astype(jnp.int32).reshape(1)
    across = swap(passage_lengths, 1)
    message, spots = encode(
        me,
        query_hidden,
        query_lengths,
        inner_weight,
        outer_weight,
        norm_gain,
        embed_weight,
        passage_vectors.shape[0],
        passage_row,
        candidates,
        slots,
        color,
    )
    message, across, raw = lax.optimization_barrier((message, across, passage_vectors))
    raw = swap(raw, 1)

    line = [message] + [send(message, d) for d in range(slots - inner, 0, -inner)][::-1]
    got = [line[s // inner] if s % inner == 0 else send(line[s // inner], s % inner) for s in range(slots)]
    own, other = mask((passage_lengths, across), (passage_vectors, raw), got[inner + 1])
    sums = score(me, got, own, other, query_hidden.shape[1])
    back = lax.all_to_all(sums, "shard", split_axis=0, concat_axis=0, axis_index_groups=groups, tiled=True)
    return finish(back, spots)


def solution(mesh):
    in_specs = (
        P(("groups", "shard"), None, None),
        P(("groups", "shard")),
        P(),
        P(),
        P(),
        P(),
        P(("groups", "shard"), None, None),
        P(("groups", "shard")),
        P("groups"),
        P(("groups", "shard"), None),
    )
    out_specs = (P(("groups", "shard"), None), P(("groups", "shard"), None))
    return jax.shard_map(
        per_device, mesh=mesh, in_specs=in_specs, out_specs=out_specs, check_vma=False
    )
```

```python
import jax
import jax.numpy as jnp
from jax import lax
from jax.experimental import pallas as pl
from jax.experimental.pallas import tpu as pltpu
from jax.sharding import PartitionSpec as P

TOPN = 10
F32 = jnp.float32
BF16 = jnp.bfloat16
NT = (((1,), (1,)), ((), ()))
VMEM = pl.BlockSpec(memory_space=pltpu.VMEM)
SMEM = pl.BlockSpec(memory_space=pltpu.SMEM)
ANY = pl.BlockSpec(memory_space=pl.ANY)


def split3(value):
    high = value.astype(BF16)
    rest = value - high.astype(F32)
    middle = rest.astype(BF16)
    low = (rest - middle.astype(F32)).astype(BF16)
    return high, middle, low


def mask_into(out_ref, pass_ref, len_ref, first, count):
    def mask(p, carry):
        block = pass_ref[p]
        keep = lax.broadcasted_iota(jnp.int32, block.shape, 0) < len_ref[p]
        block = block.astype(F32)
        out_ref[p] = jnp.where(keep, block, jnp.broadcast_to(block[0:1], block.shape)).astype(BF16)
        return carry

    if count <= 8:
        for p in range(first, first + count):
            mask(p, 0)
    else:
        lax.fori_loop(first, first + count, mask, 0, unroll=16)


def encode_kernel(
    half,
    color,
    me_ref,
    lens_hbm,
    row_hbm,
    cand_hbm,
    x_hbm,
    w1_ref,
    w2_ref,
    gain_hbm,
    embed_hbm,
    out_ref,
    spot_ref,
    w1_buf,
    w2_buf,
    lens_ref,
    row_ref,
    place_ref,
    cand_ref,
    x_ref,
    gain_ref,
    embed_ref,
    table,
    table_v,
    sems,
    small_sems,
    place_sem,
    table_sem,
):
    chunks, _, width = w1_buf.shape
    slots, lanes = table_v.shape
    query_count, token_count, width_in = x_ref.shape
    cand_count = cand_ref.shape[1]
    table_v[...] = jnp.zeros(table_v.shape, jnp.int32)
    clear = pltpu.make_async_copy(table_v, table, table_sem)
    clear.start()
    copies = []
    for c in range(chunks):
        first = pltpu.make_async_copy(w1_ref.at[:, pl.ds(c * width, width)], w1_buf.at[c], sems.at[0, c])
        second = pltpu.make_async_copy(w2_ref.at[pl.ds(c * width, width), :], w2_buf.at[c], sems.at[1, c])
        copies.append((first, second))
    small = [
        pltpu.make_async_copy(source, target, small_sems.at[n])
        for n, (source, target) in enumerate(
            (
                (x_hbm, x_ref),
                (row_hbm, row_ref),
                (cand_hbm, cand_ref),
                (lens_hbm, lens_ref),
                (gain_hbm, gain_ref),
                (embed_hbm, embed_ref),
            )
        )
    ]
    for copy in small[:3]:
        copy.start()
    copies[0][0].start()
    copies[1][0].start()
    copies[0][1].start()
    for c in range(2, chunks):
        copies[c][0].start()
        copies[c - 1][1].start()
    copies[-1][1].start()
    for copy in small[3:]:
        copy.start()
    clear.wait()
    small[1].wait()
    row = row_ref[...]
    owner = jnp.floor((row.astype(F32) + 0.5) * (1.0 / half)).astype(jnp.int32)
    opposite = jnp.bitwise_xor(color(owner), color(me_ref[0]))
    row_ref[...] = jnp.right_shift(owner, 1) * lanes + row - owner * half + opposite * half
    placed = pltpu.make_async_copy(row_ref, place_ref, place_sem)
    placed.start()

    entries = [(i, k) for k in range(cand_count) for i in range(query_count)]
    share = -(-len(entries) // chunks)

    def enter():
        for first in range(0, share, 12):
            batch = entries[first:min(first + 12, share)]
            names = [cand_ref[i, k] for i, k in batch]
            spots = [place_ref[name] for name in names]
            for (i, k), spot in zip(batch, spots):
                table[jnp.right_shift(spot, 7), jnp.bitwise_and(spot, 127)] = i
                spot_ref[i, k] = spot
        del entries[:share]

    small[0].wait()
    x = x_ref[...].reshape(query_count * token_count, width_in)
    total = x.astype(F32)
    inner = active = None
    for step in range(chunks + 2):
        if step < chunks:
            copies[step][0].wait()
        if step >= 2:
            copies[step - 2][1].wait()
        if step == 1:
            small[2].wait()
            placed.wait()
        if step >= 1:
            enter()
        later = jnp.dot(x, w1_buf[step], preferred_element_type=F32) if step < chunks else None
        if step >= 2:
            total = total + jnp.dot(active, w2_buf[step - 2], preferred_element_type=F32)
        if 1 <= step <= chunks:
            active = (0.5 * inner * (1.0 + lax.erf(inner * (0.5 ** 0.5)))).astype(BF16)
        inner = later
        if step == chunks:
            fetch = pltpu.make_async_copy(table, table_v, table_sem)
            fetch.start()

    for copy in small[3:]:
        copy.wait()
    centered = total - jnp.mean(total, axis=-1, keepdims=True)
    variance = jnp.mean(jnp.square(centered), axis=-1, keepdims=True)
    layer_out = (centered * lax.rsqrt(variance + 1e-12) * gain_ref[...].reshape(1, width_in)).astype(BF16)
    embedded = jnp.dot(layer_out, embed_ref[...], preferred_element_type=F32)
    length = jnp.sum(jnp.square(embedded), axis=-1, keepdims=True)
    vectors = embedded * lax.rsqrt(length + 1e-06)
    token = lax.broadcasted_iota(jnp.int32, vectors.shape, 0)
    for i in range(query_count):
        padded = (token >= i * token_count + lens_ref[i]) & (token < (i + 1) * token_count)
        vectors = jnp.where(padded, 0.0, vectors)
    vectors = vectors.astype(BF16)
    fetch.wait()
    tokens = query_count * token_count
    wanted = table_v[...].astype(F32).astype(BF16)
    out_ref[pl.ds(0, tokens), :] = vectors
    out_ref[pl.ds(tokens, slots), :] = wanted


def encode(
    me,
    query_hidden,
    query_lengths,
    inner_weight,
    outer_weight,
    norm_gain,
    embed_weight,
    half,
    passage_row,
    candidates,
    slots,
    color,
):
    query_count, token_count, d = query_hidden.shape
    ff = inner_weight.shape[1]
    e = embed_weight.shape[1]
    slots = -(-slots // 16) * 16
    assert 2 * half <= e == 128
    chunks = 4
    width = ff // chunks
    tokens = query_count * token_count

    def kernel(*refs):
        encode_kernel(half, color, *refs)

    return pl.pallas_call(
        kernel,
        out_shape=(
            jax.ShapeDtypeStruct((tokens + slots, e), BF16),
            jax.ShapeDtypeStruct(candidates.shape, jnp.int32),
        ),
        in_specs=[SMEM] + [ANY] * 8,
        out_specs=(VMEM, SMEM),
        scratch_shapes=[
            pltpu.VMEM((chunks, d, width), BF16),
            pltpu.VMEM((chunks, width, d), BF16),
            pltpu.SMEM(query_lengths.shape, jnp.int32),
            pltpu.VMEM(passage_row.shape, jnp.int32),
            pltpu.SMEM(passage_row.shape, jnp.int32),
            pltpu.SMEM(candidates.shape, jnp.int32),
            pltpu.VMEM(query_hidden.shape, BF16),
            pltpu.VMEM(norm_gain.shape, F32),
            pltpu.VMEM(embed_weight.shape, BF16),
            pltpu.SMEM((slots, e), jnp.int32),
            pltpu.VMEM((slots, e), jnp.int32),
            pltpu.SemaphoreType.DMA((2, chunks)),
            pltpu.SemaphoreType.DMA((6,)),
            pltpu.SemaphoreType.DMA,
            pltpu.SemaphoreType.DMA,
        ],
        compiler_params=pltpu.CompilerParams(vmem_limit_bytes=60 * 2 ** 20),
        cost_estimate=pl.CostEstimate(
            flops=4 * tokens * d * ff, bytes_accessed=4 * d * ff, transcendentals=tokens * ff
        ),
        name="encode",
    )(
        me,
        query_lengths,
        passage_row,
        candidates,
        query_hidden,
        inner_weight,
        outer_weight,
        norm_gain,
        embed_weight,
    )


def mask_kernel(len0_ref, len1_ref, pass0_ref, pass1_ref, _, out0_ref, out1_ref):
    mask_into(out0_ref, pass0_ref, len0_ref, 0, pass0_ref.shape[0])
    mask_into(out1_ref, pass1_ref, len1_ref, 0, pass1_ref.shape[0])


def mask(lengths, passages, late):
    shape = passages[0].shape
    size = 2 * passages[0].size
    return pl.pallas_call(
        mask_kernel,
        out_shape=[jax.ShapeDtypeStruct(shape, BF16)] * 2,
        in_specs=[SMEM, SMEM, VMEM, VMEM, VMEM],
        out_specs=[VMEM, VMEM],
        compiler_params=pltpu.CompilerParams(vmem_limit_bytes=2 ** 22),
        cost_estimate=pl.CostEstimate(flops=8 * size, bytes_accessed=4 * size, transcendentals=0),
        name="mask",
    )(*lengths, *passages, late)


def score_kernel(order, token_count, me_ref, own_ref, other_ref, *refs):
    slots = len(order)
    got_refs = refs[:slots]
    out_ref, best_ref, index_v, index, sem = refs[slots:]
    message, lanes = got_refs[0].shape
    half = own_ref.shape[0]
    rows = -(-slots // 16) * 16
    tokens = message - rows
    group = min(slots, 256 // token_count)
    unroll = half if slots == group else 8
    chip = jnp.right_shift(me_ref[0], 1)
    mine = lax.broadcasted_iota(jnp.int32, (rows, lanes), 0) == chip
    for s in range(slots):
        table = got_refs[s][pl.ds(tokens, rows), :].astype(F32)
        query = jnp.sum(jnp.where(mine, table, 0.0), axis=0, keepdims=True)
        index_v[s:s + 1, :] = query.astype(jnp.int32) * token_count
    copy = pltpu.make_async_copy(index_v, index, sem)
    copy.start()
    copy.wait()

    for first, pass_ref in ((half, other_ref), (0, own_ref)):

        def several(step, carry):
            for part in range(slots // group):
                rows = []
                for j in range(unroll):
                    p = step * unroll + j
                    picked = jnp.concatenate(
                        [
                            got_refs[s][pl.ds(pl.multiple_of(index[s, first + p], token_count), token_count), :]
                            for s in range(part * group, (part + 1) * group)
                        ],
                        axis=0,
                    )
                    similar = lax.dot_general(pass_ref[p], picked, NT, preferred_element_type=F32)
                    rows.append(jnp.max(similar, axis=0, keepdims=True))
                    if len(rows) == 8:
                        best_ref[
                            pl.ds(pl.multiple_of(first + step * unroll + j - 7, 8), 8),
                            pl.ds(part * group * token_count, group * token_count),
                        ] = jnp.concatenate(rows, axis=0)
                        rows = []
            return carry

        if unroll == half:
            several(0, 0)
        else:
            lax.fori_loop(0, half // unroll, several, 0)
    wide = best_ref.shape[1]
    source = lax.broadcasted_iota(jnp.int32, (slots, wide), 0)
    column = lax.broadcasted_iota(jnp.int32, (slots, wide), 1)
    start = source * token_count
    ones = jnp.where((column >= start) & (column < start + token_count), 1.0, 0.0).astype(BF16)
    total = sum(lax.dot_general(ones, part, NT, preferred_element_type=F32) for part in split3(best_ref[...]))
    out_ref[...] = jnp.zeros(out_ref.shape, F32)
    for s in range(slots):
        out_ref[pl.ds(jnp.bitwise_xor(chip, order[s]), 1), pl.ds(0, 2 * half)] = total[s:s + 1]


def score(me, got, order, own, other, token_count):
    half, plen, e = own.shape
    passage_count = 2 * half
    slots = len(got)

    def kernel(*refs):
        score_kernel(order, token_count, *refs)

    return pl.pallas_call(
        kernel,
        out_shape=jax.ShapeDtypeStruct((slots, e), F32),
        in_specs=[SMEM, VMEM, VMEM] + [VMEM] * slots,
        out_specs=VMEM,
        scratch_shapes=[
            pltpu.VMEM((passage_count, slots * token_count), F32),
            pltpu.VMEM((slots, e), jnp.int32),
            pltpu.SMEM((slots, e), jnp.int32),
            pltpu.SemaphoreType.DMA,
        ],
        compiler_params=pltpu.CompilerParams(vmem_limit_bytes=12 * 2 ** 20),
        cost_estimate=pl.CostEstimate(
            flops=2 * passage_count * slots * token_count * plen * e,
            bytes_accessed=4 * own.size,
            transcendentals=0,
        ),
        name="score",
    )(me, own, other, *[got[s] for s in order])


def finish_kernel(got_ref, spot_ref, scores_ref, best_ref):
    slots, lanes = got_ref.shape
    query_count, cand_count = scores_ref.shape
    parts = split3(got_ref[...])
    slot_iota = lax.broadcasted_iota(jnp.int32, (slots, cand_count), 0) * lanes
    lane_iota = lax.broadcasted_iota(jnp.int32, (lanes, cand_count), 0)
    row_iota = lax.broadcasted_iota(jnp.int32, (cand_count, cand_count), 0)
    col_iota = lax.broadcasted_iota(jnp.int32, (cand_count, cand_count), 1)
    place = lax.broadcasted_iota(jnp.int32, (cand_count, 128), 1)
    for i in range(query_count):
        spot = spot_ref[i:i + 1, :]
        lane = jnp.bitwise_and(spot, lanes - 1)
        onehot = jnp.where(lane_iota == lane, 1.0, 0.0).astype(BF16)
        picked = sum(jnp.dot(part, onehot, preferred_element_type=F32) for part in parts)
        score_row = jnp.sum(jnp.where(slot_iota == spot - lane, picked, 0.0), axis=0, keepdims=True)
        scores_ref[i:i + 1, :] = score_row
        across = jnp.broadcast_to(score_row, (cand_count, cand_count))
        score_col = jnp.sum(jnp.where(row_iota == col_iota, across, 0.0), axis=1, keepdims=True)
        ahead = (across > score_col) | ((across == score_col) & (col_iota < row_iota))
        rank = jnp.sum(jnp.where(ahead, 1.0, 0.0), axis=1, keepdims=True).astype(jnp.int32)
        ordered = jnp.sum(jnp.where(rank == place, score_col, 0.0), axis=0, keepdims=True)
        best_ref[i:i + 1, :] = ordered[:, :TOPN]


def finish(got, spots):
    return pl.pallas_call(
        finish_kernel,
        out_shape=(
            jax.ShapeDtypeStruct(spots.shape, F32),
            jax.ShapeDtypeStruct((spots.shape[0], TOPN), F32),
        ),
        in_specs=[VMEM, VMEM],
        out_specs=(VMEM, VMEM),
        compiler_params=pltpu.CompilerParams(vmem_limit_bytes=2 ** 21),
        name="finish",
    )(got, spots)


def swap(value, distance):
    size = lax.axis_size("shard")
    return lax.ppermute(value, "shard", [(i, i ^ distance) for i in range(size)])


def per_device(
    query_hidden,
    query_lengths,
    inner_weight,
    outer_weight,
    norm_gain,
    embed_weight,
    passage_vectors,
    passage_lengths,
    passage_row,
    candidates,
):
    size = lax.axis_size("shard")
    slots = size // 2
    inner = 1
    while 4 * inner * inner <= slots:
        inner *= 2
    shift = inner.bit_length()

    def color(index):
        return (index ^ (index >> 1) ^ (index >> shift)) & 1

    groups = [[i for i in range(size) if color(i) == c] for c in range(2)]

    def send(value, distance):
        return swap(value, 2 * distance + color(2 * distance))

    me = lax.axis_index("shard").astype(jnp.int32).reshape(1)
    across = swap(passage_lengths, 1)
    message, spots = encode(
        me,
        query_hidden,
        query_lengths,
        inner_weight,
        outer_weight,
        norm_gain,
        embed_weight,
        passage_vectors.shape[0],
        passage_row,
        candidates,
        slots,
        color,
    )
    message, across, raw = lax.optimization_barrier((message, across, passage_vectors))
    raw = swap(raw, 1)

    line = [message] + [send(message, d) for d in range(slots - inner, 0, -inner)][::-1]
    got = [line[s // inner] if s % inner == 0 else send(line[s // inner], s % inner) for s in range(slots)]
    own, other = mask((passage_lengths, across), (passage_vectors, raw), got[-1])
    order = [z + y for z in [0, *range(slots - inner, 0, -inner)] for y in range(inner)]
    sums = score(me, got, order, own, other, query_hidden.shape[1])
    back = lax.all_to_all(sums, "shard", split_axis=0, concat_axis=0, axis_index_groups=groups, tiled=True)
    return finish(back, spots)


def solution(mesh):
    in_specs = (
        P(("groups", "shard"), None, None),
        P(("groups", "shard")),
        P(),
        P(),
        P(),
        P(),
        P(("groups", "shard"), None, None),
        P(("groups", "shard")),
        P("groups"),
        P(("groups", "shard"), None),
    )
    out_specs = (P(("groups", "shard"), None), P(("groups", "shard"), None))
    return jax.shard_map(
        per_device, mesh=mesh, in_specs=in_specs, out_specs=out_specs, check_vma=False
    )
```

```python
import jax
import jax.numpy as jnp
from jax import lax
from jax.experimental import pallas as pl
from jax.experimental.pallas import tpu as pltpu
from jax.sharding import PartitionSpec as P

TOPN = 10
F32 = jnp.float32
BF16 = jnp.bfloat16
NT = (((1,), (1,)), ((), ()))
VMEM = pl.BlockSpec(memory_space=pltpu.VMEM)
SMEM = pl.BlockSpec(memory_space=pltpu.SMEM)
ANY = pl.BlockSpec(memory_space=pl.ANY)


def split3(value):
    high = value.astype(BF16)
    rest = value - high.astype(F32)
    middle = rest.astype(BF16)
    low = (rest - middle.astype(F32)).astype(BF16)
    return high, middle, low


def mask_into(out_ref, pass_ref, len_ref, first, count):
    def mask(p, carry):
        block = pass_ref[p]
        keep = lax.broadcasted_iota(jnp.int32, block.shape, 0) < len_ref[p]
        block = block.astype(F32)
        out_ref[p] = jnp.where(keep, block, jnp.broadcast_to(block[0:1], block.shape)).astype(BF16)
        return carry

    if count <= 8:
        for p in range(first, first + count):
            mask(p, 0)
    else:
        lax.fori_loop(first, first + count, mask, 0, unroll=16)


def encode_kernel(
    half,
    color,
    me_ref,
    lens_hbm,
    row_hbm,
    cand_hbm,
    x_hbm,
    w1_ref,
    w2_ref,
    gain_hbm,
    embed_hbm,
    out_ref,
    spot_ref,
    w1_buf,
    w2_buf,
    lens_ref,
    row_ref,
    place_ref,
    cand_ref,
    x_ref,
    gain_ref,
    embed_ref,
    table,
    table_v,
    sems,
    small_sems,
    place_sem,
    table_sem,
):
    chunks, _, width = w1_buf.shape
    slots, lanes = table_v.shape
    query_count, token_count, width_in = x_ref.shape
    cand_count = cand_ref.shape[1]
    table_v[...] = jnp.zeros(table_v.shape, jnp.int32)
    clear = pltpu.make_async_copy(table_v, table, table_sem)
    clear.start()
    copies = []
    for c in range(chunks):
        first = pltpu.make_async_copy(w1_ref.at[:, pl.ds(c * width, width)], w1_buf.at[c], sems.at[0, c])
        second = pltpu.make_async_copy(w2_ref.at[pl.ds(c * width, width), :], w2_buf.at[c], sems.at[1, c])
        copies.append((first, second))
    small = [
        pltpu.make_async_copy(source, target, small_sems.at[n])
        for n, (source, target) in enumerate(
            (
                (x_hbm, x_ref),
                (row_hbm, row_ref),
                (cand_hbm, cand_ref),
                (lens_hbm, lens_ref),
                (gain_hbm, gain_ref),
                (embed_hbm, embed_ref),
            )
        )
    ]
    for copy in small[:3]:
        copy.start()
    copies[0][0].start()
    copies[1][0].start()
    copies[0][1].start()
    for c in range(2, chunks):
        copies[c][0].start()
        copies[c - 1][1].start()
    copies[-1][1].start()
    for copy in small[3:]:
        copy.start()
    clear.wait()
    small[1].wait()
    row = row_ref[...]
    owner = jnp.floor((row.astype(F32) + 0.5) * (1.0 / half)).astype(jnp.int32)
    opposite = jnp.bitwise_xor(color(owner), color(me_ref[0]))
    row_ref[...] = jnp.right_shift(owner, 1) * lanes + row - owner * half + opposite * half
    placed = pltpu.make_async_copy(row_ref, place_ref, place_sem)
    placed.start()

    entries = [(i, k) for k in range(cand_count) for i in range(query_count)]
    share = -(-len(entries) // chunks)

    def enter():
        for first in range(0, share, 12):
            batch = entries[first:min(first + 12, share)]
            names = [cand_ref[i, k] for i, k in batch]
            spots = [place_ref[name] for name in names]
            for (i, k), spot in zip(batch, spots):
                table[jnp.right_shift(spot, 7), jnp.bitwise_and(spot, 127)] = i
                spot_ref[i, k] = spot
        del entries[:share]

    small[0].wait()
    x = x_ref[...].reshape(query_count * token_count, width_in)
    total = x.astype(F32)
    inner = active = None
    for step in range(chunks + 2):
        if step < chunks:
            copies[step][0].wait()
        if step >= 2:
            copies[step - 2][1].wait()
        if step == 1:
            small[2].wait()
            placed.wait()
        if step >= 1:
            enter()
        later = jnp.dot(x, w1_buf[step], preferred_element_type=F32) if step < chunks else None
        if step >= 2:
            total = total + jnp.dot(active, w2_buf[step - 2], preferred_element_type=F32)
        if 1 <= step <= chunks:
            active = (0.5 * inner * (1.0 + lax.erf(inner * (0.5 ** 0.5)))).astype(BF16)
        inner = later
        if step == chunks:
            fetch = pltpu.make_async_copy(table, table_v, table_sem)
            fetch.start()

    for copy in small[3:]:
        copy.wait()
    centered = total - jnp.mean(total, axis=-1, keepdims=True)
    variance = jnp.mean(jnp.square(centered), axis=-1, keepdims=True)
    layer_out = (centered * lax.rsqrt(variance + 1e-12) * gain_ref[...].reshape(1, width_in)).astype(BF16)
    embedded = jnp.dot(layer_out, embed_ref[...], preferred_element_type=F32)
    length = jnp.sum(jnp.square(embedded), axis=-1, keepdims=True)
    vectors = embedded * lax.rsqrt(length + 1e-06)
    token = lax.broadcasted_iota(jnp.int32, vectors.shape, 0)
    for i in range(query_count):
        padded = (token >= i * token_count + lens_ref[i]) & (token < (i + 1) * token_count)
        vectors = jnp.where(padded, 0.0, vectors)
    vectors = vectors.astype(BF16)
    fetch.wait()
    tokens = query_count * token_count
    wanted = table_v[...].astype(F32).astype(BF16)
    out_ref[pl.ds(0, tokens), :] = vectors
    out_ref[pl.ds(tokens, slots), :] = wanted


def encode(
    me,
    query_hidden,
    query_lengths,
    inner_weight,
    outer_weight,
    norm_gain,
    embed_weight,
    half,
    passage_row,
    candidates,
    slots,
    color,
):
    query_count, token_count, d = query_hidden.shape
    ff = inner_weight.shape[1]
    e = embed_weight.shape[1]
    slots = -(-slots // 16) * 16
    assert 2 * half <= e == 128
    chunks = 4
    width = ff // chunks
    tokens = query_count * token_count

    def kernel(*refs):
        encode_kernel(half, color, *refs)

    return pl.pallas_call(
        kernel,
        out_shape=(
            jax.ShapeDtypeStruct((tokens + slots, e), BF16),
            jax.ShapeDtypeStruct(candidates.shape, jnp.int32),
        ),
        in_specs=[SMEM] + [ANY] * 8,
        out_specs=(VMEM, SMEM),
        scratch_shapes=[
            pltpu.VMEM((chunks, d, width), BF16),
            pltpu.VMEM((chunks, width, d), BF16),
            pltpu.SMEM(query_lengths.shape, jnp.int32),
            pltpu.VMEM(passage_row.shape, jnp.int32),
            pltpu.SMEM(passage_row.shape, jnp.int32),
            pltpu.SMEM(candidates.shape, jnp.int32),
            pltpu.VMEM(query_hidden.shape, BF16),
            pltpu.VMEM(norm_gain.shape, F32),
            pltpu.VMEM(embed_weight.shape, BF16),
            pltpu.SMEM((slots, e), jnp.int32),
            pltpu.VMEM((slots, e), jnp.int32),
            pltpu.SemaphoreType.DMA((2, chunks)),
            pltpu.SemaphoreType.DMA((6,)),
            pltpu.SemaphoreType.DMA,
            pltpu.SemaphoreType.DMA,
        ],
        compiler_params=pltpu.CompilerParams(vmem_limit_bytes=60 * 2 ** 20),
        cost_estimate=pl.CostEstimate(
            flops=4 * tokens * d * ff, bytes_accessed=4 * d * ff, transcendentals=tokens * ff
        ),
        name="encode",
    )(
        me,
        query_lengths,
        passage_row,
        candidates,
        query_hidden,
        inner_weight,
        outer_weight,
        norm_gain,
        embed_weight,
    )


def mask_kernel(len0_ref, len1_ref, pass0_ref, pass1_ref, _, out0_ref, out1_ref):
    mask_into(out0_ref, pass0_ref, len0_ref, 0, pass0_ref.shape[0])
    mask_into(out1_ref, pass1_ref, len1_ref, 0, pass1_ref.shape[0])


def mask(lengths, passages, late):
    shape = passages[0].shape
    size = 2 * passages[0].size
    return pl.pallas_call(
        mask_kernel,
        out_shape=[jax.ShapeDtypeStruct(shape, BF16)] * 2,
        in_specs=[SMEM, SMEM, VMEM, VMEM, VMEM],
        out_specs=[VMEM, VMEM],
        compiler_params=pltpu.CompilerParams(vmem_limit_bytes=2 ** 22),
        cost_estimate=pl.CostEstimate(flops=8 * size, bytes_accessed=4 * size, transcendentals=0),
        name="mask",
    )(*lengths, *passages, late)


def score_kernel(order, token_count, me_ref, own_ref, other_ref, *refs):
    slots = len(order)
    got_refs = refs[:slots]
    out_ref, best_ref, index_v, index, sem = refs[slots:]
    message, lanes = got_refs[0].shape
    half = own_ref.shape[0]
    rows = -(-slots // 16) * 16
    tokens = message - rows
    group = min(slots, 256 // token_count)
    unroll = half if slots == group else 8
    chip = jnp.right_shift(me_ref[0], 1)
    mine = lax.broadcasted_iota(jnp.int32, (rows, lanes), 0) == chip
    for s in range(slots):
        table = got_refs[s][pl.ds(tokens, rows), :].astype(F32)
        query = jnp.sum(jnp.where(mine, table, 0.0), axis=0, keepdims=True)
        index_v[s:s + 1, :] = query.astype(jnp.int32) * token_count
    copy = pltpu.make_async_copy(index_v, index, sem)
    copy.start()
    copy.wait()

    for first, pass_ref in ((half, other_ref), (0, own_ref)):

        def several(step, carry):
            for part in range(slots // group):
                rows = []
                for j in range(unroll):
                    p = step * unroll + j
                    picked = jnp.concatenate(
                        [
                            got_refs[s][pl.ds(pl.multiple_of(index[s, first + p], token_count), token_count), :]
                            for s in range(part * group, (part + 1) * group)
                        ],
                        axis=0,
                    )
                    similar = lax.dot_general(pass_ref[p], picked, NT, preferred_element_type=F32)
                    rows.append(jnp.max(similar, axis=0, keepdims=True))
                    if len(rows) == 8:
                        best_ref[
                            pl.ds(pl.multiple_of(first + step * unroll + j - 7, 8), 8),
                            pl.ds(part * group * token_count, group * token_count),
                        ] = jnp.concatenate(rows, axis=0)
                        rows = []
            return carry

        if unroll == half:
            several(0, 0)
        else:
            lax.fori_loop(0, half // unroll, several, 0)
    wide = best_ref.shape[1]
    source = lax.broadcasted_iota(jnp.int32, (slots, wide), 0)
    column = lax.broadcasted_iota(jnp.int32, (slots, wide), 1)
    start = source * token_count
    ones = jnp.where((column >= start) & (column < start + token_count), 1.0, 0.0).astype(BF16)
    total = sum(lax.dot_general(ones, part, NT, preferred_element_type=F32) for part in split3(best_ref[...]))
    out_ref[...] = jnp.zeros(out_ref.shape, F32)
    for s in range(slots):
        out_ref[pl.ds(jnp.bitwise_xor(chip, order[s]), 1), pl.ds(0, 2 * half)] = total[s:s + 1]


def score(me, got, order, own, other, token_count):
    half, plen, e = own.shape
    passage_count = 2 * half
    slots = len(got)

    def kernel(*refs):
        score_kernel(order, token_count, *refs)

    return pl.pallas_call(
        kernel,
        out_shape=jax.ShapeDtypeStruct((slots, e), F32),
        in_specs=[SMEM, VMEM, VMEM] + [VMEM] * slots,
        out_specs=VMEM,
        scratch_shapes=[
            pltpu.VMEM((passage_count, slots * token_count), F32),
            pltpu.VMEM((slots, e), jnp.int32),
            pltpu.SMEM((slots, e), jnp.int32),
            pltpu.SemaphoreType.DMA,
        ],
        compiler_params=pltpu.CompilerParams(vmem_limit_bytes=12 * 2 ** 20),
        cost_estimate=pl.CostEstimate(
            flops=2 * passage_count * slots * token_count * plen * e,
            bytes_accessed=4 * own.size,
            transcendentals=0,
        ),
        name="score",
    )(me, own, other, *[got[s] for s in order])


def finish_kernel(got_ref, spot_ref, scores_ref, best_ref):
    slots, lanes = got_ref.shape
    query_count, cand_count = scores_ref.shape
    parts = split3(got_ref[...])
    slot_iota = lax.broadcasted_iota(jnp.int32, (slots, cand_count), 0) * lanes
    lane_iota = lax.broadcasted_iota(jnp.int32, (lanes, cand_count), 0)
    row_iota = lax.broadcasted_iota(jnp.int32, (cand_count, cand_count), 0)
    col_iota = lax.broadcasted_iota(jnp.int32, (cand_count, cand_count), 1)
    place = lax.broadcasted_iota(jnp.int32, (cand_count, 128), 1)
    for i in range(query_count):
        spot = spot_ref[i:i + 1, :]
        lane = jnp.bitwise_and(spot, lanes - 1)
        onehot = jnp.where(lane_iota == lane, 1.0, 0.0).astype(BF16)
        picked = sum(jnp.dot(part, onehot, preferred_element_type=F32) for part in parts)
        score_row = jnp.sum(jnp.where(slot_iota == spot - lane, picked, 0.0), axis=0, keepdims=True)
        scores_ref[i:i + 1, :] = score_row
        across = jnp.broadcast_to(score_row, (cand_count, cand_count))
        score_col = jnp.sum(jnp.where(row_iota == col_iota, across, 0.0), axis=1, keepdims=True)
        ahead = (across > score_col) | ((across == score_col) & (col_iota < row_iota))
        rank = jnp.sum(jnp.where(ahead, 1.0, 0.0), axis=1, keepdims=True).astype(jnp.int32)
        ordered = jnp.sum(jnp.where(rank == place, score_col, 0.0), axis=0, keepdims=True)
        best_ref[i:i + 1, :] = ordered[:, :TOPN]


def finish(got, spots):
    return pl.pallas_call(
        finish_kernel,
        out_shape=(
            jax.ShapeDtypeStruct(spots.shape, F32),
            jax.ShapeDtypeStruct((spots.shape[0], TOPN), F32),
        ),
        in_specs=[VMEM, VMEM],
        out_specs=(VMEM, VMEM),
        compiler_params=pltpu.CompilerParams(vmem_limit_bytes=2 ** 21),
        name="finish",
    )(got, spots)


def swap(value, distance):
    size = lax.axis_size("shard")
    return lax.ppermute(value, "shard", [(i, i ^ distance) for i in range(size)])


def per_device(
    query_hidden,
    query_lengths,
    inner_weight,
    outer_weight,
    norm_gain,
    embed_weight,
    passage_vectors,
    passage_lengths,
    passage_row,
    candidates,
):
    size = lax.axis_size("shard")
    slots = size // 2
    inner = 1
    while 4 * inner * inner <= slots:
        inner *= 2
    shift = inner.bit_length()

    def color(index):
        return (index ^ (index >> 1) ^ (index >> shift)) & 1

    groups = [[i for i in range(size) if color(i) == c] for c in range(2)]

    def send(value, distance):
        return swap(value, 2 * distance + color(2 * distance))

    me = lax.axis_index("shard").astype(jnp.int32).reshape(1)
    across = swap(passage_lengths, 1)
    message, spots = encode(
        me,
        query_hidden,
        query_lengths,
        inner_weight,
        outer_weight,
        norm_gain,
        embed_weight,
        passage_vectors.shape[0],
        passage_row,
        candidates,
        slots,
        color,
    )
    message, across, raw = lax.optimization_barrier((message, across, passage_vectors))
    raw = swap(raw, 1)

    line = [message] + [send(message, d) for d in range(slots - inner, 0, -inner)][::-1]
    got = [line[s // inner] if s % inner == 0 else send(line[s // inner], s % inner) for s in range(slots)]
    own, other = mask((passage_lengths, across), (passage_vectors, raw), got[inner + 1])
    order = [z + y for z in [0, *range(slots - inner, 0, -inner)] for y in range(inner)]
    sums = score(me, got, order, own, other, query_hidden.shape[1])
    back = lax.all_to_all(sums, "shard", split_axis=0, concat_axis=0, axis_index_groups=groups, tiled=True)
    return finish(back, spots)


def solution(mesh):
    in_specs = (
        P(("groups", "shard"), None, None),
        P(("groups", "shard")),
        P(),
        P(),
        P(),
        P(),
        P(("groups", "shard"), None, None),
        P(("groups", "shard")),
        P("groups"),
        P(("groups", "shard"), None),
    )
    out_specs = (P(("groups", "shard"), None), P(("groups", "shard"), None))
    return jax.shard_map(
        per_device, mesh=mesh, in_specs=in_specs, out_specs=out_specs, check_vma=False
    )
```

```python
import jax
import jax.numpy as jnp
from jax import lax
from jax.experimental import pallas as pl
from jax.experimental.pallas import tpu as pltpu
from jax.sharding import PartitionSpec as P

TOPN = 10
F32 = jnp.float32
BF16 = jnp.bfloat16
NT = (((1,), (1,)), ((), ()))
VMEM = pl.BlockSpec(memory_space=pltpu.VMEM)
SMEM = pl.BlockSpec(memory_space=pltpu.SMEM)
ANY = pl.BlockSpec(memory_space=pl.ANY)


def split3(value):
    high = value.astype(BF16)
    rest = value - high.astype(F32)
    middle = rest.astype(BF16)
    low = (rest - middle.astype(F32)).astype(BF16)
    return high, middle, low


def mask_into(out_ref, pass_ref, len_ref, first, count):
    def mask(p, carry):
        block = pass_ref[p]
        keep = lax.broadcasted_iota(jnp.int32, block.shape, 0) < len_ref[p]
        block = block.astype(F32)
        out_ref[p] = jnp.where(keep, block, jnp.broadcast_to(block[0:1], block.shape)).astype(BF16)
        return carry

    if count <= 8:
        for p in range(first, first + count):
            mask(p, 0)
    else:
        lax.fori_loop(first, first + count, mask, 0, unroll=16)


def encode_kernel(
    half,
    color,
    me_ref,
    lens_hbm,
    row_hbm,
    cand_hbm,
    x_hbm,
    w1_ref,
    w2_ref,
    gain_hbm,
    embed_hbm,
    out_ref,
    spot_ref,
    w1_buf,
    w2_buf,
    lens_ref,
    row_ref,
    place_ref,
    cand_ref,
    x_ref,
    gain_ref,
    embed_ref,
    table,
    table_v,
    sems,
    small_sems,
    place_sem,
    table_sem,
):
    chunks, _, width = w1_buf.shape
    slots, lanes = table_v.shape
    query_count, token_count, width_in = x_ref.shape
    cand_count = cand_ref.shape[1]
    table_v[...] = jnp.zeros(table_v.shape, jnp.int32)
    clear = pltpu.make_async_copy(table_v, table, table_sem)
    clear.start()
    copies = []
    for c in range(chunks):
        first = pltpu.make_async_copy(w1_ref.at[:, pl.ds(c * width, width)], w1_buf.at[c], sems.at[0, c])
        second = pltpu.make_async_copy(w2_ref.at[pl.ds(c * width, width), :], w2_buf.at[c], sems.at[1, c])
        copies.append((first, second))
    small = [
        pltpu.make_async_copy(source, target, small_sems.at[n])
        for n, (source, target) in enumerate(
            (
                (x_hbm, x_ref),
                (row_hbm, row_ref),
                (cand_hbm, cand_ref),
                (lens_hbm, lens_ref),
                (gain_hbm, gain_ref),
                (embed_hbm, embed_ref),
            )
        )
    ]
    for copy in small[:3]:
        copy.start()
    copies[0][0].start()
    copies[1][0].start()
    copies[0][1].start()
    for c in range(2, chunks):
        copies[c][0].start()
        copies[c - 1][1].start()
    copies[-1][1].start()
    for copy in small[3:]:
        copy.start()
    clear.wait()
    small[1].wait()
    row = row_ref[...]
    owner = jnp.floor((row.astype(F32) + 0.5) * (1.0 / half)).astype(jnp.int32)
    opposite = jnp.bitwise_xor(color(owner), color(me_ref[0]))
    row_ref[...] = jnp.right_shift(owner, 1) * lanes + row - owner * half + opposite * half
    placed = pltpu.make_async_copy(row_ref, place_ref, place_sem)
    placed.start()

    entries = [(i, k) for k in range(cand_count) for i in range(query_count)]
    share = -(-len(entries) // chunks)

    def enter():
        for first in range(0, share, 12):
            batch = entries[first:min(first + 12, share)]
            names = [cand_ref[i, k] for i, k in batch]
            spots = [place_ref[name] for name in names]
            for (i, k), spot in zip(batch, spots):
                table[jnp.right_shift(spot, 7), jnp.bitwise_and(spot, 127)] = i
                spot_ref[i, k] = spot
        del entries[:share]

    small[0].wait()
    x = x_ref[...].reshape(query_count * token_count, width_in)
    total = x.astype(F32)
    inner = None
    for step in range(chunks + 1):
        if step < chunks:
            copies[step][0].wait()
        if step == 1:
            small[2].wait()
            placed.wait()
        if step >= 1:
            copies[step - 1][1].wait()
            enter()
        later = jnp.dot(x, w1_buf[step], preferred_element_type=F32) if step < chunks else None
        if step >= 1:
            active = (0.5 * inner * (1.0 + lax.erf(inner * (0.5 ** 0.5)))).astype(BF16)
            total = total + jnp.dot(active, w2_buf[step - 1], preferred_element_type=F32)
        inner = later
        if step == chunks:
            fetch = pltpu.make_async_copy(table, table_v, table_sem)
            fetch.start()

    for copy in small[3:]:
        copy.wait()
    centered = total - jnp.mean(total, axis=-1, keepdims=True)
    variance = jnp.mean(jnp.square(centered), axis=-1, keepdims=True)
    layer_out = (centered * lax.rsqrt(variance + 1e-12) * gain_ref[...].reshape(1, width_in)).astype(BF16)
    embedded = jnp.dot(layer_out, embed_ref[...], preferred_element_type=F32)
    length = jnp.sum(jnp.square(embedded), axis=-1, keepdims=True)
    vectors = embedded * lax.rsqrt(length + 1e-06)
    token = lax.broadcasted_iota(jnp.int32, vectors.shape, 0)
    for i in range(query_count):
        padded = (token >= i * token_count + lens_ref[i]) & (token < (i + 1) * token_count)
        vectors = jnp.where(padded, 0.0, vectors)
    vectors = vectors.astype(BF16)
    fetch.wait()
    tokens = query_count * token_count
    wanted = table_v[...].astype(F32).astype(BF16)
    out_ref[pl.ds(0, tokens), :] = vectors
    out_ref[pl.ds(tokens, slots), :] = wanted


def encode(
    me,
    query_hidden,
    query_lengths,
    inner_weight,
    outer_weight,
    norm_gain,
    embed_weight,
    half,
    passage_row,
    candidates,
    slots,
    color,
):
    query_count, token_count, d = query_hidden.shape
    ff = inner_weight.shape[1]
    e = embed_weight.shape[1]
    slots = -(-slots // 16) * 16
    assert 2 * half <= e == 128
    chunks = 4
    width = ff // chunks
    tokens = query_count * token_count

    def kernel(*refs):
        encode_kernel(half, color, *refs)

    return pl.pallas_call(
        kernel,
        out_shape=(
            jax.ShapeDtypeStruct((tokens + slots, e), BF16),
            jax.ShapeDtypeStruct(candidates.shape, jnp.int32),
        ),
        in_specs=[SMEM] + [ANY] * 8,
        out_specs=(VMEM, SMEM),
        scratch_shapes=[
            pltpu.VMEM((chunks, d, width), BF16),
            pltpu.VMEM((chunks, width, d), BF16),
            pltpu.SMEM(query_lengths.shape, jnp.int32),
            pltpu.VMEM(passage_row.shape, jnp.int32),
            pltpu.SMEM(passage_row.shape, jnp.int32),
            pltpu.SMEM(candidates.shape, jnp.int32),
            pltpu.VMEM(query_hidden.shape, BF16),
            pltpu.VMEM(norm_gain.shape, F32),
            pltpu.VMEM(embed_weight.shape, BF16),
            pltpu.SMEM((slots, e), jnp.int32),
            pltpu.VMEM((slots, e), jnp.int32),
            pltpu.SemaphoreType.DMA((2, chunks)),
            pltpu.SemaphoreType.DMA((6,)),
            pltpu.SemaphoreType.DMA,
            pltpu.SemaphoreType.DMA,
        ],
        compiler_params=pltpu.CompilerParams(vmem_limit_bytes=60 * 2 ** 20),
        cost_estimate=pl.CostEstimate(
            flops=4 * tokens * d * ff, bytes_accessed=4 * d * ff, transcendentals=tokens * ff
        ),
        name="encode",
    )(
        me,
        query_lengths,
        passage_row,
        candidates,
        query_hidden,
        inner_weight,
        outer_weight,
        norm_gain,
        embed_weight,
    )


def mask_kernel(len0_ref, len1_ref, pass0_ref, pass1_ref, _, out0_ref, out1_ref):
    mask_into(out0_ref, pass0_ref, len0_ref, 0, pass0_ref.shape[0])
    mask_into(out1_ref, pass1_ref, len1_ref, 0, pass1_ref.shape[0])


def mask(lengths, passages, late):
    shape = passages[0].shape
    size = 2 * passages[0].size
    return pl.pallas_call(
        mask_kernel,
        out_shape=[jax.ShapeDtypeStruct(shape, BF16)] * 2,
        in_specs=[SMEM, SMEM, VMEM, VMEM, VMEM],
        out_specs=[VMEM, VMEM],
        compiler_params=pltpu.CompilerParams(vmem_limit_bytes=2 ** 22),
        cost_estimate=pl.CostEstimate(flops=8 * size, bytes_accessed=4 * size, transcendentals=0),
        name="mask",
    )(*lengths, *passages, late)


def score_kernel(order, token_count, me_ref, own_ref, other_ref, *refs):
    slots = len(order)
    got_refs = refs[:slots]
    out_ref, best_ref, index_v, index, sem = refs[slots:]
    message, lanes = got_refs[0].shape
    half = own_ref.shape[0]
    rows = -(-slots // 16) * 16
    tokens = message - rows
    group = min(slots, 256 // token_count)
    unroll = half if slots == group else 8
    chip = jnp.right_shift(me_ref[0], 1)
    mine = lax.broadcasted_iota(jnp.int32, (rows, lanes), 0) == chip
    for s in range(slots):
        table = got_refs[s][pl.ds(tokens, rows), :].astype(F32)
        query = jnp.sum(jnp.where(mine, table, 0.0), axis=0, keepdims=True)
        index_v[s:s + 1, :] = query.astype(jnp.int32) * token_count
    copy = pltpu.make_async_copy(index_v, index, sem)
    copy.start()
    copy.wait()

    for first, pass_ref in ((half, other_ref), (0, own_ref)):

        def several(step, carry):
            for part in range(slots // group):
                rows = []
                for j in range(unroll):
                    p = step * unroll + j
                    picked = jnp.concatenate(
                        [
                            got_refs[s][pl.ds(pl.multiple_of(index[s, first + p], token_count), token_count), :]
                            for s in range(part * group, (part + 1) * group)
                        ],
                        axis=0,
                    )
                    similar = lax.dot_general(pass_ref[p], picked, NT, preferred_element_type=F32)
                    rows.append(jnp.max(similar, axis=0, keepdims=True))
                    if len(rows) == 8:
                        best_ref[
                            pl.ds(pl.multiple_of(first + step * unroll + j - 7, 8), 8),
                            pl.ds(part * group * token_count, group * token_count),
                        ] = jnp.concatenate(rows, axis=0)
                        rows = []
            return carry

        if unroll == half:
            several(0, 0)
        else:
            lax.fori_loop(0, half // unroll, several, 0)
    wide = best_ref.shape[1]
    source = lax.broadcasted_iota(jnp.int32, (slots, wide), 0)
    column = lax.broadcasted_iota(jnp.int32, (slots, wide), 1)
    start = source * token_count
    ones = jnp.where((column >= start) & (column < start + token_count), 1.0, 0.0).astype(BF16)
    total = sum(lax.dot_general(ones, part, NT, preferred_element_type=F32) for part in split3(best_ref[...]))
    out_ref[...] = jnp.zeros(out_ref.shape, F32)
    for s in range(slots):
        out_ref[pl.ds(jnp.bitwise_xor(chip, order[s]), 1), pl.ds(0, 2 * half)] = total[s:s + 1]


def score(me, got, order, own, other, token_count):
    half, plen, e = own.shape
    passage_count = 2 * half
    slots = len(got)

    def kernel(*refs):
        score_kernel(order, token_count, *refs)

    return pl.pallas_call(
        kernel,
        out_shape=jax.ShapeDtypeStruct((slots, e), F32),
        in_specs=[SMEM, VMEM, VMEM] + [VMEM] * slots,
        out_specs=VMEM,
        scratch_shapes=[
            pltpu.VMEM((passage_count, slots * token_count), F32),
            pltpu.VMEM((slots, e), jnp.int32),
            pltpu.SMEM((slots, e), jnp.int32),
            pltpu.SemaphoreType.DMA,
        ],
        compiler_params=pltpu.CompilerParams(vmem_limit_bytes=12 * 2 ** 20),
        cost_estimate=pl.CostEstimate(
            flops=2 * passage_count * slots * token_count * plen * e,
            bytes_accessed=4 * own.size,
            transcendentals=0,
        ),
        name="score",
    )(me, own, other, *[got[s] for s in order])


def finish_kernel(got_ref, spot_ref, scores_ref, best_ref):
    slots, lanes = got_ref.shape
    query_count, cand_count = scores_ref.shape
    parts = split3(got_ref[...])
    slot_iota = lax.broadcasted_iota(jnp.int32, (slots, cand_count), 0) * lanes
    lane_iota = lax.broadcasted_iota(jnp.int32, (lanes, cand_count), 0)
    row_iota = lax.broadcasted_iota(jnp.int32, (cand_count, cand_count), 0)
    col_iota = lax.broadcasted_iota(jnp.int32, (cand_count, cand_count), 1)
    place = lax.broadcasted_iota(jnp.int32, (cand_count, 128), 1)
    for i in range(query_count):
        spot = spot_ref[i:i + 1, :]
        lane = jnp.bitwise_and(spot, lanes - 1)
        onehot = jnp.where(lane_iota == lane, 1.0, 0.0).astype(BF16)
        picked = sum(jnp.dot(part, onehot, preferred_element_type=F32) for part in parts)
        score_row = jnp.sum(jnp.where(slot_iota == spot - lane, picked, 0.0), axis=0, keepdims=True)
        scores_ref[i:i + 1, :] = score_row
        across = jnp.broadcast_to(score_row, (cand_count, cand_count))
        score_col = jnp.sum(jnp.where(row_iota == col_iota, across, 0.0), axis=1, keepdims=True)
        ahead = (across > score_col) | ((across == score_col) & (col_iota < row_iota))
        rank = jnp.sum(jnp.where(ahead, 1.0, 0.0), axis=1, keepdims=True).astype(jnp.int32)
        ordered = jnp.sum(jnp.where(rank == place, score_col, 0.0), axis=0, keepdims=True)
        best_ref[i:i + 1, :] = ordered[:, :TOPN]


def finish(got, spots):
    return pl.pallas_call(
        finish_kernel,
        out_shape=(
            jax.ShapeDtypeStruct(spots.shape, F32),
            jax.ShapeDtypeStruct((spots.shape[0], TOPN), F32),
        ),
        in_specs=[VMEM, VMEM],
        out_specs=(VMEM, VMEM),
        compiler_params=pltpu.CompilerParams(vmem_limit_bytes=2 ** 21),
        name="finish",
    )(got, spots)


def swap(value, distance):
    size = lax.axis_size("shard")
    return lax.ppermute(value, "shard", [(i, i ^ distance) for i in range(size)])


def per_device(
    query_hidden,
    query_lengths,
    inner_weight,
    outer_weight,
    norm_gain,
    embed_weight,
    passage_vectors,
    passage_lengths,
    passage_row,
    candidates,
):
    size = lax.axis_size("shard")
    slots = size // 2
    inner = 1
    while 4 * inner * inner <= slots:
        inner *= 2
    shift = inner.bit_length()

    def color(index):
        return (index ^ (index >> 1) ^ (index >> shift)) & 1

    groups = [[i for i in range(size) if color(i) == c] for c in range(2)]

    def send(value, distance):
        return swap(value, 2 * distance + color(2 * distance))

    me = lax.axis_index("shard").astype(jnp.int32).reshape(1)
    across = swap(passage_lengths, 1)
    message, spots = encode(
        me,
        query_hidden,
        query_lengths,
        inner_weight,
        outer_weight,
        norm_gain,
        embed_weight,
        passage_vectors.shape[0],
        passage_row,
        candidates,
        slots,
        color,
    )
    message, across, raw = lax.optimization_barrier((message, across, passage_vectors))
    raw = swap(raw, 1)

    line = [message] + [send(message, d) for d in range(slots - inner, 0, -inner)][::-1]
    got = [line[s // inner] if s % inner == 0 else send(line[s // inner], s % inner) for s in range(slots)]
    own, other = mask((passage_lengths, across), (passage_vectors, raw), got[inner + 1])
    order = [z + y for z in [0, *range(slots - inner, 0, -inner)] for y in range(inner)]
    sums = score(me, got, order, own, other, query_hidden.shape[1])
    back = lax.all_to_all(sums, "shard", split_axis=0, concat_axis=0, axis_index_groups=groups, tiled=True)
    return finish(back, spots)


def solution(mesh):
    in_specs = (
        P(("groups", "shard"), None, None),
        P(("groups", "shard")),
        P(),
        P(),
        P(),
        P(),
        P(("groups", "shard"), None, None),
        P(("groups", "shard")),
        P("groups"),
        P(("groups", "shard"), None),
    )
    out_specs = (P(("groups", "shard"), None), P(("groups", "shard"), None))
    return jax.shard_map(
        per_device, mesh=mesh, in_specs=in_specs, out_specs=out_specs, check_vma=False
    )
```

```python
import jax
import jax.numpy as jnp
from jax import lax
from jax.experimental import pallas as pl
from jax.experimental.pallas import tpu as pltpu
from jax.sharding import PartitionSpec as P

TOPN = 10
F32 = jnp.float32
BF16 = jnp.bfloat16
NT = (((1,), (1,)), ((), ()))
VMEM = pl.BlockSpec(memory_space=pltpu.VMEM)
SMEM = pl.BlockSpec(memory_space=pltpu.SMEM)
ANY = pl.BlockSpec(memory_space=pl.ANY)


def split3(value):
    high = value.astype(BF16)
    rest = value - high.astype(F32)
    middle = rest.astype(BF16)
    low = (rest - middle.astype(F32)).astype(BF16)
    return high, middle, low


def mask_into(out_ref, pass_ref, len_ref, first, count):
    def mask(p, carry):
        block = pass_ref[p]
        keep = lax.broadcasted_iota(jnp.int32, block.shape, 0) < len_ref[p]
        block = block.astype(F32)
        out_ref[p] = jnp.where(keep, block, jnp.broadcast_to(block[0:1], block.shape)).astype(BF16)
        return carry

    if count <= 8:
        for p in range(first, first + count):
            mask(p, 0)
    else:
        lax.fori_loop(first, first + count, mask, 0, unroll=16)


def encode_kernel(
    half,
    color,
    me_ref,
    lens_hbm,
    row_hbm,
    cand_hbm,
    x_hbm,
    w1_ref,
    w2_ref,
    gain_hbm,
    embed_hbm,
    out_ref,
    spot_ref,
    w1_buf,
    w2_buf,
    lens_ref,
    row_ref,
    place_ref,
    cand_ref,
    x_ref,
    gain_ref,
    embed_ref,
    table,
    table_v,
    sems,
    small_sems,
    place_sem,
    table_sem,
):
    chunks, _, width = w1_buf.shape
    slots, lanes = table_v.shape
    query_count, token_count, width_in = x_ref.shape
    cand_count = cand_ref.shape[1]
    table_v[...] = jnp.zeros(table_v.shape, jnp.int32)
    clear = pltpu.make_async_copy(table_v, table, table_sem)
    clear.start()
    copies = []
    for c in range(chunks):
        first = pltpu.make_async_copy(w1_ref.at[:, pl.ds(c * width, width)], w1_buf.at[c], sems.at[0, c])
        second = pltpu.make_async_copy(w2_ref.at[pl.ds(c * width, width), :], w2_buf.at[c], sems.at[1, c])
        copies.append((first, second))
    small = [
        pltpu.make_async_copy(source, target, small_sems.at[n])
        for n, (source, target) in enumerate(
            (
                (x_hbm, x_ref),
                (row_hbm, row_ref),
                (cand_hbm, cand_ref),
                (lens_hbm, lens_ref),
                (gain_hbm, gain_ref),
                (embed_hbm, embed_ref),
            )
        )
    ]
    for copy in small[:3]:
        copy.start()
    copies[0][0].start()
    copies[1][0].start()
    copies[0][1].start()
    for c in range(2, chunks):
        copies[c][0].start()
        copies[c - 1][1].start()
    for copy in small[3:]:
        copy.start()
    copies[-1][1].start()
    clear.wait()
    small[1].wait()
    row = row_ref[...]
    owner = jnp.floor((row.astype(F32) + 0.5) * (1.0 / half)).astype(jnp.int32)
    opposite = jnp.bitwise_xor(color(owner), color(me_ref[0]))
    row_ref[...] = jnp.right_shift(owner, 1) * lanes + row - owner * half + opposite * half
    placed = pltpu.make_async_copy(row_ref, place_ref, place_sem)
    placed.start()

    entries = [(i, k) for k in range(cand_count) for i in range(query_count)]
    share = -(-len(entries) // chunks)

    def enter():
        for first in range(0, share, 12):
            batch = entries[first:min(first + 12, share)]
            names = [cand_ref[i, k] for i, k in batch]
            spots = [place_ref[name] for name in names]
            for (i, k), spot in zip(batch, spots):
                table[jnp.right_shift(spot, 7), jnp.bitwise_and(spot, 127)] = i
                spot_ref[i, k] = spot
        del entries[:share]

    small[0].wait()
    x = x_ref[...].reshape(query_count * token_count, width_in)
    total = x.astype(F32)
    inner = active = None
    for step in range(chunks + 2):
        if step < chunks:
            copies[step][0].wait()
        if step == 1:
            small[2].wait()
            placed.wait()
        if step == chunks + 1:
            for copy in small[3:]:
                copy.wait()
            fetch.wait()
        if step >= 2:
            copies[step - 2][1].wait()
        if step >= 1:
            enter()
        later = jnp.dot(x, w1_buf[step], preferred_element_type=F32) if step < chunks else None
        if step >= 2:
            total = total + jnp.dot(active, w2_buf[step - 2], preferred_element_type=F32)
        if 1 <= step <= chunks:
            active = (0.5 * inner * (1.0 + lax.erf(inner * (0.5 ** 0.5)))).astype(BF16)
        inner = later
        if step == chunks:
            fetch = pltpu.make_async_copy(table, table_v, table_sem)
            fetch.start()

    centered = total - jnp.mean(total, axis=-1, keepdims=True)
    variance = jnp.mean(jnp.square(centered), axis=-1, keepdims=True)
    layer_out = (centered * lax.rsqrt(variance + 1e-12) * gain_ref[...].reshape(1, width_in)).astype(BF16)
    embedded = jnp.dot(layer_out, embed_ref[...], preferred_element_type=F32)
    length = jnp.sum(jnp.square(embedded), axis=-1, keepdims=True)
    vectors = embedded * lax.rsqrt(length + 1e-06)
    token = lax.broadcasted_iota(jnp.int32, vectors.shape, 0)
    for i in range(query_count):
        padded = (token >= i * token_count + lens_ref[i]) & (token < (i + 1) * token_count)
        vectors = jnp.where(padded, 0.0, vectors)
    vectors = vectors.astype(BF16)
    tokens = query_count * token_count
    wanted = table_v[...].astype(F32).astype(BF16)
    out_ref[pl.ds(0, tokens), :] = vectors
    out_ref[pl.ds(tokens, slots), :] = wanted


def encode(
    me,
    query_hidden,
    query_lengths,
    inner_weight,
    outer_weight,
    norm_gain,
    embed_weight,
    half,
    passage_row,
    candidates,
    slots,
    color,
):
    query_count, token_count, d = query_hidden.shape
    ff = inner_weight.shape[1]
    e = embed_weight.shape[1]
    slots = -(-slots // 16) * 16
    assert 2 * half <= e == 128
    chunks = 4
    width = ff // chunks
    tokens = query_count * token_count

    def kernel(*refs):
        encode_kernel(half, color, *refs)

    return pl.pallas_call(
        kernel,
        out_shape=(
            jax.ShapeDtypeStruct((tokens + slots, e), BF16),
            jax.ShapeDtypeStruct(candidates.shape, jnp.int32),
        ),
        in_specs=[SMEM] + [ANY] * 8,
        out_specs=(VMEM, SMEM),
        scratch_shapes=[
            pltpu.VMEM((chunks, d, width), BF16),
            pltpu.VMEM((chunks, width, d), BF16),
            pltpu.SMEM(query_lengths.shape, jnp.int32),
            pltpu.VMEM(passage_row.shape, jnp.int32),
            pltpu.SMEM(passage_row.shape, jnp.int32),
            pltpu.SMEM(candidates.shape, jnp.int32),
            pltpu.VMEM(query_hidden.shape, BF16),
            pltpu.VMEM(norm_gain.shape, F32),
            pltpu.VMEM(embed_weight.shape, BF16),
            pltpu.SMEM((slots, e), jnp.int32),
            pltpu.VMEM((slots, e), jnp.int32),
            pltpu.SemaphoreType.DMA((2, chunks)),
            pltpu.SemaphoreType.DMA((6,)),
            pltpu.SemaphoreType.DMA,
            pltpu.SemaphoreType.DMA,
        ],
        compiler_params=pltpu.CompilerParams(vmem_limit_bytes=60 * 2 ** 20),
        cost_estimate=pl.CostEstimate(
            flops=4 * tokens * d * ff, bytes_accessed=4 * d * ff, transcendentals=tokens * ff
        ),
        name="encode",
    )(
        me,
        query_lengths,
        passage_row,
        candidates,
        query_hidden,
        inner_weight,
        outer_weight,
        norm_gain,
        embed_weight,
    )


def mask_kernel(len0_ref, len1_ref, pass0_ref, pass1_ref, _, out0_ref, out1_ref):
    mask_into(out0_ref, pass0_ref, len0_ref, 0, pass0_ref.shape[0])
    mask_into(out1_ref, pass1_ref, len1_ref, 0, pass1_ref.shape[0])


def mask(lengths, passages, late):
    shape = passages[0].shape
    size = 2 * passages[0].size
    return pl.pallas_call(
        mask_kernel,
        out_shape=[jax.ShapeDtypeStruct(shape, BF16)] * 2,
        in_specs=[SMEM, SMEM, VMEM, VMEM, VMEM],
        out_specs=[VMEM, VMEM],
        compiler_params=pltpu.CompilerParams(vmem_limit_bytes=2 ** 22),
        cost_estimate=pl.CostEstimate(flops=8 * size, bytes_accessed=4 * size, transcendentals=0),
        name="mask",
    )(*lengths, *passages, late)


def score_kernel(slots, token_count, me_ref, own_ref, other_ref, *refs):
    got_refs = refs[:slots]
    out_ref, best_ref, index_v, index, sem = refs[slots:]
    message, lanes = got_refs[0].shape
    half = own_ref.shape[0]
    rows = -(-slots // 16) * 16
    tokens = message - rows
    group = min(slots, 256 // token_count)
    unroll = half if slots == group else 8
    chip = jnp.right_shift(me_ref[0], 1)
    mine = lax.broadcasted_iota(jnp.int32, (rows, lanes), 0) == chip
    for s in range(slots):
        table = got_refs[s][pl.ds(tokens, rows), :].astype(F32)
        query = jnp.sum(jnp.where(mine, table, 0.0), axis=0, keepdims=True)
        index_v[s:s + 1, :] = query.astype(jnp.int32) * token_count
    copy = pltpu.make_async_copy(index_v, index, sem)
    copy.start()
    copy.wait()

    for first, pass_ref in ((half, other_ref), (0, own_ref)):

        def several(step, carry):
            for part in range(slots // group):
                rows = []
                for j in range(unroll):
                    p = step * unroll + j
                    picked = jnp.concatenate(
                        [
                            got_refs[s][pl.ds(pl.multiple_of(index[s, first + p], token_count), token_count), :]
                            for s in range(part * group, (part + 1) * group)
                        ],
                        axis=0,
                    )
                    similar = lax.dot_general(pass_ref[p], picked, NT, preferred_element_type=F32)
                    rows.append(jnp.max(similar, axis=0, keepdims=True))
                    if len(rows) == 8:
                        best_ref[
                            pl.ds(pl.multiple_of(first + step * unroll + j - 7, 8), 8),
                            pl.ds(part * group * token_count, group * token_count),
                        ] = jnp.concatenate(rows, axis=0)
                        rows = []
            return carry

        if unroll == half:
            several(0, 0)
        else:
            lax.fori_loop(0, half // unroll, several, 0)
    wide = best_ref.shape[1]
    source = lax.broadcasted_iota(jnp.int32, (slots, wide), 0)
    column = lax.broadcasted_iota(jnp.int32, (slots, wide), 1)
    start = source * token_count
    ones = jnp.where((column >= start) & (column < start + token_count), 1.0, 0.0).astype(BF16)
    total = sum(lax.dot_general(ones, part, NT, preferred_element_type=F32) for part in split3(best_ref[...]))
    out_ref[...] = jnp.zeros(out_ref.shape, F32)
    for s in range(slots):
        out_ref[pl.ds(jnp.bitwise_xor(chip, s), 1), pl.ds(0, 2 * half)] = total[s:s + 1]


def score(me, got, own, other, token_count):
    half, plen, e = own.shape
    passage_count = 2 * half
    slots = len(got)

    def kernel(*refs):
        score_kernel(slots, token_count, *refs)

    return pl.pallas_call(
        kernel,
        out_shape=jax.ShapeDtypeStruct((slots, e), F32),
        in_specs=[SMEM, VMEM, VMEM] + [VMEM] * slots,
        out_specs=VMEM,
        scratch_shapes=[
            pltpu.VMEM((passage_count, slots * token_count), F32),
            pltpu.VMEM((slots, e), jnp.int32),
            pltpu.SMEM((slots, e), jnp.int32),
            pltpu.SemaphoreType.DMA,
        ],
        compiler_params=pltpu.CompilerParams(vmem_limit_bytes=12 * 2 ** 20),
        cost_estimate=pl.CostEstimate(
            flops=2 * passage_count * slots * token_count * plen * e,
            bytes_accessed=4 * own.size,
            transcendentals=0,
        ),
        name="score",
    )(me, own, other, *got)


def finish_kernel(got_ref, spot_ref, scores_ref, best_ref):
    slots, lanes = got_ref.shape
    query_count, cand_count = scores_ref.shape
    parts = split3(got_ref[...])
    slot_iota = lax.broadcasted_iota(jnp.int32, (slots, cand_count), 0) * lanes
    lane_iota = lax.broadcasted_iota(jnp.int32, (lanes, cand_count), 0)
    row_iota = lax.broadcasted_iota(jnp.int32, (cand_count, cand_count), 0)
    col_iota = lax.broadcasted_iota(jnp.int32, (cand_count, cand_count), 1)
    place = lax.broadcasted_iota(jnp.int32, (cand_count, 128), 1)
    for i in range(query_count):
        spot = spot_ref[i:i + 1, :]
        lane = jnp.bitwise_and(spot, lanes - 1)
        onehot = jnp.where(lane_iota == lane, 1.0, 0.0).astype(BF16)
        picked = sum(jnp.dot(part, onehot, preferred_element_type=F32) for part in parts)
        score_row = jnp.sum(jnp.where(slot_iota == spot - lane, picked, 0.0), axis=0, keepdims=True)
        scores_ref[i:i + 1, :] = score_row
        across = jnp.broadcast_to(score_row, (cand_count, cand_count))
        score_col = jnp.sum(jnp.where(row_iota == col_iota, across, 0.0), axis=1, keepdims=True)
        ahead = (across > score_col) | ((across == score_col) & (col_iota < row_iota))
        rank = jnp.sum(jnp.where(ahead, 1.0, 0.0), axis=1, keepdims=True).astype(jnp.int32)
        ordered = jnp.sum(jnp.where(rank == place, score_col, 0.0), axis=0, keepdims=True)
        best_ref[i:i + 1, :] = ordered[:, :TOPN]


def finish(got, spots):
    return pl.pallas_call(
        finish_kernel,
        out_shape=(
            jax.ShapeDtypeStruct(spots.shape, F32),
            jax.ShapeDtypeStruct((spots.shape[0], TOPN), F32),
        ),
        in_specs=[VMEM, VMEM],
        out_specs=(VMEM, VMEM),
        compiler_params=pltpu.CompilerParams(vmem_limit_bytes=2 ** 21),
        name="finish",
    )(got, spots)


def swap(value, distance):
    size = lax.axis_size("shard")
    return lax.ppermute(value, "shard", [(i, i ^ distance) for i in range(size)])


def per_device(
    query_hidden,
    query_lengths,
    inner_weight,
    outer_weight,
    norm_gain,
    embed_weight,
    passage_vectors,
    passage_lengths,
    passage_row,
    candidates,
):
    size = lax.axis_size("shard")
    slots = size // 2
    inner = 1
    while 4 * inner * inner <= slots:
        inner *= 2
    shift = inner.bit_length()

    def color(index):
        return (index ^ (index >> 1) ^ (index >> shift)) & 1

    groups = [[i for i in range(size) if color(i) == c] for c in range(2)]

    def send(value, distance):
        return swap(value, 2 * distance + color(2 * distance))

    me = lax.axis_index("shard").astype(jnp.int32).reshape(1)
    across = swap(passage_lengths, 1)
    message, spots = encode(
        me,
        query_hidden,
        query_lengths,
        inner_weight,
        outer_weight,
        norm_gain,
        embed_weight,
        passage_vectors.shape[0],
        passage_row,
        candidates,
        slots,
        color,
    )
    message, across, raw = lax.optimization_barrier((message, across, passage_vectors))
    raw = swap(raw, 1)

    line = [message] + [send(message, d) for d in range(slots - inner, 0, -inner)][::-1]
    got = [line[s // inner] if s % inner == 0 else send(line[s // inner], s % inner) for s in range(slots)]
    own, other = mask((passage_lengths, across), (passage_vectors, raw), got[inner + 1])
    sums = score(me, got, own, other, query_hidden.shape[1])
    back = lax.all_to_all(sums, "shard", split_axis=0, concat_axis=0, axis_index_groups=groups, tiled=True)
    return finish(back, spots)


def solution(mesh):
    in_specs = (
        P(("groups", "shard"), None, None),
        P(("groups", "shard")),
        P(),
        P(),
        P(),
        P(),
        P(("groups", "shard"), None, None),
        P(("groups", "shard")),
        P("groups"),
        P(("groups", "shard"), None),
    )
    out_specs = (P(("groups", "shard"), None), P(("groups", "shard"), None))
    return jax.shard_map(
        per_device, mesh=mesh, in_specs=in_specs, out_specs=out_specs, check_vma=False
    )
```

```python
import jax
import jax.numpy as jnp
from jax import lax
from jax.experimental import pallas as pl
from jax.experimental.pallas import tpu as pltpu
from jax.sharding import PartitionSpec as P

TOPN = 10
F32 = jnp.float32
BF16 = jnp.bfloat16
NT = (((1,), (1,)), ((), ()))
VMEM = pl.BlockSpec(memory_space=pltpu.VMEM)
SMEM = pl.BlockSpec(memory_space=pltpu.SMEM)
ANY = pl.BlockSpec(memory_space=pl.ANY)


def split3(value):
    high = value.astype(BF16)
    rest = value - high.astype(F32)
    middle = rest.astype(BF16)
    low = (rest - middle.astype(F32)).astype(BF16)
    return high, middle, low


def mask_into(out_ref, pass_ref, len_ref, first, count):
    def mask(p, carry):
        block = pass_ref[p]
        keep = lax.broadcasted_iota(jnp.int32, block.shape, 0) < len_ref[p]
        block = block.astype(F32)
        out_ref[p] = jnp.where(keep, block, jnp.broadcast_to(block[0:1], block.shape)).astype(BF16)
        return carry

    if count <= 8:
        for p in range(first, first + count):
            mask(p, 0)
    else:
        lax.fori_loop(first, first + count, mask, 0, unroll=16)


def encode_kernel(
    half,
    color,
    me_ref,
    lens_hbm,
    row_hbm,
    cand_hbm,
    x_hbm,
    w1_ref,
    w2_ref,
    gain_hbm,
    embed_hbm,
    out_ref,
    spot_ref,
    w1_buf,
    w2_buf,
    lens_ref,
    row_ref,
    place_ref,
    cand_ref,
    x_ref,
    gain_ref,
    embed_ref,
    table,
    table_v,
    sems,
    small_sems,
    place_sem,
    table_sem,
):
    chunks, _, width = w1_buf.shape
    slots, lanes = table_v.shape
    query_count, token_count, width_in = x_ref.shape
    cand_count = cand_ref.shape[1]
    table_v[...] = jnp.zeros(table_v.shape, jnp.int32)
    clear = pltpu.make_async_copy(table_v, table, table_sem)
    clear.start()
    copies = []
    for c in range(chunks):
        first = pltpu.make_async_copy(w1_ref.at[:, pl.ds(c * width, width)], w1_buf.at[c], sems.at[0, c])
        second = pltpu.make_async_copy(w2_ref.at[pl.ds(c * width, width), :], w2_buf.at[c], sems.at[1, c])
        copies.append((first, second))
    small = [
        pltpu.make_async_copy(source, target, small_sems.at[n])
        for n, (source, target) in enumerate(
            (
                (x_hbm, x_ref),
                (row_hbm, row_ref),
                (cand_hbm, cand_ref),
                (lens_hbm, lens_ref),
                (gain_hbm, gain_ref),
                (embed_hbm, embed_ref),
            )
        )
    ]
    for copy in small[:3]:
        copy.start()
    copies[0][0].start()
    copies[1][0].start()
    copies[0][1].start()
    for c in range(2, chunks):
        copies[c][0].start()
        copies[c - 1][1].start()
    for copy in small[3:]:
        copy.start()
    copies[-1][1].start()
    clear.wait()
    small[1].wait()
    row = row_ref[...]
    owner = jnp.floor((row.astype(F32) + 0.5) * (1.0 / half)).astype(jnp.int32)
    opposite = jnp.bitwise_xor(color(owner), color(me_ref[0]))
    row_ref[...] = jnp.right_shift(owner, 1) * lanes + row - owner * half + opposite * half
    placed = pltpu.make_async_copy(row_ref, place_ref, place_sem)
    placed.start()

    entries = [(i, k) for k in range(cand_count) for i in range(query_count)]
    share = -(-len(entries) // chunks)

    def enter():
        for first in range(0, share, 12):
            batch = entries[first:min(first + 12, share)]
            names = [cand_ref[i, k] for i, k in batch]
            spots = [place_ref[name] for name in names]
            for (i, k), spot in zip(batch, spots):
                table[jnp.right_shift(spot, 7), jnp.bitwise_and(spot, 127)] = i
                spot_ref[i, k] = spot
        del entries[:share]

    small[0].wait()
    x = x_ref[...].reshape(query_count * token_count, width_in)
    total = x.astype(F32)
    inner = active = None
    for step in range(chunks + 2):
        if step < chunks:
            copies[step][0].wait()
        if step == 1:
            small[2].wait()
            placed.wait()
        if step == chunks:
            for copy in small[3:]:
                copy.wait()
        if step >= 2:
            copies[step - 2][1].wait()
        if step >= 1:
            enter()
        later = jnp.dot(x, w1_buf[step], preferred_element_type=F32) if step < chunks else None
        if step >= 2:
            total = total + jnp.dot(active, w2_buf[step - 2], preferred_element_type=F32)
        if 1 <= step <= chunks:
            active = (0.5 * inner * (1.0 + lax.erf(inner * (0.5 ** 0.5)))).astype(BF16)
        inner = later
        if step == chunks:
            fetch = pltpu.make_async_copy(table, table_v, table_sem)
            fetch.start()

    centered = total - jnp.mean(total, axis=-1, keepdims=True)
    variance = jnp.mean(jnp.square(centered), axis=-1, keepdims=True)
    layer_out = (centered * lax.rsqrt(variance + 1e-12) * gain_ref[...].reshape(1, width_in)).astype(BF16)
    embedded = jnp.dot(layer_out, embed_ref[...], preferred_element_type=F32)
    length = jnp.sum(jnp.square(embedded), axis=-1, keepdims=True)
    vectors = embedded * lax.rsqrt(length + 1e-06)
    token = lax.broadcasted_iota(jnp.int32, vectors.shape, 0)
    for i in range(query_count):
        padded = (token >= i * token_count + lens_ref[i]) & (token < (i + 1) * token_count)
        vectors = jnp.where(padded, 0.0, vectors)
    vectors = vectors.astype(BF16)
    tokens = query_count * token_count
    fetch.wait()
    wanted = table_v[...].astype(F32).astype(BF16)
    out_ref[pl.ds(0, tokens), :] = vectors
    out_ref[pl.ds(tokens, slots), :] = wanted


def encode(
    me,
    query_hidden,
    query_lengths,
    inner_weight,
    outer_weight,
    norm_gain,
    embed_weight,
    half,
    passage_row,
    candidates,
    slots,
    color,
):
    query_count, token_count, d = query_hidden.shape
    ff = inner_weight.shape[1]
    e = embed_weight.shape[1]
    slots = -(-slots // 16) * 16
    assert 2 * half <= e == 128
    chunks = 4
    width = ff // chunks
    tokens = query_count * token_count

    def kernel(*refs):
        encode_kernel(half, color, *refs)

    return pl.pallas_call(
        kernel,
        out_shape=(
            jax.ShapeDtypeStruct((tokens + slots, e), BF16),
            jax.ShapeDtypeStruct(candidates.shape, jnp.int32),
        ),
        in_specs=[SMEM] + [ANY] * 8,
        out_specs=(VMEM, SMEM),
        scratch_shapes=[
            pltpu.VMEM((chunks, d, width), BF16),
            pltpu.VMEM((chunks, width, d), BF16),
            pltpu.SMEM(query_lengths.shape, jnp.int32),
            pltpu.VMEM(passage_row.shape, jnp.int32),
            pltpu.SMEM(passage_row.shape, jnp.int32),
            pltpu.SMEM(candidates.shape, jnp.int32),
            pltpu.VMEM(query_hidden.shape, BF16),
            pltpu.VMEM(norm_gain.shape, F32),
            pltpu.VMEM(embed_weight.shape, BF16),
            pltpu.SMEM((slots, e), jnp.int32),
            pltpu.VMEM((slots, e), jnp.int32),
            pltpu.SemaphoreType.DMA((2, chunks)),
            pltpu.SemaphoreType.DMA((6,)),
            pltpu.SemaphoreType.DMA,
            pltpu.SemaphoreType.DMA,
        ],
        compiler_params=pltpu.CompilerParams(vmem_limit_bytes=60 * 2 ** 20),
        cost_estimate=pl.CostEstimate(
            flops=4 * tokens * d * ff, bytes_accessed=4 * d * ff, transcendentals=tokens * ff
        ),
        name="encode",
    )(
        me,
        query_lengths,
        passage_row,
        candidates,
        query_hidden,
        inner_weight,
        outer_weight,
        norm_gain,
        embed_weight,
    )


def mask_kernel(len0_ref, len1_ref, pass0_ref, pass1_ref, _, out0_ref, out1_ref):
    mask_into(out0_ref, pass0_ref, len0_ref, 0, pass0_ref.shape[0])
    mask_into(out1_ref, pass1_ref, len1_ref, 0, pass1_ref.shape[0])


def mask(lengths, passages, late):
    shape = passages[0].shape
    size = 2 * passages[0].size
    return pl.pallas_call(
        mask_kernel,
        out_shape=[jax.ShapeDtypeStruct(shape, BF16)] * 2,
        in_specs=[SMEM, SMEM, VMEM, VMEM, VMEM],
        out_specs=[VMEM, VMEM],
        compiler_params=pltpu.CompilerParams(vmem_limit_bytes=2 ** 22),
        cost_estimate=pl.CostEstimate(flops=8 * size, bytes_accessed=4 * size, transcendentals=0),
        name="mask",
    )(*lengths, *passages, late)


def score_kernel(slots, token_count, me_ref, own_ref, other_ref, *refs):
    got_refs = refs[:slots]
    out_ref, best_ref, index_v, index, sem = refs[slots:]
    message, lanes = got_refs[0].shape
    half = own_ref.shape[0]
    rows = -(-slots // 16) * 16
    tokens = message - rows
    group = min(slots, 256 // token_count)
    unroll = half if slots == group else 8
    chip = jnp.right_shift(me_ref[0], 1)
    mine = lax.broadcasted_iota(jnp.int32, (rows, lanes), 0) == chip
    for s in range(slots):
        table = got_refs[s][pl.ds(tokens, rows), :].astype(F32)
        query = jnp.sum(jnp.where(mine, table, 0.0), axis=0, keepdims=True)
        index_v[s:s + 1, :] = query.astype(jnp.int32) * token_count
    copy = pltpu.make_async_copy(index_v, index, sem)
    copy.start()
    copy.wait()

    for first, pass_ref in ((half, other_ref), (0, own_ref)):

        def several(step, carry):
            for part in range(slots // group):
                rows = []
                for j in range(unroll):
                    p = step * unroll + j
                    picked = jnp.concatenate(
                        [
                            got_refs[s][pl.ds(pl.multiple_of(index[s, first + p], token_count), token_count), :]
                            for s in range(part * group, (part + 1) * group)
                        ],
                        axis=0,
                    )
                    similar = lax.dot_general(pass_ref[p], picked, NT, preferred_element_type=F32)
                    rows.append(jnp.max(similar, axis=0, keepdims=True))
                    if len(rows) == 8:
                        best_ref[
                            pl.ds(pl.multiple_of(first + step * unroll + j - 7, 8), 8),
                            pl.ds(part * group * token_count, group * token_count),
                        ] = jnp.concatenate(rows, axis=0)
                        rows = []
            return carry

        if unroll == half:
            several(0, 0)
        else:
            lax.fori_loop(0, half // unroll, several, 0)
    wide = best_ref.shape[1]
    source = lax.broadcasted_iota(jnp.int32, (slots, wide), 0)
    column = lax.broadcasted_iota(jnp.int32, (slots, wide), 1)
    start = source * token_count
    ones = jnp.where((column >= start) & (column < start + token_count), 1.0, 0.0).astype(BF16)
    total = sum(lax.dot_general(ones, part, NT, preferred_element_type=F32) for part in split3(best_ref[...]))
    out_ref[...] = jnp.zeros(out_ref.shape, F32)
    for s in range(slots):
        out_ref[pl.ds(jnp.bitwise_xor(chip, s), 1), pl.ds(0, 2 * half)] = total[s:s + 1]


def score(me, got, own, other, token_count):
    half, plen, e = own.shape
    passage_count = 2 * half
    slots = len(got)

    def kernel(*refs):
        score_kernel(slots, token_count, *refs)

    return pl.pallas_call(
        kernel,
        out_shape=jax.ShapeDtypeStruct((slots, e), F32),
        in_specs=[SMEM, VMEM, VMEM] + [VMEM] * slots,
        out_specs=VMEM,
        scratch_shapes=[
            pltpu.VMEM((passage_count, slots * token_count), F32),
            pltpu.VMEM((slots, e), jnp.int32),
            pltpu.SMEM((slots, e), jnp.int32),
            pltpu.SemaphoreType.DMA,
        ],
        compiler_params=pltpu.CompilerParams(vmem_limit_bytes=12 * 2 ** 20),
        cost_estimate=pl.CostEstimate(
            flops=2 * passage_count * slots * token_count * plen * e,
            bytes_accessed=4 * own.size,
            transcendentals=0,
        ),
        name="score",
    )(me, own, other, *got)


def finish_kernel(got_ref, spot_ref, scores_ref, best_ref):
    slots, lanes = got_ref.shape
    query_count, cand_count = scores_ref.shape
    parts = split3(got_ref[...])
    slot_iota = lax.broadcasted_iota(jnp.int32, (slots, cand_count), 0) * lanes
    lane_iota = lax.broadcasted_iota(jnp.int32, (lanes, cand_count), 0)
    row_iota = lax.broadcasted_iota(jnp.int32, (cand_count, cand_count), 0)
    col_iota = lax.broadcasted_iota(jnp.int32, (cand_count, cand_count), 1)
    place = lax.broadcasted_iota(jnp.int32, (cand_count, 128), 1)
    for i in range(query_count):
        spot = spot_ref[i:i + 1, :]
        lane = jnp.bitwise_and(spot, lanes - 1)
        onehot = jnp.where(lane_iota == lane, 1.0, 0.0).astype(BF16)
        picked = sum(jnp.dot(part, onehot, preferred_element_type=F32) for part in parts)
        score_row = jnp.sum(jnp.where(slot_iota == spot - lane, picked, 0.0), axis=0, keepdims=True)
        scores_ref[i:i + 1, :] = score_row
        across = jnp.broadcast_to(score_row, (cand_count, cand_count))
        score_col = jnp.sum(jnp.where(row_iota == col_iota, across, 0.0), axis=1, keepdims=True)
        ahead = (across > score_col) | ((across == score_col) & (col_iota < row_iota))
        rank = jnp.sum(jnp.where(ahead, 1.0, 0.0), axis=1, keepdims=True).astype(jnp.int32)
        ordered = jnp.sum(jnp.where(rank == place, score_col, 0.0), axis=0, keepdims=True)
        best_ref[i:i + 1, :] = ordered[:, :TOPN]


def finish(got, spots):
    return pl.pallas_call(
        finish_kernel,
        out_shape=(
            jax.ShapeDtypeStruct(spots.shape, F32),
            jax.ShapeDtypeStruct((spots.shape[0], TOPN), F32),
        ),
        in_specs=[VMEM, VMEM],
        out_specs=(VMEM, VMEM),
        compiler_params=pltpu.CompilerParams(vmem_limit_bytes=2 ** 21),
        name="finish",
    )(got, spots)


def swap(value, distance):
    size = lax.axis_size("shard")
    return lax.ppermute(value, "shard", [(i, i ^ distance) for i in range(size)])


def per_device(
    query_hidden,
    query_lengths,
    inner_weight,
    outer_weight,
    norm_gain,
    embed_weight,
    passage_vectors,
    passage_lengths,
    passage_row,
    candidates,
):
    size = lax.axis_size("shard")
    slots = size // 2
    inner = 1
    while 4 * inner * inner <= slots:
        inner *= 2
    shift = inner.bit_length()

    def color(index):
        return (index ^ (index >> 1) ^ (index >> shift)) & 1

    groups = [[i for i in range(size) if color(i) == c] for c in range(2)]

    def send(value, distance):
        return swap(value, 2 * distance + color(2 * distance))

    me = lax.axis_index("shard").astype(jnp.int32).reshape(1)
    across = swap(passage_lengths, 1)
    message, spots = encode(
        me,
        query_hidden,
        query_lengths,
        inner_weight,
        outer_weight,
        norm_gain,
        embed_weight,
        passage_vectors.shape[0],
        passage_row,
        candidates,
        slots,
        color,
    )
    message, across, raw = lax.optimization_barrier((message, across, passage_vectors))
    raw = swap(raw, 1)

    line = [message] + [send(message, d) for d in range(slots - inner, 0, -inner)][::-1]
    got = [line[s // inner] if s % inner == 0 else send(line[s // inner], s % inner) for s in range(slots)]
    own, other = mask((passage_lengths, across), (passage_vectors, raw), got[inner + 1])
    sums = score(me, got, own, other, query_hidden.shape[1])
    back = lax.all_to_all(sums, "shard", split_axis=0, concat_axis=0, axis_index_groups=groups, tiled=True)
    return finish(back, spots)


def solution(mesh):
    in_specs = (
        P(("groups", "shard"), None, None),
        P(("groups", "shard")),
        P(),
        P(),
        P(),
        P(),
        P(("groups", "shard"), None, None),
        P(("groups", "shard")),
        P("groups"),
        P(("groups", "shard"), None),
    )
    out_specs = (P(("groups", "shard"), None), P(("groups", "shard"), None))
    return jax.shard_map(
        per_device, mesh=mesh, in_specs=in_specs, out_specs=out_specs, check_vma=False
    )
```

```python
import jax
import jax.numpy as jnp
from jax import lax
from jax.experimental import pallas as pl
from jax.experimental.pallas import tpu as pltpu
from jax.sharding import PartitionSpec as P

TOPN = 10
F32 = jnp.float32
BF16 = jnp.bfloat16
NT = (((1,), (1,)), ((), ()))
VMEM = pl.BlockSpec(memory_space=pltpu.VMEM)
SMEM = pl.BlockSpec(memory_space=pltpu.SMEM)
ANY = pl.BlockSpec(memory_space=pl.ANY)


def split3(value):
    high = value.astype(BF16)
    rest = value - high.astype(F32)
    middle = rest.astype(BF16)
    low = (rest - middle.astype(F32)).astype(BF16)
    return high, middle, low


def mask_into(out_ref, pass_ref, len_ref, first, count):
    def mask(p, carry):
        block = pass_ref[p]
        keep = lax.broadcasted_iota(jnp.int32, block.shape, 0) < len_ref[p]
        block = block.astype(F32)
        out_ref[p] = jnp.where(keep, block, jnp.broadcast_to(block[0:1], block.shape)).astype(BF16)
        return carry

    if count <= 8:
        for p in range(first, first + count):
            mask(p, 0)
    else:
        lax.fori_loop(first, first + count, mask, 0, unroll=16)


def encode_kernel(
    half,
    color,
    me_ref,
    lens_hbm,
    row_hbm,
    cand_hbm,
    x_hbm,
    w1_ref,
    w2_ref,
    gain_hbm,
    embed_hbm,
    out_ref,
    spot_ref,
    w1_buf,
    w2_buf,
    lens_ref,
    row_ref,
    place_ref,
    cand_ref,
    x_ref,
    gain_ref,
    embed_ref,
    table,
    table_v,
    sems,
    small_sems,
    place_sem,
    table_sem,
):
    chunks, _, width = w1_buf.shape
    slots, lanes = table_v.shape
    query_count, token_count, width_in = x_ref.shape
    cand_count = cand_ref.shape[1]
    table_v[...] = jnp.zeros(table_v.shape, jnp.int32)
    clear = pltpu.make_async_copy(table_v, table, table_sem)
    clear.start()
    copies = []
    for c in range(chunks):
        first = pltpu.make_async_copy(w1_ref.at[:, pl.ds(c * width, width)], w1_buf.at[c], sems.at[0, c])
        second = pltpu.make_async_copy(w2_ref.at[pl.ds(c * width, width), :], w2_buf.at[c], sems.at[1, c])
        copies.append((first, second))
    small = [
        pltpu.make_async_copy(source, target, small_sems.at[n])
        for n, (source, target) in enumerate(
            (
                (x_hbm, x_ref),
                (row_hbm, row_ref),
                (cand_hbm, cand_ref),
                (lens_hbm, lens_ref),
                (gain_hbm, gain_ref),
                (embed_hbm, embed_ref),
            )
        )
    ]
    for copy in small[:3]:
        copy.start()
    copies[0][0].start()
    copies[1][0].start()
    copies[0][1].start()
    for c in range(2, chunks):
        copies[c][0].start()
        copies[c - 1][1].start()
    for copy in small[3:]:
        copy.start()
    copies[-1][1].start()
    clear.wait()
    small[1].wait()
    row = row_ref[...]
    owner = jnp.floor((row.astype(F32) + 0.5) * (1.0 / half)).astype(jnp.int32)
    opposite = jnp.bitwise_xor(color(owner), color(me_ref[0]))
    row_ref[...] = jnp.right_shift(owner, 1) * lanes + row - owner * half + opposite * half
    placed = pltpu.make_async_copy(row_ref, place_ref, place_sem)
    placed.start()

    entries = [(i, k) for k in range(cand_count) for i in range(query_count)]
    share = -(-len(entries) // chunks)

    def enter():
        for first in range(0, share, 12):
            batch = entries[first:min(first + 12, share)]
            names = [cand_ref[i, k] for i, k in batch]
            spots = [place_ref[name] for name in names]
            for (i, k), spot in zip(batch, spots):
                table[jnp.right_shift(spot, 7), jnp.bitwise_and(spot, 127)] = i
                spot_ref[i, k] = spot
        del entries[:share]

    small[0].wait()
    x = x_ref[...].reshape(query_count * token_count, width_in)
    total = x.astype(F32)
    inner = active = None
    for step in range(chunks + 2):
        if step < chunks:
            copies[step][0].wait()
        if step == 1:
            small[2].wait()
            placed.wait()
        if step == chunks:
            for copy in small[3:]:
                copy.wait()
        if step >= 2:
            copies[step - 2][1].wait()
        if step >= 1:
            enter()
        later = jnp.dot(x, w1_buf[step], preferred_element_type=F32) if step < chunks else None
        if step >= 2:
            total = total + jnp.dot(active, w2_buf[step - 2], preferred_element_type=F32)
        if 1 <= step <= chunks:
            active = (0.5 * inner * (1.0 + lax.erf(inner * (0.5 ** 0.5)))).astype(BF16)
        inner = later
        if step == chunks:
            fetch = pltpu.make_async_copy(table, table_v, table_sem)
            fetch.start()

    centered = total - jnp.mean(total, axis=-1, keepdims=True)
    variance = jnp.mean(jnp.square(centered), axis=-1, keepdims=True)
    layer_out = (centered * lax.rsqrt(variance + 1e-12) * gain_ref[...].reshape(1, width_in)).astype(BF16)
    embedded = jnp.dot(layer_out, embed_ref[...], preferred_element_type=F32)
    length = jnp.sum(jnp.square(embedded), axis=-1, keepdims=True)
    vectors = embedded * lax.rsqrt(length + 1e-06)
    token = lax.broadcasted_iota(jnp.int32, vectors.shape, 0)
    for i in range(query_count):
        padded = (token >= i * token_count + lens_ref[i]) & (token < (i + 1) * token_count)
        vectors = jnp.where(padded, 0.0, vectors)
    vectors = vectors.astype(BF16)
    tokens = query_count * token_count
    fetch.wait()
    wanted = table_v[...].astype(F32).astype(BF16)
    out_ref[pl.ds(0, tokens), :] = vectors
    out_ref[pl.ds(tokens, slots), :] = wanted


def encode(
    me,
    query_hidden,
    query_lengths,
    inner_weight,
    outer_weight,
    norm_gain,
    embed_weight,
    half,
    passage_row,
    candidates,
    slots,
    color,
):
    query_count, token_count, d = query_hidden.shape
    ff = inner_weight.shape[1]
    e = embed_weight.shape[1]
    slots = -(-slots // 16) * 16
    assert 2 * half <= e == 128
    chunks = 4
    width = ff // chunks
    tokens = query_count * token_count

    def kernel(*refs):
        encode_kernel(half, color, *refs)

    return pl.pallas_call(
        kernel,
        out_shape=(
            jax.ShapeDtypeStruct((tokens + slots, e), BF16),
            jax.ShapeDtypeStruct(candidates.shape, jnp.int32),
        ),
        in_specs=[SMEM] + [ANY] * 8,
        out_specs=(VMEM, SMEM),
        scratch_shapes=[
            pltpu.VMEM((chunks, d, width), BF16),
            pltpu.VMEM((chunks, width, d), BF16),
            pltpu.SMEM(query_lengths.shape, jnp.int32),
            pltpu.VMEM(passage_row.shape, jnp.int32),
            pltpu.SMEM(passage_row.shape, jnp.int32),
            pltpu.SMEM(candidates.shape, jnp.int32),
            pltpu.VMEM(query_hidden.shape, BF16),
            pltpu.VMEM(norm_gain.shape, F32),
            pltpu.VMEM(embed_weight.shape, BF16),
            pltpu.SMEM((slots, e), jnp.int32),
            pltpu.VMEM((slots, e), jnp.int32),
            pltpu.SemaphoreType.DMA((2, chunks)),
            pltpu.SemaphoreType.DMA((6,)),
            pltpu.SemaphoreType.DMA,
            pltpu.SemaphoreType.DMA,
        ],
        compiler_params=pltpu.CompilerParams(vmem_limit_bytes=60 * 2 ** 20),
        cost_estimate=pl.CostEstimate(
            flops=4 * tokens * d * ff, bytes_accessed=4 * d * ff, transcendentals=tokens * ff
        ),
        name="encode",
    )(
        me,
        query_lengths,
        passage_row,
        candidates,
        query_hidden,
        inner_weight,
        outer_weight,
        norm_gain,
        embed_weight,
    )


def mask_kernel(len0_ref, len1_ref, pass0_ref, pass1_ref, _, out0_ref, out1_ref):
    mask_into(out0_ref, pass0_ref, len0_ref, 0, pass0_ref.shape[0])
    mask_into(out1_ref, pass1_ref, len1_ref, 0, pass1_ref.shape[0])


def mask(lengths, passages, late):
    shape = passages[0].shape
    size = 2 * passages[0].size
    return pl.pallas_call(
        mask_kernel,
        out_shape=[jax.ShapeDtypeStruct(shape, BF16)] * 2,
        in_specs=[SMEM, SMEM, VMEM, VMEM, VMEM],
        out_specs=[VMEM, VMEM],
        compiler_params=pltpu.CompilerParams(vmem_limit_bytes=2 ** 22),
        cost_estimate=pl.CostEstimate(flops=8 * size, bytes_accessed=4 * size, transcendentals=0),
        name="mask",
    )(*lengths, *passages, late)


def score_kernel(slots, token_count, me_ref, own_ref, other_ref, *refs):
    got_refs = refs[:slots]
    out_ref, best_ref, index_v, index, sem = refs[slots:]
    message, lanes = got_refs[0].shape
    half = own_ref.shape[0]
    rows = -(-slots // 16) * 16
    tokens = message - rows
    group = min(slots, 256 // token_count)
    unroll = half if slots == group else 8
    chip = jnp.right_shift(me_ref[0], 1)
    mine = lax.broadcasted_iota(jnp.int32, (rows, lanes), 0) == chip
    for s in range(slots):
        table = got_refs[s][pl.ds(tokens, rows), :].astype(F32)
        query = jnp.sum(jnp.where(mine, table, 0.0), axis=0, keepdims=True)
        index_v[s:s + 1, :] = query.astype(jnp.int32) * token_count
    copy = pltpu.make_async_copy(index_v, index, sem)
    copy.start()
    copy.wait()

    for first, pass_ref in ((half, other_ref), (0, own_ref)):

        def several(step, carry):
            for part in range(slots // group):
                rows = []
                for j in range(unroll):
                    p = step * unroll + j
                    picked = jnp.concatenate(
                        [
                            got_refs[s][pl.ds(pl.multiple_of(index[s, first + p], token_count), token_count), :]
                            for s in range(part * group, (part + 1) * group)
                        ],
                        axis=0,
                    )
                    similar = lax.dot_general(pass_ref[p], picked, NT, preferred_element_type=F32)
                    rows.append(jnp.max(similar, axis=0, keepdims=True))
                    if len(rows) == 8:
                        best_ref[
                            pl.ds(pl.multiple_of(first + step * unroll + j - 7, 8), 8),
                            pl.ds(part * group * token_count, group * token_count),
                        ] = jnp.concatenate(rows, axis=0)
                        rows = []
            return carry

        if unroll == half:
            several(0, 0)
        else:
            lax.fori_loop(0, half // unroll, several, 0)
    wide = best_ref.shape[1]
    source = lax.broadcasted_iota(jnp.int32, (slots, wide), 0)
    column = lax.broadcasted_iota(jnp.int32, (slots, wide), 1)
    start = source * token_count
    ones = jnp.where((column >= start) & (column < start + token_count), 1.0, 0.0).astype(BF16)
    total = sum(lax.dot_general(ones, part, NT, preferred_element_type=F32) for part in split3(best_ref[...]))
    out_ref[...] = jnp.zeros(out_ref.shape, F32)
    for s in range(slots):
        out_ref[pl.ds(jnp.bitwise_xor(chip, s), 1), pl.ds(0, 2 * half)] = total[s:s + 1]


def score(me, got, own, other, token_count):
    half, plen, e = own.shape
    passage_count = 2 * half
    slots = len(got)

    def kernel(*refs):
        score_kernel(slots, token_count, *refs)

    return pl.pallas_call(
        kernel,
        out_shape=jax.ShapeDtypeStruct((slots, e), F32),
        in_specs=[SMEM, VMEM, VMEM] + [VMEM] * slots,
        out_specs=VMEM,
        scratch_shapes=[
            pltpu.VMEM((passage_count, slots * token_count), F32),
            pltpu.VMEM((slots, e), jnp.int32),
            pltpu.SMEM((slots, e), jnp.int32),
            pltpu.SemaphoreType.DMA,
        ],
        compiler_params=pltpu.CompilerParams(vmem_limit_bytes=12 * 2 ** 20),
        cost_estimate=pl.CostEstimate(
            flops=2 * passage_count * slots * token_count * plen * e,
            bytes_accessed=4 * own.size,
            transcendentals=0,
        ),
        name="score",
    )(me, own, other, *got)


def finish_kernel(got_ref, spot_ref, scores_ref, best_ref):
    slots, lanes = got_ref.shape
    query_count, cand_count = scores_ref.shape
    parts = jnp.concatenate([part.astype(F32) for part in split3(got_ref[...])], axis=0).astype(BF16)
    spots = jnp.concatenate([spot_ref[i:i + 1, :] for i in range(query_count)], axis=1)
    entry_count = query_count * cand_count
    lane = jnp.bitwise_and(spots, lanes - 1)
    lane_iota = lax.broadcasted_iota(jnp.int32, (lanes, entry_count), 0)
    slot_iota = lax.broadcasted_iota(jnp.int32, (slots, entry_count), 0) * lanes
    onehot = jnp.where(lane_iota == lane, 1.0, 0.0).astype(BF16)
    picked = jnp.dot(parts, onehot, preferred_element_type=F32)
    picked = picked[:slots] + picked[slots:2 * slots] + picked[2 * slots:]
    picked = jnp.sum(jnp.where(slot_iota == spots - lane, picked, 0.0), axis=0, keepdims=True)
    row_iota = lax.broadcasted_iota(jnp.int32, (cand_count, cand_count), 0)
    col_iota = lax.broadcasted_iota(jnp.int32, (cand_count, cand_count), 1)
    place = lax.broadcasted_iota(jnp.int32, (cand_count, 128), 1)
    for i in range(query_count):
        score_row = picked[:, i * cand_count:(i + 1) * cand_count]
        scores_ref[i:i + 1, :] = score_row
        across = jnp.broadcast_to(score_row, (cand_count, cand_count))
        score_col = jnp.sum(jnp.where(row_iota == col_iota, across, 0.0), axis=1, keepdims=True)
        ahead = (across > score_col) | ((across == score_col) & (col_iota < row_iota))
        rank = jnp.sum(jnp.where(ahead, 1.0, 0.0), axis=1, keepdims=True).astype(jnp.int32)
        ordered = jnp.sum(jnp.where(rank == place, score_col, 0.0), axis=0, keepdims=True)
        best_ref[i:i + 1, :] = ordered[:, :TOPN]


def finish(got, spots):
    return pl.pallas_call(
        finish_kernel,
        out_shape=(
            jax.ShapeDtypeStruct(spots.shape, F32),
            jax.ShapeDtypeStruct((spots.shape[0], TOPN), F32),
        ),
        in_specs=[VMEM, VMEM],
        out_specs=(VMEM, VMEM),
        compiler_params=pltpu.CompilerParams(vmem_limit_bytes=2 ** 21),
        name="finish",
    )(got, spots)


def swap(value, distance):
    size = lax.axis_size("shard")
    return lax.ppermute(value, "shard", [(i, i ^ distance) for i in range(size)])


def per_device(
    query_hidden,
    query_lengths,
    inner_weight,
    outer_weight,
    norm_gain,
    embed_weight,
    passage_vectors,
    passage_lengths,
    passage_row,
    candidates,
):
    size = lax.axis_size("shard")
    slots = size // 2
    inner = 1
    while 4 * inner * inner <= slots:
        inner *= 2
    shift = inner.bit_length()

    def color(index):
        return (index ^ (index >> 1) ^ (index >> shift)) & 1

    groups = [[i for i in range(size) if color(i) == c] for c in range(2)]

    def send(value, distance):
        return swap(value, 2 * distance + color(2 * distance))

    me = lax.axis_index("shard").astype(jnp.int32).reshape(1)
    across = swap(passage_lengths, 1)
    message, spots = encode(
        me,
        query_hidden,
        query_lengths,
        inner_weight,
        outer_weight,
        norm_gain,
        embed_weight,
        passage_vectors.shape[0],
        passage_row,
        candidates,
        slots,
        color,
    )
    message, across, raw = lax.optimization_barrier((message, across, passage_vectors))
    raw = swap(raw, 1)

    line = [message] + [send(message, d) for d in range(slots - inner, 0, -inner)][::-1]
    got = [line[s // inner] if s % inner == 0 else send(line[s // inner], s % inner) for s in range(slots)]
    own, other = mask((passage_lengths, across), (passage_vectors, raw), got[inner + 1])
    sums = score(me, got, own, other, query_hidden.shape[1])
    back = lax.all_to_all(sums, "shard", split_axis=0, concat_axis=0, axis_index_groups=groups, tiled=True)
    return finish(back, spots)


def solution(mesh):
    in_specs = (
        P(("groups", "shard"), None, None),
        P(("groups", "shard")),
        P(),
        P(),
        P(),
        P(),
        P(("groups", "shard"), None, None),
        P(("groups", "shard")),
        P("groups"),
        P(("groups", "shard"), None),
    )
    out_specs = (P(("groups", "shard"), None), P(("groups", "shard"), None))
    return jax.shard_map(
        per_device, mesh=mesh, in_specs=in_specs, out_specs=out_specs, check_vma=False
    )
```

```python
import jax
import jax.numpy as jnp
from jax import lax
from jax.experimental import pallas as pl
from jax.experimental.pallas import tpu as pltpu
from jax.sharding import PartitionSpec as P

TOPN = 10
F32 = jnp.float32
BF16 = jnp.bfloat16
NT = (((1,), (1,)), ((), ()))
VMEM = pl.BlockSpec(memory_space=pltpu.VMEM)
SMEM = pl.BlockSpec(memory_space=pltpu.SMEM)
ANY = pl.BlockSpec(memory_space=pl.ANY)


def split3(value):
    high = value.astype(BF16)
    rest = value - high.astype(F32)
    middle = rest.astype(BF16)
    low = (rest - middle.astype(F32)).astype(BF16)
    return high, middle, low


def mask_into(out_ref, pass_ref, len_ref, first, count):
    def mask(p, carry):
        block = pass_ref[p]
        keep = lax.broadcasted_iota(jnp.int32, block.shape, 0) < len_ref[p]
        block = block.astype(F32)
        out_ref[p] = jnp.where(keep, block, jnp.broadcast_to(block[0:1], block.shape)).astype(BF16)
        return carry

    if count <= 8:
        for p in range(first, first + count):
            mask(p, 0)
    else:
        lax.fori_loop(first, first + count, mask, 0, unroll=16)


def encode_kernel(
    half,
    color,
    me_ref,
    lens_hbm,
    row_hbm,
    cand_hbm,
    x_hbm,
    w1_ref,
    w2_ref,
    gain_hbm,
    embed_hbm,
    out_ref,
    spot_ref,
    w1_buf,
    w2_buf,
    lens_ref,
    row_ref,
    place_ref,
    cand_ref,
    x_ref,
    gain_ref,
    embed_ref,
    table,
    table_v,
    sems,
    small_sems,
    place_sem,
    table_sem,
):
    chunks, _, width = w1_buf.shape
    slots, lanes = table_v.shape
    query_count, token_count, width_in = x_ref.shape
    cand_count = cand_ref.shape[1]
    table_v[...] = jnp.zeros(table_v.shape, jnp.int32)
    clear = pltpu.make_async_copy(table_v, table, table_sem)
    clear.start()
    copies = []
    for c in range(chunks):
        first = pltpu.make_async_copy(w1_ref.at[:, pl.ds(c * width, width)], w1_buf.at[c], sems.at[0, c])
        second = pltpu.make_async_copy(w2_ref.at[pl.ds(c * width, width), :], w2_buf.at[c], sems.at[1, c])
        copies.append((first, second))
    small = [
        pltpu.make_async_copy(source, target, small_sems.at[n])
        for n, (source, target) in enumerate(
            (
                (x_hbm, x_ref),
                (row_hbm, row_ref),
                (cand_hbm, cand_ref),
                (lens_hbm, lens_ref),
                (gain_hbm, gain_ref),
                (embed_hbm, embed_ref),
            )
        )
    ]
    for copy in small[:3]:
        copy.start()
    copies[0][0].start()
    copies[1][0].start()
    copies[0][1].start()
    for c in range(2, chunks):
        copies[c][0].start()
        copies[c - 1][1].start()
    for copy in small[3:]:
        copy.start()
    copies[-1][1].start()
    clear.wait()
    small[1].wait()
    row = row_ref[...]
    owner = jnp.floor((row.astype(F32) + 0.5) * (1.0 / half)).astype(jnp.int32)
    opposite = jnp.bitwise_xor(color(owner), color(me_ref[0]))
    row_ref[...] = jnp.right_shift(owner, 1) * lanes + row - owner * half + opposite * half
    placed = pltpu.make_async_copy(row_ref, place_ref, place_sem)
    placed.start()

    entries = [(i, k) for k in range(cand_count) for i in range(query_count)]
    share = -(-len(entries) // chunks)

    def enter():
        for first in range(0, share, 12):
            batch = entries[first:min(first + 12, share)]
            names = [cand_ref[i, k] for i, k in batch]
            spots = [place_ref[name] for name in names]
            for (i, k), spot in zip(batch, spots):
                table[jnp.right_shift(spot, 7), jnp.bitwise_and(spot, 127)] = i
                spot_ref[i, k] = spot
        del entries[:share]

    small[0].wait()
    x = x_ref[...].reshape(query_count * token_count, width_in)
    total = x.astype(F32)
    inner = active = None
    for step in range(chunks + 2):
        if step < chunks:
            copies[step][0].wait()
        if step == 1:
            small[2].wait()
            placed.wait()
        if step == chunks:
            for copy in small[3:]:
                copy.wait()
        if step >= 2:
            copies[step - 2][1].wait()
        if step >= 1:
            enter()
        later = jnp.dot(x, w1_buf[step], preferred_element_type=F32) if step < chunks else None
        if step >= 2:
            total = total + jnp.dot(active, w2_buf[step - 2], preferred_element_type=F32)
        if 1 <= step <= chunks:
            active = (0.5 * inner * (1.0 + lax.erf(inner * (0.5 ** 0.5)))).astype(BF16)
        inner = later
        if step == chunks:
            fetch = pltpu.make_async_copy(table, table_v, table_sem)
            fetch.start()

    centered = total - jnp.mean(total, axis=-1, keepdims=True)
    variance = jnp.mean(jnp.square(centered), axis=-1, keepdims=True)
    layer_out = (centered * lax.rsqrt(variance + 1e-12) * gain_ref[...].reshape(1, width_in)).astype(BF16)
    embedded = jnp.dot(layer_out, embed_ref[...], preferred_element_type=F32)
    length = jnp.sum(jnp.square(embedded), axis=-1, keepdims=True)
    vectors = embedded * lax.rsqrt(length + 1e-06)
    token = lax.broadcasted_iota(jnp.int32, vectors.shape, 0)
    for i in range(query_count):
        padded = (token >= i * token_count + lens_ref[i]) & (token < (i + 1) * token_count)
        vectors = jnp.where(padded, 0.0, vectors)
    vectors = vectors.astype(BF16)
    tokens = query_count * token_count
    fetch.wait()
    wanted = table_v[...].astype(F32).astype(BF16)
    out_ref[pl.ds(0, tokens), :] = vectors
    out_ref[pl.ds(tokens, slots), :] = wanted


def encode(
    me,
    query_hidden,
    query_lengths,
    inner_weight,
    outer_weight,
    norm_gain,
    embed_weight,
    half,
    passage_row,
    candidates,
    slots,
    color,
):
    query_count, token_count, d = query_hidden.shape
    ff = inner_weight.shape[1]
    e = embed_weight.shape[1]
    slots = -(-slots // 16) * 16
    assert 2 * half <= e == 128
    chunks = 4
    width = ff // chunks
    tokens = query_count * token_count

    def kernel(*refs):
        encode_kernel(half, color, *refs)

    return pl.pallas_call(
        kernel,
        out_shape=(
            jax.ShapeDtypeStruct((tokens + slots, e), BF16),
            jax.ShapeDtypeStruct(candidates.shape, jnp.int32),
        ),
        in_specs=[SMEM] + [ANY] * 8,
        out_specs=(VMEM, SMEM),
        scratch_shapes=[
            pltpu.VMEM((chunks, d, width), BF16),
            pltpu.VMEM((chunks, width, d), BF16),
            pltpu.SMEM(query_lengths.shape, jnp.int32),
            pltpu.VMEM(passage_row.shape, jnp.int32),
            pltpu.SMEM(passage_row.shape, jnp.int32),
            pltpu.SMEM(candidates.shape, jnp.int32),
            pltpu.VMEM(query_hidden.shape, BF16),
            pltpu.VMEM(norm_gain.shape, F32),
            pltpu.VMEM(embed_weight.shape, BF16),
            pltpu.SMEM((slots, e), jnp.int32),
            pltpu.VMEM((slots, e), jnp.int32),
            pltpu.SemaphoreType.DMA((2, chunks)),
            pltpu.SemaphoreType.DMA((6,)),
            pltpu.SemaphoreType.DMA,
            pltpu.SemaphoreType.DMA,
        ],
        compiler_params=pltpu.CompilerParams(vmem_limit_bytes=60 * 2 ** 20),
        cost_estimate=pl.CostEstimate(
            flops=4 * tokens * d * ff, bytes_accessed=4 * d * ff, transcendentals=tokens * ff
        ),
        name="encode",
    )(
        me,
        query_lengths,
        passage_row,
        candidates,
        query_hidden,
        inner_weight,
        outer_weight,
        norm_gain,
        embed_weight,
    )


def mask_kernel(len0_ref, len1_ref, pass0_ref, pass1_ref, _, out0_ref, out1_ref):
    mask_into(out0_ref, pass0_ref, len0_ref, 0, pass0_ref.shape[0])
    mask_into(out1_ref, pass1_ref, len1_ref, 0, pass1_ref.shape[0])


def mask(lengths, passages, late):
    shape = passages[0].shape
    size = 2 * passages[0].size
    return pl.pallas_call(
        mask_kernel,
        out_shape=[jax.ShapeDtypeStruct(shape, BF16)] * 2,
        in_specs=[SMEM, SMEM, VMEM, VMEM, VMEM],
        out_specs=[VMEM, VMEM],
        compiler_params=pltpu.CompilerParams(vmem_limit_bytes=2 ** 22),
        cost_estimate=pl.CostEstimate(flops=8 * size, bytes_accessed=4 * size, transcendentals=0),
        name="mask",
    )(*lengths, *passages, late)


def score_kernel(slots, middle, token_count, me_ref, own_ref, other_ref, *refs):
    got_refs = refs[:slots]
    out_ref, best_ref, index_v, index, sem = refs[slots:]
    message, lanes = got_refs[0].shape
    half = own_ref.shape[0]
    rows = -(-slots // 16) * 16
    tokens = message - rows
    group = min(slots, 256 // token_count)
    unroll = half if slots == group else 8
    chip = jnp.right_shift(me_ref[0], 1)
    mine = lax.broadcasted_iota(jnp.int32, (rows, lanes), 0) == chip
    for s in range(slots):
        table = got_refs[s][pl.ds(tokens, rows), :].astype(F32)
        query = jnp.sum(jnp.where(mine, table, 0.0), axis=0, keepdims=True)
        index_v[s:s + 1, :] = query.astype(jnp.int32) * token_count
    copy = pltpu.make_async_copy(index_v, index, sem)
    copy.start()
    copy.wait()

    for first, pass_ref in ((half, other_ref), (0, own_ref)):

        def several(step, carry):
            for part in range(slots // group):
                rows = []
                for j in range(unroll):
                    p = step * unroll + j
                    picked = jnp.concatenate(
                        [
                            got_refs[s][pl.ds(pl.multiple_of(index[s, first + p], token_count), token_count), :]
                            for s in range(part * group, (part + 1) * group)
                        ],
                        axis=0,
                    )
                    similar = lax.dot_general(pass_ref[p], picked, NT, preferred_element_type=F32)
                    rows.append(jnp.max(similar, axis=0, keepdims=True))
                    if len(rows) == 8:
                        best_ref[
                            pl.ds(pl.multiple_of(first + step * unroll + j - 7, 8), 8),
                            pl.ds(part * group * token_count, group * token_count),
                        ] = jnp.concatenate(rows, axis=0)
                        rows = []
            return carry

        if unroll == half:
            several(0, 0)
        else:
            lax.fori_loop(0, half // unroll, several, 0)
    wide = best_ref.shape[1]
    source = lax.broadcasted_iota(jnp.int32, (slots, wide), 0)
    column = lax.broadcasted_iota(jnp.int32, (slots, wide), 1)
    start = source * token_count
    ones = jnp.where((column >= start) & (column < start + token_count), 1.0, 0.0).astype(BF16)
    total = sum(lax.dot_general(ones, part, NT, preferred_element_type=F32) for part in split3(best_ref[...]))
    out_ref[...] = jnp.zeros(out_ref.shape, F32)
    for s in range(slots):
        out_ref[pl.ds(jnp.bitwise_xor(chip, s ^ middle), 1), pl.ds(0, 2 * half)] = total[s:s + 1]


def score(me, got, own, other, middle, token_count):
    half, plen, e = own.shape
    passage_count = 2 * half
    slots = len(got)

    def kernel(*refs):
        score_kernel(slots, middle, token_count, *refs)

    return pl.pallas_call(
        kernel,
        out_shape=jax.ShapeDtypeStruct((slots, e), F32),
        in_specs=[SMEM, VMEM, VMEM] + [VMEM] * slots,
        out_specs=VMEM,
        scratch_shapes=[
            pltpu.VMEM((passage_count, slots * token_count), F32),
            pltpu.VMEM((slots, e), jnp.int32),
            pltpu.SMEM((slots, e), jnp.int32),
            pltpu.SemaphoreType.DMA,
        ],
        compiler_params=pltpu.CompilerParams(vmem_limit_bytes=12 * 2 ** 20),
        cost_estimate=pl.CostEstimate(
            flops=2 * passage_count * slots * token_count * plen * e,
            bytes_accessed=4 * own.size,
            transcendentals=0,
        ),
        name="score",
    )(me, own, other, *got)


def finish_kernel(middle, got_ref, spot_ref, scores_ref, best_ref):
    slots, lanes = got_ref.shape
    query_count, cand_count = scores_ref.shape
    parts = split3(got_ref[...])
    slot_iota = lax.broadcasted_iota(jnp.int32, (slots, cand_count), 0) * lanes
    lane_iota = lax.broadcasted_iota(jnp.int32, (lanes, cand_count), 0)
    row_iota = lax.broadcasted_iota(jnp.int32, (cand_count, cand_count), 0)
    col_iota = lax.broadcasted_iota(jnp.int32, (cand_count, cand_count), 1)
    place = lax.broadcasted_iota(jnp.int32, (cand_count, 128), 1)
    for i in range(query_count):
        spot = jnp.bitwise_xor(spot_ref[i:i + 1, :], middle * lanes)
        lane = jnp.bitwise_and(spot, lanes - 1)
        onehot = jnp.where(lane_iota == lane, 1.0, 0.0).astype(BF16)
        picked = sum(jnp.dot(part, onehot, preferred_element_type=F32) for part in parts)
        score_row = jnp.sum(jnp.where(slot_iota == spot - lane, picked, 0.0), axis=0, keepdims=True)
        scores_ref[i:i + 1, :] = score_row
        across = jnp.broadcast_to(score_row, (cand_count, cand_count))
        score_col = jnp.sum(jnp.where(row_iota == col_iota, across, 0.0), axis=1, keepdims=True)
        ahead = (across > score_col) | ((across == score_col) & (col_iota < row_iota))
        rank = jnp.sum(jnp.where(ahead, 1.0, 0.0), axis=1, keepdims=True).astype(jnp.int32)
        ordered = jnp.sum(jnp.where(rank == place, score_col, 0.0), axis=0, keepdims=True)
        best_ref[i:i + 1, :] = ordered[:, :TOPN]


def finish(got, spots, middle):
    def kernel(*refs):
        finish_kernel(middle, *refs)

    return pl.pallas_call(
        kernel,
        out_shape=(
            jax.ShapeDtypeStruct(spots.shape, F32),
            jax.ShapeDtypeStruct((spots.shape[0], TOPN), F32),
        ),
        in_specs=[VMEM, VMEM],
        out_specs=(VMEM, VMEM),
        compiler_params=pltpu.CompilerParams(vmem_limit_bytes=2 ** 21),
        name="finish",
    )(got, spots)


def swap(value, distance):
    size = lax.axis_size("shard")
    return lax.ppermute(value, "shard", [(i, i ^ distance) for i in range(size)])


def per_device(
    query_hidden,
    query_lengths,
    inner_weight,
    outer_weight,
    norm_gain,
    embed_weight,
    passage_vectors,
    passage_lengths,
    passage_row,
    candidates,
):
    size = lax.axis_size("shard")
    slots = size // 2
    inner = 1
    while 4 * inner * inner <= slots:
        inner *= 2
    shift = inner.bit_length()

    def color(index):
        return (index ^ (index >> 1) ^ (index >> shift)) & 1

    middle = inner * (slots // inner // 2 - 1)
    groups = [[2 * (p ^ middle) + (c ^ color(2 * (p ^ middle))) for p in range(slots)] for c in range(2)]

    def send(value, distance):
        return swap(value, 2 * distance + color(2 * distance))

    me = lax.axis_index("shard").astype(jnp.int32).reshape(1)
    across = swap(passage_lengths, 1)
    message, spots = encode(
        me,
        query_hidden,
        query_lengths,
        inner_weight,
        outer_weight,
        norm_gain,
        embed_weight,
        passage_vectors.shape[0],
        passage_row,
        candidates,
        slots,
        color,
    )
    message, across, raw = lax.optimization_barrier((message, across, passage_vectors))
    raw = swap(raw, 1)

    line = [message] + [send(message, d) for d in range(slots - inner, 0, -inner)][::-1]
    got = [line[s // inner] if s % inner == 0 else send(line[s // inner], s % inner) for s in range(slots)]
    own, other = mask((passage_lengths, across), (passage_vectors, raw), got[inner + 1])
    sums = score(me, got, own, other, middle, query_hidden.shape[1])
    back = lax.all_to_all(sums, "shard", split_axis=0, concat_axis=0, axis_index_groups=groups, tiled=True)
    return finish(back, spots, middle)


def solution(mesh):
    in_specs = (
        P(("groups", "shard"), None, None),
        P(("groups", "shard")),
        P(),
        P(),
        P(),
        P(),
        P(("groups", "shard"), None, None),
        P(("groups", "shard")),
        P("groups"),
        P(("groups", "shard"), None),
    )
    out_specs = (P(("groups", "shard"), None), P(("groups", "shard"), None))
    return jax.shard_map(
        per_device, mesh=mesh, in_specs=in_specs, out_specs=out_specs, check_vma=False
    )
```

```python
import jax
import jax.numpy as jnp
from jax import lax
from jax.experimental import pallas as pl
from jax.experimental.pallas import tpu as pltpu
from jax.sharding import PartitionSpec as P

TOPN = 10
F32 = jnp.float32
BF16 = jnp.bfloat16
NT = (((1,), (1,)), ((), ()))
VMEM = pl.BlockSpec(memory_space=pltpu.VMEM)
SMEM = pl.BlockSpec(memory_space=pltpu.SMEM)
ANY = pl.BlockSpec(memory_space=pl.ANY)


def split3(value):
    high = value.astype(BF16)
    rest = value - high.astype(F32)
    leader = rest.astype(BF16)
    low = (rest - leader.astype(F32)).astype(BF16)
    return high, leader, low


def mask_into(out_ref, pass_ref, len_ref, first, count):
    def mask(p, carry):
        block = pass_ref[p]
        keep = lax.broadcasted_iota(jnp.int32, block.shape, 0) < len_ref[p]
        block = block.astype(F32)
        out_ref[p] = jnp.where(keep, block, jnp.broadcast_to(block[0:1], block.shape)).astype(BF16)
        return carry

    if count <= 8:
        for p in range(first, first + count):
            mask(p, 0)
    else:
        lax.fori_loop(first, first + count, mask, 0, unroll=16)


def encode_kernel(
    half,
    color,
    me_ref,
    lens_hbm,
    row_hbm,
    cand_hbm,
    x_hbm,
    w1_ref,
    w2_ref,
    gain_hbm,
    embed_hbm,
    out_ref,
    spot_ref,
    w1_buf,
    w2_buf,
    lens_ref,
    row_ref,
    place_ref,
    cand_ref,
    x_ref,
    gain_ref,
    embed_ref,
    table,
    table_v,
    sems,
    small_sems,
    place_sem,
    table_sem,
):
    chunks, _, width = w1_buf.shape
    slots, lanes = table_v.shape
    query_count, token_count, width_in = x_ref.shape
    cand_count = cand_ref.shape[1]
    table_v[...] = jnp.zeros(table_v.shape, jnp.int32)
    clear = pltpu.make_async_copy(table_v, table, table_sem)
    clear.start()
    copies = []
    for c in range(chunks):
        first = pltpu.make_async_copy(w1_ref.at[:, pl.ds(c * width, width)], w1_buf.at[c], sems.at[0, c])
        second = pltpu.make_async_copy(w2_ref.at[pl.ds(c * width, width), :], w2_buf.at[c], sems.at[1, c])
        copies.append((first, second))
    small = [
        pltpu.make_async_copy(source, target, small_sems.at[n])
        for n, (source, target) in enumerate(
            (
                (x_hbm, x_ref),
                (row_hbm, row_ref),
                (cand_hbm, cand_ref),
                (lens_hbm, lens_ref),
                (gain_hbm, gain_ref),
                (embed_hbm, embed_ref),
            )
        )
    ]
    for copy in small[:3]:
        copy.start()
    copies[0][0].start()
    copies[1][0].start()
    copies[0][1].start()
    for c in range(2, chunks):
        copies[c][0].start()
        copies[c - 1][1].start()
    for copy in small[3:]:
        copy.start()
    copies[-1][1].start()
    clear.wait()
    small[1].wait()
    row = row_ref[...]
    owner = jnp.floor((row.astype(F32) + 0.5) * (1.0 / half)).astype(jnp.int32)
    opposite = jnp.bitwise_xor(color(owner), color(me_ref[0]))
    row_ref[...] = jnp.right_shift(owner, 1) * lanes + row - owner * half + opposite * half
    placed = pltpu.make_async_copy(row_ref, place_ref, place_sem)
    placed.start()

    entries = [(i, k) for k in range(cand_count) for i in range(query_count)]
    share = -(-len(entries) // chunks)

    def enter():
        for first in range(0, share, 12):
            batch = entries[first:min(first + 12, share)]
            names = [cand_ref[i, k] for i, k in batch]
            spots = [place_ref[name] for name in names]
            for (i, k), spot in zip(batch, spots):
                table[jnp.right_shift(spot, 7), jnp.bitwise_and(spot, 127)] = i
                spot_ref[i, k] = spot
        del entries[:share]

    small[0].wait()
    x = x_ref[...].reshape(query_count * token_count, width_in)
    total = x.astype(F32)
    inner = active = None
    for step in range(chunks + 2):
        if step < chunks:
            copies[step][0].wait()
        if step == 1:
            small[2].wait()
            placed.wait()
        if step == chunks:
            for copy in small[3:]:
                copy.wait()
        if step >= 2:
            copies[step - 2][1].wait()
        if step >= 1:
            enter()
        later = jnp.dot(x, w1_buf[step], preferred_element_type=F32) if step < chunks else None
        if step >= 2:
            total = total + jnp.dot(active, w2_buf[step - 2], preferred_element_type=F32)
        if 1 <= step <= chunks:
            active = (0.5 * inner * (1.0 + lax.erf(inner * (0.5 ** 0.5)))).astype(BF16)
        inner = later
        if step == chunks:
            fetch = pltpu.make_async_copy(table, table_v, table_sem)
            fetch.start()

    centered = total - jnp.mean(total, axis=-1, keepdims=True)
    variance = jnp.mean(jnp.square(centered), axis=-1, keepdims=True)
    layer_out = (centered * lax.rsqrt(variance + 1e-12) * gain_ref[...].reshape(1, width_in)).astype(BF16)
    embedded = jnp.dot(layer_out, embed_ref[...], preferred_element_type=F32)
    length = jnp.sum(jnp.square(embedded), axis=-1, keepdims=True)
    vectors = embedded * lax.rsqrt(length + 1e-06)
    token = lax.broadcasted_iota(jnp.int32, vectors.shape, 0)
    for i in range(query_count):
        padded = (token >= i * token_count + lens_ref[i]) & (token < (i + 1) * token_count)
        vectors = jnp.where(padded, 0.0, vectors)
    vectors = vectors.astype(BF16)
    tokens = query_count * token_count
    fetch.wait()
    wanted = table_v[...].astype(F32).astype(BF16)
    out_ref[pl.ds(0, tokens), :] = vectors
    out_ref[pl.ds(tokens, slots), :] = wanted


def encode(
    me,
    query_hidden,
    query_lengths,
    inner_weight,
    outer_weight,
    norm_gain,
    embed_weight,
    half,
    passage_row,
    candidates,
    slots,
    color,
):
    query_count, token_count, d = query_hidden.shape
    ff = inner_weight.shape[1]
    e = embed_weight.shape[1]
    slots = -(-slots // 16) * 16
    assert 2 * half <= e == 128
    chunks = 4
    width = ff // chunks
    tokens = query_count * token_count

    def kernel(*refs):
        encode_kernel(half, color, *refs)

    return pl.pallas_call(
        kernel,
        out_shape=(
            jax.ShapeDtypeStruct((tokens + slots, e), BF16),
            jax.ShapeDtypeStruct(candidates.shape, jnp.int32),
        ),
        in_specs=[SMEM] + [ANY] * 8,
        out_specs=(VMEM, SMEM),
        scratch_shapes=[
            pltpu.VMEM((chunks, d, width), BF16),
            pltpu.VMEM((chunks, width, d), BF16),
            pltpu.SMEM(query_lengths.shape, jnp.int32),
            pltpu.VMEM(passage_row.shape, jnp.int32),
            pltpu.SMEM(passage_row.shape, jnp.int32),
            pltpu.SMEM(candidates.shape, jnp.int32),
            pltpu.VMEM(query_hidden.shape, BF16),
            pltpu.VMEM(norm_gain.shape, F32),
            pltpu.VMEM(embed_weight.shape, BF16),
            pltpu.SMEM((slots, e), jnp.int32),
            pltpu.VMEM((slots, e), jnp.int32),
            pltpu.SemaphoreType.DMA((2, chunks)),
            pltpu.SemaphoreType.DMA((6,)),
            pltpu.SemaphoreType.DMA,
            pltpu.SemaphoreType.DMA,
        ],
        compiler_params=pltpu.CompilerParams(vmem_limit_bytes=60 * 2 ** 20),
        cost_estimate=pl.CostEstimate(
            flops=4 * tokens * d * ff, bytes_accessed=4 * d * ff, transcendentals=tokens * ff
        ),
        name="encode",
    )(
        me,
        query_lengths,
        passage_row,
        candidates,
        query_hidden,
        inner_weight,
        outer_weight,
        norm_gain,
        embed_weight,
    )


def mask_kernel(len0_ref, len1_ref, pass0_ref, pass1_ref, _, out0_ref, out1_ref):
    mask_into(out0_ref, pass0_ref, len0_ref, 0, pass0_ref.shape[0])
    mask_into(out1_ref, pass1_ref, len1_ref, 0, pass1_ref.shape[0])


def mask(lengths, passages, late):
    shape = passages[0].shape
    size = 2 * passages[0].size
    return pl.pallas_call(
        mask_kernel,
        out_shape=[jax.ShapeDtypeStruct(shape, BF16)] * 2,
        in_specs=[SMEM, SMEM, VMEM, VMEM, VMEM],
        out_specs=[VMEM, VMEM],
        compiler_params=pltpu.CompilerParams(vmem_limit_bytes=2 ** 22),
        cost_estimate=pl.CostEstimate(flops=8 * size, bytes_accessed=4 * size, transcendentals=0),
        name="mask",
    )(*lengths, *passages, late)


def score_kernel(slots, leader, token_count, me_ref, own_ref, other_ref, *refs):
    got_refs = refs[:slots]
    out_ref, best_ref, index_v, index, sem = refs[slots:]
    message, lanes = got_refs[0].shape
    half = own_ref.shape[0]
    rows = -(-slots // 16) * 16
    tokens = message - rows
    group = min(slots, 256 // token_count)
    unroll = half if slots == group else 8
    chip = jnp.right_shift(me_ref[0], 1)
    mine = lax.broadcasted_iota(jnp.int32, (rows, lanes), 0) == chip
    for s in range(slots):
        table = got_refs[s][pl.ds(tokens, rows), :].astype(F32)
        query = jnp.sum(jnp.where(mine, table, 0.0), axis=0, keepdims=True)
        index_v[s:s + 1, :] = query.astype(jnp.int32) * token_count
    copy = pltpu.make_async_copy(index_v, index, sem)
    copy.start()
    copy.wait()

    for first, pass_ref in ((half, other_ref), (0, own_ref)):

        def several(step, carry):
            for part in range(slots // group):
                rows = []
                for j in range(unroll):
                    p = step * unroll + j
                    picked = jnp.concatenate(
                        [
                            got_refs[s][pl.ds(pl.multiple_of(index[s, first + p], token_count), token_count), :]
                            for s in range(part * group, (part + 1) * group)
                        ],
                        axis=0,
                    )
                    similar = lax.dot_general(pass_ref[p], picked, NT, preferred_element_type=F32)
                    rows.append(jnp.max(similar, axis=0, keepdims=True))
                    if len(rows) == 8:
                        best_ref[
                            pl.ds(pl.multiple_of(first + step * unroll + j - 7, 8), 8),
                            pl.ds(part * group * token_count, group * token_count),
                        ] = jnp.concatenate(rows, axis=0)
                        rows = []
            return carry

        if unroll == half:
            several(0, 0)
        else:
            lax.fori_loop(0, half // unroll, several, 0)
    wide = best_ref.shape[1]
    source = lax.broadcasted_iota(jnp.int32, (slots, wide), 0)
    column = lax.broadcasted_iota(jnp.int32, (slots, wide), 1)
    start = source * token_count
    ones = jnp.where((column >= start) & (column < start + token_count), 1.0, 0.0).astype(BF16)
    total = sum(lax.dot_general(ones, part, NT, preferred_element_type=F32) for part in split3(best_ref[...]))
    out_ref[...] = jnp.zeros(out_ref.shape, F32)
    for s in range(slots):
        out_ref[pl.ds(jnp.bitwise_xor(chip, s ^ leader), 1), pl.ds(0, 2 * half)] = total[s:s + 1]


def score(me, got, own, other, leader, token_count):
    half, plen, e = own.shape
    passage_count = 2 * half
    slots = len(got)

    def kernel(*refs):
        score_kernel(slots, leader, token_count, *refs)

    return pl.pallas_call(
        kernel,
        out_shape=jax.ShapeDtypeStruct((slots, e), F32),
        in_specs=[SMEM, VMEM, VMEM] + [VMEM] * slots,
        out_specs=VMEM,
        scratch_shapes=[
            pltpu.VMEM((passage_count, slots * token_count), F32),
            pltpu.VMEM((slots, e), jnp.int32),
            pltpu.SMEM((slots, e), jnp.int32),
            pltpu.SemaphoreType.DMA,
        ],
        compiler_params=pltpu.CompilerParams(vmem_limit_bytes=12 * 2 ** 20),
        cost_estimate=pl.CostEstimate(
            flops=2 * passage_count * slots * token_count * plen * e,
            bytes_accessed=4 * own.size,
            transcendentals=0,
        ),
        name="score",
    )(me, own, other, *got)


def finish_kernel(leader, got_ref, spot_ref, scores_ref, best_ref):
    slots, lanes = got_ref.shape
    query_count, cand_count = scores_ref.shape
    parts = split3(got_ref[...])
    slot_iota = lax.broadcasted_iota(jnp.int32, (slots, cand_count), 0) * lanes
    lane_iota = lax.broadcasted_iota(jnp.int32, (lanes, cand_count), 0)
    row_iota = lax.broadcasted_iota(jnp.int32, (cand_count, cand_count), 0)
    col_iota = lax.broadcasted_iota(jnp.int32, (cand_count, cand_count), 1)
    place = lax.broadcasted_iota(jnp.int32, (cand_count, 128), 1)
    for i in range(query_count):
        spot = jnp.bitwise_xor(spot_ref[i:i + 1, :], leader * lanes)
        lane = jnp.bitwise_and(spot, lanes - 1)
        onehot = jnp.where(lane_iota == lane, 1.0, 0.0).astype(BF16)
        picked = sum(jnp.dot(part, onehot, preferred_element_type=F32) for part in parts)
        score_row = jnp.sum(jnp.where(slot_iota == spot - lane, picked, 0.0), axis=0, keepdims=True)
        scores_ref[i:i + 1, :] = score_row
        across = jnp.broadcast_to(score_row, (cand_count, cand_count))
        score_col = jnp.sum(jnp.where(row_iota == col_iota, across, 0.0), axis=1, keepdims=True)
        ahead = (across > score_col) | ((across == score_col) & (col_iota < row_iota))
        rank = jnp.sum(jnp.where(ahead, 1.0, 0.0), axis=1, keepdims=True).astype(jnp.int32)
        ordered = jnp.sum(jnp.where(rank == place, score_col, 0.0), axis=0, keepdims=True)
        best_ref[i:i + 1, :] = ordered[:, :TOPN]


def finish(got, spots, leader):
    def kernel(*refs):
        finish_kernel(leader, *refs)

    return pl.pallas_call(
        kernel,
        out_shape=(
            jax.ShapeDtypeStruct(spots.shape, F32),
            jax.ShapeDtypeStruct((spots.shape[0], TOPN), F32),
        ),
        in_specs=[VMEM, VMEM],
        out_specs=(VMEM, VMEM),
        compiler_params=pltpu.CompilerParams(vmem_limit_bytes=2 ** 21),
        name="finish",
    )(got, spots)


def swap(value, distance):
    size = lax.axis_size("shard")
    return lax.ppermute(value, "shard", [(i, i ^ distance) for i in range(size)])


def per_device(
    query_hidden,
    query_lengths,
    inner_weight,
    outer_weight,
    norm_gain,
    embed_weight,
    passage_vectors,
    passage_lengths,
    passage_row,
    candidates,
):
    size = lax.axis_size("shard")
    slots = size // 2
    inner = 1
    while 4 * inner * inner <= slots:
        inner *= 2
    shift = inner.bit_length()

    def color(index):
        return (index ^ (index >> 1) ^ (index >> shift)) & 1

    leader = slots - inner
    groups = [[2 * (p ^ leader) + (c ^ color(2 * (p ^ leader))) for p in range(slots)] for c in range(2)]

    def send(value, distance):
        return swap(value, 2 * distance + color(2 * distance))

    me = lax.axis_index("shard").astype(jnp.int32).reshape(1)
    across = swap(passage_lengths, 1)
    message, spots = encode(
        me,
        query_hidden,
        query_lengths,
        inner_weight,
        outer_weight,
        norm_gain,
        embed_weight,
        passage_vectors.shape[0],
        passage_row,
        candidates,
        slots,
        color,
    )
    message, across, raw = lax.optimization_barrier((message, across, passage_vectors))
    raw = swap(raw, 1)

    line = [message] + [send(message, d) for d in range(slots - inner, 0, -inner)][::-1]
    got = [line[s // inner] if s % inner == 0 else send(line[s // inner], s % inner) for s in range(slots)]
    own, other = mask((passage_lengths, across), (passage_vectors, raw), got[inner + 1])
    sums = score(me, got, own, other, leader, query_hidden.shape[1])
    back = lax.all_to_all(sums, "shard", split_axis=0, concat_axis=0, axis_index_groups=groups, tiled=True)
    return finish(back, spots, leader)


def solution(mesh):
    in_specs = (
        P(("groups", "shard"), None, None),
        P(("groups", "shard")),
        P(),
        P(),
        P(),
        P(),
        P(("groups", "shard"), None, None),
        P(("groups", "shard")),
        P("groups"),
        P(("groups", "shard"), None),
    )
    out_specs = (P(("groups", "shard"), None), P(("groups", "shard"), None))
    return jax.shard_map(
        per_device, mesh=mesh, in_specs=in_specs, out_specs=out_specs, check_vma=False
    )
```

```python
import jax
import jax.numpy as jnp
from jax import lax
from jax.experimental import pallas as pl
from jax.experimental.pallas import tpu as pltpu
from jax.sharding import PartitionSpec as P

TOPN = 10
F32 = jnp.float32
BF16 = jnp.bfloat16
NT = (((1,), (1,)), ((), ()))
VMEM = pl.BlockSpec(memory_space=pltpu.VMEM)
SMEM = pl.BlockSpec(memory_space=pltpu.SMEM)
ANY = pl.BlockSpec(memory_space=pl.ANY)


def split3(value):
    high = value.astype(BF16)
    rest = value - high.astype(F32)
    middle = rest.astype(BF16)
    low = (rest - middle.astype(F32)).astype(BF16)
    return high, middle, low


def mask_into(out_ref, pass_ref, len_ref, first, count):
    def mask(p, carry):
        block = pass_ref[p]
        keep = lax.broadcasted_iota(jnp.int32, block.shape, 0) < len_ref[p]
        block = block.astype(F32)
        out_ref[p] = jnp.where(keep, block, jnp.broadcast_to(block[0:1], block.shape)).astype(BF16)
        return carry

    if count <= 8:
        for p in range(first, first + count):
            mask(p, 0)
    else:
        lax.fori_loop(first, first + count, mask, 0, unroll=16)


def encode_kernel(
    half,
    color,
    me_ref,
    lens_hbm,
    row_hbm,
    cand_hbm,
    x_hbm,
    w1_ref,
    w2_ref,
    gain_hbm,
    embed_hbm,
    out_ref,
    spot_ref,
    w1_buf,
    w2_buf,
    lens_ref,
    row_ref,
    place_ref,
    cand_ref,
    x_ref,
    gain_ref,
    embed_ref,
    table,
    table_v,
    sems,
    small_sems,
    place_sem,
    table_sem,
):
    chunks, _, width = w1_buf.shape
    slots, lanes = table_v.shape
    query_count, token_count, width_in = x_ref.shape
    cand_count = cand_ref.shape[1]
    table_v[...] = jnp.zeros(table_v.shape, jnp.int32)
    clear = pltpu.make_async_copy(table_v, table, table_sem)
    clear.start()
    copies = []
    for c in range(chunks):
        first = pltpu.make_async_copy(w1_ref.at[:, pl.ds(c * width, width)], w1_buf.at[c], sems.at[0, c])
        second = pltpu.make_async_copy(w2_ref.at[pl.ds(c * width, width), :], w2_buf.at[c], sems.at[1, c])
        copies.append((first, second))
    small = [
        pltpu.make_async_copy(source, target, small_sems.at[n])
        for n, (source, target) in enumerate(
            (
                (x_hbm, x_ref),
                (row_hbm, row_ref),
                (cand_hbm, cand_ref),
                (lens_hbm, lens_ref),
                (gain_hbm, gain_ref),
                (embed_hbm, embed_ref),
            )
        )
    ]
    for copy in small[:3]:
        copy.start()
    copies[0][0].start()
    copies[1][0].start()
    copies[0][1].start()
    for c in range(2, chunks):
        copies[c][0].start()
        copies[c - 1][1].start()
    for copy in small[3:]:
        copy.start()
    copies[-1][1].start()
    clear.wait()
    small[1].wait()
    row = row_ref[...]
    owner = jnp.floor((row.astype(F32) + 0.5) * (1.0 / half)).astype(jnp.int32)
    opposite = jnp.bitwise_xor(color(owner), color(me_ref[0]))
    row_ref[...] = jnp.right_shift(owner, 1) * lanes + row - owner * half + opposite * half
    placed = pltpu.make_async_copy(row_ref, place_ref, place_sem)
    placed.start()

    entries = [(i, k) for k in range(cand_count) for i in range(query_count)]
    share = -(-len(entries) // chunks)

    def enter():
        for first in range(0, share, 12):
            batch = entries[first:min(first + 12, share)]
            names = [cand_ref[i, k] for i, k in batch]
            spots = [place_ref[name] for name in names]
            for (i, k), spot in zip(batch, spots):
                table[jnp.right_shift(spot, 7), jnp.bitwise_and(spot, 127)] = i
                spot_ref[i, k] = spot
        del entries[:share]

    small[0].wait()
    x = x_ref[...].reshape(query_count * token_count, width_in)
    total = x.astype(F32)
    inner = active = None
    for step in range(chunks + 2):
        if step < chunks:
            copies[step][0].wait()
        if step == 1:
            small[2].wait()
            placed.wait()
        if step == chunks:
            for copy in small[3:]:
                copy.wait()
        if step >= 2:
            copies[step - 2][1].wait()
        if step >= 1:
            enter()
        later = jnp.dot(x, w1_buf[step], preferred_element_type=F32) if step < chunks else None
        if step >= 2:
            total = total + jnp.dot(active, w2_buf[step - 2], preferred_element_type=F32)
        if 1 <= step <= chunks:
            active = (0.5 * inner * (1.0 + lax.erf(inner * (0.5 ** 0.5)))).astype(BF16)
        inner = later
        if step == chunks:
            fetch = pltpu.make_async_copy(table, table_v, table_sem)
            fetch.start()

    centered = total - jnp.mean(total, axis=-1, keepdims=True)
    variance = jnp.mean(jnp.square(centered), axis=-1, keepdims=True)
    layer_out = (centered * lax.rsqrt(variance + 1e-12) * gain_ref[...].reshape(1, width_in)).astype(BF16)
    embedded = jnp.dot(layer_out, embed_ref[...], preferred_element_type=F32)
    length = jnp.sum(jnp.square(embedded), axis=-1, keepdims=True)
    vectors = embedded * lax.rsqrt(length + 1e-06)
    token = lax.broadcasted_iota(jnp.int32, vectors.shape, 0)
    for i in range(query_count):
        padded = (token >= i * token_count + lens_ref[i]) & (token < (i + 1) * token_count)
        vectors = jnp.where(padded, 0.0, vectors)
    vectors = vectors.astype(BF16)
    tokens = query_count * token_count
    fetch.wait()
    wanted = table_v[...].astype(F32).astype(BF16)
    out_ref[pl.ds(0, tokens), :] = vectors
    out_ref[pl.ds(tokens, slots), :] = wanted


def encode(
    me,
    query_hidden,
    query_lengths,
    inner_weight,
    outer_weight,
    norm_gain,
    embed_weight,
    half,
    passage_row,
    candidates,
    slots,
    color,
):
    query_count, token_count, d = query_hidden.shape
    ff = inner_weight.shape[1]
    e = embed_weight.shape[1]
    slots = -(-slots // 16) * 16
    assert 2 * half <= e == 128
    chunks = 4
    width = ff // chunks
    tokens = query_count * token_count

    def kernel(*refs):
        encode_kernel(half, color, *refs)

    return pl.pallas_call(
        kernel,
        out_shape=(
            jax.ShapeDtypeStruct((tokens + slots, e), BF16),
            jax.ShapeDtypeStruct(candidates.shape, jnp.int32),
        ),
        in_specs=[SMEM] + [ANY] * 8,
        out_specs=(VMEM, SMEM),
        scratch_shapes=[
            pltpu.VMEM((chunks, d, width), BF16),
            pltpu.VMEM((chunks, width, d), BF16),
            pltpu.SMEM(query_lengths.shape, jnp.int32),
            pltpu.VMEM(passage_row.shape, jnp.int32),
            pltpu.SMEM(passage_row.shape, jnp.int32),
            pltpu.SMEM(candidates.shape, jnp.int32),
            pltpu.VMEM(query_hidden.shape, BF16),
            pltpu.VMEM(norm_gain.shape, F32),
            pltpu.VMEM(embed_weight.shape, BF16),
            pltpu.SMEM((slots, e), jnp.int32),
            pltpu.VMEM((slots, e), jnp.int32),
            pltpu.SemaphoreType.DMA((2, chunks)),
            pltpu.SemaphoreType.DMA((6,)),
            pltpu.SemaphoreType.DMA,
            pltpu.SemaphoreType.DMA,
        ],
        compiler_params=pltpu.CompilerParams(vmem_limit_bytes=60 * 2 ** 20),
        cost_estimate=pl.CostEstimate(
            flops=4 * tokens * d * ff, bytes_accessed=4 * d * ff, transcendentals=tokens * ff
        ),
        name="encode",
    )(
        me,
        query_lengths,
        passage_row,
        candidates,
        query_hidden,
        inner_weight,
        outer_weight,
        norm_gain,
        embed_weight,
    )


def mask_kernel(len0_ref, len1_ref, pass0_ref, pass1_ref, _, out0_ref, out1_ref):
    mask_into(out0_ref, pass0_ref, len0_ref, 0, pass0_ref.shape[0])
    mask_into(out1_ref, pass1_ref, len1_ref, 0, pass1_ref.shape[0])


def mask(lengths, passages, late):
    shape = passages[0].shape
    size = 2 * passages[0].size
    return pl.pallas_call(
        mask_kernel,
        out_shape=[jax.ShapeDtypeStruct(shape, BF16)] * 2,
        in_specs=[SMEM, SMEM, VMEM, VMEM, VMEM],
        out_specs=[VMEM, VMEM],
        compiler_params=pltpu.CompilerParams(vmem_limit_bytes=2 ** 22),
        cost_estimate=pl.CostEstimate(flops=8 * size, bytes_accessed=4 * size, transcendentals=0),
        name="mask",
    )(*lengths, *passages, late)


def score_kernel(slots, leader, token_count, me_ref, own_ref, other_ref, *refs):
    got_refs = refs[:slots]
    out_ref, best_ref, index_v, index, sem = refs[slots:]
    message, lanes = got_refs[0].shape
    half = own_ref.shape[0]
    rows = -(-slots // 16) * 16
    tokens = message - rows
    group = min(slots, 256 // token_count)
    unroll = half if slots == group else 8
    chip = jnp.right_shift(me_ref[0], 1)
    mine = lax.broadcasted_iota(jnp.int32, (rows, lanes), 0) == chip
    for s in range(slots):
        table = got_refs[s][pl.ds(tokens, rows), :].astype(F32)
        query = jnp.sum(jnp.where(mine, table, 0.0), axis=0, keepdims=True)
        index_v[s:s + 1, :] = query.astype(jnp.int32) * token_count
    copy = pltpu.make_async_copy(index_v, index, sem)
    copy.start()
    copy.wait()

    for first, pass_ref in ((half, other_ref), (0, own_ref)):

        def several(step, carry):
            for part in range(slots // group):
                rows = []
                for j in range(unroll):
                    p = step * unroll + j
                    picked = jnp.concatenate(
                        [
                            got_refs[s][pl.ds(pl.multiple_of(index[s, first + p], token_count), token_count), :]
                            for s in range(part * group, (part + 1) * group)
                        ],
                        axis=0,
                    )
                    similar = lax.dot_general(pass_ref[p], picked, NT, preferred_element_type=F32)
                    rows.append(jnp.max(similar, axis=0, keepdims=True))
                    if len(rows) == 8:
                        best_ref[
                            pl.ds(pl.multiple_of(first + step * unroll + j - 7, 8), 8),
                            pl.ds(part * group * token_count, group * token_count),
                        ] = jnp.concatenate(rows, axis=0)
                        rows = []
            return carry

        if unroll == half:
            several(0, 0)
        else:
            lax.fori_loop(0, half // unroll, several, 0)
    wide = best_ref.shape[1]
    source = lax.broadcasted_iota(jnp.int32, (slots, wide), 0)
    column = lax.broadcasted_iota(jnp.int32, (slots, wide), 1)
    start = source * token_count
    ones = jnp.where((column >= start) & (column < start + token_count), 1.0, 0.0).astype(BF16)
    total = sum(lax.dot_general(ones, part, NT, preferred_element_type=F32) for part in split3(best_ref[...]))
    out_ref[...] = jnp.zeros(out_ref.shape, F32)
    for s in range(slots):
        out_ref[pl.ds(jnp.bitwise_xor(chip, s ^ leader), 1), pl.ds(0, 2 * half)] = total[s:s + 1]


def score(me, got, own, other, leader, token_count):
    half, plen, e = own.shape
    passage_count = 2 * half
    slots = len(got)

    def kernel(*refs):
        score_kernel(slots, leader, token_count, *refs)

    return pl.pallas_call(
        kernel,
        out_shape=jax.ShapeDtypeStruct((slots, e), F32),
        in_specs=[SMEM, VMEM, VMEM] + [VMEM] * slots,
        out_specs=VMEM,
        scratch_shapes=[
            pltpu.VMEM((passage_count, slots * token_count), F32),
            pltpu.VMEM((slots, e), jnp.int32),
            pltpu.SMEM((slots, e), jnp.int32),
            pltpu.SemaphoreType.DMA,
        ],
        compiler_params=pltpu.CompilerParams(vmem_limit_bytes=12 * 2 ** 20),
        cost_estimate=pl.CostEstimate(
            flops=2 * passage_count * slots * token_count * plen * e,
            bytes_accessed=4 * own.size,
            transcendentals=0,
        ),
        name="score",
    )(me, own, other, *got)


def finish_kernel(leader, got_ref, spot_ref, scores_ref, best_ref):
    slots, lanes = got_ref.shape
    query_count, cand_count = scores_ref.shape
    parts = split3(got_ref[...])
    slot_iota = lax.broadcasted_iota(jnp.int32, (slots, cand_count), 0) * lanes
    lane_iota = lax.broadcasted_iota(jnp.int32, (lanes, cand_count), 0)
    row_iota = lax.broadcasted_iota(jnp.int32, (cand_count, cand_count), 0)
    col_iota = lax.broadcasted_iota(jnp.int32, (cand_count, cand_count), 1)
    place = lax.broadcasted_iota(jnp.int32, (cand_count, 128), 1)
    for i in range(query_count):
        spot = jnp.bitwise_xor(spot_ref[i:i + 1, :], leader * lanes)
        lane = jnp.bitwise_and(spot, lanes - 1)
        onehot = jnp.where(lane_iota == lane, 1.0, 0.0).astype(BF16)
        picked = sum(jnp.dot(part, onehot, preferred_element_type=F32) for part in parts)
        score_row = jnp.sum(jnp.where(slot_iota == spot - lane, picked, 0.0), axis=0, keepdims=True)
        scores_ref[i:i + 1, :] = score_row
        across = jnp.broadcast_to(score_row, (cand_count, cand_count))
        score_col = jnp.sum(jnp.where(row_iota == col_iota, across, 0.0), axis=1, keepdims=True)
        ahead = (across > score_col) | ((across == score_col) & (col_iota < row_iota))
        rank = jnp.sum(jnp.where(ahead, 1.0, 0.0), axis=1, keepdims=True).astype(jnp.int32)
        ordered = jnp.sum(jnp.where(rank == place, score_col, 0.0), axis=0, keepdims=True)
        best_ref[i:i + 1, :] = ordered[:, :TOPN]


def finish(got, spots, leader):
    def kernel(*refs):
        finish_kernel(leader, *refs)

    return pl.pallas_call(
        kernel,
        out_shape=(
            jax.ShapeDtypeStruct(spots.shape, F32),
            jax.ShapeDtypeStruct((spots.shape[0], TOPN), F32),
        ),
        in_specs=[VMEM, VMEM],
        out_specs=(VMEM, VMEM),
        compiler_params=pltpu.CompilerParams(vmem_limit_bytes=2 ** 21),
        name="finish",
    )(got, spots)


def swap(value, distance):
    size = lax.axis_size("shard")
    return lax.ppermute(value, "shard", [(i, i ^ distance) for i in range(size)])


def per_device(
    query_hidden,
    query_lengths,
    inner_weight,
    outer_weight,
    norm_gain,
    embed_weight,
    passage_vectors,
    passage_lengths,
    passage_row,
    candidates,
):
    size = lax.axis_size("shard")
    slots = size // 2
    inner = 1
    while 4 * inner * inner <= slots:
        inner *= 2
    shift = inner.bit_length()

    def color(index):
        return (index ^ (index >> 1) ^ (index >> shift)) & 1

    leader = inner * (slots // inner // 2)
    groups = [[2 * (p ^ leader) + (c ^ color(2 * (p ^ leader))) for p in range(slots)] for c in range(2)]

    def send(value, distance):
        return swap(value, 2 * distance + color(2 * distance))

    me = lax.axis_index("shard").astype(jnp.int32).reshape(1)
    across = swap(passage_lengths, 1)
    message, spots = encode(
        me,
        query_hidden,
        query_lengths,
        inner_weight,
        outer_weight,
        norm_gain,
        embed_weight,
        passage_vectors.shape[0],
        passage_row,
        candidates,
        slots,
        color,
    )
    message, across, raw = lax.optimization_barrier((message, across, passage_vectors))
    raw = swap(raw, 1)

    line = [message] + [send(message, d) for d in range(slots - inner, 0, -inner)][::-1]
    got = [line[s // inner] if s % inner == 0 else send(line[s // inner], s % inner) for s in range(slots)]
    own, other = mask((passage_lengths, across), (passage_vectors, raw), got[inner + 1])
    sums = score(me, got, own, other, leader, query_hidden.shape[1])
    back = lax.all_to_all(sums, "shard", split_axis=0, concat_axis=0, axis_index_groups=groups, tiled=True)
    return finish(back, spots, leader)


def solution(mesh):
    in_specs = (
        P(("groups", "shard"), None, None),
        P(("groups", "shard")),
        P(),
        P(),
        P(),
        P(),
        P(("groups", "shard"), None, None),
        P(("groups", "shard")),
        P("groups"),
        P(("groups", "shard"), None),
    )
    out_specs = (P(("groups", "shard"), None), P(("groups", "shard"), None))
    return jax.shard_map(
        per_device, mesh=mesh, in_specs=in_specs, out_specs=out_specs, check_vma=False
    )
```

```python
import jax
import jax.numpy as jnp
from jax import lax
from jax.experimental import pallas as pl
from jax.experimental.pallas import tpu as pltpu
from jax.sharding import PartitionSpec as P

TOPN = 10
F32 = jnp.float32
BF16 = jnp.bfloat16
NT = (((1,), (1,)), ((), ()))
VMEM = pl.BlockSpec(memory_space=pltpu.VMEM)
SMEM = pl.BlockSpec(memory_space=pltpu.SMEM)
ANY = pl.BlockSpec(memory_space=pl.ANY)


def split3(value):
    high = value.astype(BF16)
    rest = value - high.astype(F32)
    middle = rest.astype(BF16)
    low = (rest - middle.astype(F32)).astype(BF16)
    return high, middle, low


def mask_into(out_ref, pass_ref, len_ref, first, count):
    def mask(p, carry):
        block = pass_ref[p]
        keep = lax.broadcasted_iota(jnp.int32, block.shape, 0) < len_ref[p]
        block = block.astype(F32)
        out_ref[p] = jnp.where(keep, block, jnp.broadcast_to(block[0:1], block.shape)).astype(BF16)
        return carry

    if count <= 8:
        for p in range(first, first + count):
            mask(p, 0)
    else:
        lax.fori_loop(first, first + count, mask, 0, unroll=16)


def encode_kernel(
    half,
    color,
    me_ref,
    lens_hbm,
    row_hbm,
    cand_hbm,
    x_hbm,
    w1_ref,
    w2_ref,
    gain_hbm,
    embed_hbm,
    out_ref,
    spot_ref,
    w1_buf,
    w2_buf,
    lens_ref,
    row_ref,
    place_ref,
    cand_ref,
    x_ref,
    gain_ref,
    embed_ref,
    table,
    table_v,
    sems,
    small_sems,
    place_sem,
    table_sem,
):
    chunks, _, width = w1_buf.shape
    slots, lanes = table_v.shape
    query_count, token_count, width_in = x_ref.shape
    cand_count = cand_ref.shape[1]
    table_v[...] = jnp.zeros(table_v.shape, jnp.int32)
    clear = pltpu.make_async_copy(table_v, table, table_sem)
    clear.start()
    copies = []
    for c in range(chunks):
        first = pltpu.make_async_copy(w1_ref.at[:, pl.ds(c * width, width)], w1_buf.at[c], sems.at[0, c])
        second = pltpu.make_async_copy(w2_ref.at[pl.ds(c * width, width), :], w2_buf.at[c], sems.at[1, c])
        copies.append((first, second))
    small = [
        pltpu.make_async_copy(source, target, small_sems.at[n])
        for n, (source, target) in enumerate(
            (
                (x_hbm, x_ref),
                (row_hbm, row_ref),
                (cand_hbm, cand_ref),
                (lens_hbm, lens_ref),
                (gain_hbm, gain_ref),
                (embed_hbm, embed_ref),
            )
        )
    ]
    for copy in small[:3]:
        copy.start()
    copies[0][0].start()
    copies[1][0].start()
    copies[0][1].start()
    for c in range(2, chunks):
        copies[c][0].start()
        copies[c - 1][1].start()
    for copy in small[3:]:
        copy.start()
    copies[-1][1].start()
    clear.wait()
    small[1].wait()
    row = row_ref[...]
    owner = jnp.floor((row.astype(F32) + 0.5) * (1.0 / half)).astype(jnp.int32)
    opposite = jnp.bitwise_xor(color(owner), color(me_ref[0]))
    row_ref[...] = jnp.right_shift(owner, 1) * lanes + row - owner * half + opposite * half
    placed = pltpu.make_async_copy(row_ref, place_ref, place_sem)
    placed.start()

    entries = [(i, k) for k in range(cand_count) for i in range(query_count)]
    share = -(-len(entries) // chunks)

    def enter():
        for first in range(0, share, 12):
            batch = entries[first:min(first + 12, share)]
            names = [cand_ref[i, k] for i, k in batch]
            spots = [place_ref[name] for name in names]
            for (i, k), spot in zip(batch, spots):
                table[jnp.right_shift(spot, 7), jnp.bitwise_and(spot, 127)] = i
                spot_ref[i, k] = spot
        del entries[:share]

    small[0].wait()
    x = x_ref[...].reshape(query_count * token_count, width_in)
    total = x.astype(F32)
    inner = active = None
    for step in range(chunks + 2):
        if step < chunks:
            copies[step][0].wait()
        if step == 1:
            small[2].wait()
            placed.wait()
        if step == chunks:
            for copy in small[3:]:
                copy.wait()
        if step >= 2:
            copies[step - 2][1].wait()
        if step >= 1:
            enter()
        later = jnp.dot(x, w1_buf[step], preferred_element_type=F32) if step < chunks else None
        if step >= 2:
            total = total + jnp.dot(active, w2_buf[step - 2], preferred_element_type=F32)
        if 1 <= step <= chunks:
            active = (0.5 * inner * (1.0 + lax.erf(inner * (0.5 ** 0.5)))).astype(BF16)
        inner = later
        if step == chunks:
            fetch = pltpu.make_async_copy(table, table_v, table_sem)
            fetch.start()

    centered = total - jnp.mean(total, axis=-1, keepdims=True)
    variance = jnp.mean(jnp.square(centered), axis=-1, keepdims=True)
    layer_out = (centered * lax.rsqrt(variance + 1e-12) * gain_ref[...].reshape(1, width_in)).astype(BF16)
    embedded = jnp.dot(layer_out, embed_ref[...], preferred_element_type=F32)
    length = jnp.sum(jnp.square(embedded), axis=-1, keepdims=True)
    vectors = embedded * lax.rsqrt(length + 1e-06)
    token = lax.broadcasted_iota(jnp.int32, vectors.shape, 0)
    for i in range(query_count):
        padded = (token >= i * token_count + lens_ref[i]) & (token < (i + 1) * token_count)
        vectors = jnp.where(padded, 0.0, vectors)
    vectors = vectors.astype(BF16)
    tokens = query_count * token_count
    fetch.wait()
    wanted = table_v[...].astype(F32).astype(BF16)
    out_ref[pl.ds(0, tokens), :] = vectors
    out_ref[pl.ds(tokens, slots), :] = wanted


def encode(
    me,
    query_hidden,
    query_lengths,
    inner_weight,
    outer_weight,
    norm_gain,
    embed_weight,
    half,
    passage_row,
    candidates,
    slots,
    color,
):
    query_count, token_count, d = query_hidden.shape
    ff = inner_weight.shape[1]
    e = embed_weight.shape[1]
    slots = -(-slots // 16) * 16
    assert 2 * half <= e == 128
    chunks = 4
    width = ff // chunks
    tokens = query_count * token_count

    def kernel(*refs):
        encode_kernel(half, color, *refs)

    return pl.pallas_call(
        kernel,
        out_shape=(
            jax.ShapeDtypeStruct((tokens + slots, e), BF16),
            jax.ShapeDtypeStruct(candidates.shape, jnp.int32),
        ),
        in_specs=[SMEM] + [ANY] * 8,
        out_specs=(VMEM, SMEM),
        scratch_shapes=[
            pltpu.VMEM((chunks, d, width), BF16),
            pltpu.VMEM((chunks, width, d), BF16),
            pltpu.SMEM(query_lengths.shape, jnp.int32),
            pltpu.VMEM(passage_row.shape, jnp.int32),
            pltpu.SMEM(passage_row.shape, jnp.int32),
            pltpu.SMEM(candidates.shape, jnp.int32),
            pltpu.VMEM(query_hidden.shape, BF16),
            pltpu.VMEM(norm_gain.shape, F32),
            pltpu.VMEM(embed_weight.shape, BF16),
            pltpu.SMEM((slots, e), jnp.int32),
            pltpu.VMEM((slots, e), jnp.int32),
            pltpu.SemaphoreType.DMA((2, chunks)),
            pltpu.SemaphoreType.DMA((6,)),
            pltpu.SemaphoreType.DMA,
            pltpu.SemaphoreType.DMA,
        ],
        compiler_params=pltpu.CompilerParams(vmem_limit_bytes=60 * 2 ** 20),
        cost_estimate=pl.CostEstimate(
            flops=4 * tokens * d * ff, bytes_accessed=4 * d * ff, transcendentals=tokens * ff
        ),
        name="encode",
    )(
        me,
        query_lengths,
        passage_row,
        candidates,
        query_hidden,
        inner_weight,
        outer_weight,
        norm_gain,
        embed_weight,
    )


def mask_kernel(len0_ref, len1_ref, pass0_ref, pass1_ref, _, out0_ref, out1_ref):
    mask_into(out0_ref, pass0_ref, len0_ref, 0, pass0_ref.shape[0])
    mask_into(out1_ref, pass1_ref, len1_ref, 0, pass1_ref.shape[0])


def mask(lengths, passages, late):
    shape = passages[0].shape
    size = 2 * passages[0].size
    return pl.pallas_call(
        mask_kernel,
        out_shape=[jax.ShapeDtypeStruct(shape, BF16)] * 2,
        in_specs=[SMEM, SMEM, VMEM, VMEM, VMEM],
        out_specs=[VMEM, VMEM],
        compiler_params=pltpu.CompilerParams(vmem_limit_bytes=2 ** 22),
        cost_estimate=pl.CostEstimate(flops=8 * size, bytes_accessed=4 * size, transcendentals=0),
        name="mask",
    )(*lengths, *passages, late)


def score_kernel(slots, leader, token_count, me_ref, own_ref, other_ref, *refs):
    got_refs = refs[:slots]
    out_ref, best_ref, index_v, index, sem = refs[slots:]
    message, lanes = got_refs[0].shape
    half = own_ref.shape[0]
    rows = -(-slots // 16) * 16
    tokens = message - rows
    group = min(slots, 256 // token_count)
    unroll = half if slots == group else 8
    chip = jnp.right_shift(me_ref[0], 1)
    mine = lax.broadcasted_iota(jnp.int32, (rows, lanes), 0) == chip
    for s in range(slots):
        table = got_refs[s][pl.ds(tokens, rows), :].astype(F32)
        query = jnp.sum(jnp.where(mine, table, 0.0), axis=0, keepdims=True)
        index_v[s:s + 1, :] = query.astype(jnp.int32) * token_count
    copy = pltpu.make_async_copy(index_v, index, sem)
    copy.start()
    copy.wait()

    for first, pass_ref in ((half, other_ref), (0, own_ref)):

        def several(step, carry):
            for part in range(slots // group):
                rows = []
                for j in range(unroll):
                    p = step * unroll + j
                    picked = jnp.concatenate(
                        [
                            got_refs[s][pl.ds(pl.multiple_of(index[s, first + p], token_count), token_count), :]
                            for s in range(part * group, (part + 1) * group)
                        ],
                        axis=0,
                    )
                    similar = lax.dot_general(pass_ref[p], picked, NT, preferred_element_type=F32)
                    rows.append(jnp.max(similar, axis=0, keepdims=True))
                    if len(rows) == 8:
                        best_ref[
                            pl.ds(pl.multiple_of(first + step * unroll + j - 7, 8), 8),
                            pl.ds(part * group * token_count, group * token_count),
                        ] = jnp.concatenate(rows, axis=0)
                        rows = []
            return carry

        if unroll == half:
            several(0, 0)
        else:
            lax.fori_loop(0, half // unroll, several, 0)
    wide = best_ref.shape[1]
    source = lax.broadcasted_iota(jnp.int32, (slots, wide), 0)
    column = lax.broadcasted_iota(jnp.int32, (slots, wide), 1)
    start = source * token_count
    ones = jnp.where((column >= start) & (column < start + token_count), 1.0, 0.0).astype(BF16)
    total = sum(lax.dot_general(ones, part, NT, preferred_element_type=F32) for part in split3(best_ref[...]))
    out_ref[...] = jnp.zeros(out_ref.shape, F32)
    for s in range(slots):
        out_ref[pl.ds(jnp.bitwise_xor(chip, s ^ leader), 1), pl.ds(0, 2 * half)] = total[s:s + 1]


def score(me, got, own, other, leader, token_count):
    half, plen, e = own.shape
    passage_count = 2 * half
    slots = len(got)

    def kernel(*refs):
        score_kernel(slots, leader, token_count, *refs)

    return pl.pallas_call(
        kernel,
        out_shape=jax.ShapeDtypeStruct((slots, e), F32),
        in_specs=[SMEM, VMEM, VMEM] + [VMEM] * slots,
        out_specs=VMEM,
        scratch_shapes=[
            pltpu.VMEM((passage_count, slots * token_count), F32),
            pltpu.VMEM((slots, e), jnp.int32),
            pltpu.SMEM((slots, e), jnp.int32),
            pltpu.SemaphoreType.DMA,
        ],
        compiler_params=pltpu.CompilerParams(vmem_limit_bytes=12 * 2 ** 20),
        cost_estimate=pl.CostEstimate(
            flops=2 * passage_count * slots * token_count * plen * e,
            bytes_accessed=4 * own.size,
            transcendentals=0,
        ),
        name="score",
    )(me, own, other, *got)


def finish_kernel(leader, got_ref, spot_ref, scores_ref, best_ref):
    slots, lanes = got_ref.shape
    query_count, cand_count = scores_ref.shape
    parts = split3(got_ref[...])
    slot_iota = lax.broadcasted_iota(jnp.int32, (slots, cand_count), 0) * lanes
    lane_iota = lax.broadcasted_iota(jnp.int32, (lanes, cand_count), 0)
    row_iota = lax.broadcasted_iota(jnp.int32, (cand_count, cand_count), 0)
    col_iota = lax.broadcasted_iota(jnp.int32, (cand_count, cand_count), 1)
    place = lax.broadcasted_iota(jnp.int32, (cand_count, 128), 1)
    for i in range(query_count):
        spot = jnp.bitwise_xor(spot_ref[i:i + 1, :], leader * lanes)
        lane = jnp.bitwise_and(spot, lanes - 1)
        onehot = jnp.where(lane_iota == lane, 1.0, 0.0).astype(BF16)
        picked = sum(jnp.dot(part, onehot, preferred_element_type=F32) for part in parts)
        score_row = jnp.sum(jnp.where(slot_iota == spot - lane, picked, 0.0), axis=0, keepdims=True)
        scores_ref[i:i + 1, :] = score_row
        across = jnp.broadcast_to(score_row, (cand_count, cand_count))
        score_col = jnp.sum(jnp.where(row_iota == col_iota, across, 0.0), axis=1, keepdims=True)
        ahead = (across > score_col) | ((across == score_col) & (col_iota < row_iota))
        rank = jnp.sum(jnp.where(ahead, 1.0, 0.0), axis=1, keepdims=True).astype(jnp.int32)
        ordered = jnp.sum(jnp.where(rank == place, score_col, 0.0), axis=0, keepdims=True)
        best_ref[i:i + 1, :] = ordered[:, :TOPN]


def finish(got, spots, leader):
    def kernel(*refs):
        finish_kernel(leader, *refs)

    return pl.pallas_call(
        kernel,
        out_shape=(
            jax.ShapeDtypeStruct(spots.shape, F32),
            jax.ShapeDtypeStruct((spots.shape[0], TOPN), F32),
        ),
        in_specs=[VMEM, VMEM],
        out_specs=(VMEM, VMEM),
        compiler_params=pltpu.CompilerParams(vmem_limit_bytes=2 ** 21),
        name="finish",
    )(got, spots)


def swap(value, distance):
    size = lax.axis_size("shard")
    return lax.ppermute(value, "shard", [(i, i ^ distance) for i in range(size)])


def per_device(
    query_hidden,
    query_lengths,
    inner_weight,
    outer_weight,
    norm_gain,
    embed_weight,
    passage_vectors,
    passage_lengths,
    passage_row,
    candidates,
):
    size = lax.axis_size("shard")
    slots = size // 2
    inner = 1
    while 4 * inner * inner <= slots:
        inner *= 2
    shift = inner.bit_length()

    def color(index):
        return (index ^ (index >> 1) ^ (index >> shift)) & 1

    leader = slots - 1
    groups = [[2 * (p ^ leader) + (c ^ color(2 * (p ^ leader))) for p in range(slots)] for c in range(2)]

    def send(value, distance):
        return swap(value, 2 * distance + color(2 * distance))

    me = lax.axis_index("shard").astype(jnp.int32).reshape(1)
    across = swap(passage_lengths, 1)
    message, spots = encode(
        me,
        query_hidden,
        query_lengths,
        inner_weight,
        outer_weight,
        norm_gain,
        embed_weight,
        passage_vectors.shape[0],
        passage_row,
        candidates,
        slots,
        color,
    )
    message, across, raw = lax.optimization_barrier((message, across, passage_vectors))
    raw = swap(raw, 1)

    line = [message] + [send(message, d) for d in range(slots - inner, 0, -inner)][::-1]
    got = [line[s // inner] if s % inner == 0 else send(line[s // inner], s % inner) for s in range(slots)]
    own, other = mask((passage_lengths, across), (passage_vectors, raw), got[inner + 1])
    sums = score(me, got, own, other, leader, query_hidden.shape[1])
    back = lax.all_to_all(sums, "shard", split_axis=0, concat_axis=0, axis_index_groups=groups, tiled=True)
    return finish(back, spots, leader)


def solution(mesh):
    in_specs = (
        P(("groups", "shard"), None, None),
        P(("groups", "shard")),
        P(),
        P(),
        P(),
        P(),
        P(("groups", "shard"), None, None),
        P(("groups", "shard")),
        P("groups"),
        P(("groups", "shard"), None),
    )
    out_specs = (P(("groups", "shard"), None), P(("groups", "shard"), None))
    return jax.shard_map(
        per_device, mesh=mesh, in_specs=in_specs, out_specs=out_specs, check_vma=False
    )
```
